32 devices in a mesh: pipe: 2 (over core), batch: 4 (over y, x), space: 4 (over z).
Axes of the slice: x: 2, y: 2, z: 4, core: 2. Of those that a mesh axis runs over, the one named last changes fastest.
Arguments:
- images: bfloat16 [64, 8, 64, 256], P('batch', 'space'), may hold values from -6 to 6
- image_counts: int32 [4, 4], P('batch'), may hold values from 1 to 4, as said below
- labels: int32 [64, 40], P('batch'), may hold values 0 or 1
- fw_picks: int32 [20], replicated, may hold values from 0 to 39
- conv_down: bfloat16 [3, 3, 256, 512], replicated, may hold values from -0.125 to 0.125
- conv_mid: bfloat16 [3, 3, 512, 512], replicated, may hold values from -0.09375 to 0.09375
- shortcut: bfloat16 [256, 512], replicated, may hold values from -0.375 to 0.375
- gains_down: float32 [3, 512], replicated, may hold values from 0.5 to 1.5
- biases_down: float32 [3, 512], replicated, may hold values from -3 to 3
- conv_first: bfloat16 [3, 3, 512, 512], replicated, may hold values from -0.09375 to 0.09375
- conv_second: bfloat16 [3, 3, 512, 512], replicated, may hold values from -0.09375 to 0.09375
- gains_plain: float32 [2, 512], replicated, may hold values from 0.5 to 1.5
- biases_plain: float32 [2, 512], replicated, may hold values from -3 to 3
- head_weight: float32 [512, 40], replicated, may hold values from -0.25 to 0.25
- head_bias: float32 [40], replicated, may hold values from -3 to 3
Outputs:
- pooled: float32 [64, 512], P('batch', 'pipe')
- images_grad: float32 [64, 8, 64, 256], P('batch', 'space', None, 'pipe')
- conv_down_grad: float32 [3, 3, 256, 512], P(None, None, None, 'pipe')
- conv_mid_grad: float32 [3, 3, 512, 512], P(None, None, None, 'pipe')
- shortcut_grad: float32 [256, 512], P(None, 'pipe')
- gains_down_grad: float32 [3, 512], P(None, 'pipe')
- biases_down_grad: float32 [3, 512], P(None, 'pipe')
- conv_first_grad: float32 [3, 3, 512, 512], P(None, None, None, 'pipe')
- conv_second_grad: float32 [3, 3, 512, 512], P(None, None, None, 'pipe')
- gains_plain_grad: float32 [2, 512], P(None, 'pipe')
- biases_plain_grad: float32 [2, 512], P(None, 'pipe')
- head_weight_grad: float32 [512, 40], P('pipe')
- head_bias_grad: float32 [40], P('pipe')
The draws below stay inside these ranges and needn't reach their ends.
Inputs may be any that keep to these rules, and one draw needn't show every extreme that they name: Within each batch index and micro-batch the first image_counts slots are live; some batch index fills all 4 slots of some micro-batch.
All inputs are finite; a program needn't handle non-finite values. No bound on the sum of `labels` on one device may be relied on, other than what follows from the above.
Results may differ from the reference program's by a relative error of at most 0.013.
Values may be sent and summed in bfloat16 or wider, within the bound.
No kernel may reach another device: no remote copies, remote signals or barrier semaphores. Data moves between devices by JAX's collectives and lax.ppermute only.
A program may use at most 448 MiB of HBM per device.

```python
import jax
import jax.numpy as jnp
from jax import lax

IN_CHANNELS = 256
CHANNELS = 512
TASKS = 40
IMG_DEV = 4
MICRO = 4
ROWS_DEV = 1
WIDTH_OUT = 32
FW_STEPS = 20
IMAGES = 64
HEIGHT = 8
WIDTH = 64
N_BATCH = 4
N_SPACE = 4


def draw_image_counts(key, part):
    key = jax.random.fold_in(key, 11)
    key_counts, key_chosen = jax.random.split(key)
    counts = jax.random.randint(key_counts, (N_BATCH * MICRO,), 1, IMG_DEV + 1)
    chosen = jax.random.randint(key_chosen, (), 0, N_BATCH * MICRO)
    flattened = jnp.where(jnp.arange(N_BATCH * MICRO) == chosen, IMG_DEV, counts)
    return flattened.reshape(N_BATCH, MICRO).astype(jnp.int32)


def set_ends(drawn, own_key, low, largest):
    shape = drawn.shape
    index_at = [jax.random.randint(jax.random.fold_in(own_key, axis), (), 0, shape[axis]) for axis in range(len(shape))]
    drawn = drawn.at[tuple(index_at)].set(low)
    longest = shape.index(max(shape))
    index_at[longest] = (index_at[longest] + 1) % shape[longest]
    return drawn.at[tuple(index_at)].set(largest)


def block_scale(key, shape, cuts, least, high):
    loudness, own = 1.0, jax.random.fold_in(key, 6)
    for position, blocks in cuts:
        steps = jnp.exp(jax.random.uniform(jax.random.fold_in(own, position), (blocks,), jnp.float32, least / len(cuts), high / len(cuts)))
        loudness = loudness * jnp.repeat(steps, shape[position] // blocks).reshape([-1 if axis == position else 1 for axis in range(len(shape))])
    return loudness


def normal_values(stream_key, shape, deviation, reach, cuts=(), held_as=jnp.bfloat16):
    values = deviation * jax.random.normal(stream_key, shape, jnp.float32)
    if cuts:
        values = values * block_scale(stream_key, shape, cuts, -0.22, 0.18)
    return jnp.clip(values, -reach, reach).astype(held_as)


def setup_inputs(seed: int = 0) -> dict:
    arg_keys = jax.random.split(jax.random.key(seed), 16)
    images = normal_values(arg_keys[0], (IMAGES, HEIGHT, WIDTH, IN_CHANNELS), 1.0, 6.0, ((0, 4), (1, 4)))
    image_counts = draw_image_counts(jax.random.fold_in(arg_keys[15], 71), 0)
    labels = set_ends((jax.random.randint(arg_keys[2], (IMAGES, TASKS), 0, 2) < 1).astype(jnp.int32), jax.random.fold_in(arg_keys[2], 1), 0, 1)
    fw_picks = set_ends(jax.random.randint(arg_keys[3], (FW_STEPS,), 0, TASKS), jax.random.fold_in(arg_keys[3], 1), 0, TASKS - 1).astype(jnp.int32)
    conv_down = normal_values(arg_keys[4], (3, 3, IN_CHANNELS, CHANNELS), (9 * IN_CHANNELS) ** -0.5, 0.125)
    conv_mid = normal_values(arg_keys[5], (3, 3, CHANNELS, CHANNELS), (9 * CHANNELS) ** -0.5, 0.09375)
    shortcut = normal_values(arg_keys[6], (IN_CHANNELS, CHANNELS), IN_CHANNELS ** -0.5, 0.375)
    gains_down = jnp.clip(1.0 + 0.1 * jax.random.normal(arg_keys[7], (3, CHANNELS), jnp.float32), 0.5, 1.5)
    biases_down = normal_values(arg_keys[8], (3, CHANNELS), 0.5, 3.0, (), jnp.float32)
    conv_first = normal_values(arg_keys[9], (3, 3, CHANNELS, CHANNELS), (9 * CHANNELS) ** -0.5, 0.09375)
    conv_second = normal_values(arg_keys[10], (3, 3, CHANNELS, CHANNELS), (9 * CHANNELS) ** -0.5, 0.09375)
    gains_plain = jnp.clip(1.0 + 0.1 * jax.random.normal(arg_keys[11], (2, CHANNELS), jnp.float32), 0.5, 1.5)
    biases_plain = normal_values(arg_keys[12], (2, CHANNELS), 0.5, 3.0, (), jnp.float32)
    head_weight = normal_values(arg_keys[13], (CHANNELS, TASKS), CHANNELS ** -0.5, 0.25, (), jnp.float32)
    head_bias = normal_values(arg_keys[14], (TASKS,), 0.5, 3.0, (), jnp.float32)
    return {"images": images, "image_counts": image_counts, "labels": labels, "fw_picks": fw_picks, "conv_down": conv_down, "conv_mid": conv_mid, "shortcut": shortcut, "gains_down": gains_down, "biases_down": biases_down, "conv_first": conv_first, "conv_second": conv_second, "gains_plain": gains_plain, "biases_plain": biases_plain, "head_weight": head_weight, "head_bias": head_bias}


EPSILON = 1e-05
NUMBERS = ('NHWC', 'HWIO', 'NHWC')
HIGHEST = lax.Precision.HIGHEST

@jax.custom_vjp
def low(v):
    return lax.optimization_barrier(v.astype(jnp.bfloat16)).astype(jnp.float32)

@jax.custom_vjp
def low_back(v):
    return v

def low_keep(v):
    return (low(v), None)

def low_pass(kept, grad):
    return (grad,)

def back_keep(v):
    return (v, None)

def back_low(kept, grad):
    return (low(grad),)
low.defvjp(low_keep, low_pass)
low_back.defvjp(back_keep, back_low)

def conv_same(inputs, kernel, stride):
    return lax.conv_general_dilated(inputs, kernel, (stride, stride), ((1, 1), (1, 1)), dimension_numbers=NUMBERS, precision=HIGHEST)

def batch_norm(conv_out, gain, bias, living):
    weight = living[:, None, None, None]
    counted = jnp.sum(living) * conv_out.shape[1] * conv_out.shape[2]
    average = lax.optimization_barrier(jnp.sum(conv_out * weight, axis=(0, 1, 2))) / counted
    centered = conv_out - average
    variance = lax.optimization_barrier(jnp.sum(centered * centered * weight, axis=(0, 1, 2))) / counted
    return centered * lax.rsqrt(variance + EPSILON) * gain + bias

def frank_wolfe(gram, picks):
    tasks = gram.shape[0]
    labels_index = jnp.arange(tasks, dtype=jnp.int32)

    def advance(step_index, weights):
        chosen = picks[step_index]
        pulled = jnp.dot(gram, weights, precision=HIGHEST)
        energy = jnp.dot(weights, pulled, precision=HIGHEST)
        onehot = (labels_index == chosen).astype(jnp.float32)
        toward = jnp.sum(pulled * onehot)
        corner = jnp.sum(jnp.diagonal(gram) * onehot)
        denom = jnp.maximum(energy - 2.0 * toward + corner, 0.05 * corner)
        ratio = jnp.clip((energy - toward) / denom, 0.0, 1.0)
        return (1.0 - ratio) * weights + ratio * onehot
    return lax.fori_loop(0, picks.shape[0], advance, jnp.full((tasks,), 1.0 / tasks, jnp.float32))

def down_block(images_mb, living, conv_down, conv_mid, shortcut, gains_down, biases_down):
    down_conv = low_back(conv_same(images_mb, conv_down, 2))
    down_act = low(jax.nn.silu(batch_norm(down_conv, gains_down[0], biases_down[0], living)))
    mid_conv = low_back(conv_same(down_act, conv_mid, 1))
    short_conv = low_back(jnp.einsum('nhwi,io->nhwo', images_mb[:, ::2, ::2], shortcut, precision=HIGHEST))
    joined = batch_norm(mid_conv, gains_down[1], biases_down[1], living) + batch_norm(short_conv, gains_down[2], biases_down[2], living)
    return low_back(low(jax.nn.silu(joined)))

def plain_block(entry, living, conv_first, conv_second, gains_plain, biases_plain):
    first_conv = low_back(conv_same(entry, conv_first, 1))
    plain_act = low(jax.nn.silu(batch_norm(first_conv, gains_plain[0], biases_plain[0], living)))
    second_conv = low_back(conv_same(plain_act, conv_second, 1))
    return jax.nn.silu(batch_norm(second_conv, gains_plain[1], biases_plain[1], living) + entry)

def reference(images, image_counts, labels, fw_picks, conv_down, conv_mid, shortcut, gains_down, biases_down, conv_first, conv_second, gains_plain, biases_plain, head_weight, head_bias):
    slots = jnp.arange(IMG_DEV, dtype=jnp.int32)
    living_all = (slots[None, None, :] < image_counts[:, :, None]).astype(jnp.float32)
    image_mask = living_all.reshape(IMAGES)
    targets = labels.astype(jnp.float32)

    def forward(images_f, down_w, mid_w, short_w, gains_d, biases_d, first_w, second_w, gains_p, biases_p, head_w, head_b):
        shaped = images_f.reshape(N_BATCH, MICRO, IMG_DEV, HEIGHT, WIDTH, IN_CHANNELS)
        pooled_list = []
        for moment in range(MICRO):
            images_mb = shaped[:, moment].reshape(N_BATCH * IMG_DEV, HEIGHT, WIDTH, IN_CHANNELS)
            living = living_all[:, moment].reshape(N_BATCH * IMG_DEV)
            entry = down_block(images_mb, living, down_w, mid_w, short_w, gains_d, biases_d)
            output = plain_block(entry, living, first_w, second_w, gains_p, biases_p)
            pooled_list.append(lax.optimization_barrier(jnp.mean(output, axis=(1, 2))).reshape(N_BATCH, 1, IMG_DEV, CHANNELS))
        pooled = jnp.concatenate(pooled_list, axis=1).reshape(IMAGES, CHANNELS)
        logits = jnp.dot(pooled, head_w, precision=HIGHEST) + head_b
        errors = image_mask[:, None] * (jax.nn.sigmoid(logits) - targets)
        gram = jnp.dot(errors.T, errors, precision=HIGHEST) * jnp.dot(head_w.T, head_w, precision=HIGHEST)
        alpha = frank_wolfe(gram, fw_picks)
        return (pooled, logits, alpha)
    params = (images.astype(jnp.float32), conv_down.astype(jnp.float32), conv_mid.astype(jnp.float32), shortcut.astype(jnp.float32), gains_down, biases_down, conv_first.astype(jnp.float32), conv_second.astype(jnp.float32), gains_plain, biases_plain, head_weight, head_bias)
    (pooled, logits, alpha), pull = jax.vjp(forward, *params)

    def task_losses(values):
        return lax.optimization_barrier(jnp.sum(image_mask[:, None] * (jax.nn.softplus(values) - targets * values), axis=0))
    losses, loss_pull = jax.vjp(task_losses, logits)
    scale = float(ROWS_DEV * N_SPACE * WIDTH_OUT * TASKS)
    grad_logits = loss_pull(scale * alpha)[0]
    grads = pull((jnp.zeros_like(pooled), grad_logits, jnp.zeros_like(alpha)))
    return (pooled, grads[0], grads[1], grads[2], grads[3], grads[4], grads[5], grads[6], grads[7], grads[8], grads[9], grads[10], grads[11])
```

```python
import jax
import jax.numpy as jnp
from jax import lax
from jax.experimental import pallas as pl
from jax.experimental.pallas import tpu as pltpu
from jax.sharding import PartitionSpec as P

EPSILON = 1e-05
NUMBERS = ("NHWC", "HWIO", "NHWC")
HIGHEST = lax.Precision.HIGHEST
F32 = jnp.float32
BF16 = jnp.bfloat16


def silu_slope(values):
    sigmoid = jax.nn.sigmoid(values)
    return sigmoid * (1.0 + values * (1.0 - sigmoid))


def frank_wolfe_kernel(picks_ref, gram_ref, alpha_ref):
    tasks = gram_ref.shape[0]
    lanes = lax.broadcasted_iota(jnp.int32, (1, tasks), 1)
    gram = gram_ref[...]
    alpha = jnp.full((1, tasks), 1.0 / tasks, F32)
    pulled = jnp.sum(gram, axis=0, keepdims=True) * (1.0 / tasks)
    energy = jnp.sum(pulled * alpha, axis=1, keepdims=True)

    def advance(step, carry):
        alpha, pulled, energy = carry
        chosen = picks_ref[step]
        row = gram_ref[pl.ds(chosen, 1), :]
        onehot = (lanes == chosen).astype(F32)
        toward = jnp.sum(pulled * onehot, axis=1, keepdims=True)
        corner = jnp.sum(row * onehot, axis=1, keepdims=True)
        denom = jnp.maximum(energy - 2.0 * toward + corner, 0.05 * corner)
        ratio = jnp.clip((energy - toward) / denom, 0.0, 1.0)
        rest = 1.0 - ratio
        alpha = rest * alpha + ratio * onehot
        pulled = rest * pulled + ratio * row
        energy = rest * rest * energy + 2.0 * rest * ratio * toward + ratio * ratio * corner
        return alpha, pulled, energy

    alpha, _, _ = lax.fori_loop(0, picks_ref.shape[0], advance, (alpha, pulled, energy))
    alpha_ref[...] = alpha


def frank_wolfe(gram, picks):
    tasks = gram.shape[0]
    return pl.pallas_call(
        frank_wolfe_kernel,
        out_shape=jax.ShapeDtypeStruct((1, tasks), F32),
        in_specs=[
            pl.BlockSpec(memory_space=pltpu.SMEM),
            pl.BlockSpec(memory_space=pltpu.VMEM),
        ],
        out_specs=pl.BlockSpec(memory_space=pltpu.VMEM),
    )(picks, gram)


class Layout:
    def __init__(self, micros):
        self.micros = micros
        self.spaces = lax.axis_size("space")
        self.groups = self.spaces // micros
        self.inner = [
            [group * micros + zone for zone in range(micros)] for group in range(self.groups)
        ]
        self.outer = [
            [group * micros + zone for group in range(self.groups)] for zone in range(micros)
        ]
        self.zone = lax.axis_index("space") % micros

    def group_sum(self, tree):
        if self.groups == 1:
            return tree
        return lax.psum(tree, "space", axis_index_groups=self.outer)

    def row_from(self, block, step):
        span = step * self.micros
        route = [
            (i, i + span) for i in range(self.spaces) if 0 <= i + span < self.spaces
        ]
        if not route:
            return jnp.zeros_like(block)
        return lax.ppermute(block, "space", route)

    def rims(self, tensor):
        above = self.row_from(tensor[:, -1:], 1)
        below = self.row_from(tensor[:, :1], -1)
        grown = jnp.concatenate([above, tensor, below], axis=1)
        return jnp.pad(grown, ((0, 0), (0, 0), (1, 1), (0, 0)))


def conv_valid(extended, kernel, stride):
    return lax.conv_general_dilated(
        extended,
        kernel,
        (stride, stride),
        "VALID",
        dimension_numbers=NUMBERS,
        preferred_element_type=F32,
    )


def flipped(kernel):
    return jnp.swapaxes(kernel[::-1, ::-1], 2, 3)


def kernel_grad(extended, grad_low, stride):
    rows, cols = grad_low.shape[1], grad_low.shape[2]
    taps = []
    for row_tap in range(3):
        for col_tap in range(3):
            window = extended[
                :,
                row_tap : row_tap + stride * (rows - 1) + 1 : stride,
                col_tap : col_tap + stride * (cols - 1) + 1 : stride,
            ]
            taps.append(jnp.einsum("nhwi,nhwo->io", window, grad_low, preferred_element_type=F32))
    return jnp.stack(taps)


def norm_forward(layout, conv_out, weight, counted):
    total = layout.group_sum(jnp.sum(conv_out * weight, axis=(0, 1, 2)))
    centered = conv_out - total / counted
    spread = layout.group_sum(jnp.sum(centered * centered * weight, axis=(0, 1, 2)))
    inverse = lax.rsqrt(spread / counted + EPSILON)
    return centered * inverse, inverse


def norm_back(layout, upstream, normed, inverse, gain, weight, counted):
    grad_sum = jnp.sum(upstream * weight, axis=(0, 1, 2))
    cross_sum = jnp.sum(upstream * normed * weight, axis=(0, 1, 2))
    grad_total, cross_total = layout.group_sum((grad_sum, cross_sum))
    correction = weight * (grad_total / counted + normed * (cross_total / counted))
    low = (gain * inverse * (upstream - correction)).astype(BF16)
    return low, cross_sum, grad_sum


def per_device(
    images,
    image_counts,
    labels,
    fw_picks,
    conv_down,
    conv_mid,
    shortcut,
    gains_down,
    biases_down,
    conv_first,
    conv_second,
    gains_plain,
    biases_plain,
    head_weight,
    head_bias,
):
    layout = Layout(image_counts.shape[1])
    micros, zone = layout.micros, layout.zone
    batches, pipes = lax.axis_size("batch"), lax.axis_size("pipe")
    batch = lax.axis_index("batch")
    pipe = lax.axis_index("pipe")
    per_micro = images.shape[0] // micros
    count = per_micro * batches
    entering, channels = conv_down.shape[2], conv_mid.shape[3]
    tasks = head_weight.shape[1]
    half = channels // pipes
    own = pipe * half

    def own_out(kernel, axis):
        size = kernel.shape[axis] // pipes
        return lax.dynamic_slice_in_dim(kernel, pipe * size, size, axis)

    def whole(tensor, axis=3):
        return lax.all_gather(tensor, "pipe", axis=axis, tiled=True)

    def share(tensor):
        size = tensor.shape[3] // batches
        return lax.dynamic_slice_in_dim(tensor, batch * size, size, 3)

    mine = lax.all_to_all(
        images, "space", 0, 1, axis_index_groups=layout.inner, tiled=True
    )
    mine = lax.all_gather(mine, "batch", axis=0, tiled=True)
    counts = lax.all_gather(image_counts, "batch", axis=0, tiled=True)
    counts = lax.dynamic_slice_in_dim(counts, zone, 1, 1)[:, 0]
    marks = lax.dynamic_slice_in_dim(labels, zone * per_micro, per_micro, 0)
    targets = lax.all_gather(marks, "batch", axis=0, tiled=True).astype(F32)
    slots = jnp.arange(per_micro, dtype=jnp.int32)
    living = (slots[None, :] < counts[:, None]).astype(F32).reshape(count)
    weight = living[:, None, None, None]
    out_rows, out_cols = mine.shape[1] // 2, mine.shape[2] // 2
    image_pixels = out_rows * layout.groups * out_cols
    counted = jnp.sum(living) * image_pixels
    scale = float(image_pixels * tasks)

    gain_d, bias_d = own_out(gains_down, 1), own_out(biases_down, 1)
    gain_p, bias_p = own_out(gains_plain, 1), own_out(biases_plain, 1)

    above = layout.row_from(mine[:, -1:], 1)
    down_ext = jnp.pad(
        jnp.concatenate([above, mine], axis=1), ((0, 0), (0, 0), (1, 0), (0, 0))
    )
    down_out = conv_valid(down_ext, own_out(conv_down, 3), 2)
    down_norm, down_inv = norm_forward(layout, down_out, weight, counted)
    down_pre = down_norm * gain_d[0] + bias_d[0]
    mid_ext = layout.rims(whole(jax.nn.silu(down_pre).astype(BF16)))
    mid_out = conv_valid(mid_ext, own_out(conv_mid, 3), 1)
    short_in = mine[:, ::2, ::2]
    short_out = jnp.einsum(
        "nhwi,io->nhwo", short_in, own_out(shortcut, 1), preferred_element_type=F32
    )
    mid_norm, mid_inv = norm_forward(layout, mid_out, weight, counted)
    short_norm, short_inv = norm_forward(layout, short_out, weight, counted)
    section_pre = mid_norm * gain_d[1] + bias_d[1] + short_norm * gain_d[2] + bias_d[2]
    section = jax.nn.silu(section_pre).astype(BF16)
    first_ext = layout.rims(whole(section))
    first_out = conv_valid(first_ext, own_out(conv_first, 3), 1)
    first_norm, first_inv = norm_forward(layout, first_out, weight, counted)
    first_pre = first_norm * gain_p[0] + bias_p[0]
    second_ext = layout.rims(whole(jax.nn.silu(first_pre).astype(BF16)))
    second_out = conv_valid(second_ext, own_out(conv_second, 3), 1)
    second_norm, second_inv = norm_forward(layout, second_out, weight, counted)
    block_pre = second_norm * gain_p[1] + bias_p[1] + section.astype(F32)
    pooled = layout.group_sum(jnp.sum(jax.nn.silu(block_pre), axis=(1, 2))) / image_pixels

    pooled_all = whole(pooled, 1)
    logits = jnp.dot(pooled_all, head_weight, precision=HIGHEST) + head_bias
    errors = living[:, None] * (jax.nn.sigmoid(logits) - targets)
    cross = jnp.einsum("nt,ns->ts", errors, errors, precision=HIGHEST)
    cross = lax.psum(cross, "space", axis_index_groups=layout.inner)
    gram = cross * jnp.dot(head_weight.T, head_weight, precision=HIGHEST)
    alpha = frank_wolfe(gram, fw_picks)
    grad_logits = scale * alpha * errors
    head_w = jnp.einsum("nc,nt->ct", pooled, grad_logits, precision=HIGHEST)
    head_b = jnp.sum(grad_logits, axis=0)
    head_own = own_out(head_weight, 0)
    grad_pool = jnp.einsum("nt,ct->nc", grad_logits, head_own, precision=HIGHEST) / image_pixels

    grad_block = grad_pool[:, None, None, :] * silu_slope(block_pre)
    second_low, second_cross, second_sum = norm_back(
        layout, grad_block, second_norm, second_inv, gain_p[1], weight, counted
    )
    second_kernel = kernel_grad(share(second_ext), second_low, 1)
    act_grad = conv_valid(layout.rims(whole(second_low)), flipped(own_out(conv_second, 2)), 1)
    first_low, first_cross, first_sum = norm_back(
        layout, act_grad * silu_slope(first_pre), first_norm, first_inv, gain_p[0], weight, counted
    )
    first_kernel = kernel_grad(share(first_ext), first_low, 1)
    entry_grad = conv_valid(layout.rims(whole(first_low)), flipped(own_out(conv_first, 2)), 1)
    entry_grad = (entry_grad + grad_block).astype(BF16).astype(F32)
    grad_section = entry_grad * silu_slope(section_pre)
    mid_low, mid_cross, mid_sum = norm_back(
        layout, grad_section, mid_norm, mid_inv, gain_d[1], weight, counted
    )
    short_low, short_cross, short_sum = norm_back(
        layout, grad_section, short_norm, short_inv, gain_d[2], weight, counted
    )
    mid_kernel = kernel_grad(share(mid_ext), mid_low, 1)
    short_kernel = jnp.einsum(
        "nhwi,nhwo->io", share(short_in), short_low, preferred_element_type=F32
    )
    act_grad = conv_valid(layout.rims(whole(mid_low)), flipped(own_out(conv_mid, 2)), 1)
    down_low, down_cross, down_sum = norm_back(
        layout, act_grad * silu_slope(down_pre), down_norm, down_inv, gain_d[0], weight, counted
    )
    down_kernel = kernel_grad(share(down_ext), down_low, 2)

    kept = lax.dynamic_slice_in_dim(whole(down_low), batch * per_micro, per_micro, 0)
    below = layout.row_from(kept[:, :1], -1)
    spread = lax.conv_general_dilated(
        jnp.concatenate([kept, below], axis=1),
        flipped(own_out(conv_down, 2)),
        (1, 1),
        ((2, 2), (2, 2)),
        lhs_dilation=(2, 2),
        dimension_numbers=NUMBERS,
        preferred_element_type=F32,
    )[:, 1 : 2 * out_rows + 1, 1:]
    short_kept = lax.dynamic_slice_in_dim(whole(short_low), batch * per_micro, per_micro, 0)
    spread = spread.at[:, ::2, ::2].add(
        jnp.einsum(
            "nhwo,io->nhwi", short_kept, own_out(shortcut, 0), preferred_element_type=F32
        )
    )
    images_grad = lax.all_to_all(
        spread.astype(BF16), "space", 1, 0, axis_index_groups=layout.inner, tiled=True
    ).astype(F32)

    def total(kernel, axis):
        summed = lax.psum(kernel.astype(BF16), "space")
        return lax.all_gather(summed, "batch", axis=axis, tiled=True).astype(F32)

    pooled_out = lax.dynamic_slice_in_dim(pooled, batch * per_micro, per_micro, 0)
    pooled_out = lax.all_gather(
        pooled_out, "space", axis_index_groups=layout.inner, axis=0, tiled=True
    )
    head_w, head_b = lax.psum((head_w, head_b), "space", axis_index_groups=layout.inner)
    gains_d, sums_d, gains_p, sums_p = lax.psum(
        (
            jnp.stack([down_cross, mid_cross, short_cross]),
            jnp.stack([down_sum, mid_sum, short_sum]),
            jnp.stack([first_cross, second_cross]),
            jnp.stack([first_sum, second_sum]),
        ),
        "space",
    )
    return (
        pooled_out,
        images_grad,
        total(down_kernel, 1).reshape(3, 3, entering, half),
        total(mid_kernel, 1).reshape(3, 3, channels, half),
        total(short_kernel, 0),
        gains_d,
        sums_d,
        total(first_kernel, 1).reshape(3, 3, channels, half),
        total(second_kernel, 1).reshape(3, 3, channels, half),
        gains_p,
        sums_p,
        head_w,
        own_out(head_b, 0),
    )


def solution(mesh):
    placed = (
        P("batch", "space", None, None),
        P("batch", None),
        P("batch", None),
    ) + (P(),) * 12
    return jax.shard_map(
        per_device,
        mesh=mesh,
        in_specs=placed,
        out_specs=(
            P("batch", "pipe"),
            P("batch", "space", None, "pipe"),
            P(None, None, None, "pipe"),
            P(None, None, None, "pipe"),
            P(None, "pipe"),
            P(None, "pipe"),
            P(None, "pipe"),
            P(None, None, None, "pipe"),
            P(None, None, None, "pipe"),
            P(None, "pipe"),
            P(None, "pipe"),
            P("pipe", None),
            P("pipe"),
        ),
        check_vma=False,
    )
```

```python
import jax
import jax.numpy as jnp
from jax import lax
from jax.experimental import pallas as pl
from jax.experimental.pallas import tpu as pltpu
from jax.sharding import PartitionSpec as P

EPSILON = 1e-05
NUMBERS = ("NHWC", "HWIO", "NHWC")
HIGHEST = lax.Precision.HIGHEST
F32 = jnp.float32
BF16 = jnp.bfloat16


def silu_slope(values):
    sigmoid = jax.nn.sigmoid(values)
    return sigmoid * (1.0 + values * (1.0 - sigmoid))


def frank_wolfe_kernel(picks_ref, gram_ref, alpha_ref):
    tasks = gram_ref.shape[0]
    lanes = lax.broadcasted_iota(jnp.int32, (1, tasks), 1)
    gram = gram_ref[...]
    alpha = jnp.full((1, tasks), 1.0 / tasks, F32)
    pulled = jnp.sum(gram, axis=0, keepdims=True) * (1.0 / tasks)
    energy = jnp.sum(pulled * alpha, axis=1, keepdims=True)

    def advance(step, carry):
        alpha, pulled, energy = carry
        chosen = picks_ref[step]
        row = gram_ref[pl.ds(chosen, 1), :]
        onehot = (lanes == chosen).astype(F32)
        toward = jnp.sum(pulled * onehot, axis=1, keepdims=True)
        corner = jnp.sum(row * onehot, axis=1, keepdims=True)
        denom = jnp.maximum(energy - 2.0 * toward + corner, 0.05 * corner)
        ratio = jnp.clip((energy - toward) / denom, 0.0, 1.0)
        rest = 1.0 - ratio
        alpha = rest * alpha + ratio * onehot
        pulled = rest * pulled + ratio * row
        energy = rest * rest * energy + 2.0 * rest * ratio * toward + ratio * ratio * corner
        return alpha, pulled, energy

    alpha, _, _ = lax.fori_loop(0, picks_ref.shape[0], advance, (alpha, pulled, energy))
    alpha_ref[...] = alpha


def frank_wolfe(gram, picks):
    tasks = gram.shape[0]
    return pl.pallas_call(
        frank_wolfe_kernel,
        out_shape=jax.ShapeDtypeStruct((1, tasks), F32),
        in_specs=[
            pl.BlockSpec(memory_space=pltpu.SMEM),
            pl.BlockSpec(memory_space=pltpu.VMEM),
        ],
        out_specs=pl.BlockSpec(memory_space=pltpu.VMEM),
    )(picks, gram)


class Layout:
    def __init__(self, micros):
        self.micros = micros
        self.spaces = lax.axis_size("space")
        self.groups = self.spaces // micros
        self.inner = [
            [group * micros + zone for zone in range(micros)] for group in range(self.groups)
        ]
        self.outer = [
            [group * micros + zone for group in range(self.groups)] for zone in range(micros)
        ]
        self.zone = lax.axis_index("space") % micros

    def group_sum(self, tree):
        if self.groups == 1:
            return tree
        return lax.psum(tree, "space", axis_index_groups=self.outer)

    def row_from(self, block, step):
        span = step * self.micros
        route = [
            (i, i + span) for i in range(self.spaces) if 0 <= i + span < self.spaces
        ]
        if not route:
            return jnp.zeros_like(block)
        return lax.ppermute(block, "space", route)

    def rims(self, tensor):
        above = self.row_from(tensor[:, -1:], 1)
        below = self.row_from(tensor[:, :1], -1)
        grown = jnp.concatenate([above, tensor, below], axis=1)
        return jnp.pad(grown, ((0, 0), (0, 0), (1, 1), (0, 0)))


def conv_valid(extended, kernel, stride):
    return lax.conv_general_dilated(
        extended,
        kernel,
        (stride, stride),
        "VALID",
        dimension_numbers=NUMBERS,
        preferred_element_type=F32,
    )


def flipped(kernel):
    return jnp.swapaxes(kernel[::-1, ::-1], 2, 3)


def kernel_grad(extended, grad_low, stride):
    rows, cols = grad_low.shape[1], grad_low.shape[2]
    taps = []
    for row_tap in range(3):
        for col_tap in range(3):
            window = extended[
                :,
                row_tap : row_tap + stride * (rows - 1) + 1 : stride,
                col_tap : col_tap + stride * (cols - 1) + 1 : stride,
            ]
            taps.append(jnp.einsum("nhwi,nhwo->io", window, grad_low, preferred_element_type=F32))
    return jnp.stack(taps)


def norm_forward(layout, conv_out, weight, counted):
    total = layout.group_sum(jnp.sum(conv_out * weight, axis=(0, 1, 2)))
    centered = conv_out - total / counted
    spread = layout.group_sum(jnp.sum(centered * centered * weight, axis=(0, 1, 2)))
    inverse = lax.rsqrt(spread / counted + EPSILON)
    return centered * inverse, inverse


def norm_back(layout, upstream, normed, inverse, gain, weight, counted):
    grad_sum = jnp.sum(upstream * weight, axis=(0, 1, 2))
    cross_sum = jnp.sum(upstream * normed * weight, axis=(0, 1, 2))
    grad_total, cross_total = layout.group_sum((grad_sum, cross_sum))
    correction = weight * (grad_total / counted + normed * (cross_total / counted))
    low = (gain * inverse * (upstream - correction)).astype(BF16)
    return low, cross_sum, grad_sum


MESH_LIMIT = 56 * 2**20
VM = pl.BlockSpec(memory_space=pltpu.VMEM)
SM = pl.BlockSpec(memory_space=pltpu.SMEM)
NT = (((1,), (1,)), ((), ()))
TN = (((0,), (0,)), ((), ()))
OWN_PX, OTHER_PX, ALL_PX = 8, 9, 10


def call(kernel, outs, operands, scratch=(), flops=0, name=None):
    nbytes = sum(x.size * x.dtype.itemsize for x in operands)
    return pl.pallas_call(
        kernel,
        out_shape=tuple(jax.ShapeDtypeStruct(shape, dtype) for shape, dtype in outs),
        in_specs=[SM if x.ndim == 1 else VM for x in operands],
        out_specs=tuple(VM for _ in outs),
        scratch_shapes=list(scratch),
        compiler_params=pltpu.CompilerParams(vmem_limit_bytes=MESH_LIMIT),
        cost_estimate=pl.CostEstimate(
            flops=int(flops), bytes_accessed=int(nbytes), transcendentals=0
        ),
        name=name,
    )(*operands)


def fold(rows):
    return rows[0:8] + rows[8:16] + rows[16:24] + rows[24:32]


def total_row(part):
    return jnp.sum(part, axis=0, keepdims=True)


def band(row):
    return slice(row * 32, row * 32 + 32)


def put_band(x_ref, image, row, value):
    zero = jnp.zeros_like(value)
    x_ref[image, band(row), 512:1024] = value
    if row < 3:
        x_ref[image, band(row + 1), 0:512] = value
    else:
        x_ref[image, band(0), 0:512] = zero
    if row > 0:
        x_ref[image, band(row - 1), 1024:1536] = value
    else:
        x_ref[image, band(3), 1024:1536] = zero


def columns_joined(left, middle, right):
    count = middle.shape[0]
    column = lax.broadcasted_iota(jnp.int32, (count, 1), 0) % 32
    joined = middle
    if left is not None:
        joined = joined + jnp.where(column == 0, 0.0, pltpu.roll(left, 1, 0))
    if right is not None:
        joined = joined + jnp.where(column == 31, 0.0, pltpu.roll(right, count - 1, 0))
    return joined


def conv_core(x_ref, w_ref, out_ref, back):
    for part in range(2):
        images = slice(4 * part, 4 * part + 4)

        def tap(col):
            value = None
            for row in range(3):
                lhs = x_ref[images, :, row * 512 : (row + 1) * 512].reshape(512, 512)
                if back:
                    term = lax.dot_general(
                        lhs, w_ref[2 - row, 2 - col], NT, preferred_element_type=F32
                    )
                else:
                    term = jnp.dot(lhs, w_ref[row, col], preferred_element_type=F32)
                value = term if value is None else value + term
            return value

        out = columns_joined(tap(0), tap(1), tap(2))
        out_ref[images] = out.reshape(4, 128, 512)


def stats_of(facts_ref, out_ref, stat_ref, row):
    def add(image, part):
        for r in range(4):
            part = part + fold(out_ref[image, band(r), :]) * facts_ref[image]
        return part

    first = total_row(lax.fori_loop(0, 8, add, jnp.zeros((8, 512), F32)))
    mean = first / jnp.maximum(facts_ref[OWN_PX], 1.0)

    def deviate(image, part):
        for r in range(4):
            away = out_ref[image, band(r), :] - mean
            part = part + fold(away * away) * facts_ref[image]
        return part

    second = total_row(lax.fori_loop(0, 8, deviate, jnp.zeros((8, 512), F32)))
    stat_ref[row : row + 1, :] = first
    stat_ref[row + 1 : row + 2, :] = second


def norm_of(facts_ref, own_ref, other_ref, row):
    own_px, other_px, all_px = facts_ref[OWN_PX], facts_ref[OTHER_PX], facts_ref[ALL_PX]
    own, other = own_ref[row : row + 1, :], other_ref[row : row + 1, :]
    mean = (own + other) / all_px
    apart = own / jnp.maximum(own_px, 1.0) - other / jnp.maximum(other_px, 1.0)
    spread = own_ref[row + 1 : row + 2, :] + other_ref[row + 1 : row + 2, :]
    variance = (spread + apart * apart * (own_px * other_px / all_px)) / all_px
    return mean, lax.rsqrt(variance + EPSILON)


def sigmoid(values):
    return 1.0 / (1.0 + jnp.exp(-values))


def slope_of(values):
    gate = sigmoid(values)
    return gate * (1.0 + values * (1.0 - gate))


def pieces_kernel(where_ref, images_ref, o0, o1, o2, o3, wide):
    pipe, zone = where_ref[0], where_ref[2]
    for rel, out in enumerate((o0, o1, o2, o3)):
        first = (zone ^ rel) * 4 + pipe * 2
        for i in range(2):
            for row in range(2):
                for part in range(2):
                    lanes = slice(part * 128, part * 128 + 128)
                    wide[...] = images_ref[first + i, row, :, lanes].astype(F32)
                    for par in range(2):
                        value = wide[pl.ds(par, 32, stride=2), :]
                        start = par * 256 + part * 128
                        out[i, row, :, start : start + 128] = value.astype(BF16)


def down_kernel(facts_ref, where_ref, *refs):
    pieces, (w_ref, s_ref, img_ref, out_ref, short_ref, stat_ref, x_ref) = refs[:16], refs[16:]
    batch, zone = where_ref[1], where_ref[2]
    for kb in range(4):
        for kz in range(4):
            piece = pieces[kb * 4 + kz]
            row = zone ^ kz
            here = pl.ds(pl.multiple_of(row * 32, 32), 32)
            after = pl.ds(pl.multiple_of(((row + 1) % 4) * 32, 32), 32)
            for i in range(2):
                image = (batch ^ kb) * 2 + i
                odd = piece[i, 1]
                img_ref[image, here, 0:512] = piece[i, 0]
                img_ref[image, here, 512:1024] = odd
                x_ref[image, after, :] = jnp.where(row == 3, jnp.zeros_like(odd), odd)
    for part in range(2):
        images = slice(4 * part, 4 * part + 4)
        blocks = (
            x_ref[images].reshape(512, 512),
            img_ref[images, :, 0:512].reshape(512, 512),
            img_ref[images, :, 512:1024].reshape(512, 512),
        )
        left, middle = None, None
        for row in range(3):
            a = jnp.dot(blocks[row][:, 256:], w_ref[row, 0], preferred_element_type=F32)
            m = jnp.dot(
                blocks[row], w_ref[row, 1:3].reshape(512, 512), preferred_element_type=F32
            )
            left = a if left is None else left + a
            middle = m if middle is None else middle + m
        out_ref[images] = columns_joined(left, middle, None).reshape(4, 128, 512)
        short = jnp.dot(blocks[1][:, :256], s_ref[...], preferred_element_type=F32)
        short_ref[images] = short.reshape(4, 128, 512)
    stats_of(facts_ref, out_ref, stat_ref, 0)
    stats_of(facts_ref, short_ref, stat_ref, 2)
    stat_ref[4:8, :] = jnp.zeros((4, 512), F32)


def layer_kernel(which, facts_ref, in_ref, own_ref, other_ref, g_ref, b_ref, w_ref,
                 act_ref, out_ref, stat_ref, norm_ref, x_ref):
    mean, inverse = norm_of(facts_ref, own_ref, other_ref, 0)
    gain, bias = g_ref[which : which + 1, :], b_ref[which : which + 1, :]

    def activate(image, carry):
        for r in range(4):
            pre = (in_ref[image, band(r), :] - mean) * inverse * gain + bias
            act = (pre * sigmoid(pre)).astype(BF16)
            act_ref[image, band(r), :] = act
            put_band(x_ref, image, r, act)
        return carry

    lax.fori_loop(0, 8, activate, 0)
    norm_ref[0:1, :] = mean
    norm_ref[1:2, :] = inverse
    norm_ref[2:8, :] = jnp.zeros((6, 512), F32)
    conv_core(x_ref, w_ref, out_ref, False)
    stats_of(facts_ref, out_ref, stat_ref, 0)
    stat_ref[2:8, :] = jnp.zeros((6, 512), F32)


def join_kernel(facts_ref, mid_ref, short_ref, own_m, other_m, own_d, other_d, g_ref, b_ref,
                w_ref, act_ref, out_ref, stat_ref, norm_ref, x_ref):
    mean_m, inv_m = norm_of(facts_ref, own_m, other_m, 0)
    mean_s, inv_s = norm_of(facts_ref, own_d, other_d, 2)
    gain_m, gain_s = g_ref[1:2, :], g_ref[2:3, :]
    bias_m, bias_s = b_ref[1:2, :], b_ref[2:3, :]

    def activate(image, carry):
        for r in range(4):
            pre = (mid_ref[image, band(r), :] - mean_m) * inv_m * gain_m + bias_m
            pre = pre + (short_ref[image, band(r), :] - mean_s) * inv_s * gain_s + bias_s
            act = (pre * sigmoid(pre)).astype(BF16)
            act_ref[image, band(r), :] = act
            put_band(x_ref, image, r, act)
        return carry

    lax.fori_loop(0, 8, activate, 0)
    norm_ref[0:1, :] = mean_m
    norm_ref[1:2, :] = inv_m
    norm_ref[2:3, :] = mean_s
    norm_ref[3:4, :] = inv_s
    norm_ref[4:8, :] = jnp.zeros((4, 512), F32)
    conv_core(x_ref, w_ref, out_ref, False)
    stats_of(facts_ref, out_ref, stat_ref, 0)
    stat_ref[2:8, :] = jnp.zeros((6, 512), F32)


def block_kernel(facts_ref, in_ref, section_ref, own_ref, other_ref, g_ref, b_ref,
                 pack_ref, norm_ref):
    mean, inverse = norm_of(facts_ref, own_ref, other_ref, 0)
    gain, bias = g_ref[1:2, :], b_ref[1:2, :]
    norm_ref[0:1, :] = mean
    norm_ref[1:2, :] = inverse
    norm_ref[2:8, :] = jnp.zeros((6, 512), F32)

    def gather(image, carry):
        pooled = jnp.zeros((8, 512), F32)
        slopes, crossed = pooled, pooled
        for r in range(4):
            normed = (in_ref[image, band(r), :] - mean) * inverse
            pre = normed * gain + bias + section_ref[image, band(r), :].astype(F32)
            gate = sigmoid(pre)
            slope = gate * (1.0 + pre * (1.0 - gate))
            pooled = pooled + fold(pre * gate)
            slopes = slopes + fold(slope)
            crossed = crossed + fold(slope * normed)
        pack_ref[pl.ds(image, 1), :] = total_row(pooled) / 128.0
        pack_ref[pl.ds(image + 8, 1), :] = total_row(slopes)
        pack_ref[pl.ds(image + 16, 1), :] = total_row(crossed)
        return carry

    lax.fori_loop(0, 8, gather, 0)


def logits_kernel(where_ref, own_ref, other_ref, living_ref, labels_ref, hw_ref, hb_ref,
                  all_ref, errors_ref, cross_ref):
    pipe = where_ref[0]
    for block in range(3):
        rows = slice(block * 8, block * 8 + 8)
        all_ref[block, pl.ds(pl.multiple_of(pipe * 8, 8), 8), :] = own_ref[rows, :]
        all_ref[block, pl.ds(pl.multiple_of((1 - pipe) * 8, 8), 8), :] = other_ref[rows, :]
    logits = (
        jnp.dot(all_ref[0], hw_ref[...], precision=HIGHEST, preferred_element_type=F32)
        + hb_ref[...]
    )
    errors = living_ref[...] * (sigmoid(logits) - labels_ref[...])
    errors_ref[...] = errors
    cross_ref[...] = lax.dot_general(
        errors, errors, TN, precision=HIGHEST, preferred_element_type=F32
    )


def head_kernel(picks_ref, where_ref, facts_ref, c0, c1, c2, c3, heads_ref, hw_ref, errors_ref,
                all_ref, in_ref, section_ref, norm_ref, g_ref, b_ref,
                low_ref, pool_ref, small_ref, alpha_ref, gram_ref):
    tasks = gram_ref.shape[0]
    pipe = where_ref[0]
    gram_ref[...] = ((c0[...] + c1[...]) + (c2[...] + c3[...])) * heads_ref[...]
    frank_wolfe_kernel(picks_ref, gram_ref, alpha_ref)
    grad_logits = (128.0 * tasks) * alpha_ref[...] * errors_ref[...]
    pooled, slopes, crossed = all_ref[0], all_ref[1], all_ref[2]
    grad_pool = (
        lax.dot_general(
            grad_logits, hw_ref[...], NT, precision=HIGHEST, preferred_element_type=F32
        )
        / 128.0
    )
    grad_sum = total_row(grad_pool * slopes)
    cross_sum = total_row(grad_pool * crossed)
    small_ref[0:tasks, :] = lax.dot_general(
        grad_logits, pooled, TN, precision=HIGHEST, preferred_element_type=F32
    )
    small_ref[tasks : tasks + 1, :] = grad_sum
    small_ref[tasks + 1 : tasks + 2, :] = cross_sum
    small_ref[tasks + 2 :, :] = jnp.zeros((small_ref.shape[0] - tasks - 2, 512), F32)
    for start in (0, 256):
        small_ref[tasks + 2 : tasks + 3, start : start + tasks] = total_row(grad_logits)
    pool_ref[...] = jnp.where(pipe == 0, grad_pool[0:8], grad_pool[8:16])

    mean, inverse = norm_ref[0:1, :], norm_ref[1:2, :]
    gain, bias = g_ref[1:2, :], b_ref[1:2, :]
    all_px = facts_ref[ALL_PX]
    front = gain * inverse
    mean_grad, mean_cross = grad_sum / all_px, cross_sum / all_px

    def back(image, carry):
        up = pool_ref[pl.ds(image, 1), :]
        for r in range(4):
            normed = (in_ref[image, band(r), :] - mean) * inverse
            pre = normed * gain + bias + section_ref[image, band(r), :].astype(F32)
            grad = up * slope_of(pre)
            fix = facts_ref[image] * (mean_grad + normed * mean_cross)
            low_ref[image, band(r), :] = (front * (grad - fix)).astype(BF16)
        return carry

    lax.fori_loop(0, 8, back, 0)


def back_norm(facts_ref, in_ref, up_ref, norm_ref, own_ref, other_ref, gain, rows, sinks):
    mean, inverse = norm_ref[rows : rows + 1, :], norm_ref[rows + 1 : rows + 2, :]
    all_px = facts_ref[ALL_PX]
    front = gain * inverse
    cross_row = 1 + rows // 2
    mean_grad = (own_ref[0:1, :] + other_ref[0:1, :]) / all_px
    mean_cross = (
        own_ref[cross_row : cross_row + 1, :] + other_ref[cross_row : cross_row + 1, :]
    ) / all_px

    def back(image, carry):
        for r in range(4):
            normed = (in_ref[image, band(r), :] - mean) * inverse
            fix = facts_ref[image] * (mean_grad + normed * mean_cross)
            sinks(image, r, (front * (up_ref[image, band(r), :] - fix)).astype(BF16))
        return carry

    lax.fori_loop(0, 8, back, 0)


def second_back_kernel(facts_ref, low_ref, in_ref, norm_ref, g_ref, b_ref, w_ref,
                       up_ref, sum_ref, x_ref, conv_ref):
    def fill(image, carry):
        for r in range(4):
            put_band(x_ref, image, r, low_ref[image, band(r), :])
        return carry

    lax.fori_loop(0, 8, fill, 0)
    conv_core(x_ref, w_ref, conv_ref, True)
    slope_sums(facts_ref, in_ref, norm_ref, g_ref[0:1, :], b_ref[0:1, :], conv_ref, up_ref, sum_ref)


def slope_sums(facts_ref, in_ref, norm_ref, gain, bias, conv_ref, up_ref, sum_ref):
    mean, inverse = norm_ref[0:1, :], norm_ref[1:2, :]

    def slope(image, carry):
        grads, crosses = carry
        for r in range(4):
            normed = (in_ref[image, band(r), :] - mean) * inverse
            up = conv_ref[image, band(r), :] * slope_of(normed * gain + bias)
            up_ref[image, band(r), :] = up
            living = facts_ref[image]
            grads = grads + fold(up) * living
            crosses = crosses + fold(up * normed) * living
        return grads, crosses

    zero = jnp.zeros((8, 512), F32)
    grads, crosses = lax.fori_loop(0, 8, slope, (zero, zero))
    sum_ref[0:1, :] = total_row(grads)
    sum_ref[1:2, :] = total_row(crosses)
    sum_ref[2:8, :] = jnp.zeros((6, 512), F32)


def first_back_kernel(facts_ref, up_in, in_ref, norm_ref, own_ref, other_ref, gp_ref, w_ref,
                      second_ref, norm2_ref, section_ref, bp_ref, pool_ref,
                      mid_ref, short_ref, normd_ref, gd_ref, bd_ref,
                      low_ref, up_ref, sum_ref, x_ref, conv_ref):
    def keep(image, r, low):
        low_ref[image, band(r), :] = low
        put_band(x_ref, image, r, low)

    back_norm(facts_ref, in_ref, up_in, norm_ref, own_ref, other_ref, gp_ref[0:1, :], 0, keep)
    conv_core(x_ref, w_ref, conv_ref, True)
    mean2, inv2 = norm2_ref[0:1, :], norm2_ref[1:2, :]
    gain2, bias2 = gp_ref[1:2, :], bp_ref[1:2, :]
    mean_m, inv_m = normd_ref[0:1, :], normd_ref[1:2, :]
    mean_s, inv_s = normd_ref[2:3, :], normd_ref[3:4, :]
    gain_m, gain_s = gd_ref[1:2, :], gd_ref[2:3, :]
    bias_m, bias_s = bd_ref[1:2, :], bd_ref[2:3, :]

    def join(image, carry):
        grads, cross_m, cross_s = carry
        pool = pool_ref[pl.ds(image, 1), :]
        for r in range(4):
            pre2 = (second_ref[image, band(r), :] - mean2) * inv2 * gain2 + bias2
            pre2 = pre2 + section_ref[image, band(r), :].astype(F32)
            entry = conv_ref[image, band(r), :] + pool * slope_of(pre2)
            entry = entry.astype(BF16).astype(F32)
            norm_m = (mid_ref[image, band(r), :] - mean_m) * inv_m
            norm_s = (short_ref[image, band(r), :] - mean_s) * inv_s
            pre = norm_m * gain_m + bias_m + norm_s * gain_s + bias_s
            up = entry * slope_of(pre)
            up_ref[image, band(r), :] = up
            living = facts_ref[image]
            grads = grads + fold(up) * living
            cross_m = cross_m + fold(up * norm_m) * living
            cross_s = cross_s + fold(up * norm_s) * living
        return grads, cross_m, cross_s

    zero = jnp.zeros((8, 512), F32)
    grads, cross_m, cross_s = lax.fori_loop(0, 8, join, (zero, zero, zero))
    sum_ref[0:1, :] = total_row(grads)
    sum_ref[1:2, :] = total_row(cross_m)
    sum_ref[2:3, :] = total_row(cross_s)
    sum_ref[3:8, :] = jnp.zeros((5, 512), F32)


def mid_back_kernel(facts_ref, up_in, mid_ref, short_ref, normd_ref, own_ref, other_ref, gd_ref,
                    w_ref, in_ref, norm1_ref, bd_ref,
                    low_ref, low_s_ref, up_ref, sum_ref, x_ref, conv_ref):
    def keep(image, r, low):
        low_ref[image, band(r), :] = low
        put_band(x_ref, image, r, low)

    def keep_short(image, r, low):
        low_s_ref[image, band(r), :] = low

    back_norm(facts_ref, mid_ref, up_in, normd_ref, own_ref, other_ref, gd_ref[1:2, :], 0, keep)
    back_norm(
        facts_ref, short_ref, up_in, normd_ref, own_ref, other_ref, gd_ref[2:3, :], 2, keep_short
    )
    conv_core(x_ref, w_ref, conv_ref, True)
    slope_sums(
        facts_ref, in_ref, norm1_ref, gd_ref[0:1, :], bd_ref[0:1, :], conv_ref, up_ref, sum_ref
    )


def down_back_kernel(where_ref, facts_ref, up_in, in_ref, norm1_ref, own_ref, other_ref, gd_ref,
                     low_s_ref, w_ref, s_ref, low_ref, own_out, other_out):
    pipe, batch, zone = where_ref[0], where_ref[1], where_ref[2]

    def keep(image, r, low):
        low_ref[image, band(r), :] = low

    back_norm(facts_ref, in_ref, up_in, norm1_ref, own_ref, other_ref, gd_ref[0:1, :], 0, keep)
    mine = pl.ds(batch * 2, 2)
    here = low_ref[mine]
    below = jnp.concatenate([here[:, 32:], jnp.zeros((2, 32, 512), BF16)], axis=1)
    here, below = here.reshape(256, 512), below.reshape(256, 512)
    short = low_s_ref[mine].reshape(256, 512)

    def back(lhs, row, col):
        return lax.dot_general(lhs, w_ref[row, col], NT, preferred_element_type=F32)

    even_even = back(here, 1, 1) + lax.dot_general(
        short, s_ref[...], NT, preferred_element_type=F32
    )
    even_odd = columns_joined(None, back(here, 1, 2), back(here, 1, 0))
    odd_even = back(here, 2, 1) + back(below, 0, 1)
    odd_odd = columns_joined(
        None, back(here, 2, 2) + back(below, 0, 2), back(here, 2, 0) + back(below, 0, 0)
    )
    planes = ((even_even, even_odd), (odd_even, odd_odd))
    for row in range(2):
        for par in range(2):
            plane = planes[row][par].reshape(2, 4, 32, 256).astype(BF16)
            halves = (plane[..., 0:128], plane[..., 128:256])
            own = jnp.where(pipe == 0, halves[0], halves[1])
            other = jnp.where(pipe == 0, halves[1], halves[0])
            lanes = slice(par * 128, par * 128 + 128)
            for z in range(4):
                own_out[z ^ zone, :, row, :, lanes] = own[:, z]
                other_out[z ^ zone, :, row, :, lanes] = other[:, z]


def image_grad_kernel(where_ref, *refs):
    pieces, out_ref = refs[:8], refs[8]
    pipe, zone = where_ref[0], where_ref[2]
    for rel in range(4):
        for side in range(2):
            first = (zone ^ rel) * 4 + (pipe if side == 0 else 1 - pipe) * 2
            for i in range(2):
                for row in range(2):
                    for par in range(2):
                        out_ref[first + i, row, pl.ds(par, 32, stride=2), :] = pieces[
                            rel * 2 + side
                        ][i, row, :, par * 128 : (par + 1) * 128].astype(F32)


def slot_of(quarter, zone):
    rel = quarter ^ zone
    return (rel >> 1) | ((rel & 1) << 1)


def shifted_window(turned, down, right):
    pixel = lax.broadcasted_iota(jnp.int32, (1, 128), 1)
    column, row = pixel % 32 + right, pixel // 32 + down
    inside = (column >= 0) & (column < 32) & (row >= 0) & (row < 4)
    amount = (256 - down * 32 - right) % 128
    moved = turned if isinstance(amount, int) and amount == 0 else pltpu.roll(turned, amount, 1)
    return jnp.where(inside, moved, 0.0).astype(BF16)


def split_out(pipe, zone, unit, result_own, result_other, own_ref, other_ref):
    for quarter in range(4):
        slot = slot_of(quarter, zone)
        rows = slice(quarter * 32, quarter * 32 + 32)
        own_ref[slot, unit] = result_own[rows]
        other_ref[slot, unit] = result_other[rows].astype(BF16)


def kernel_grad_kernel(where_ref, act_ref, low_ref, own_ref, other_ref, turned_ref):
    pipe, batch, zone = where_ref[0], where_ref[1], where_ref[2]
    lanes = pl.ds(pl.multiple_of(batch * 128, 128), 128)

    def turn(image, carry):
        turned = act_ref[image, :, lanes].astype(F32).T
        pixels = pl.ds(pl.multiple_of(image * 128, 128), 128)
        for row in range(3):
            for col in range(3):
                turned_ref[row * 3 + col, :, pixels] = shifted_window(turned, row - 1, col - 1)
        return carry

    lax.fori_loop(0, 8, turn, 0)
    lhs = turned_ref[...].reshape(9 * 128, 1024)
    results = []
    for side in (pipe, 1 - pipe):
        columns = pl.ds(pl.multiple_of(side * 256, 256), 256)
        rhs = low_ref[:, :, columns].reshape(1024, 256)
        results.append(jnp.dot(lhs, rhs, preferred_element_type=F32))
    for unit in range(9):
        rows = slice(unit * 128, unit * 128 + 128)
        split_out(pipe, zone, unit, results[0][rows], results[1][rows], own_ref, other_ref)


DOWN_UNITS = (
    ((0, 0, 0, 4), (2, -1, 0, 1), (2, 0, 0, 7), (0, 0, 0, 9), (1, 0, 0, 5)),
    ((1, 0, -1, 3), (3, -1, -1, 0), (3, -1, 0, 2), (3, 0, -1, 6), (3, 0, 0, 8)),
)


def down_grad_kernel(where_ref, img_ref, low_ref, low_s_ref, own_ref, other_ref, turned_ref):
    pipe, batch, zone = where_ref[0], where_ref[1], where_ref[2]
    upper, part = batch // 2, batch % 2

    for turn_kind in range(2):

        @pl.when(upper == turn_kind)
        def _(units=DOWN_UNITS[turn_kind]):
            def turn(image, carry):
                pixels = pl.ds(pl.multiple_of(image * 128, 128), 128)
                seen = {}
                for unit, (plane, down, right, _) in enumerate(units):
                    if plane not in seen:
                        lanes = pl.ds(pl.multiple_of(plane * 256 + part * 128, 128), 128)
                        seen[plane] = img_ref[image, :, lanes].astype(F32).T
                    turned_ref[unit, :, pixels] = shifted_window(seen[plane], down, right)
                return carry

            lax.fori_loop(0, 8, turn, 0)

    short_unit = [tap for _, _, _, tap in DOWN_UNITS[0]].index(9)
    for unit in range(5):
        lhs = turned_ref[unit]
        results = []
        for side in (pipe, 1 - pipe):
            columns = pl.ds(pl.multiple_of(side * 256, 256), 256)
            rhs = low_ref[:, :, columns].reshape(1024, 256)
            if unit == short_unit:
                rhs_s = low_s_ref[:, :, columns].reshape(1024, 256)
                rhs = jnp.where(upper == 0, rhs_s, rhs)
            results.append(jnp.dot(lhs, rhs, preferred_element_type=F32))
        split_out(pipe, zone, unit, results[0], results[1], own_ref, other_ref)


def gathered_blocks(zone, batch, refs):
    fin, near = refs[0], refs[1]
    sets = {0: (None, refs[2]), 1: (refs[3], refs[6]), 2: (refs[4], refs[7]), 3: (refs[5], refs[8])}
    for kb in range(4):
        first, second = sets[kb]
        for rel in range(4):
            owner, quarter = batch ^ kb, zone ^ rel
            if rel % 2 == 1:
                yield owner, quarter, second, rel // 2
            elif first is not None:
                yield owner, quarter, first, rel // 2
            else:
                yield owner, quarter, (fin if rel == 0 else near), None


def assemble_kernel(where_ref, *refs):
    pieces, out_ref = refs[:9], refs[9]
    batch, zone = where_ref[1], where_ref[2]
    for owner, quarter, ref, index in gathered_blocks(zone, batch, pieces):
        rows = pl.ds(pl.multiple_of(owner * 128 + quarter * 32, 32), 32)
        value = ref[...] if index is None else ref[index]
        out_ref[:, rows, :] = value.astype(F32)


def assemble_down_kernel(where_ref, *refs):
    pieces, (out_ref, short_ref) = refs[:9], refs[9:]
    batch, zone = where_ref[1], where_ref[2]
    for owner, quarter, ref, index in gathered_blocks(zone, batch, pieces):
        upper, part = owner // 2, owner % 2
        rows = pl.ds(pl.multiple_of(part * 128 + quarter * 32, 32), 32)
        value = (ref[...] if index is None else ref[index]).astype(F32)
        for kind in range(2):

            @pl.when(upper == kind)
            def _(value=value, rows=rows, units=DOWN_UNITS[kind]):
                for unit, (_, _, _, tap) in enumerate(units):
                    if tap == 9:
                        short_ref[rows, :] = value[unit]
                    else:
                        out_ref[tap, rows, :] = value[unit]


def fast_device(images, image_counts, labels, fw_picks, conv_down, conv_mid, shortcut, gains_down,
                biases_down, conv_first, conv_second, gains_plain, biases_plain, head_weight,
                head_bias):
    pipe, batch, zone = (lax.axis_index(axis) for axis in ("pipe", "batch", "space"))
    tasks = head_weight.shape[1]

    def over(axis, rel, x):
        size = lax.axis_size(axis)
        return lax.ppermute(x, axis, [(i, i ^ rel) for i in range(size)])

    def by_index(parts, own):
        stacked = jnp.stack(parts)
        return jnp.take(stacked, jnp.arange(4) ^ own, axis=0)

    where = jnp.stack([pipe, batch, zone, zone]).astype(jnp.int32)

    pieces = call(
        pieces_kernel,
        [((2, 2, 32, 512), BF16)] * 4,
        [where, images],
        [pltpu.VMEM((64, 128), F32)],
        name="pieces",
    )
    moved = [pieces[0]] + [over("space", rel, pieces[rel]) for rel in (1, 2, 3)]
    gathered = [[moved[rel] for rel in range(4)]]
    for kb in (1, 2, 3):
        gathered.append([over("batch", kb, moved[rel]) for rel in range(4)])

    marks = lax.dynamic_slice_in_dim(labels, zone * 4, 4, 0)
    count = lax.dynamic_slice_in_dim(image_counts, zone, 1, 1)
    marks = jnp.concatenate([marks, jnp.broadcast_to(count, (1, tasks))], axis=0)
    marks = by_index([marks] + [over("batch", kb, marks) for kb in (1, 2, 3)], batch)
    counts = marks[:, 4, 0]
    slots = jnp.arange(4, dtype=jnp.int32).reshape(2, 1, 2)
    living = (slots < counts[None, :, None]).astype(F32).reshape(2, 8)
    targets = marks[:, :4].reshape(4, 2, 2, tasks).transpose(1, 0, 2, 3).reshape(16, tasks)
    targets = targets.astype(F32)
    alive = jnp.sum(living, axis=1) * 128.0
    mine = jnp.where(pipe == 0, living[0], living[1])
    own_px = jnp.where(pipe == 0, alive[0], alive[1])
    facts = jnp.concatenate(
        [mine, jnp.stack([own_px, alive[0] + alive[1] - own_px, alive[0] + alive[1]])]
    )
    facts = jnp.pad(facts, (0, 5))

    big = ((8, 128, 512), F32)
    low = ((8, 128, 512), BF16)
    rows = ((8, 512), F32)
    x_scratch = pltpu.VMEM((8, 128, 1536), BF16)
    conv_scratch = pltpu.VMEM((8, 128, 512), F32)
    conv_flops = 2 * 1024 * 4608 * 512

    def partner(x):
        return over("pipe", 1, x)

    img, down_out, short_out, stat_d = call(
        down_kernel,
        [((8, 128, 1024), BF16), big, big, rows],
        [facts, where] + [piece for line in gathered for piece in line] + [conv_down, shortcut],
        [pltpu.VMEM((8, 128, 512), BF16)],
        conv_flops // 2,
        "down",
    )
    other_d = partner(stat_d)
    down_act, mid_out, stat_m, norm_d = call(
        lambda *refs: layer_kernel(0, *refs),
        [low, big, rows, rows],
        [facts, down_out, stat_d, other_d, gains_down, biases_down, conv_mid],
        [x_scratch],
        conv_flops,
        "mid",
    )
    other_m = partner(stat_m)
    section, first_out, stat_f, norm_j = call(
        join_kernel,
        [low, big, rows, rows],
        [facts, mid_out, short_out, stat_m, other_m, stat_d, other_d, gains_down, biases_down,
         conv_first],
        [x_scratch],
        conv_flops,
        "first",
    )
    other_f = partner(stat_f)
    plain_act, second_out, stat_s, norm_f = call(
        lambda *refs: layer_kernel(0, *refs),
        [low, big, rows, rows],
        [facts, first_out, stat_f, other_f, gains_plain, biases_plain, conv_second],
        [x_scratch],
        conv_flops,
        "second",
    )
    other_s = partner(stat_s)
    pack, norm_s = call(
        block_kernel,
        [((24, 512), F32), rows],
        [facts, second_out, section, stat_s, other_s, gains_plain, biases_plain],
        name="block",
    )
    other_pack = partner(pack)
    all_pack, errors, cross = call(
        logits_kernel,
        [((3, 16, 512), F32), ((16, tasks), F32), ((tasks, tasks), F32)],
        [where, pack, other_pack, living.reshape(16, 1), targets, head_weight,
         head_bias.reshape(1, tasks)],
        name="logits",
    )
    crosses = [cross] + [over("space", rel, cross) for rel in (1, 2, 3)]
    heads = jnp.dot(head_weight.T, head_weight, precision=HIGHEST)
    second_low, grad_pool, small = call(
        head_kernel,
        [low, rows, ((tasks + 8, 512), F32)],
        [fw_picks, where, facts] + crosses
        + [heads, head_weight, errors, all_pack, second_out, section, norm_s, gains_plain,
           biases_plain],
        [pltpu.VMEM((1, tasks), F32), pltpu.VMEM((tasks, tasks), F32)],
        name="head",
    )

    def summed(own, other):
        got = partner(other)
        both = own + got.astype(F32)
        near = both[:2] + over("space", 1, both[2:].astype(BF16)).astype(F32)
        mine = near[0] + over("space", 2, near[1].astype(BF16)).astype(F32)
        final = mine.astype(BF16)
        far = over("space", 2, final)
        a = jnp.stack([final, far])
        b = over("space", 1, a)
        ax, ay = over("batch", 1, a), over("batch", 2, a)
        bx, by = over("batch", 1, b), over("batch", 2, b)
        axy, bxy = over("batch", 2, ax), over("batch", 1, by)
        return [where, final, far, b, ax, ay, axy, bx, by, bxy]

    def kernel_grad_of(act, low_grad, name):
        own, other = call(
            kernel_grad_kernel,
            [((4, 9, 32, 256), F32), ((4, 9, 32, 256), BF16)],
            [where, act, low_grad],
            [pltpu.VMEM((9, 128, 1024), BF16)],
            conv_flops // 4,
            name,
        )
        return summed(own, other)

    def assembled(blocks, name):
        (out,) = call(assemble_kernel, [((9, 512, 256), F32)], blocks, name=name)
        return out.reshape(3, 3, 512, 256)

    second_blocks = kernel_grad_of(plain_act, second_low, "second_grad")
    up_f, sum_f = call(
        second_back_kernel,
        [big, rows],
        [facts, second_low, first_out, norm_f, gains_plain, biases_plain, conv_second],
        [x_scratch, conv_scratch],
        conv_flops,
        "second_back",
    )
    other_sf = partner(sum_f)
    first_low, up_j, sum_j = call(
        first_back_kernel,
        [low, big, rows],
        [facts, up_f, first_out, norm_f, sum_f, other_sf, gains_plain, conv_first,
         second_out, norm_s, section, biases_plain, grad_pool,
         mid_out, short_out, norm_j, gains_down, biases_down],
        [x_scratch, conv_scratch],
        conv_flops,
        "first_back",
    )
    other_sj = partner(sum_j)
    first_blocks = kernel_grad_of(section, first_low, "first_grad")
    mid_low, short_low, up_d, sum_d = call(
        mid_back_kernel,
        [low, low, big, rows],
        [facts, up_j, mid_out, short_out, norm_j, sum_j, other_sj, gains_down, conv_mid,
         down_out, norm_d, biases_down],
        [x_scratch, conv_scratch],
        conv_flops,
        "mid_back",
    )
    other_sd = partner(sum_d)
    mid_blocks = kernel_grad_of(down_act, mid_low, "mid_grad")
    down_low, own_img, other_img = call(
        down_back_kernel,
        [low, ((4, 2, 2, 32, 256), BF16), ((4, 2, 2, 32, 256), BF16)],
        [where, facts, up_d, down_out, norm_d, sum_d, other_sd, gains_down, short_low, conv_down,
         shortcut],
        [],
        conv_flops // 8,
        "down_back",
    )
    own, other = call(
        down_grad_kernel,
        [((4, 5, 32, 256), F32), ((4, 5, 32, 256), BF16)],
        [where, img, down_low, short_low],
        [pltpu.VMEM((5, 128, 1024), BF16)],
        conv_flops // 8,
        "down_grad",
    )
    down_blocks = summed(own, other)

    got_img = partner(other_img)
    image_pieces = []
    for rel in range(4):
        for block in (own_img, got_img):
            part = block[rel]
            image_pieces.append(part if rel == 0 else over("space", rel, part))
    (images_grad,) = call(
        image_grad_kernel,
        [((16, 2, 64, 128), F32)],
        [where] + image_pieces,
        name="image_grad",
    )

    def own_lanes(x):
        return lax.dynamic_slice_in_dim(x, pipe * 256, 256, x.ndim - 1)

    pooled_mine = lax.dynamic_slice_in_dim(
        all_pack[0].reshape(2, 4, 2, 512), batch, 1, 1
    ).reshape(4, 512)
    sums = jnp.concatenate(
        [
            small,
            sum_f[0:2] + other_sf[0:2],
            sum_j[0:3] + other_sj[0:3],
            sum_d[0:2] + other_sd[0:2],
        ]
    )
    sent = jnp.concatenate([own_lanes(sums), own_lanes(pooled_mine)])
    parts = [sent] + [over("space", rel, sent) for rel in (1, 2, 3)]
    summed_up = (parts[0] + parts[1]) + (parts[2] + parts[3])
    pooled = by_index([part[-4:] for part in parts], zone).reshape(16, 256)
    row = tasks + 8
    second_sum, second_cross, head_b = (summed_up[tasks + i] for i in range(3))
    first_sum, first_cross = summed_up[row], summed_up[row + 1]
    join_sum, mid_cross, short_cross = (summed_up[row + 2 + i] for i in range(3))
    down_sum, down_cross = summed_up[row + 5], summed_up[row + 6]
    down_grad, short_grad = call(
        assemble_down_kernel,
        [((9, 256, 256), F32), ((256, 256), F32)],
        down_blocks,
        name="down_out",
    )
    return (
        pooled,
        images_grad,
        down_grad.reshape(3, 3, 256, 256),
        assembled(mid_blocks, "mid_out"),
        short_grad,
        jnp.stack([down_cross, mid_cross, short_cross]),
        jnp.stack([down_sum, join_sum, join_sum]),
        assembled(first_blocks, "first_out"),
        assembled(second_blocks, "second_out"),
        jnp.stack([first_cross, second_cross]),
        jnp.stack([first_sum, second_sum]),
        summed_up[:tasks].T,
        lax.dynamic_slice_in_dim(head_b, pipe * (tasks // 2), tasks // 2, 0),
    )


def per_device(
    images,
    image_counts,
    labels,
    fw_picks,
    conv_down,
    conv_mid,
    shortcut,
    gains_down,
    biases_down,
    conv_first,
    conv_second,
    gains_plain,
    biases_plain,
    head_weight,
    head_bias,
):
    layout = Layout(image_counts.shape[1])
    micros, zone = layout.micros, layout.zone
    sizes = (images.shape, conv_down.shape, lax.axis_size("pipe"), lax.axis_size("batch"))
    if layout.groups == 1 and sizes == ((16, 2, 64, 256), (3, 3, 256, 512), 2, 4):
        return fast_device(
            images, image_counts, labels, fw_picks, conv_down, conv_mid, shortcut, gains_down,
            biases_down, conv_first, conv_second, gains_plain, biases_plain, head_weight,
            head_bias,
        )
    batches, pipes = lax.axis_size("batch"), lax.axis_size("pipe")
    batch = lax.axis_index("batch")
    pipe = lax.axis_index("pipe")
    per_micro = images.shape[0] // micros
    count = per_micro * batches
    entering, channels = conv_down.shape[2], conv_mid.shape[3]
    tasks = head_weight.shape[1]
    half = channels // pipes
    own = pipe * half

    def own_out(kernel, axis):
        size = kernel.shape[axis] // pipes
        return lax.dynamic_slice_in_dim(kernel, pipe * size, size, axis)

    def whole(tensor, axis=3):
        return lax.all_gather(tensor, "pipe", axis=axis, tiled=True)

    def share(tensor):
        size = tensor.shape[3] // batches
        return lax.dynamic_slice_in_dim(tensor, batch * size, size, 3)

    mine = lax.all_to_all(
        images, "space", 0, 1, axis_index_groups=layout.inner, tiled=True
    )
    mine = lax.all_gather(mine, "batch", axis=0, tiled=True)
    counts = lax.all_gather(image_counts, "batch", axis=0, tiled=True)
    counts = lax.dynamic_slice_in_dim(counts, zone, 1, 1)[:, 0]
    marks = lax.dynamic_slice_in_dim(labels, zone * per_micro, per_micro, 0)
    targets = lax.all_gather(marks, "batch", axis=0, tiled=True).astype(F32)
    slots = jnp.arange(per_micro, dtype=jnp.int32)
    living = (slots[None, :] < counts[:, None]).astype(F32).reshape(count)
    weight = living[:, None, None, None]
    out_rows, out_cols = mine.shape[1] // 2, mine.shape[2] // 2
    image_pixels = out_rows * layout.groups * out_cols
    counted = jnp.sum(living) * image_pixels
    scale = float(image_pixels * tasks)

    gain_d, bias_d = own_out(gains_down, 1), own_out(biases_down, 1)
    gain_p, bias_p = own_out(gains_plain, 1), own_out(biases_plain, 1)

    above = layout.row_from(mine[:, -1:], 1)
    down_ext = jnp.pad(
        jnp.concatenate([above, mine], axis=1), ((0, 0), (0, 0), (1, 0), (0, 0))
    )
    down_out = conv_valid(down_ext, own_out(conv_down, 3), 2)
    down_norm, down_inv = norm_forward(layout, down_out, weight, counted)
    down_pre = down_norm * gain_d[0] + bias_d[0]
    mid_ext = layout.rims(whole(jax.nn.silu(down_pre).astype(BF16)))
    mid_out = conv_valid(mid_ext, own_out(conv_mid, 3), 1)
    short_in = mine[:, ::2, ::2]
    short_out = jnp.einsum(
        "nhwi,io->nhwo", short_in, own_out(shortcut, 1), preferred_element_type=F32
    )
    mid_norm, mid_inv = norm_forward(layout, mid_out, weight, counted)
    short_norm, short_inv = norm_forward(layout, short_out, weight, counted)
    section_pre = mid_norm * gain_d[1] + bias_d[1] + short_norm * gain_d[2] + bias_d[2]
    section = jax.nn.silu(section_pre).astype(BF16)
    first_ext = layout.rims(whole(section))
    first_out = conv_valid(first_ext, own_out(conv_first, 3), 1)
    first_norm, first_inv = norm_forward(layout, first_out, weight, counted)
    first_pre = first_norm * gain_p[0] + bias_p[0]
    second_ext = layout.rims(whole(jax.nn.silu(first_pre).astype(BF16)))
    second_out = conv_valid(second_ext, own_out(conv_second, 3), 1)
    second_norm, second_inv = norm_forward(layout, second_out, weight, counted)
    block_pre = second_norm * gain_p[1] + bias_p[1] + section.astype(F32)
    pooled = layout.group_sum(jnp.sum(jax.nn.silu(block_pre), axis=(1, 2))) / image_pixels

    pooled_all = whole(pooled, 1)
    logits = jnp.dot(pooled_all, head_weight, precision=HIGHEST) + head_bias
    errors = living[:, None] * (jax.nn.sigmoid(logits) - targets)
    cross = jnp.einsum("nt,ns->ts", errors, errors, precision=HIGHEST)
    cross = lax.psum(cross, "space", axis_index_groups=layout.inner)
    gram = cross * jnp.dot(head_weight.T, head_weight, precision=HIGHEST)
    alpha = frank_wolfe(gram, fw_picks)
    grad_logits = scale * alpha * errors
    head_w = jnp.einsum("nc,nt->ct", pooled, grad_logits, precision=HIGHEST)
    head_b = jnp.sum(grad_logits, axis=0)
    head_own = own_out(head_weight, 0)
    grad_pool = jnp.einsum("nt,ct->nc", grad_logits, head_own, precision=HIGHEST) / image_pixels

    grad_block = grad_pool[:, None, None, :] * silu_slope(block_pre)
    second_low, second_cross, second_sum = norm_back(
        layout, grad_block, second_norm, second_inv, gain_p[1], weight, counted
    )
    second_kernel = kernel_grad(share(second_ext), second_low, 1)
    act_grad = conv_valid(layout.rims(whole(second_low)), flipped(own_out(conv_second, 2)), 1)
    first_low, first_cross, first_sum = norm_back(
        layout, act_grad * silu_slope(first_pre), first_norm, first_inv, gain_p[0], weight, counted
    )
    first_kernel = kernel_grad(share(first_ext), first_low, 1)
    entry_grad = conv_valid(layout.rims(whole(first_low)), flipped(own_out(conv_first, 2)), 1)
    entry_grad = (entry_grad + grad_block).astype(BF16).astype(F32)
    grad_section = entry_grad * silu_slope(section_pre)
    mid_low, mid_cross, mid_sum = norm_back(
        layout, grad_section, mid_norm, mid_inv, gain_d[1], weight, counted
    )
    short_low, short_cross, short_sum = norm_back(
        layout, grad_section, short_norm, short_inv, gain_d[2], weight, counted
    )
    mid_kernel = kernel_grad(share(mid_ext), mid_low, 1)
    short_kernel = jnp.einsum(
        "nhwi,nhwo->io", share(short_in), short_low, preferred_element_type=F32
    )
    act_grad = conv_valid(layout.rims(whole(mid_low)), flipped(own_out(conv_mid, 2)), 1)
    down_low, down_cross, down_sum = norm_back(
        layout, act_grad * silu_slope(down_pre), down_norm, down_inv, gain_d[0], weight, counted
    )
    down_kernel = kernel_grad(share(down_ext), down_low, 2)

    kept = lax.dynamic_slice_in_dim(whole(down_low), batch * per_micro, per_micro, 0)
    below = layout.row_from(kept[:, :1], -1)
    spread = lax.conv_general_dilated(
        jnp.concatenate([kept, below], axis=1),
        flipped(own_out(conv_down, 2)),
        (1, 1),
        ((2, 2), (2, 2)),
        lhs_dilation=(2, 2),
        dimension_numbers=NUMBERS,
        preferred_element_type=F32,
    )[:, 1 : 2 * out_rows + 1, 1:]
    short_kept = lax.dynamic_slice_in_dim(whole(short_low), batch * per_micro, per_micro, 0)
    spread = spread.at[:, ::2, ::2].add(
        jnp.einsum(
            "nhwo,io->nhwi", short_kept, own_out(shortcut, 0), preferred_element_type=F32
        )
    )
    images_grad = lax.all_to_all(
        spread.astype(BF16), "space", 1, 0, axis_index_groups=layout.inner, tiled=True
    ).astype(F32)

    def total(kernel, axis):
        summed = lax.psum(kernel.astype(BF16), "space")
        return lax.all_gather(summed, "batch", axis=axis, tiled=True).astype(F32)

    pooled_out = lax.dynamic_slice_in_dim(pooled, batch * per_micro, per_micro, 0)
    pooled_out = lax.all_gather(
        pooled_out, "space", axis_index_groups=layout.inner, axis=0, tiled=True
    )
    head_w, head_b = lax.psum((head_w, head_b), "space", axis_index_groups=layout.inner)
    gains_d, sums_d, gains_p, sums_p = lax.psum(
        (
            jnp.stack([down_cross, mid_cross, short_cross]),
            jnp.stack([down_sum, mid_sum, short_sum]),
            jnp.stack([first_cross, second_cross]),
            jnp.stack([first_sum, second_sum]),
        ),
        "space",
    )
    return (
        pooled_out,
        images_grad,
        total(down_kernel, 1).reshape(3, 3, entering, half),
        total(mid_kernel, 1).reshape(3, 3, channels, half),
        total(short_kernel, 0),
        gains_d,
        sums_d,
        total(first_kernel, 1).reshape(3, 3, channels, half),
        total(second_kernel, 1).reshape(3, 3, channels, half),
        gains_p,
        sums_p,
        head_w,
        own_out(head_b, 0),
    )


def solution(mesh):
    placed = (
        P("batch", "space", None, None),
        P("batch", None),
        P("batch", None),
    ) + (P(),) * 12
    return jax.shard_map(
        per_device,
        mesh=mesh,
        in_specs=placed,
        out_specs=(
            P("batch", "pipe"),
            P("batch", "space", None, "pipe"),
            P(None, None, None, "pipe"),
            P(None, None, None, "pipe"),
            P(None, "pipe"),
            P(None, "pipe"),
            P(None, "pipe"),
            P(None, None, None, "pipe"),
            P(None, None, None, "pipe"),
            P(None, "pipe"),
            P(None, "pipe"),
            P("pipe", None),
            P("pipe"),
        ),
        check_vma=False,
    )
```

```python
import jax
import jax.numpy as jnp
from jax import lax
from jax.experimental import pallas as pl
from jax.experimental.pallas import tpu as pltpu
from jax.sharding import PartitionSpec as P

EPSILON = 1e-05
NUMBERS = ("NHWC", "HWIO", "NHWC")
HIGHEST = lax.Precision.HIGHEST
F32 = jnp.float32
BF16 = jnp.bfloat16


def silu_slope(values):
    sigmoid = jax.nn.sigmoid(values)
    return sigmoid * (1.0 + values * (1.0 - sigmoid))


def frank_wolfe_kernel(picks_ref, gram_ref, alpha_ref):
    tasks = gram_ref.shape[0]
    lanes = lax.broadcasted_iota(jnp.int32, (1, tasks), 1)
    gram = gram_ref[...]
    alpha = jnp.full((1, tasks), 1.0 / tasks, F32)
    pulled = jnp.sum(gram, axis=0, keepdims=True) * (1.0 / tasks)
    energy = jnp.sum(pulled * alpha, axis=1, keepdims=True)

    def advance(step, carry):
        alpha, pulled, energy = carry
        chosen = picks_ref[step]
        row = gram_ref[pl.ds(chosen, 1), :]
        onehot = (lanes == chosen).astype(F32)
        toward = jnp.sum(pulled * onehot, axis=1, keepdims=True)
        corner = jnp.sum(row * onehot, axis=1, keepdims=True)
        denom = jnp.maximum(energy - 2.0 * toward + corner, 0.05 * corner)
        ratio = jnp.clip((energy - toward) / denom, 0.0, 1.0)
        rest = 1.0 - ratio
        alpha = rest * alpha + ratio * onehot
        pulled = rest * pulled + ratio * row
        energy = rest * rest * energy + 2.0 * rest * ratio * toward + ratio * ratio * corner
        return alpha, pulled, energy

    alpha, _, _ = lax.fori_loop(0, picks_ref.shape[0], advance, (alpha, pulled, energy))
    alpha_ref[...] = alpha


def frank_wolfe(gram, picks):
    tasks = gram.shape[0]
    return pl.pallas_call(
        frank_wolfe_kernel,
        out_shape=jax.ShapeDtypeStruct((1, tasks), F32),
        in_specs=[
            pl.BlockSpec(memory_space=pltpu.SMEM),
            pl.BlockSpec(memory_space=pltpu.VMEM),
        ],
        out_specs=pl.BlockSpec(memory_space=pltpu.VMEM),
    )(picks, gram)


class Layout:
    def __init__(self, micros):
        self.micros = micros
        self.spaces = lax.axis_size("space")
        self.groups = self.spaces // micros
        self.inner = [
            [group * micros + zone for zone in range(micros)] for group in range(self.groups)
        ]
        self.outer = [
            [group * micros + zone for group in range(self.groups)] for zone in range(micros)
        ]
        self.zone = lax.axis_index("space") % micros

    def group_sum(self, tree):
        if self.groups == 1:
            return tree
        return lax.psum(tree, "space", axis_index_groups=self.outer)

    def row_from(self, block, step):
        span = step * self.micros
        route = [
            (i, i + span) for i in range(self.spaces) if 0 <= i + span < self.spaces
        ]
        if not route:
            return jnp.zeros_like(block)
        return lax.ppermute(block, "space", route)

    def rims(self, tensor):
        above = self.row_from(tensor[:, -1:], 1)
        below = self.row_from(tensor[:, :1], -1)
        grown = jnp.concatenate([above, tensor, below], axis=1)
        return jnp.pad(grown, ((0, 0), (0, 0), (1, 1), (0, 0)))


def conv_valid(extended, kernel, stride):
    return lax.conv_general_dilated(
        extended,
        kernel,
        (stride, stride),
        "VALID",
        dimension_numbers=NUMBERS,
        preferred_element_type=F32,
    )


def flipped(kernel):
    return jnp.swapaxes(kernel[::-1, ::-1], 2, 3)


def kernel_grad(extended, grad_low, stride):
    rows, cols = grad_low.shape[1], grad_low.shape[2]
    taps = []
    for row_tap in range(3):
        for col_tap in range(3):
            window = extended[
                :,
                row_tap : row_tap + stride * (rows - 1) + 1 : stride,
                col_tap : col_tap + stride * (cols - 1) + 1 : stride,
            ]
            taps.append(jnp.einsum("nhwi,nhwo->io", window, grad_low, preferred_element_type=F32))
    return jnp.stack(taps)


def norm_forward(layout, conv_out, weight, counted):
    total = layout.group_sum(jnp.sum(conv_out * weight, axis=(0, 1, 2)))
    centered = conv_out - total / counted
    spread = layout.group_sum(jnp.sum(centered * centered * weight, axis=(0, 1, 2)))
    inverse = lax.rsqrt(spread / counted + EPSILON)
    return centered * inverse, inverse


def norm_back(layout, upstream, normed, inverse, gain, weight, counted):
    grad_sum = jnp.sum(upstream * weight, axis=(0, 1, 2))
    cross_sum = jnp.sum(upstream * normed * weight, axis=(0, 1, 2))
    grad_total, cross_total = layout.group_sum((grad_sum, cross_sum))
    correction = weight * (grad_total / counted + normed * (cross_total / counted))
    low = (gain * inverse * (upstream - correction)).astype(BF16)
    return low, cross_sum, grad_sum


KERNEL_LIMIT = 24 * 2**20
VM = pl.BlockSpec(memory_space=pltpu.VMEM)
SM = pl.BlockSpec(memory_space=pltpu.SMEM)
NT = (((1,), (1,)), ((), ()))
TN = (((0,), (0,)), ((), ()))
OWN_PX, OTHER_PX, ALL_PX = 8, 9, 10
G_DOWN, G_MID, G_SHORT, B_DOWN, B_MID, B_SHORT, G_FIRST, G_SECOND, B_FIRST, B_SECOND = range(10)


def param(params_ref, row):
    return params_ref[row : row + 1, :]


def call(kernel, outs, operands, scratch=(), flops=0, name=None, after=(), specs=None):
    count = len(operands)
    nbytes = sum(x.size * x.dtype.itemsize for x in operands)
    specs = specs or {}

    def body(*refs):
        kernel(*refs[:count], *refs[count + len(after) :])

    return pl.pallas_call(
        body,
        out_shape=tuple(jax.ShapeDtypeStruct(shape, dtype) for shape, dtype in outs),
        in_specs=[specs.get(i, SM if x.ndim == 1 else VM) for i, x in enumerate(operands)]
        + [pl.BlockSpec(memory_space=pl.ANY)] * len(after),
        out_specs=tuple(SM if len(shape) == 1 else VM for shape, _ in outs),
        scratch_shapes=list(scratch),
        compiler_params=pltpu.CompilerParams(vmem_limit_bytes=KERNEL_LIMIT),
        cost_estimate=pl.CostEstimate(
            flops=int(flops), bytes_accessed=int(nbytes), transcendentals=0
        ),
        name=name,
    )(*operands, *after)


def fold(rows):
    return rows[0:8] + rows[8:16] + rows[16:24] + rows[24:32]


def total_row(part):
    return jnp.sum(part, axis=0, keepdims=True)


def band(row):
    return slice(row * 32, row * 32 + 32)


def put_band(x_ref, image, row, value):
    zero = jnp.zeros_like(value)
    x_ref[image, band(row), 512:1024] = value
    if row < 3:
        x_ref[image, band(row + 1), 0:512] = value
    else:
        x_ref[image, band(0), 0:512] = zero
    if row > 0:
        x_ref[image, band(row - 1), 1024:1536] = value
    else:
        x_ref[image, band(3), 1024:1536] = zero


def columns_joined(left, middle, right):
    count = middle.shape[0]
    column = lax.broadcasted_iota(jnp.int32, (count, 1), 0) % 32
    joined = middle
    if left is not None:
        joined = joined + jnp.where(column == 0, 0.0, pltpu.roll(left, 1, 0))
    if right is not None:
        joined = joined + jnp.where(column == 31, 0.0, pltpu.roll(right, count - 1, 0))
    return joined


def conv_core(x_ref, w_ref, out_ref, back):
    for part in range(2):
        images = slice(4 * part, 4 * part + 4)

        def tap(col):
            value = None
            for row in range(3):
                lhs = x_ref[images, :, row * 512 : (row + 1) * 512].reshape(512, 512)
                if back:
                    term = lax.dot_general(
                        lhs, w_ref[2 - row, 2 - col], NT, preferred_element_type=F32
                    )
                else:
                    term = jnp.dot(lhs, w_ref[row, col], preferred_element_type=F32)
                value = term if value is None else value + term
            return value

        out = columns_joined(tap(0), tap(1), tap(2))
        out_ref[images] = out.reshape(4, 128, 512)


def stats_of(facts_ref, out_ref, stat_ref, row):
    def add(image, part):
        for r in range(4):
            part = part + fold(out_ref[image, band(r), :]) * facts_ref[image]
        return part

    first = total_row(lax.fori_loop(0, 8, add, jnp.zeros((8, 512), F32)))
    mean = first / jnp.maximum(facts_ref[OWN_PX], 1.0)

    def deviate(image, part):
        for r in range(4):
            away = out_ref[image, band(r), :] - mean
            part = part + fold(away * away) * facts_ref[image]
        return part

    second = total_row(lax.fori_loop(0, 8, deviate, jnp.zeros((8, 512), F32)))
    stat_ref[row : row + 1, :] = first
    stat_ref[row + 1 : row + 2, :] = second


def norm_of(facts_ref, own_ref, other_ref, row):
    own_px, other_px, all_px = facts_ref[OWN_PX], facts_ref[OTHER_PX], facts_ref[ALL_PX]
    own, other = own_ref[row : row + 1, :], other_ref[row : row + 1, :]
    mean = (own + other) / all_px
    apart = own / jnp.maximum(own_px, 1.0) - other / jnp.maximum(other_px, 1.0)
    spread = own_ref[row + 1 : row + 2, :] + other_ref[row + 1 : row + 2, :]
    variance = (spread + apart * apart * (own_px * other_px / all_px)) / all_px
    return mean, lax.rsqrt(variance + EPSILON)


def sigmoid(values):
    return 1.0 / (1.0 + jnp.exp(-values))


def slope_of(values):
    gate = sigmoid(values)
    return gate * (1.0 + values * (1.0 - gate))


MARKS = 128


def pieces_kernel(where_ref, images_ref, labels_ref, count_ref, o0, o1, o2, o3, wide):
    pipe, zone = where_ref[0], where_ref[2]
    tasks = labels_ref.shape[1]
    o0[MARKS:, :] = jnp.zeros((16, 512), BF16)
    for rel, out in enumerate((o0, o1, o2, o3)):
        first = (zone ^ rel) * 4 + pipe * 2
        for i in range(2):
            for row in range(2):
                lines = slice((i * 2 + row) * 32, (i * 2 + row) * 32 + 32)
                for part in range(2):
                    lanes = slice(part * 128, part * 128 + 128)
                    wide[...] = images_ref[first + i, row, :, lanes].astype(F32)
                    for par in range(2):
                        value = wide[pl.ds(par, 32, stride=2), :]
                        start = par * 256 + part * 128
                        out[lines, start : start + 128] = value.astype(BF16)
    marks = jnp.concatenate(
        [
            labels_ref[...].astype(F32),
            jnp.broadcast_to(count_ref[...].astype(F32), (4, tasks)),
            jnp.zeros((8, tasks), F32),
        ]
    )
    o0[MARKS:, 0:tasks] = marks.astype(BF16)


def down_kernel(facts_ref, where_ref, *refs):
    pieces, (w_ref, s_ref, img_ref, out_ref, short_ref, stat_ref, x_ref) = refs[:12], refs[12:]
    batch, zone = where_ref[1], where_ref[2]
    for kb in range(4):
        for kz in range(4):
            piece, base = pieces[kb * 3 + min(kz, 2)], (128 if kz == 3 else 0)
            row = zone ^ kz
            here = pl.ds(pl.multiple_of(row * 32, 32), 32)
            after = pl.ds(pl.multiple_of(((row + 1) % 4) * 32, 32), 32)
            for i in range(2):
                image = (batch ^ kb) * 2 + i
                start = base + i * 64
                odd = piece[start + 32 : start + 64, :]
                img_ref[image, here, 0:512] = piece[start : start + 32, :]
                img_ref[image, here, 512:1024] = odd
                x_ref[image, after, :] = jnp.where(row == 3, jnp.zeros_like(odd), odd)
    for part in range(2):
        images = slice(4 * part, 4 * part + 4)
        blocks = (
            x_ref[images].reshape(512, 512),
            img_ref[images, :, 0:512].reshape(512, 512),
            img_ref[images, :, 512:1024].reshape(512, 512),
        )
        left, middle = None, None
        for row in range(3):
            a = jnp.dot(blocks[row][:, 256:], w_ref[row, 0], preferred_element_type=F32)
            m = jnp.dot(
                blocks[row], w_ref[row, 1:3].reshape(512, 512), preferred_element_type=F32
            )
            left = a if left is None else left + a
            middle = m if middle is None else middle + m
        out_ref[images] = columns_joined(left, middle, None).reshape(4, 128, 512)
        short = jnp.dot(blocks[1][:, :256], s_ref[...], preferred_element_type=F32)
        short_ref[images] = short.reshape(4, 128, 512)
    stats_of(facts_ref, out_ref, stat_ref, 0)
    stats_of(facts_ref, short_ref, stat_ref, 2)
    stat_ref[4:8, :] = jnp.zeros((4, 512), F32)


def layer_kernel(g_row, b_row, facts_ref, in_ref, own_ref, other_ref, params_ref, w_ref,
                 act_ref, out_ref, stat_ref, norm_ref, x_ref):
    mean, inverse = norm_of(facts_ref, own_ref, other_ref, 0)
    gain, bias = param(params_ref, g_row), param(params_ref, b_row)

    def activate(image, carry):
        for r in range(4):
            pre = (in_ref[image, band(r), :] - mean) * inverse * gain + bias
            act = (pre * sigmoid(pre)).astype(BF16)
            act_ref[image, band(r), :] = act
            put_band(x_ref, image, r, act)
        return carry

    lax.fori_loop(0, 8, activate, 0)
    norm_ref[0:1, :] = mean
    norm_ref[1:2, :] = inverse
    norm_ref[2:8, :] = jnp.zeros((6, 512), F32)
    conv_core(x_ref, w_ref, out_ref, False)
    stats_of(facts_ref, out_ref, stat_ref, 0)
    stat_ref[2:8, :] = jnp.zeros((6, 512), F32)


def join_kernel(facts_ref, mid_ref, short_ref, own_m, other_m, own_d, other_d, params_ref,
                w_ref, act_ref, out_ref, stat_ref, norm_ref, x_ref):
    mean_m, inv_m = norm_of(facts_ref, own_m, other_m, 0)
    mean_s, inv_s = norm_of(facts_ref, own_d, other_d, 2)
    gain_m, gain_s = param(params_ref, G_MID), param(params_ref, G_SHORT)
    bias_m, bias_s = param(params_ref, B_MID), param(params_ref, B_SHORT)

    def activate(image, carry):
        for r in range(4):
            pre = (mid_ref[image, band(r), :] - mean_m) * inv_m * gain_m + bias_m
            pre = pre + (short_ref[image, band(r), :] - mean_s) * inv_s * gain_s + bias_s
            act = (pre * sigmoid(pre)).astype(BF16)
            act_ref[image, band(r), :] = act
            put_band(x_ref, image, r, act)
        return carry

    lax.fori_loop(0, 8, activate, 0)
    norm_ref[0:1, :] = mean_m
    norm_ref[1:2, :] = inv_m
    norm_ref[2:3, :] = mean_s
    norm_ref[3:4, :] = inv_s
    norm_ref[4:8, :] = jnp.zeros((4, 512), F32)
    conv_core(x_ref, w_ref, out_ref, False)
    stats_of(facts_ref, out_ref, stat_ref, 0)
    stat_ref[2:8, :] = jnp.zeros((6, 512), F32)


def block_kernel(facts_ref, in_ref, section_ref, own_ref, other_ref, params_ref,
                 pack_ref, norm_ref):
    mean, inverse = norm_of(facts_ref, own_ref, other_ref, 0)
    gain, bias = param(params_ref, G_SECOND), param(params_ref, B_SECOND)
    norm_ref[0:1, :] = mean
    norm_ref[1:2, :] = inverse
    norm_ref[2:8, :] = jnp.zeros((6, 512), F32)

    def gather(image, carry):
        pooled = jnp.zeros((8, 512), F32)
        slopes, crossed = pooled, pooled
        for r in range(4):
            normed = (in_ref[image, band(r), :] - mean) * inverse
            pre = normed * gain + bias + section_ref[image, band(r), :].astype(F32)
            gate = sigmoid(pre)
            slope = gate * (1.0 + pre * (1.0 - gate))
            pooled = pooled + fold(pre * gate)
            slopes = slopes + fold(slope)
            crossed = crossed + fold(slope * normed)
        pack_ref[pl.ds(image, 1), :] = total_row(pooled) / 128.0
        pack_ref[pl.ds(image + 8, 1), :] = total_row(slopes)
        pack_ref[pl.ds(image + 16, 1), :] = total_row(crossed)
        return carry

    lax.fori_loop(0, 8, gather, 0)


def logits_kernel(where_ref, own_ref, other_ref, living_ref, labels_ref, hw_ref, hb_ref,
                  all_ref, errors_ref, cross_ref):
    pipe = where_ref[0]
    for block in range(3):
        rows = slice(block * 8, block * 8 + 8)
        all_ref[block, pl.ds(pl.multiple_of(pipe * 8, 8), 8), :] = own_ref[rows, :]
        all_ref[block, pl.ds(pl.multiple_of((1 - pipe) * 8, 8), 8), :] = other_ref[rows, :]
    logits = (
        lax.dot_general(
            all_ref[0], hw_ref[...], NT, precision=HIGHEST, preferred_element_type=F32
        )
        + hb_ref[...]
    )
    errors = living_ref[...] * (sigmoid(logits) - labels_ref[...])
    errors_ref[...] = errors
    cross_ref[...] = lax.dot_general(
        errors, errors, TN, precision=HIGHEST, preferred_element_type=F32
    )


def head_kernel(picks_ref, where_ref, facts_ref, c0, c1, c2, c3, heads_ref, hw_ref, errors_ref,
                all_ref, in_ref, section_ref, norm_ref, params_ref,
                low_ref, pool_ref, small_ref, alpha_ref, gram_ref):
    tasks = gram_ref.shape[0]
    pipe = where_ref[0]
    gram_ref[...] = ((c0[...] + c1[...]) + (c2[...] + c3[...])) * heads_ref[...]
    frank_wolfe_kernel(picks_ref, gram_ref, alpha_ref)
    grad_logits = (128.0 * tasks) * alpha_ref[...] * errors_ref[...]
    pooled, slopes, crossed = all_ref[0], all_ref[1], all_ref[2]
    grad_pool = (
        jnp.dot(grad_logits, hw_ref[...], precision=HIGHEST, preferred_element_type=F32)
        / 128.0
    )
    grad_sum = total_row(grad_pool * slopes)
    cross_sum = total_row(grad_pool * crossed)
    small_ref[0:tasks, :] = lax.dot_general(
        grad_logits, pooled, TN, precision=HIGHEST, preferred_element_type=F32
    )
    small_ref[tasks : tasks + 1, :] = grad_sum
    small_ref[tasks + 1 : tasks + 2, :] = cross_sum
    small_ref[tasks + 2 :, :] = jnp.zeros((small_ref.shape[0] - tasks - 2, 512), F32)
    for start in (0, 256):
        small_ref[tasks + 2 : tasks + 3, start : start + tasks] = total_row(grad_logits)
    pool_ref[...] = jnp.where(pipe == 0, grad_pool[0:8], grad_pool[8:16])

    mean, inverse = norm_ref[0:1, :], norm_ref[1:2, :]
    gain, bias = param(params_ref, G_SECOND), param(params_ref, B_SECOND)
    all_px = facts_ref[ALL_PX]
    front = gain * inverse
    mean_grad, mean_cross = grad_sum / all_px, cross_sum / all_px

    def back(image, carry):
        up = pool_ref[pl.ds(image, 1), :]
        for r in range(4):
            normed = (in_ref[image, band(r), :] - mean) * inverse
            pre = normed * gain + bias + section_ref[image, band(r), :].astype(F32)
            grad = up * slope_of(pre)
            fix = facts_ref[image] * (mean_grad + normed * mean_cross)
            low_ref[image, band(r), :] = (front * (grad - fix)).astype(BF16)
        return carry

    lax.fori_loop(0, 8, back, 0)


def back_norm(facts_ref, in_ref, up_ref, norm_ref, own_ref, other_ref, gain, rows, sinks):
    mean, inverse = norm_ref[rows : rows + 1, :], norm_ref[rows + 1 : rows + 2, :]
    all_px = facts_ref[ALL_PX]
    front = gain * inverse
    cross_row = 1 + rows // 2
    mean_grad = (own_ref[0:1, :] + other_ref[0:1, :]) / all_px
    mean_cross = (
        own_ref[cross_row : cross_row + 1, :] + other_ref[cross_row : cross_row + 1, :]
    ) / all_px

    def back(image, carry):
        for r in range(4):
            normed = (in_ref[image, band(r), :] - mean) * inverse
            fix = facts_ref[image] * (mean_grad + normed * mean_cross)
            sinks(image, r, (front * (up_ref[image, band(r), :] - fix)).astype(BF16))
        return carry

    lax.fori_loop(0, 8, back, 0)


def second_back_kernel(facts_ref, low_ref, in_ref, norm_ref, params_ref, w_ref,
                       up_ref, sum_ref, x_ref, conv_ref):
    def fill(image, carry):
        for r in range(4):
            put_band(x_ref, image, r, low_ref[image, band(r), :])
        return carry

    lax.fori_loop(0, 8, fill, 0)
    conv_core(x_ref, w_ref, conv_ref, True)
    gain, bias = param(params_ref, G_FIRST), param(params_ref, B_FIRST)
    slope_sums(facts_ref, in_ref, norm_ref, gain, bias, conv_ref, up_ref, sum_ref)


def slope_sums(facts_ref, in_ref, norm_ref, gain, bias, conv_ref, up_ref, sum_ref):
    mean, inverse = norm_ref[0:1, :], norm_ref[1:2, :]

    def slope(image, carry):
        grads, crosses = carry
        for r in range(4):
            normed = (in_ref[image, band(r), :] - mean) * inverse
            up = conv_ref[image, band(r), :] * slope_of(normed * gain + bias)
            up_ref[image, band(r), :] = up
            living = facts_ref[image]
            grads = grads + fold(up) * living
            crosses = crosses + fold(up * normed) * living
        return grads, crosses

    zero = jnp.zeros((8, 512), F32)
    grads, crosses = lax.fori_loop(0, 8, slope, (zero, zero))
    sum_ref[0:1, :] = total_row(grads)
    sum_ref[1:2, :] = total_row(crosses)
    sum_ref[2:8, :] = jnp.zeros((6, 512), F32)


def first_back_kernel(facts_ref, up_in, in_ref, norm_ref, own_ref, other_ref, params_ref, w_ref,
                      second_ref, norm2_ref, section_ref, pool_ref, mid_ref, short_ref, normd_ref,
                      low_ref, up_ref, sum_ref, x_ref, conv_ref):
    def keep(image, r, low):
        low_ref[image, band(r), :] = low
        put_band(x_ref, image, r, low)

    back_norm(facts_ref, in_ref, up_in, norm_ref, own_ref, other_ref, param(params_ref, G_FIRST),
              0, keep)
    conv_core(x_ref, w_ref, conv_ref, True)
    mean2, inv2 = norm2_ref[0:1, :], norm2_ref[1:2, :]
    gain2, bias2 = param(params_ref, G_SECOND), param(params_ref, B_SECOND)
    mean_m, inv_m = normd_ref[0:1, :], normd_ref[1:2, :]
    mean_s, inv_s = normd_ref[2:3, :], normd_ref[3:4, :]
    gain_m, gain_s = param(params_ref, G_MID), param(params_ref, G_SHORT)
    bias_m, bias_s = param(params_ref, B_MID), param(params_ref, B_SHORT)

    def join(image, carry):
        grads, cross_m, cross_s = carry
        pool = pool_ref[pl.ds(image, 1), :]
        for r in range(4):
            pre2 = (second_ref[image, band(r), :] - mean2) * inv2 * gain2 + bias2
            pre2 = pre2 + section_ref[image, band(r), :].astype(F32)
            entry = conv_ref[image, band(r), :] + pool * slope_of(pre2)
            entry = entry.astype(BF16).astype(F32)
            norm_m = (mid_ref[image, band(r), :] - mean_m) * inv_m
            norm_s = (short_ref[image, band(r), :] - mean_s) * inv_s
            pre = norm_m * gain_m + bias_m + norm_s * gain_s + bias_s
            up = entry * slope_of(pre)
            up_ref[image, band(r), :] = up
            living = facts_ref[image]
            grads = grads + fold(up) * living
            cross_m = cross_m + fold(up * norm_m) * living
            cross_s = cross_s + fold(up * norm_s) * living
        return grads, cross_m, cross_s

    zero = jnp.zeros((8, 512), F32)
    grads, cross_m, cross_s = lax.fori_loop(0, 8, join, (zero, zero, zero))
    sum_ref[0:1, :] = total_row(grads)
    sum_ref[1:2, :] = total_row(cross_m)
    sum_ref[2:3, :] = total_row(cross_s)
    sum_ref[3:8, :] = jnp.zeros((5, 512), F32)


def mid_back_kernel(facts_ref, up_in, mid_ref, short_ref, normd_ref, own_ref, other_ref, params_ref,
                    w_ref, in_ref, norm1_ref,
                    low_ref, low_s_ref, up_ref, sum_ref, x_ref, conv_ref):
    def keep(image, r, low):
        low_ref[image, band(r), :] = low
        put_band(x_ref, image, r, low)

    def keep_short(image, r, low):
        low_s_ref[image, band(r), :] = low

    gain_m, gain_s = param(params_ref, G_MID), param(params_ref, G_SHORT)
    back_norm(facts_ref, mid_ref, up_in, normd_ref, own_ref, other_ref, gain_m, 0, keep)
    back_norm(facts_ref, short_ref, up_in, normd_ref, own_ref, other_ref, gain_s, 2, keep_short)
    conv_core(x_ref, w_ref, conv_ref, True)
    gain, bias = param(params_ref, G_DOWN), param(params_ref, B_DOWN)
    slope_sums(facts_ref, in_ref, norm1_ref, gain, bias, conv_ref, up_ref, sum_ref)


def down_back_kernel(where_ref, facts_ref, up_in, in_ref, norm1_ref, own_ref, other_ref, params_ref,
                     low_s_ref, w_ref, s_ref, low_ref, o0, o1, o2, o3, stage_ref):
    pipe, batch, zone = where_ref[0], where_ref[1], where_ref[2]

    def keep(image, r, low):
        low_ref[image, band(r), :] = low

    gain = param(params_ref, G_DOWN)
    back_norm(facts_ref, in_ref, up_in, norm1_ref, own_ref, other_ref, gain, 0, keep)
    mine = pl.ds(batch * 2, 2)
    here = low_ref[mine]
    below = jnp.concatenate([here[:, 32:], jnp.zeros((2, 32, 512), BF16)], axis=1)
    here, below = here.reshape(256, 512), below.reshape(256, 512)
    short = low_s_ref[mine].reshape(256, 512)

    def back(lhs, row, col):
        return lax.dot_general(lhs, w_ref[row, col], NT, preferred_element_type=F32)

    even_even = back(here, 1, 1) + lax.dot_general(
        short, s_ref[...], NT, preferred_element_type=F32
    )
    even_odd = columns_joined(None, back(here, 1, 2), back(here, 1, 0))
    odd_even = back(here, 2, 1) + back(below, 0, 1)
    odd_odd = columns_joined(
        None, back(here, 2, 2) + back(below, 0, 2), back(here, 2, 0) + back(below, 0, 0)
    )
    planes = ((even_even, even_odd), (odd_even, odd_odd))
    for row in range(2):
        for par in range(2):
            plane = planes[row][par].reshape(2, 4, 32, 256).astype(BF16)
            lanes = slice(par * 128, par * 128 + 128)
            for side in range(2):
                half = plane[..., side * 128 : side * 128 + 128]
                for z in range(4):
                    stage_ref[z ^ zone, side ^ pipe, :, row, :, lanes] = half[:, z]
    for rel, out in enumerate((o0, o1, o2, o3)):
        out[...] = stage_ref[rel]


def image_grad_kernel(where_ref, own_ref, got_ref, out_ref):
    pipe, zone = where_ref[0], where_ref[2]
    for rel in range(4):
        for side, pieces in enumerate((own_ref, got_ref)):
            first = (zone ^ rel) * 4 + (pipe if side == 0 else 1 - pipe) * 2
            for i in range(2):
                for row in range(2):
                    for par in range(2):
                        out_ref[first + i, row, pl.ds(par, 32, stride=2), :] = pieces[
                            rel, i, row, :, par * 128 : (par + 1) * 128
                        ].astype(F32)


def slot_of(quarter, zone):
    rel = quarter ^ zone
    return (rel >> 1) | ((rel & 1) << 1)


def shifted_window(turned, down, right):
    pixel = lax.broadcasted_iota(jnp.int32, (1, 128), 1)
    column, row = pixel % 32 + right, pixel // 32 + down
    inside = (column >= 0) & (column < 32) & (row >= 0) & (row < 4)
    amount = (256 - down * 32 - right) % 128
    moved = turned if isinstance(amount, int) and amount == 0 else pltpu.roll(turned, amount, 1)
    return jnp.where(inside, moved, 0.0).astype(BF16)


def split_out(pipe, zone, unit, result_own, result_other, own_ref, other_ref):
    for quarter in range(4):
        slot = slot_of(quarter, zone)
        rows = slice(quarter * 32, quarter * 32 + 32)
        own_ref[slot, unit] = result_own[rows]
        other_ref[slot, unit] = result_other[rows].astype(BF16)


def turned_taps(batch, act_ref, turned_ref):
    lanes = pl.ds(pl.multiple_of(batch * 128, 128), 128)

    def turn(image, carry):
        turned = act_ref[image, :, lanes].astype(F32).T
        pixels = pl.ds(pl.multiple_of(image * 128, 128), 128)
        for row in range(3):
            for col in range(3):
                turned_ref[row * 3 + col, :, pixels] = shifted_window(turned, row - 1, col - 1)
        return carry

    lax.fori_loop(0, 8, turn, 0)


def tap_products(pipe, zone, low_ref, turned_ref, own_ref, other_ref):
    lhs = turned_ref[0:9].reshape(9 * 128, 1024)
    results = []
    for side in (pipe, 1 - pipe):
        columns = pl.ds(pl.multiple_of(side * 256, 256), 256)
        rhs = low_ref[:, :, columns].reshape(1024, 256)
        results.append(jnp.dot(lhs, rhs, preferred_element_type=F32))
    for unit in range(9):
        rows = slice(unit * 128, unit * 128 + 128)
        split_out(pipe, zone, unit, results[0][rows], results[1][rows], own_ref, other_ref)


def kernel_grad_kernel(where_ref, act_ref, low_ref, own_ref, other_ref, turned_ref):
    pipe, batch, zone = where_ref[0], where_ref[1], where_ref[2]
    turned_taps(batch, act_ref, turned_ref)
    tap_products(pipe, zone, low_ref, turned_ref, own_ref, other_ref)


DOWN_UNITS = (
    ((0, 0, 0, 4), (2, -1, 0, 1), (2, 0, 0, 7), (0, 0, 0, 9), (1, 0, 0, 5)),
    ((1, 0, -1, 3), (3, -1, -1, 0), (3, -1, 0, 2), (3, 0, -1, 6), (3, 0, 0, 8)),
)


def down_grad_kernel(where_ref, img_ref, low_ref, low_s_ref, own_ref, other_ref, turned_ref):
    pipe, batch, zone = where_ref[0], where_ref[1], where_ref[2]
    upper, part = batch // 2, batch % 2

    for turn_kind in range(2):

        @pl.when(upper == turn_kind)
        def _(units=DOWN_UNITS[turn_kind]):
            def turn(image, carry):
                pixels = pl.ds(pl.multiple_of(image * 128, 128), 128)
                seen = {}
                for unit, (plane, down, right, _) in enumerate(units):
                    if plane not in seen:
                        lanes = pl.ds(pl.multiple_of(plane * 256 + part * 128, 128), 128)
                        seen[plane] = img_ref[image, :, lanes].astype(F32).T
                    turned_ref[unit, :, pixels] = shifted_window(seen[plane], down, right)
                return carry

            lax.fori_loop(0, 8, turn, 0)

    short_unit = [tap for _, _, _, tap in DOWN_UNITS[0]].index(9)
    for unit in range(5):
        lhs = turned_ref[unit]
        results = []
        for side in (pipe, 1 - pipe):
            columns = pl.ds(pl.multiple_of(side * 256, 256), 256)
            rhs = low_ref[:, :, columns].reshape(1024, 256)
            if unit == short_unit:
                rhs_s = low_s_ref[:, :, columns].reshape(1024, 256)
                rhs = jnp.where(upper == 0, rhs_s, rhs)
            results.append(jnp.dot(lhs, rhs, preferred_element_type=F32))
        split_out(pipe, zone, unit, results[0], results[1], own_ref, other_ref)


def gathered_blocks(zone, batch, refs):
    a, b, ax, by, ayy, bxx = refs
    sets = {0: (a, b, 0, 0), 1: (ax, bxx, 0, 0), 2: (ayy, by, 0, 0), 3: (ayy, bxx, 2, 2)}
    for kb in range(4):
        even, odd, base_even, base_odd = sets[kb]
        for rel in range(4):
            if rel % 2 == 1:
                yield batch ^ kb, zone ^ rel, odd, base_odd + rel // 2
            else:
                yield batch ^ kb, zone ^ rel, even, base_even + rel // 2


def assemble_kernel(where_ref, *refs):
    pieces, out_ref = refs[:6], refs[6]
    batch, zone = where_ref[1], where_ref[2]
    for owner, quarter, ref, index in gathered_blocks(zone, batch, pieces):
        rows = pl.ds(pl.multiple_of(owner * 128 + quarter * 32, 32), 32)
        out_ref[:, rows, :] = ref[index].astype(F32)


def assemble_down_kernel(where_ref, *refs):
    pieces, (out_ref, short_ref) = refs[:6], refs[6:]
    batch, zone = where_ref[1], where_ref[2]
    for owner, quarter, ref, index in gathered_blocks(zone, batch, pieces):
        upper, part = owner // 2, owner % 2
        rows = pl.ds(pl.multiple_of(part * 128 + quarter * 32, 32), 32)
        value = ref[index].astype(F32)
        for kind in range(2):

            @pl.when(upper == kind)
            def _(value=value, rows=rows, units=DOWN_UNITS[kind]):
                for unit, (_, _, _, tap) in enumerate(units):
                    if tap == 9:
                        short_ref[rows, :] = value[unit]
                    else:
                        out_ref[tap, rows, :] = value[unit]


def facts_kernel(where_ref, p0, p1, p2, p3, hw_ref, facts_ref, living_ref, targets_ref, heads_ref):
    pipe, batch = where_ref[0], where_ref[1]
    tasks = hw_ref.shape[0]
    alive = [jnp.float32(0.0), jnp.float32(0.0)]
    for rel, piece in enumerate((p0, p1, p2, p3)):
        owner = batch ^ rel
        marks = piece[MARKS:, 0:tasks].astype(F32)
        count = jnp.max(marks[4:5, :])
        for slot in range(4):
            side, place = slot // 2, owner * 2 + slot % 2
            living = (count > slot + 0.5).astype(F32)
            alive[side] = alive[side] + living
            row = pl.ds(side * 8 + place, 1)
            living_ref[row, :] = jnp.full((1, tasks), living)
            targets_ref[row, :] = marks[slot : slot + 1, :]

            @pl.when(pipe == side)
            def _(place=place, living=living):
                facts_ref[place] = living

    own = jnp.where(pipe == 0, alive[0], alive[1])
    facts_ref[OWN_PX] = own * 128.0
    facts_ref[OTHER_PX] = (alive[0] + alive[1] - own) * 128.0
    facts_ref[ALL_PX] = (alive[0] + alive[1]) * 128.0
    for rest in range(ALL_PX + 1, 16):
        facts_ref[rest] = jnp.float32(0.0)
    heads_ref[...] = lax.dot_general(
        hw_ref[...], hw_ref[...], NT, precision=HIGHEST, preferred_element_type=F32
    )


SMALL_ROWS = 64


def small_kernel(where_ref, head_ref, all_ref, sum_f, other_f, sum_j, other_j, sum_d, other_d,
                 sent_ref, wide_ref):
    pipe, batch = where_ref[0], where_ref[1]
    tasks = head_ref.shape[0] - 8
    wide_ref[...] = jnp.zeros(wide_ref.shape, F32)
    wide_ref[0 : tasks + 3, :] = head_ref[0 : tasks + 3, :]
    at = tasks + 3
    for own, other, count in ((sum_f, other_f, 2), (sum_j, other_j, 3), (sum_d, other_d, 2)):
        wide_ref[at : at + count, :] = own[0:count, :] + other[0:count, :]
        at += count
    for side in range(2):
        for slot in range(2):
            row = side * 8 + batch * 2 + slot
            at_row = SMALL_ROWS - 8 + side * 2 + slot
            wide_ref[at_row : at_row + 1, :] = all_ref[0, pl.ds(row, 1), :]
    sent_ref[...] = wide_ref[:, pl.ds(pl.multiple_of(pipe * 256, 256), 256)]


def small_out_kernel(where_ref, p0, p1, p2, p3, pooled_ref, head_ref, gd_ref, bd_ref, gp_ref, bp_ref,
                     headb_ref):
    tasks = head_ref.shape[0]
    zone = where_ref[2]
    for rel, part in enumerate((p0, p1, p2, p3)):
        pooled_ref[zone ^ rel] = part[SMALL_ROWS - 8 : SMALL_ROWS - 4, :]
    total = (p0[...] + p1[...]) + (p2[...] + p3[...])
    head_ref[...] = total[0:tasks]

    def line(at):
        return total[tasks + at : tasks + at + 1]

    headb_ref[...] = line(2)
    bp_ref[0:1, :], gp_ref[0:1, :] = line(3), line(4)
    bp_ref[1:2, :], gp_ref[1:2, :] = line(0), line(1)
    bd_ref[0:1, :], gd_ref[0:1, :] = line(8), line(9)
    bd_ref[1:2, :], gd_ref[1:2, :] = line(5), line(6)
    bd_ref[2:3, :], gd_ref[2:3, :] = line(5), line(7)


def fast_device(images, image_counts, labels, fw_picks, conv_down, conv_mid, shortcut, gains_down,
                biases_down, conv_first, conv_second, gains_plain, biases_plain, head_weight,
                head_bias):
    pipe, batch, zone = (lax.axis_index(axis) for axis in ("pipe", "batch", "space"))
    tasks = head_weight.shape[1]

    def over(axis, rel, x):
        size = lax.axis_size(axis)
        return lax.ppermute(x, axis, [(i, i ^ rel) for i in range(size)])

    where = jnp.stack([pipe, batch, zone, zone]).astype(jnp.int32)
    params = jnp.concatenate([gains_down, biases_down, gains_plain, biases_plain])
    turned_heads = head_weight.T
    bias_row = head_bias.reshape(1, tasks)

    pieces = call(
        pieces_kernel,
        [((144, 512), BF16)] + [((128, 512), BF16)] * 3,
        [where, images, lax.dynamic_slice_in_dim(labels, zone * 4, 4, 0),
         lax.dynamic_slice_in_dim(image_counts, zone, 1, 1)],
        [pltpu.VMEM((64, 128), F32)],
        name="pieces",
    )
    moved = [over("space", rel, pieces[rel]) for rel in (1, 2, 3)]
    moved = [pieces[0], moved[0], jnp.concatenate([moved[1], moved[2]])]
    gathered = [moved] + [[over("batch", kb, x) for x in moved] for kb in (1, 2, 3)]
    facts, living, targets, heads = call(
        facts_kernel,
        [((16,), F32), ((16, tasks), F32), ((16, tasks), F32), ((tasks, tasks), F32)],
        [where] + [line[0] for line in gathered] + [turned_heads],
        name="facts",
    )

    big = ((8, 128, 512), F32)
    low = ((8, 128, 512), BF16)
    rows = ((8, 512), F32)
    x_scratch = pltpu.VMEM((8, 128, 1536), BF16)
    conv_scratch = pltpu.VMEM((8, 128, 512), F32)
    conv_flops = 2 * 1024 * 4608 * 512

    def partner(x):
        return over("pipe", 1, x)

    img, down_out, short_out, stat_d = call(
        down_kernel,
        [((8, 128, 1024), BF16), big, big, rows],
        [facts, where] + [piece for line in gathered for piece in line] + [conv_down, shortcut],
        [pltpu.VMEM((8, 128, 512), BF16)],
        conv_flops // 2,
        "down",
    )
    other_d = partner(stat_d)
    down_act, mid_out, stat_m, norm_d = call(
        lambda *refs: layer_kernel(G_DOWN, B_DOWN, *refs),
        [low, big, rows, rows],
        [facts, down_out, stat_d, other_d, params, conv_mid],
        [x_scratch],
        conv_flops,
        "mid",
    )
    other_m = partner(stat_m)
    section, first_out, stat_f, norm_j = call(
        join_kernel,
        [low, big, rows, rows],
        [facts, mid_out, short_out, stat_m, other_m, stat_d, other_d, params, conv_first],
        [x_scratch],
        conv_flops,
        "first",
    )
    other_f = partner(stat_f)
    plain_act, second_out, stat_s, norm_f = call(
        lambda *refs: layer_kernel(G_FIRST, B_FIRST, *refs),
        [low, big, rows, rows],
        [facts, first_out, stat_f, other_f, params, conv_second],
        [x_scratch],
        conv_flops,
        "second",
    )
    other_s = partner(stat_s)
    pack, norm_s = call(
        block_kernel,
        [((24, 512), F32), rows],
        [facts, second_out, section, stat_s, other_s, params],
        name="block",
    )
    other_pack = partner(pack)
    all_pack, errors, cross = call(
        logits_kernel,
        [((3, 16, 512), F32), ((16, tasks), F32), ((tasks, tasks), F32)],
        [where, pack, other_pack, living, targets, turned_heads, bias_row],
        name="logits",
    )
    crosses = [cross] + [over("space", rel, cross) for rel in (1, 2, 3)]
    second_low, grad_pool, small = call(
        head_kernel,
        [low, rows, ((tasks + 8, 512), F32)],
        [fw_picks, where, facts] + crosses
        + [heads, turned_heads, errors, all_pack, second_out, section, norm_s, params],
        [pltpu.VMEM((1, tasks), F32), pltpu.VMEM((tasks, tasks), F32)],
        name="head",
    )

    class Sum:
        def __init__(self, own, other):
            self.own, self.other = own, other

        def cores(self):
            self.both = self.own + partner(self.other).astype(F32)
            self.sent = self.both[1:].astype(BF16)

        def zones(self):
            got = [over("space", rel, self.sent[slot]).astype(F32)
                   for slot, rel in ((1, 1), (0, 2), (2, 3))]
            self.final = ((self.both[0] + got[0]) + (got[1] + got[2])).astype(BF16)

        def near(self):
            self.far = over("space", 2, self.final)
            self.a = jnp.stack([self.final, self.far])

        def ends(self):
            self.b = over("space", 1, self.a)

        def plane(self):
            self.ax, self.by = over("batch", 1, self.a), over("batch", 2, self.b)

        def plane_far(self):
            self.ayy = over("batch", 2, jnp.concatenate([self.a, self.ax]))
            self.bxx = over("batch", 1, jnp.concatenate([self.b, self.by]))

        def blocks(self):
            return [where, self.a, self.b, self.ax, self.by, self.ayy, self.bxx]

    def kernel_grad_of(act, low_grad, name, after=()):
        return Sum(*call(
            kernel_grad_kernel,
            [((4, 9, 32, 256), F32), ((4, 9, 32, 256), BF16)],
            [where, act, low_grad],
            [pltpu.VMEM((9, 128, 1024), BF16)],
            conv_flops // 4,
            name,
            after,
        ))

    def assembled(blocks, name, after=()):
        (out,) = call(assemble_kernel, [((9, 512, 256), F32)], blocks, name=name, after=after)
        return out.reshape(3, 3, 512, 256)

    second = kernel_grad_of(plain_act, second_low, "second_grad")
    up_f, sum_f = call(
        second_back_kernel,
        [big, rows],
        [facts, second_low, first_out, norm_f, params, conv_second],
        [x_scratch, conv_scratch],
        conv_flops,
        "second_back",
        after=[second.other],
    )
    other_sf = partner(sum_f)
    second.cores()
    first_low, up_j, sum_j = call(
        first_back_kernel,
        [low, big, rows],
        [facts, up_f, first_out, norm_f, sum_f, other_sf, params, conv_first,
         second_out, norm_s, section, grad_pool, mid_out, short_out, norm_j],
        [x_scratch, conv_scratch],
        conv_flops,
        "first_back",
        after=[second.sent],
    )
    other_sj = partner(sum_j)
    second.zones()
    first = kernel_grad_of(section, first_low, "first_grad")
    first.cores()
    mid_low, short_low, up_d, sum_d = call(
        mid_back_kernel,
        [low, low, big, rows],
        [facts, up_j, mid_out, short_out, norm_j, sum_j, other_sj, params, conv_mid,
         down_out, norm_d],
        [x_scratch, conv_scratch],
        conv_flops,
        "mid_back",
        after=[first.sent, second.final],
    )
    other_sd = partner(sum_d)
    second.near()
    first.zones()
    mid = kernel_grad_of(down_act, mid_low, "mid_grad")
    mid.cores()
    second.ends()
    down_low, *img_pieces = call(
        down_back_kernel,
        [low] + [((2, 2, 2, 32, 256), BF16)] * 4,
        [where, facts, up_d, down_out, norm_d, sum_d, other_sd, params, short_low, conv_down,
         shortcut],
        [pltpu.VMEM((4, 2, 2, 2, 32, 256), BF16)],
        conv_flops // 8,
        "down_back",
        after=[second.a, mid.other],
    )
    down = Sum(*call(
        down_grad_kernel,
        [((4, 5, 32, 256), F32), ((4, 5, 32, 256), BF16)],
        [where, img, down_low, short_low],
        [pltpu.VMEM((5, 128, 1024), BF16)],
        conv_flops // 8,
        "down_grad",
        after=[second.b, mid.sent, first.final],
    ))
    down.cores()
    first.near()
    first.ends()
    second.plane()
    second.plane_far()
    mid.zones()
    first.plane()
    first.plane_far()
    mid.near()
    mid.ends()
    down.zones()
    down.near()
    down.ends()
    mid.plane()
    mid.plane_far()
    down.plane()
    down.plane_far()
    second_out_grad = assembled(second.blocks(), "second_out")
    first_out_grad = assembled(first.blocks(), "first_out")
    mid_out_grad = assembled(mid.blocks(), "mid_out")

    img_moved = [img_pieces[0]] + [over("space", rel, img_pieces[rel]) for rel in (1, 2, 3)]
    img_moved = jnp.stack(img_moved)
    img_got = partner(img_moved[:, 1])
    (images_grad,) = call(
        image_grad_kernel,
        [((16, 2, 64, 128), F32)],
        [where, img_moved[:, 0], img_got],
        name="image_grad",
    )

    (sent,) = call(
        small_kernel,
        [((SMALL_ROWS, 256), F32)],
        [where, small, all_pack, sum_f, other_sf, sum_j, other_sj, sum_d, other_sd],
        [pltpu.VMEM((SMALL_ROWS, 512), F32)],
        name="small",
    )
    parts = [sent] + [over("space", rel, sent) for rel in (1, 2, 3)]
    pooled, head_out, gains_d, sums_d, gains_p, sums_p, head_b = call(
        small_out_kernel,
        [((4, 4, 256), F32), ((tasks, 256), F32), ((3, 256), F32), ((3, 256), F32),
         ((2, 256), F32), ((2, 256), F32), ((1, 256), F32)],
        [where] + parts,
        name="small_out",
    )
    down_grad, short_grad = call(
        assemble_down_kernel,
        [((9, 256, 256), F32), ((256, 256), F32)],
        down.blocks(),
        name="down_out",
    )
    return (
        pooled.reshape(16, 256),
        images_grad,
        down_grad.reshape(3, 3, 256, 256),
        mid_out_grad,
        short_grad,
        gains_d,
        sums_d,
        first_out_grad,
        second_out_grad,
        gains_p,
        sums_p,
        head_out.T,
        lax.dynamic_slice_in_dim(head_b[0], pipe * (tasks // 2), tasks // 2, 0),
    )


def per_device(
    images,
    image_counts,
    labels,
    fw_picks,
    conv_down,
    conv_mid,
    shortcut,
    gains_down,
    biases_down,
    conv_first,
    conv_second,
    gains_plain,
    biases_plain,
    head_weight,
    head_bias,
):
    layout = Layout(image_counts.shape[1])
    micros, zone = layout.micros, layout.zone
    sizes = (images.shape, conv_down.shape, lax.axis_size("pipe"), lax.axis_size("batch"))
    if layout.groups == 1 and sizes == ((16, 2, 64, 256), (3, 3, 256, 512), 2, 4):
        return fast_device(
            images, image_counts, labels, fw_picks, conv_down, conv_mid, shortcut, gains_down,
            biases_down, conv_first, conv_second, gains_plain, biases_plain, head_weight,
            head_bias,
        )
    batches, pipes = lax.axis_size("batch"), lax.axis_size("pipe")
    batch = lax.axis_index("batch")
    pipe = lax.axis_index("pipe")
    per_micro = images.shape[0] // micros
    count = per_micro * batches
    entering, channels = conv_down.shape[2], conv_mid.shape[3]
    tasks = head_weight.shape[1]
    half = channels // pipes
    own = pipe * half

    def own_out(kernel, axis):
        size = kernel.shape[axis] // pipes
        return lax.dynamic_slice_in_dim(kernel, pipe * size, size, axis)

    def whole(tensor, axis=3):
        return lax.all_gather(tensor, "pipe", axis=axis, tiled=True)

    def share(tensor):
        size = tensor.shape[3] // batches
        return lax.dynamic_slice_in_dim(tensor, batch * size, size, 3)

    mine = lax.all_to_all(
        images, "space", 0, 1, axis_index_groups=layout.inner, tiled=True
    )
    mine = lax.all_gather(mine, "batch", axis=0, tiled=True)
    counts = lax.all_gather(image_counts, "batch", axis=0, tiled=True)
    counts = lax.dynamic_slice_in_dim(counts, zone, 1, 1)[:, 0]
    marks = lax.dynamic_slice_in_dim(labels, zone * per_micro, per_micro, 0)
    targets = lax.all_gather(marks, "batch", axis=0, tiled=True).astype(F32)
    slots = jnp.arange(per_micro, dtype=jnp.int32)
    living = (slots[None, :] < counts[:, None]).astype(F32).reshape(count)
    weight = living[:, None, None, None]
    out_rows, out_cols = mine.shape[1] // 2, mine.shape[2] // 2
    image_pixels = out_rows * layout.groups * out_cols
    counted = jnp.sum(living) * image_pixels
    scale = float(image_pixels * tasks)

    gain_d, bias_d = own_out(gains_down, 1), own_out(biases_down, 1)
    gain_p, bias_p = own_out(gains_plain, 1), own_out(biases_plain, 1)

    above = layout.row_from(mine[:, -1:], 1)
    down_ext = jnp.pad(
        jnp.concatenate([above, mine], axis=1), ((0, 0), (0, 0), (1, 0), (0, 0))
    )
    down_out = conv_valid(down_ext, own_out(conv_down, 3), 2)
    down_norm, down_inv = norm_forward(layout, down_out, weight, counted)
    down_pre = down_norm * gain_d[0] + bias_d[0]
    mid_ext = layout.rims(whole(jax.nn.silu(down_pre).astype(BF16)))
    mid_out = conv_valid(mid_ext, own_out(conv_mid, 3), 1)
    short_in = mine[:, ::2, ::2]
    short_out = jnp.einsum(
        "nhwi,io->nhwo", short_in, own_out(shortcut, 1), preferred_element_type=F32
    )
    mid_norm, mid_inv = norm_forward(layout, mid_out, weight, counted)
    short_norm, short_inv = norm_forward(layout, short_out, weight, counted)
    section_pre = mid_norm * gain_d[1] + bias_d[1] + short_norm * gain_d[2] + bias_d[2]
    section = jax.nn.silu(section_pre).astype(BF16)
    first_ext = layout.rims(whole(section))
    first_out = conv_valid(first_ext, own_out(conv_first, 3), 1)
    first_norm, first_inv = norm_forward(layout, first_out, weight, counted)
    first_pre = first_norm * gain_p[0] + bias_p[0]
    second_ext = layout.rims(whole(jax.nn.silu(first_pre).astype(BF16)))
    second_out = conv_valid(second_ext, own_out(conv_second, 3), 1)
    second_norm, second_inv = norm_forward(layout, second_out, weight, counted)
    block_pre = second_norm * gain_p[1] + bias_p[1] + section.astype(F32)
    pooled = layout.group_sum(jnp.sum(jax.nn.silu(block_pre), axis=(1, 2))) / image_pixels

    pooled_all = whole(pooled, 1)
    logits = jnp.dot(pooled_all, head_weight, precision=HIGHEST) + head_bias
    errors = living[:, None] * (jax.nn.sigmoid(logits) - targets)
    cross = jnp.einsum("nt,ns->ts", errors, errors, precision=HIGHEST)
    cross = lax.psum(cross, "space", axis_index_groups=layout.inner)
    gram = cross * jnp.dot(head_weight.T, head_weight, precision=HIGHEST)
    alpha = frank_wolfe(gram, fw_picks)
    grad_logits = scale * alpha * errors
    head_w = jnp.einsum("nc,nt->ct", pooled, grad_logits, precision=HIGHEST)
    head_b = jnp.sum(grad_logits, axis=0)
    head_own = own_out(head_weight, 0)
    grad_pool = jnp.einsum("nt,ct->nc", grad_logits, head_own, precision=HIGHEST) / image_pixels

    grad_block = grad_pool[:, None, None, :] * silu_slope(block_pre)
    second_low, second_cross, second_sum = norm_back(
        layout, grad_block, second_norm, second_inv, gain_p[1], weight, counted
    )
    second_kernel = kernel_grad(share(second_ext), second_low, 1)
    act_grad = conv_valid(layout.rims(whole(second_low)), flipped(own_out(conv_second, 2)), 1)
    first_low, first_cross, first_sum = norm_back(
        layout, act_grad * silu_slope(first_pre), first_norm, first_inv, gain_p[0], weight, counted
    )
    first_kernel = kernel_grad(share(first_ext), first_low, 1)
    entry_grad = conv_valid(layout.rims(whole(first_low)), flipped(own_out(conv_first, 2)), 1)
    entry_grad = (entry_grad + grad_block).astype(BF16).astype(F32)
    grad_section = entry_grad * silu_slope(section_pre)
    mid_low, mid_cross, mid_sum = norm_back(
        layout, grad_section, mid_norm, mid_inv, gain_d[1], weight, counted
    )
    short_low, short_cross, short_sum = norm_back(
        layout, grad_section, short_norm, short_inv, gain_d[2], weight, counted
    )
    mid_kernel = kernel_grad(share(mid_ext), mid_low, 1)
    short_kernel = jnp.einsum(
        "nhwi,nhwo->io", share(short_in), short_low, preferred_element_type=F32
    )
    act_grad = conv_valid(layout.rims(whole(mid_low)), flipped(own_out(conv_mid, 2)), 1)
    down_low, down_cross, down_sum = norm_back(
        layout, act_grad * silu_slope(down_pre), down_norm, down_inv, gain_d[0], weight, counted
    )
    down_kernel = kernel_grad(share(down_ext), down_low, 2)

    kept = lax.dynamic_slice_in_dim(whole(down_low), batch * per_micro, per_micro, 0)
    below = layout.row_from(kept[:, :1], -1)
    spread = lax.conv_general_dilated(
        jnp.concatenate([kept, below], axis=1),
        flipped(own_out(conv_down, 2)),
        (1, 1),
        ((2, 2), (2, 2)),
        lhs_dilation=(2, 2),
        dimension_numbers=NUMBERS,
        preferred_element_type=F32,
    )[:, 1 : 2 * out_rows + 1, 1:]
    short_kept = lax.dynamic_slice_in_dim(whole(short_low), batch * per_micro, per_micro, 0)
    spread = spread.at[:, ::2, ::2].add(
        jnp.einsum(
            "nhwo,io->nhwi", short_kept, own_out(shortcut, 0), preferred_element_type=F32
        )
    )
    images_grad = lax.all_to_all(
        spread.astype(BF16), "space", 1, 0, axis_index_groups=layout.inner, tiled=True
    ).astype(F32)

    def total(kernel, axis):
        summed = lax.psum(kernel.astype(BF16), "space")
        return lax.all_gather(summed, "batch", axis=axis, tiled=True).astype(F32)

    pooled_out = lax.dynamic_slice_in_dim(pooled, batch * per_micro, per_micro, 0)
    pooled_out = lax.all_gather(
        pooled_out, "space", axis_index_groups=layout.inner, axis=0, tiled=True
    )
    head_w, head_b = lax.psum((head_w, head_b), "space", axis_index_groups=layout.inner)
    gains_d, sums_d, gains_p, sums_p = lax.psum(
        (
            jnp.stack([down_cross, mid_cross, short_cross]),
            jnp.stack([down_sum, mid_sum, short_sum]),
            jnp.stack([first_cross, second_cross]),
            jnp.stack([first_sum, second_sum]),
        ),
        "space",
    )
    return (
        pooled_out,
        images_grad,
        total(down_kernel, 1).reshape(3, 3, entering, half),
        total(mid_kernel, 1).reshape(3, 3, channels, half),
        total(short_kernel, 0),
        gains_d,
        sums_d,
        total(first_kernel, 1).reshape(3, 3, channels, half),
        total(second_kernel, 1).reshape(3, 3, channels, half),
        gains_p,
        sums_p,
        head_w,
        own_out(head_b, 0),
    )


def solution(mesh):
    placed = (
        P("batch", "space", None, None),
        P("batch", None),
        P("batch", None),
    ) + (P(),) * 12
    return jax.shard_map(
        per_device,
        mesh=mesh,
        in_specs=placed,
        out_specs=(
            P("batch", "pipe"),
            P("batch", "space", None, "pipe"),
            P(None, None, None, "pipe"),
            P(None, None, None, "pipe"),
            P(None, "pipe"),
            P(None, "pipe"),
            P(None, "pipe"),
            P(None, None, None, "pipe"),
            P(None, None, None, "pipe"),
            P(None, "pipe"),
            P(None, "pipe"),
            P("pipe", None),
            P("pipe"),
        ),
        check_vma=False,
    )
```

```python
import jax
import jax.numpy as jnp
from jax import lax
from jax.experimental import pallas as pl
from jax.experimental.pallas import tpu as pltpu
from jax.sharding import PartitionSpec as P

EPSILON = 1e-05
NUMBERS = ("NHWC", "HWIO", "NHWC")
HIGHEST = lax.Precision.HIGHEST
F32 = jnp.float32
BF16 = jnp.bfloat16


def silu_slope(values):
    sigmoid = jax.nn.sigmoid(values)
    return sigmoid * (1.0 + values * (1.0 - sigmoid))


def frank_wolfe_kernel(picks_ref, gram_ref, alpha_ref):
    tasks = gram_ref.shape[0]
    lanes = lax.broadcasted_iota(jnp.int32, (1, tasks), 1)
    gram = gram_ref[...]
    alpha = jnp.full((1, tasks), 1.0 / tasks, F32)
    pulled = jnp.sum(gram, axis=0, keepdims=True) * (1.0 / tasks)
    energy = jnp.sum(pulled * alpha, axis=1, keepdims=True)

    def advance(step, carry):
        alpha, pulled, energy = carry
        chosen = picks_ref[step]
        row = gram_ref[pl.ds(chosen, 1), :]
        onehot = (lanes == chosen).astype(F32)
        toward = jnp.sum(pulled * onehot, axis=1, keepdims=True)
        corner = jnp.sum(row * onehot, axis=1, keepdims=True)
        denom = jnp.maximum(energy - 2.0 * toward + corner, 0.05 * corner)
        ratio = jnp.clip((energy - toward) / denom, 0.0, 1.0)
        rest = 1.0 - ratio
        alpha = rest * alpha + ratio * onehot
        pulled = rest * pulled + ratio * row
        energy = rest * rest * energy + 2.0 * rest * ratio * toward + ratio * ratio * corner
        return alpha, pulled, energy

    alpha, _, _ = lax.fori_loop(0, picks_ref.shape[0], advance, (alpha, pulled, energy))
    alpha_ref[...] = alpha


def frank_wolfe(gram, picks):
    tasks = gram.shape[0]
    return pl.pallas_call(
        frank_wolfe_kernel,
        out_shape=jax.ShapeDtypeStruct((1, tasks), F32),
        in_specs=[
            pl.BlockSpec(memory_space=pltpu.SMEM),
            pl.BlockSpec(memory_space=pltpu.VMEM),
        ],
        out_specs=pl.BlockSpec(memory_space=pltpu.VMEM),
    )(picks, gram)


class Layout:
    def __init__(self, micros):
        self.micros = micros
        self.spaces = lax.axis_size("space")
        self.groups = self.spaces // micros
        self.inner = [
            [group * micros + zone for zone in range(micros)] for group in range(self.groups)
        ]
        self.outer = [
            [group * micros + zone for group in range(self.groups)] for zone in range(micros)
        ]
        self.zone = lax.axis_index("space") % micros

    def group_sum(self, tree):
        if self.groups == 1:
            return tree
        return lax.psum(tree, "space", axis_index_groups=self.outer)

    def row_from(self, block, step):
        span = step * self.micros
        route = [
            (i, i + span) for i in range(self.spaces) if 0 <= i + span < self.spaces
        ]
        if not route:
            return jnp.zeros_like(block)
        return lax.ppermute(block, "space", route)

    def rims(self, tensor):
        above = self.row_from(tensor[:, -1:], 1)
        below = self.row_from(tensor[:, :1], -1)
        grown = jnp.concatenate([above, tensor, below], axis=1)
        return jnp.pad(grown, ((0, 0), (0, 0), (1, 1), (0, 0)))


def conv_valid(extended, kernel, stride):
    return lax.conv_general_dilated(
        extended,
        kernel,
        (stride, stride),
        "VALID",
        dimension_numbers=NUMBERS,
        preferred_element_type=F32,
    )


def flipped(kernel):
    return jnp.swapaxes(kernel[::-1, ::-1], 2, 3)


def kernel_grad(extended, grad_low, stride):
    rows, cols = grad_low.shape[1], grad_low.shape[2]
    taps = []
    for row_tap in range(3):
        for col_tap in range(3):
            window = extended[
                :,
                row_tap : row_tap + stride * (rows - 1) + 1 : stride,
                col_tap : col_tap + stride * (cols - 1) + 1 : stride,
            ]
            taps.append(jnp.einsum("nhwi,nhwo->io", window, grad_low, preferred_element_type=F32))
    return jnp.stack(taps)


def norm_forward(layout, conv_out, weight, counted):
    total = layout.group_sum(jnp.sum(conv_out * weight, axis=(0, 1, 2)))
    centered = conv_out - total / counted
    spread = layout.group_sum(jnp.sum(centered * centered * weight, axis=(0, 1, 2)))
    inverse = lax.rsqrt(spread / counted + EPSILON)
    return centered * inverse, inverse


def norm_back(layout, upstream, normed, inverse, gain, weight, counted):
    grad_sum = jnp.sum(upstream * weight, axis=(0, 1, 2))
    cross_sum = jnp.sum(upstream * normed * weight, axis=(0, 1, 2))
    grad_total, cross_total = layout.group_sum((grad_sum, cross_sum))
    correction = weight * (grad_total / counted + normed * (cross_total / counted))
    low = (gain * inverse * (upstream - correction)).astype(BF16)
    return low, cross_sum, grad_sum


KERNEL_LIMIT = 24 * 2**20
VM = pl.BlockSpec(memory_space=pltpu.VMEM)
SM = pl.BlockSpec(memory_space=pltpu.SMEM)
NT = (((1,), (1,)), ((), ()))
TN = (((0,), (0,)), ((), ()))
OWN_PX, OTHER_PX, ALL_PX = 8, 9, 10
G_DOWN, G_MID, G_SHORT, B_DOWN, B_MID, B_SHORT, G_FIRST, G_SECOND, B_FIRST, B_SECOND = range(10)


def param(params_ref, row):
    return params_ref[row : row + 1, :]


def call(kernel, outs, operands, scratch=(), flops=0, name=None, after=(), specs=None):
    count = len(operands)
    nbytes = sum(x.size * x.dtype.itemsize for x in operands)
    specs = specs or {}

    def body(*refs):
        kernel(*refs[:count], *refs[count + len(after) :])

    return pl.pallas_call(
        body,
        out_shape=tuple(jax.ShapeDtypeStruct(shape, dtype) for shape, dtype in outs),
        in_specs=[specs.get(i, SM if x.ndim == 1 else VM) for i, x in enumerate(operands)]
        + [pl.BlockSpec(memory_space=pl.ANY)] * len(after),
        out_specs=tuple(SM if len(shape) == 1 else VM for shape, _ in outs),
        scratch_shapes=list(scratch),
        compiler_params=pltpu.CompilerParams(vmem_limit_bytes=KERNEL_LIMIT),
        cost_estimate=pl.CostEstimate(
            flops=int(flops), bytes_accessed=int(nbytes), transcendentals=0
        ),
        name=name,
    )(*operands, *after)


def fold(rows):
    return rows[0:8] + rows[8:16] + rows[16:24] + rows[24:32]


def total_row(part):
    return jnp.sum(part, axis=0, keepdims=True)


def band(row):
    return slice(row * 32, row * 32 + 32)


def put_band(x_ref, image, row, value):
    zero = jnp.zeros_like(value)
    x_ref[image, band(row), 512:1024] = value
    if row < 3:
        x_ref[image, band(row + 1), 0:512] = value
    else:
        x_ref[image, band(0), 0:512] = zero
    if row > 0:
        x_ref[image, band(row - 1), 1024:1536] = value
    else:
        x_ref[image, band(3), 1024:1536] = zero


def columns_joined(left, middle, right):
    count = middle.shape[0]
    column = lax.broadcasted_iota(jnp.int32, (count, 1), 0) % 32
    joined = middle
    if left is not None:
        joined = joined + jnp.where(column == 0, 0.0, pltpu.roll(left, 1, 0))
    if right is not None:
        joined = joined + jnp.where(column == 31, 0.0, pltpu.roll(right, count - 1, 0))
    return joined


def conv_core(x_ref, w_ref, out_ref, back):
    for part in range(2):
        images = slice(4 * part, 4 * part + 4)

        def tap(col):
            value = None
            for row in range(3):
                lhs = x_ref[images, :, row * 512 : (row + 1) * 512].reshape(512, 512)
                if back:
                    term = lax.dot_general(
                        lhs, w_ref[2 - row, 2 - col], NT, preferred_element_type=F32
                    )
                else:
                    term = jnp.dot(lhs, w_ref[row, col], preferred_element_type=F32)
                value = term if value is None else value + term
            return value

        out = columns_joined(tap(0), tap(1), tap(2))
        out_ref[images] = out.reshape(4, 128, 512)


def stats_of(facts_ref, out_ref, stat_ref, row):
    def add(image, part):
        for r in range(4):
            part = part + fold(out_ref[image, band(r), :]) * facts_ref[image]
        return part

    first = total_row(lax.fori_loop(0, 8, add, jnp.zeros((8, 512), F32)))
    mean = first / jnp.maximum(facts_ref[OWN_PX], 1.0)

    def deviate(image, part):
        for r in range(4):
            away = out_ref[image, band(r), :] - mean
            part = part + fold(away * away) * facts_ref[image]
        return part

    second = total_row(lax.fori_loop(0, 8, deviate, jnp.zeros((8, 512), F32)))
    stat_ref[row : row + 1, :] = first
    stat_ref[row + 1 : row + 2, :] = second


def norm_of(facts_ref, own_ref, other_ref, row):
    own_px, other_px, all_px = facts_ref[OWN_PX], facts_ref[OTHER_PX], facts_ref[ALL_PX]
    own, other = own_ref[row : row + 1, :], other_ref[row : row + 1, :]
    mean = (own + other) / all_px
    apart = own / jnp.maximum(own_px, 1.0) - other / jnp.maximum(other_px, 1.0)
    spread = own_ref[row + 1 : row + 2, :] + other_ref[row + 1 : row + 2, :]
    variance = (spread + apart * apart * (own_px * other_px / all_px)) / all_px
    return mean, lax.rsqrt(variance + EPSILON)


def sigmoid(values):
    return 1.0 / (1.0 + jnp.exp(-values))


def slope_of(values):
    gate = sigmoid(values)
    return gate * (1.0 + values * (1.0 - gate))


MARKS = 128


def pieces_kernel(where_ref, images_ref, labels_ref, count_ref, o0, o1, o2, o3, wide):
    pipe, zone = where_ref[0], where_ref[2]
    tasks = labels_ref.shape[1]
    o0[MARKS:, :] = jnp.zeros((16, 512), BF16)
    for rel, out in enumerate((o0, o1, o2, o3)):
        first = (zone ^ rel) * 4 + pipe * 2
        for i in range(2):
            for row in range(2):
                lines = slice((i * 2 + row) * 32, (i * 2 + row) * 32 + 32)
                for part in range(2):
                    lanes = slice(part * 128, part * 128 + 128)
                    wide[...] = images_ref[first + i, row, :, lanes].astype(F32)
                    for par in range(2):
                        value = wide[pl.ds(par, 32, stride=2), :]
                        start = par * 256 + part * 128
                        out[lines, start : start + 128] = value.astype(BF16)
    marks = jnp.concatenate(
        [
            labels_ref[...].astype(F32),
            jnp.broadcast_to(count_ref[...].astype(F32), (4, tasks)),
            jnp.zeros((8, tasks), F32),
        ]
    )
    o0[MARKS:, 0:tasks] = marks.astype(BF16)


def down_kernel(facts_ref, where_ref, *refs):
    pieces, (w_ref, s_ref, img_ref, out_ref, short_ref, stat_ref, x_ref) = refs[:12], refs[12:]
    batch, zone = where_ref[1], where_ref[2]
    for kb in range(4):
        for kz in range(4):
            piece, base = pieces[kb * 3 + min(kz, 2)], (128 if kz == 3 else 0)
            row = zone ^ kz
            here = pl.ds(pl.multiple_of(row * 32, 32), 32)
            after = pl.ds(pl.multiple_of(((row + 1) % 4) * 32, 32), 32)
            for i in range(2):
                image = (batch ^ kb) * 2 + i
                start = base + i * 64
                odd = piece[start + 32 : start + 64, :]
                img_ref[image, here, 0:512] = piece[start : start + 32, :]
                img_ref[image, here, 512:1024] = odd
                x_ref[image, after, :] = jnp.where(row == 3, jnp.zeros_like(odd), odd)
    for part in range(2):
        images = slice(4 * part, 4 * part + 4)
        blocks = (
            x_ref[images].reshape(512, 512),
            img_ref[images, :, 0:512].reshape(512, 512),
            img_ref[images, :, 512:1024].reshape(512, 512),
        )
        left, middle = None, None
        for row in range(3):
            a = jnp.dot(blocks[row][:, 256:], w_ref[row, 0], preferred_element_type=F32)
            m = jnp.dot(
                blocks[row], w_ref[row, 1:3].reshape(512, 512), preferred_element_type=F32
            )
            left = a if left is None else left + a
            middle = m if middle is None else middle + m
        out_ref[images] = columns_joined(left, middle, None).reshape(4, 128, 512)
        short = jnp.dot(blocks[1][:, :256], s_ref[...], preferred_element_type=F32)
        short_ref[images] = short.reshape(4, 128, 512)
    stats_of(facts_ref, out_ref, stat_ref, 0)
    stats_of(facts_ref, short_ref, stat_ref, 2)
    stat_ref[4:8, :] = jnp.zeros((4, 512), F32)


def layer_kernel(g_row, b_row, facts_ref, in_ref, own_ref, other_ref, params_ref, w_ref,
                 act_ref, out_ref, stat_ref, norm_ref, x_ref):
    mean, inverse = norm_of(facts_ref, own_ref, other_ref, 0)
    gain, bias = param(params_ref, g_row), param(params_ref, b_row)

    def activate(image, carry):
        for r in range(4):
            pre = (in_ref[image, band(r), :] - mean) * inverse * gain + bias
            act = (pre * sigmoid(pre)).astype(BF16)
            act_ref[image, band(r), :] = act
            put_band(x_ref, image, r, act)
        return carry

    lax.fori_loop(0, 8, activate, 0)
    norm_ref[0:1, :] = mean
    norm_ref[1:2, :] = inverse
    norm_ref[2:8, :] = jnp.zeros((6, 512), F32)
    conv_core(x_ref, w_ref, out_ref, False)
    stats_of(facts_ref, out_ref, stat_ref, 0)
    stat_ref[2:8, :] = jnp.zeros((6, 512), F32)


def join_kernel(facts_ref, mid_ref, short_ref, own_m, other_m, own_d, other_d, params_ref,
                w_ref, act_ref, out_ref, stat_ref, norm_ref, x_ref):
    mean_m, inv_m = norm_of(facts_ref, own_m, other_m, 0)
    mean_s, inv_s = norm_of(facts_ref, own_d, other_d, 2)
    gain_m, gain_s = param(params_ref, G_MID), param(params_ref, G_SHORT)
    bias_m, bias_s = param(params_ref, B_MID), param(params_ref, B_SHORT)

    def activate(image, carry):
        for r in range(4):
            pre = (mid_ref[image, band(r), :] - mean_m) * inv_m * gain_m + bias_m
            pre = pre + (short_ref[image, band(r), :] - mean_s) * inv_s * gain_s + bias_s
            act = (pre * sigmoid(pre)).astype(BF16)
            act_ref[image, band(r), :] = act
            put_band(x_ref, image, r, act)
        return carry

    lax.fori_loop(0, 8, activate, 0)
    norm_ref[0:1, :] = mean_m
    norm_ref[1:2, :] = inv_m
    norm_ref[2:3, :] = mean_s
    norm_ref[3:4, :] = inv_s
    norm_ref[4:8, :] = jnp.zeros((4, 512), F32)
    conv_core(x_ref, w_ref, out_ref, False)
    stats_of(facts_ref, out_ref, stat_ref, 0)
    stat_ref[2:8, :] = jnp.zeros((6, 512), F32)


def block_kernel(facts_ref, in_ref, section_ref, own_ref, other_ref, params_ref,
                 pack_ref, norm_ref):
    mean, inverse = norm_of(facts_ref, own_ref, other_ref, 0)
    gain, bias = param(params_ref, G_SECOND), param(params_ref, B_SECOND)
    norm_ref[0:1, :] = mean
    norm_ref[1:2, :] = inverse
    norm_ref[2:8, :] = jnp.zeros((6, 512), F32)

    def gather(image, carry):
        pooled = jnp.zeros((8, 512), F32)
        slopes, crossed = pooled, pooled
        for r in range(4):
            normed = (in_ref[image, band(r), :] - mean) * inverse
            pre = normed * gain + bias + section_ref[image, band(r), :].astype(F32)
            gate = sigmoid(pre)
            slope = gate * (1.0 + pre * (1.0 - gate))
            pooled = pooled + fold(pre * gate)
            slopes = slopes + fold(slope)
            crossed = crossed + fold(slope * normed)
        pack_ref[pl.ds(image, 1), :] = total_row(pooled) / 128.0
        pack_ref[pl.ds(image + 8, 1), :] = total_row(slopes)
        pack_ref[pl.ds(image + 16, 1), :] = total_row(crossed)
        return carry

    lax.fori_loop(0, 8, gather, 0)


def logits_kernel(where_ref, own_ref, other_ref, living_ref, labels_ref, hw_ref, hb_ref,
                  all_ref, errors_ref, cross_ref):
    pipe = where_ref[0]
    for block in range(3):
        rows = slice(block * 8, block * 8 + 8)
        all_ref[block, pl.ds(pl.multiple_of(pipe * 8, 8), 8), :] = own_ref[rows, :]
        all_ref[block, pl.ds(pl.multiple_of((1 - pipe) * 8, 8), 8), :] = other_ref[rows, :]
    logits = (
        lax.dot_general(
            all_ref[0], hw_ref[...], NT, precision=HIGHEST, preferred_element_type=F32
        )
        + hb_ref[...]
    )
    errors = living_ref[...] * (sigmoid(logits) - labels_ref[...])
    errors_ref[...] = errors
    cross_ref[...] = lax.dot_general(
        errors, errors, TN, precision=HIGHEST, preferred_element_type=F32
    )


def head_kernel(picks_ref, where_ref, facts_ref, c0, c1, c2, c3, heads_ref, hw_ref, errors_ref,
                all_ref, in_ref, section_ref, norm_ref, params_ref,
                low_ref, pool_ref, small_ref, alpha_ref, gram_ref):
    tasks = gram_ref.shape[0]
    pipe = where_ref[0]
    gram_ref[...] = ((c0[...] + c1[...]) + (c2[...] + c3[...])) * heads_ref[...]
    frank_wolfe_kernel(picks_ref, gram_ref, alpha_ref)
    grad_logits = (128.0 * tasks) * alpha_ref[...] * errors_ref[...]
    pooled, slopes, crossed = all_ref[0], all_ref[1], all_ref[2]
    grad_pool = (
        jnp.dot(grad_logits, hw_ref[...], precision=HIGHEST, preferred_element_type=F32)
        / 128.0
    )
    grad_sum = total_row(grad_pool * slopes)
    cross_sum = total_row(grad_pool * crossed)
    small_ref[0:tasks, :] = lax.dot_general(
        grad_logits, pooled, TN, precision=HIGHEST, preferred_element_type=F32
    )
    small_ref[tasks : tasks + 1, :] = grad_sum
    small_ref[tasks + 1 : tasks + 2, :] = cross_sum
    small_ref[tasks + 2 :, :] = jnp.zeros((small_ref.shape[0] - tasks - 2, 512), F32)
    for start in (0, 256):
        small_ref[tasks + 2 : tasks + 3, start : start + tasks] = total_row(grad_logits)
    pool_ref[...] = jnp.where(pipe == 0, grad_pool[0:8], grad_pool[8:16])

    mean, inverse = norm_ref[0:1, :], norm_ref[1:2, :]
    gain, bias = param(params_ref, G_SECOND), param(params_ref, B_SECOND)
    all_px = facts_ref[ALL_PX]
    front = gain * inverse
    mean_grad, mean_cross = grad_sum / all_px, cross_sum / all_px

    def back(image, carry):
        up = pool_ref[pl.ds(image, 1), :]
        for r in range(4):
            normed = (in_ref[image, band(r), :] - mean) * inverse
            pre = normed * gain + bias + section_ref[image, band(r), :].astype(F32)
            grad = up * slope_of(pre)
            fix = facts_ref[image] * (mean_grad + normed * mean_cross)
            low_ref[image, band(r), :] = (front * (grad - fix)).astype(BF16)
        return carry

    lax.fori_loop(0, 8, back, 0)


def back_norm(facts_ref, in_ref, up_ref, norm_ref, own_ref, other_ref, gain, rows, sinks):
    mean, inverse = norm_ref[rows : rows + 1, :], norm_ref[rows + 1 : rows + 2, :]
    all_px = facts_ref[ALL_PX]
    front = gain * inverse
    cross_row = 1 + rows // 2
    mean_grad = (own_ref[0:1, :] + other_ref[0:1, :]) / all_px
    mean_cross = (
        own_ref[cross_row : cross_row + 1, :] + other_ref[cross_row : cross_row + 1, :]
    ) / all_px

    def back(image, carry):
        for r in range(4):
            normed = (in_ref[image, band(r), :] - mean) * inverse
            fix = facts_ref[image] * (mean_grad + normed * mean_cross)
            sinks(image, r, (front * (up_ref[image, band(r), :] - fix)).astype(BF16))
        return carry

    lax.fori_loop(0, 8, back, 0)


def second_back_kernel(facts_ref, low_ref, in_ref, norm_ref, params_ref, w_ref,
                       up_ref, sum_ref, x_ref, conv_ref):
    def fill(image, carry):
        for r in range(4):
            put_band(x_ref, image, r, low_ref[image, band(r), :])
        return carry

    lax.fori_loop(0, 8, fill, 0)
    conv_core(x_ref, w_ref, conv_ref, True)
    gain, bias = param(params_ref, G_FIRST), param(params_ref, B_FIRST)
    slope_sums(facts_ref, in_ref, norm_ref, gain, bias, conv_ref, up_ref, sum_ref)


def slope_sums(facts_ref, in_ref, norm_ref, gain, bias, conv_ref, up_ref, sum_ref):
    mean, inverse = norm_ref[0:1, :], norm_ref[1:2, :]

    def slope(image, carry):
        grads, crosses = carry
        for r in range(4):
            normed = (in_ref[image, band(r), :] - mean) * inverse
            up = conv_ref[image, band(r), :] * slope_of(normed * gain + bias)
            up_ref[image, band(r), :] = up
            living = facts_ref[image]
            grads = grads + fold(up) * living
            crosses = crosses + fold(up * normed) * living
        return grads, crosses

    zero = jnp.zeros((8, 512), F32)
    grads, crosses = lax.fori_loop(0, 8, slope, (zero, zero))
    sum_ref[0:1, :] = total_row(grads)
    sum_ref[1:2, :] = total_row(crosses)
    sum_ref[2:8, :] = jnp.zeros((6, 512), F32)


def first_back_kernel(facts_ref, up_in, in_ref, norm_ref, own_ref, other_ref, params_ref, w_ref,
                      second_ref, norm2_ref, section_ref, pool_ref, mid_ref, short_ref, normd_ref,
                      low_ref, up_ref, sum_ref, x_ref, conv_ref):
    def keep(image, r, low):
        low_ref[image, band(r), :] = low
        put_band(x_ref, image, r, low)

    back_norm(facts_ref, in_ref, up_in, norm_ref, own_ref, other_ref, param(params_ref, G_FIRST),
              0, keep)
    conv_core(x_ref, w_ref, conv_ref, True)
    mean2, inv2 = norm2_ref[0:1, :], norm2_ref[1:2, :]
    gain2, bias2 = param(params_ref, G_SECOND), param(params_ref, B_SECOND)
    mean_m, inv_m = normd_ref[0:1, :], normd_ref[1:2, :]
    mean_s, inv_s = normd_ref[2:3, :], normd_ref[3:4, :]
    gain_m, gain_s = param(params_ref, G_MID), param(params_ref, G_SHORT)
    bias_m, bias_s = param(params_ref, B_MID), param(params_ref, B_SHORT)

    def join(image, carry):
        grads, cross_m, cross_s = carry
        pool = pool_ref[pl.ds(image, 1), :]
        for r in range(4):
            pre2 = (second_ref[image, band(r), :] - mean2) * inv2 * gain2 + bias2
            pre2 = pre2 + section_ref[image, band(r), :].astype(F32)
            entry = conv_ref[image, band(r), :] + pool * slope_of(pre2)
            entry = entry.astype(BF16).astype(F32)
            norm_m = (mid_ref[image, band(r), :] - mean_m) * inv_m
            norm_s = (short_ref[image, band(r), :] - mean_s) * inv_s
            pre = norm_m * gain_m + bias_m + norm_s * gain_s + bias_s
            up = entry * slope_of(pre)
            up_ref[image, band(r), :] = up
            living = facts_ref[image]
            grads = grads + fold(up) * living
            cross_m = cross_m + fold(up * norm_m) * living
            cross_s = cross_s + fold(up * norm_s) * living
        return grads, cross_m, cross_s

    zero = jnp.zeros((8, 512), F32)
    grads, cross_m, cross_s = lax.fori_loop(0, 8, join, (zero, zero, zero))
    sum_ref[0:1, :] = total_row(grads)
    sum_ref[1:2, :] = total_row(cross_m)
    sum_ref[2:3, :] = total_row(cross_s)
    sum_ref[3:8, :] = jnp.zeros((5, 512), F32)


def mid_back_kernel(facts_ref, up_in, mid_ref, short_ref, normd_ref, own_ref, other_ref, params_ref,
                    w_ref, in_ref, norm1_ref,
                    low_ref, low_s_ref, up_ref, sum_ref, x_ref, conv_ref):
    def keep(image, r, low):
        low_ref[image, band(r), :] = low
        put_band(x_ref, image, r, low)

    def keep_short(image, r, low):
        low_s_ref[image, band(r), :] = low

    gain_m, gain_s = param(params_ref, G_MID), param(params_ref, G_SHORT)
    back_norm(facts_ref, mid_ref, up_in, normd_ref, own_ref, other_ref, gain_m, 0, keep)
    back_norm(facts_ref, short_ref, up_in, normd_ref, own_ref, other_ref, gain_s, 2, keep_short)
    conv_core(x_ref, w_ref, conv_ref, True)
    gain, bias = param(params_ref, G_DOWN), param(params_ref, B_DOWN)
    slope_sums(facts_ref, in_ref, norm1_ref, gain, bias, conv_ref, up_ref, sum_ref)


def down_back_kernel(facts_ref, up_in, in_ref, norm1_ref, own_ref, other_ref, params_ref, low_ref):
    def keep(image, r, low):
        low_ref[image, band(r), :] = low

    gain = param(params_ref, G_DOWN)
    back_norm(facts_ref, in_ref, up_in, norm1_ref, own_ref, other_ref, gain, 0, keep)


def image_back_kernel(where_ref, low_ref, low_s_ref, w_ref, s_ref, o0, o1, o2, o3, stage_ref):
    pipe, batch, zone = where_ref[0], where_ref[1], where_ref[2]
    mine = pl.ds(batch * 2, 2)
    here = low_ref[mine]
    below = jnp.concatenate([here[:, 32:], jnp.zeros((2, 32, 512), BF16)], axis=1)
    here, below = here.reshape(256, 512), below.reshape(256, 512)
    short = low_s_ref[mine].reshape(256, 512)

    def back(lhs, row, col):
        return lax.dot_general(lhs, w_ref[row, col], NT, preferred_element_type=F32)

    even_even = back(here, 1, 1) + lax.dot_general(
        short, s_ref[...], NT, preferred_element_type=F32
    )
    even_odd = columns_joined(None, back(here, 1, 2), back(here, 1, 0))
    odd_even = back(here, 2, 1) + back(below, 0, 1)
    odd_odd = columns_joined(
        None, back(here, 2, 2) + back(below, 0, 2), back(here, 2, 0) + back(below, 0, 0)
    )
    planes = ((even_even, even_odd), (odd_even, odd_odd))
    for row in range(2):
        for par in range(2):
            plane = planes[row][par].reshape(2, 4, 32, 256).astype(BF16)
            lanes = slice(par * 128, par * 128 + 128)
            for side in range(2):
                half = plane[..., side * 128 : side * 128 + 128]
                for z in range(4):
                    stage_ref[z ^ zone, side ^ pipe, :, row, :, lanes] = half[:, z]
    for rel, out in enumerate((o0, o1, o2, o3)):
        out[...] = stage_ref[rel]


def image_grad_kernel(where_ref, own_ref, got_ref, out_ref):
    pipe, zone = where_ref[0], where_ref[2]
    for rel in range(4):
        for side, pieces in enumerate((own_ref, got_ref)):
            first = (zone ^ rel) * 4 + (pipe if side == 0 else 1 - pipe) * 2
            for i in range(2):
                for row in range(2):
                    for par in range(2):
                        out_ref[first + i, row, pl.ds(par, 32, stride=2), :] = pieces[
                            rel, i, row, :, par * 128 : (par + 1) * 128
                        ].astype(F32)


def slot_of(quarter, zone):
    rel = quarter ^ zone
    return (rel >> 1) | ((rel & 1) << 1)


def shifted_window(turned, down, right):
    pixel = lax.broadcasted_iota(jnp.int32, (1, 128), 1)
    column, row = pixel % 32 + right, pixel // 32 + down
    inside = (column >= 0) & (column < 32) & (row >= 0) & (row < 4)
    amount = (256 - down * 32 - right) % 128
    moved = turned if isinstance(amount, int) and amount == 0 else pltpu.roll(turned, amount, 1)
    return jnp.where(inside, moved, 0.0).astype(BF16)


def split_out(pipe, zone, unit, result_own, result_other, own_ref, other_ref):
    for quarter in range(4):
        slot = slot_of(quarter, zone)
        rows = slice(quarter * 32, quarter * 32 + 32)
        own_ref[slot, unit] = result_own[rows]
        other_ref[slot, unit] = result_other[rows].astype(BF16)


def hand_out(other_ref, outs):
    for slot, out in enumerate(outs):
        out[...] = other_ref[slot]


def turned_taps(batch, act_ref, turned_ref):
    lanes = pl.ds(pl.multiple_of(batch * 128, 128), 128)

    def turn(image, carry):
        turned = act_ref[image, :, lanes].astype(F32).T
        pixels = pl.ds(pl.multiple_of(image * 128, 128), 128)
        for row in range(3):
            for col in range(3):
                turned_ref[row * 3 + col, :, pixels] = shifted_window(turned, row - 1, col - 1)
        return carry

    lax.fori_loop(0, 8, turn, 0)


def tap_products(pipe, zone, low_ref, turned_ref, own_ref, other_ref):
    lhs = turned_ref[0:9].reshape(9 * 128, 1024)
    results = []
    for side in (pipe, 1 - pipe):
        columns = pl.ds(pl.multiple_of(side * 256, 256), 256)
        rhs = low_ref[:, :, columns].reshape(1024, 256)
        results.append(jnp.dot(lhs, rhs, preferred_element_type=F32))
    for unit in range(9):
        rows = slice(unit * 128, unit * 128 + 128)
        split_out(pipe, zone, unit, results[0][rows], results[1][rows], own_ref, other_ref)


def kernel_grad_kernel(where_ref, act_ref, low_ref, own_ref, o0, o1, o2, o3, turned_ref, other_ref):
    pipe, batch, zone = where_ref[0], where_ref[1], where_ref[2]
    turned_taps(batch, act_ref, turned_ref)
    tap_products(pipe, zone, low_ref, turned_ref, own_ref, other_ref)
    hand_out(other_ref, (o0, o1, o2, o3))


DOWN_UNITS = (
    ((0, 0, 0, 4), (2, -1, 0, 1), (2, 0, 0, 7), (0, 0, 0, 9), (1, 0, 0, 5)),
    ((1, 0, -1, 3), (3, -1, -1, 0), (3, -1, 0, 2), (3, 0, -1, 6), (3, 0, 0, 8)),
)


def down_grad_kernel(where_ref, img_ref, low_ref, low_s_ref, own_ref, o0, o1, o2, o3,
                     turned_ref, other_ref):
    pipe, batch, zone = where_ref[0], where_ref[1], where_ref[2]
    upper, part = batch // 2, batch % 2

    for turn_kind in range(2):

        @pl.when(upper == turn_kind)
        def _(units=DOWN_UNITS[turn_kind]):
            def turn(image, carry):
                pixels = pl.ds(pl.multiple_of(image * 128, 128), 128)
                seen = {}
                for unit, (plane, down, right, _) in enumerate(units):
                    if plane not in seen:
                        lanes = pl.ds(pl.multiple_of(plane * 256 + part * 128, 128), 128)
                        seen[plane] = img_ref[image, :, lanes].astype(F32).T
                    turned_ref[unit, :, pixels] = shifted_window(seen[plane], down, right)
                return carry

            lax.fori_loop(0, 8, turn, 0)

    short_unit = [tap for _, _, _, tap in DOWN_UNITS[0]].index(9)
    for unit in range(5):
        lhs = turned_ref[unit]
        results = []
        for side in (pipe, 1 - pipe):
            columns = pl.ds(pl.multiple_of(side * 256, 256), 256)
            rhs = low_ref[:, :, columns].reshape(1024, 256)
            if unit == short_unit:
                rhs_s = low_s_ref[:, :, columns].reshape(1024, 256)
                rhs = jnp.where(upper == 0, rhs_s, rhs)
            results.append(jnp.dot(lhs, rhs, preferred_element_type=F32))
        split_out(pipe, zone, unit, results[0], results[1], own_ref, other_ref)
    hand_out(other_ref, (o0, o1, o2, o3))


def add_cores_kernel(own_ref, g0, g1, g2, g3, keep_ref, send_ref):
    for slot, got in enumerate((g0, g1)):
        keep_ref[slot] = own_ref[slot] + got[...].astype(F32)
    for slot, got in enumerate((g2, g3)):
        send_ref[slot] = (own_ref[2 + slot] + got[...].astype(F32)).astype(BF16)


def add_near_kernel(own_ref, got_ref, keep_ref, send_ref):
    keep_ref[...] = own_ref[0] + got_ref[0].astype(F32)
    send_ref[...] = (own_ref[1] + got_ref[1].astype(F32)).astype(BF16)


def add_far_kernel(own_ref, got_ref, out_ref):
    out_ref[...] = (own_ref[...] + got_ref[...].astype(F32)).astype(BF16)


def join_kernel_of(*refs):
    at = 0
    for ref in refs[:-1]:
        if len(ref.shape) == 3:
            refs[-1][at] = ref[...]
            at += 1
        else:
            refs[-1][at : at + ref.shape[0]] = ref[...]
            at += ref.shape[0]


def gathered_blocks(zone, batch, refs):
    if len(refs) == 8:
        for kb in range(4):
            for rel in range(4):
                yield batch ^ kb, zone ^ rel, refs[2 * kb + rel % 2], rel // 2
        return
    a, b, ax, by, ayy, bxx = refs
    sets = {0: (a, b, 0, 0), 1: (ax, bxx, 0, 0), 2: (ayy, by, 0, 0), 3: (ayy, bxx, 2, 2)}
    for kb in range(4):
        even, odd, base_even, base_odd = sets[kb]
        for rel in range(4):
            if rel % 2 == 1:
                yield batch ^ kb, zone ^ rel, odd, base_odd + rel // 2
            else:
                yield batch ^ kb, zone ^ rel, even, base_even + rel // 2


def assemble_kernel(where_ref, *refs):
    pieces, out_ref = refs[:-1], refs[-1]
    batch, zone = where_ref[1], where_ref[2]
    for owner, quarter, ref, index in gathered_blocks(zone, batch, pieces):
        rows = pl.ds(pl.multiple_of(owner * 128 + quarter * 32, 32), 32)
        out_ref[:, rows, :] = ref[index].astype(F32)


def assemble_down_kernel(where_ref, *refs):
    pieces, (out_ref, short_ref) = refs[:-2], refs[-2:]
    batch, zone = where_ref[1], where_ref[2]
    for owner, quarter, ref, index in gathered_blocks(zone, batch, pieces):
        upper, part = owner // 2, owner % 2
        rows = pl.ds(pl.multiple_of(part * 128 + quarter * 32, 32), 32)
        value = ref[index].astype(F32)
        for kind in range(2):

            @pl.when(upper == kind)
            def _(value=value, rows=rows, units=DOWN_UNITS[kind]):
                for unit, (_, _, _, tap) in enumerate(units):
                    if tap == 9:
                        short_ref[rows, :] = value[unit]
                    else:
                        out_ref[tap, rows, :] = value[unit]


def facts_kernel(where_ref, p0, p1, p2, p3, hw_ref, facts_ref, living_ref, targets_ref, heads_ref):
    pipe, batch = where_ref[0], where_ref[1]
    tasks = hw_ref.shape[0]
    alive = [jnp.float32(0.0), jnp.float32(0.0)]
    for rel, piece in enumerate((p0, p1, p2, p3)):
        owner = batch ^ rel
        marks = piece[MARKS:, 0:tasks].astype(F32)
        count = jnp.max(marks[4:5, :])
        for slot in range(4):
            side, place = slot // 2, owner * 2 + slot % 2
            living = (count > slot + 0.5).astype(F32)
            alive[side] = alive[side] + living
            row = pl.ds(side * 8 + place, 1)
            living_ref[row, :] = jnp.full((1, tasks), living)
            targets_ref[row, :] = marks[slot : slot + 1, :]

            @pl.when(pipe == side)
            def _(place=place, living=living):
                facts_ref[place] = living

    own = jnp.where(pipe == 0, alive[0], alive[1])
    facts_ref[OWN_PX] = own * 128.0
    facts_ref[OTHER_PX] = (alive[0] + alive[1] - own) * 128.0
    facts_ref[ALL_PX] = (alive[0] + alive[1]) * 128.0
    for rest in range(ALL_PX + 1, 16):
        facts_ref[rest] = jnp.float32(0.0)
    heads_ref[...] = lax.dot_general(
        hw_ref[...], hw_ref[...], NT, precision=HIGHEST, preferred_element_type=F32
    )


SMALL_ROWS = 64


def small_kernel(where_ref, head_ref, all_ref, sum_f, other_f, sum_j, other_j, sum_d, other_d,
                 sent_ref, wide_ref):
    pipe, batch = where_ref[0], where_ref[1]
    tasks = head_ref.shape[0] - 8
    wide_ref[...] = jnp.zeros(wide_ref.shape, F32)
    wide_ref[0 : tasks + 3, :] = head_ref[0 : tasks + 3, :]
    at = tasks + 3
    for own, other, count in ((sum_f, other_f, 2), (sum_j, other_j, 3), (sum_d, other_d, 2)):
        wide_ref[at : at + count, :] = own[0:count, :] + other[0:count, :]
        at += count
    for side in range(2):
        for slot in range(2):
            row = side * 8 + batch * 2 + slot
            at_row = SMALL_ROWS - 8 + side * 2 + slot
            wide_ref[at_row : at_row + 1, :] = all_ref[0, pl.ds(row, 1), :]
    sent_ref[...] = wide_ref[:, pl.ds(pl.multiple_of(pipe * 256, 256), 256)]


def small_out_kernel(where_ref, p0, p1, p2, p3, pooled_ref, head_ref, gd_ref, bd_ref, gp_ref, bp_ref,
                     headb_ref):
    tasks = head_ref.shape[0]
    zone = where_ref[2]
    for rel, part in enumerate((p0, p1, p2, p3)):
        pooled_ref[zone ^ rel] = part[SMALL_ROWS - 8 : SMALL_ROWS - 4, :]
    total = (p0[...] + p1[...]) + (p2[...] + p3[...])
    head_ref[...] = total[0:tasks]

    def line(at):
        return total[tasks + at : tasks + at + 1]

    headb_ref[...] = line(2)
    bp_ref[0:1, :], gp_ref[0:1, :] = line(3), line(4)
    bp_ref[1:2, :], gp_ref[1:2, :] = line(0), line(1)
    bd_ref[0:1, :], gd_ref[0:1, :] = line(8), line(9)
    bd_ref[1:2, :], gd_ref[1:2, :] = line(5), line(6)
    bd_ref[2:3, :], gd_ref[2:3, :] = line(5), line(7)


def fast_device(images, image_counts, labels, fw_picks, conv_down, conv_mid, shortcut, gains_down,
                biases_down, conv_first, conv_second, gains_plain, biases_plain, head_weight,
                head_bias):
    pipe, batch, zone = (lax.axis_index(axis) for axis in ("pipe", "batch", "space"))
    tasks = head_weight.shape[1]

    def over(axis, rel, x):
        size = lax.axis_size(axis)
        return lax.ppermute(x, axis, [(i, i ^ rel) for i in range(size)])

    where = jnp.stack([pipe, batch, zone, zone]).astype(jnp.int32)
    params = jnp.concatenate([gains_down, biases_down, gains_plain, biases_plain])
    turned_heads = head_weight.T
    bias_row = head_bias.reshape(1, tasks)

    pieces = call(
        pieces_kernel,
        [((144, 512), BF16)] + [((128, 512), BF16)] * 3,
        [where, images, lax.dynamic_slice_in_dim(labels, zone * 4, 4, 0),
         lax.dynamic_slice_in_dim(image_counts, zone, 1, 1)],
        [pltpu.VMEM((64, 128), F32)],
        name="pieces",
    )
    moved = [over("space", rel, pieces[rel]) for rel in (1, 2, 3)]
    moved = [pieces[0], moved[0], jnp.concatenate([moved[1], moved[2]])]
    gathered = [moved] + [[over("batch", kb, x) for x in moved] for kb in (1, 2, 3)]
    facts, living, targets, heads = call(
        facts_kernel,
        [((16,), F32), ((16, tasks), F32), ((16, tasks), F32), ((tasks, tasks), F32)],
        [where] + [line[0] for line in gathered] + [turned_heads],
        name="facts",
    )

    big = ((8, 128, 512), F32)
    low = ((8, 128, 512), BF16)
    rows = ((8, 512), F32)
    x_scratch = pltpu.VMEM((8, 128, 1536), BF16)
    conv_scratch = pltpu.VMEM((8, 128, 512), F32)
    conv_flops = 2 * 1024 * 4608 * 512

    def partner(x):
        return over("pipe", 1, x)

    img, down_out, short_out, stat_d = call(
        down_kernel,
        [((8, 128, 1024), BF16), big, big, rows],
        [facts, where] + [piece for line in gathered for piece in line] + [conv_down, shortcut],
        [pltpu.VMEM((8, 128, 512), BF16)],
        conv_flops // 2,
        "down",
    )
    other_d = partner(stat_d)
    down_act, mid_out, stat_m, norm_d = call(
        lambda *refs: layer_kernel(G_DOWN, B_DOWN, *refs),
        [low, big, rows, rows],
        [facts, down_out, stat_d, other_d, params, conv_mid],
        [x_scratch],
        conv_flops,
        "mid",
    )
    other_m = partner(stat_m)
    section, first_out, stat_f, norm_j = call(
        join_kernel,
        [low, big, rows, rows],
        [facts, mid_out, short_out, stat_m, other_m, stat_d, other_d, params, conv_first],
        [x_scratch],
        conv_flops,
        "first",
    )
    other_f = partner(stat_f)
    plain_act, second_out, stat_s, norm_f = call(
        lambda *refs: layer_kernel(G_FIRST, B_FIRST, *refs),
        [low, big, rows, rows],
        [facts, first_out, stat_f, other_f, params, conv_second],
        [x_scratch],
        conv_flops,
        "second",
    )
    other_s = partner(stat_s)
    pack, norm_s = call(
        block_kernel,
        [((24, 512), F32), rows],
        [facts, second_out, section, stat_s, other_s, params],
        name="block",
    )
    other_pack = partner(pack)
    all_pack, errors, cross = call(
        logits_kernel,
        [((3, 16, 512), F32), ((16, tasks), F32), ((tasks, tasks), F32)],
        [where, pack, other_pack, living, targets, turned_heads, bias_row],
        name="logits",
    )
    crosses = [cross] + [over("space", rel, cross) for rel in (1, 2, 3)]
    second_low, grad_pool, small = call(
        head_kernel,
        [low, rows, ((tasks + 8, 512), F32)],
        [fw_picks, where, facts] + crosses
        + [heads, turned_heads, errors, all_pack, second_out, section, norm_s, params],
        [pltpu.VMEM((1, tasks), F32), pltpu.VMEM((tasks, tasks), F32)],
        name="head",
    )

    class Sum:
        def __init__(self, kernel, units, operands, scratch, flops, name, after=()):
            self.units, self.name = units, name
            self.own, *self.other = call(
                kernel,
                [self.block(4, dtype=F32)] + [self.block()] * 4,
                operands,
                [scratch, pltpu.VMEM((4, units, 32, 256), BF16)],
                flops,
                name,
                after,
            )
            self.got = [partner(x) for x in self.other]

        def block(self, *lead, dtype=BF16):
            return (lead + (self.units, 32, 256), dtype)

        def cores(self, after=()):
            self.keep, sent = call(
                add_cores_kernel,
                [self.block(2, dtype=F32), self.block(2)],
                [self.own] + self.got,
                name=self.name + "_cores",
                after=after,
            )
            self.near = over("space", 1, sent)

        def zone_near(self, after=()):
            self.keep, sent = call(
                add_near_kernel,
                [self.block(dtype=F32), self.block()],
                [self.keep, self.near],
                name=self.name + "_near",
                after=after,
            )
            self.far = over("space", 2, sent)

        def zone_far(self, after=()):
            (self.final,) = call(
                add_far_kernel,
                [self.block()],
                [self.keep, self.far],
                name=self.name + "_final",
                after=after,
            )
            self.other_far = over("space", 2, self.final)

        def pair(self, after=()):
            (self.a,) = call(
                join_kernel_of,
                [self.block(2)],
                [self.final, self.other_far],
                name=self.name + "_pair",
                after=after,
            )
            self.b = over("space", 1, self.a)

        def direct(self):
            self.ra = [over("batch", rel, self.a) for rel in (1, 2, 3)]
            self.rb = [over("batch", rel, self.b) for rel in (1, 2, 3)]
            self.blocks = [where, self.a, self.b]
            for x, y in zip(self.ra, self.rb):
                self.blocks += [x, y]

        def plane(self):
            self.ax, self.by = over("batch", 1, self.a), over("batch", 2, self.b)

        def plane_far(self, after=()):
            self.fa, self.fb = [
                call(join_kernel_of, [self.block(4)], pair, name=self.name + "_cross", after=after)[0]
                for pair in ([self.a, self.ax], [self.b, self.by])
            ]
            self.ayy, self.bxx = over("batch", 2, self.fa), over("batch", 1, self.fb)
            self.blocks = [where, self.a, self.b, self.ax, self.by, self.ayy, self.bxx]

    def kernel_grad_of(act, low_grad, name, after=()):
        return Sum(
            kernel_grad_kernel, 9, [where, act, low_grad], pltpu.VMEM((9, 128, 1024), BF16),
            conv_flops // 4, name, after,
        )

    def assembled(blocks, name, after=()):
        (out,) = call(assemble_kernel, [((9, 512, 256), F32)], blocks, name=name, after=after)
        return out.reshape(3, 3, 512, 256)

    second = kernel_grad_of(plain_act, second_low, "second_grad")
    second.cores()
    up_f, sum_f = call(
        second_back_kernel,
        [big, rows],
        [facts, second_low, first_out, norm_f, params, conv_second],
        [x_scratch, conv_scratch],
        conv_flops,
        "second_back",
        after=[second.keep],
    )
    other_sf = partner(sum_f)
    second.zone_near(after=[sum_f])
    first_low, up_j, sum_j = call(
        first_back_kernel,
        [low, big, rows],
        [facts, up_f, first_out, norm_f, sum_f, other_sf, params, conv_first,
         second_out, norm_s, section, grad_pool, mid_out, short_out, norm_j],
        [x_scratch, conv_scratch],
        conv_flops,
        "first_back",
        after=[second.keep],
    )
    other_sj = partner(sum_j)
    second.zone_far(after=[sum_j])
    first = kernel_grad_of(section, first_low, "first_grad", after=[second.final])
    second.pair(after=first.other[0:1])
    second.direct()
    first.cores(after=[second.a])
    mid_low, short_low, up_d, sum_d = call(
        mid_back_kernel,
        [low, low, big, rows],
        [facts, up_j, mid_out, short_out, norm_j, sum_j, other_sj, params, conv_mid,
         down_out, norm_d],
        [x_scratch, conv_scratch],
        conv_flops,
        "mid_back",
        after=[first.keep],
    )
    other_sd = partner(sum_d)
    first.zone_near(after=[sum_d, second.b])
    mid = kernel_grad_of(down_act, mid_low, "mid_grad", after=[first.keep] + second.ra)
    first.zone_far(after=mid.other[0:1])
    mid.cores(after=[first.final])
    (down_low,) = call(
        down_back_kernel,
        [low],
        [facts, up_d, down_out, norm_d, sum_d, other_sd, params],
        name="down_back",
        after=[mid.keep],
    )
    down = Sum(
        down_grad_kernel, 5, [where, img, down_low, short_low], pltpu.VMEM((5, 128, 1024), BF16),
        conv_flops // 8, "down_grad",
    )
    first.pair(after=down.other[0:1])
    down.cores(after=[first.a])
    mid.zone_near(after=[down.keep])
    first.plane()
    second_out_grad = assembled(second.blocks, "second_out", after=[mid.keep])
    down.zone_near(after=[second_out_grad])
    mid.zone_far(after=[down.keep])
    img_pieces = call(
        image_back_kernel,
        [((2, 2, 2, 32, 256), BF16)] * 4,
        [where, down_low, short_low, conv_down, shortcut],
        [pltpu.VMEM((4, 2, 2, 2, 32, 256), BF16)],
        conv_flops // 8,
        "image_back",
        after=[mid.final],
    )
    first.plane_far(after=[img_pieces[0]])
    down.zone_far(after=[first.fa, first.fb])
    mid.pair(after=[down.final])
    mid.plane()
    down.pair(after=[mid.a])
    down.plane()
    first_out_grad = assembled(first.blocks, "first_out", after=[down.a])
    mid.plane_far(after=[first_out_grad])
    down.plane_far(after=[mid.fa, mid.fb])
    mid_out_grad = assembled(mid.blocks, "mid_out", after=[down.fa])

    img_moved = [img_pieces[0]] + [over("space", rel, img_pieces[rel]) for rel in (1, 2, 3)]
    img_moved = jnp.stack(img_moved)
    img_got = partner(img_moved[:, 1])
    (images_grad,) = call(
        image_grad_kernel,
        [((16, 2, 64, 128), F32)],
        [where, img_moved[:, 0], img_got],
        name="image_grad",
    )

    (sent,) = call(
        small_kernel,
        [((SMALL_ROWS, 256), F32)],
        [where, small, all_pack, sum_f, other_sf, sum_j, other_sj, sum_d, other_sd],
        [pltpu.VMEM((SMALL_ROWS, 512), F32)],
        name="small",
        after=[down.final],
    )
    parts = [sent] + [over("space", rel, sent) for rel in (1, 2, 3)]
    pooled, head_out, gains_d, sums_d, gains_p, sums_p, head_b = call(
        small_out_kernel,
        [((4, 4, 256), F32), ((tasks, 256), F32), ((3, 256), F32), ((3, 256), F32),
         ((2, 256), F32), ((2, 256), F32), ((1, 256), F32)],
        [where] + parts,
        name="small_out",
    )
    down_grad, short_grad = call(
        assemble_down_kernel,
        [((9, 256, 256), F32), ((256, 256), F32)],
        down.blocks,
        name="down_out",
    )
    return (
        pooled.reshape(16, 256),
        images_grad,
        down_grad.reshape(3, 3, 256, 256),
        mid_out_grad,
        short_grad,
        gains_d,
        sums_d,
        first_out_grad,
        second_out_grad,
        gains_p,
        sums_p,
        head_out.T,
        lax.dynamic_slice_in_dim(head_b[0], pipe * (tasks // 2), tasks // 2, 0),
    )


def per_device(
    images,
    image_counts,
    labels,
    fw_picks,
    conv_down,
    conv_mid,
    shortcut,
    gains_down,
    biases_down,
    conv_first,
    conv_second,
    gains_plain,
    biases_plain,
    head_weight,
    head_bias,
):
    layout = Layout(image_counts.shape[1])
    micros, zone = layout.micros, layout.zone
    sizes = (images.shape, conv_down.shape, lax.axis_size("pipe"), lax.axis_size("batch"))
    if layout.groups == 1 and sizes == ((16, 2, 64, 256), (3, 3, 256, 512), 2, 4):
        return fast_device(
            images, image_counts, labels, fw_picks, conv_down, conv_mid, shortcut, gains_down,
            biases_down, conv_first, conv_second, gains_plain, biases_plain, head_weight,
            head_bias,
        )
    batches, pipes = lax.axis_size("batch"), lax.axis_size("pipe")
    batch = lax.axis_index("batch")
    pipe = lax.axis_index("pipe")
    per_micro = images.shape[0] // micros
    count = per_micro * batches
    entering, channels = conv_down.shape[2], conv_mid.shape[3]
    tasks = head_weight.shape[1]
    half = channels // pipes
    own = pipe * half

    def own_out(kernel, axis):
        size = kernel.shape[axis] // pipes
        return lax.dynamic_slice_in_dim(kernel, pipe * size, size, axis)

    def whole(tensor, axis=3):
        return lax.all_gather(tensor, "pipe", axis=axis, tiled=True)

    def share(tensor):
        size = tensor.shape[3] // batches
        return lax.dynamic_slice_in_dim(tensor, batch * size, size, 3)

    mine = lax.all_to_all(
        images, "space", 0, 1, axis_index_groups=layout.inner, tiled=True
    )
    mine = lax.all_gather(mine, "batch", axis=0, tiled=True)
    counts = lax.all_gather(image_counts, "batch", axis=0, tiled=True)
    counts = lax.dynamic_slice_in_dim(counts, zone, 1, 1)[:, 0]
    marks = lax.dynamic_slice_in_dim(labels, zone * per_micro, per_micro, 0)
    targets = lax.all_gather(marks, "batch", axis=0, tiled=True).astype(F32)
    slots = jnp.arange(per_micro, dtype=jnp.int32)
    living = (slots[None, :] < counts[:, None]).astype(F32).reshape(count)
    weight = living[:, None, None, None]
    out_rows, out_cols = mine.shape[1] // 2, mine.shape[2] // 2
    image_pixels = out_rows * layout.groups * out_cols
    counted = jnp.sum(living) * image_pixels
    scale = float(image_pixels * tasks)

    gain_d, bias_d = own_out(gains_down, 1), own_out(biases_down, 1)
    gain_p, bias_p = own_out(gains_plain, 1), own_out(biases_plain, 1)

    above = layout.row_from(mine[:, -1:], 1)
    down_ext = jnp.pad(
        jnp.concatenate([above, mine], axis=1), ((0, 0), (0, 0), (1, 0), (0, 0))
    )
    down_out = conv_valid(down_ext, own_out(conv_down, 3), 2)
    down_norm, down_inv = norm_forward(layout, down_out, weight, counted)
    down_pre = down_norm * gain_d[0] + bias_d[0]
    mid_ext = layout.rims(whole(jax.nn.silu(down_pre).astype(BF16)))
    mid_out = conv_valid(mid_ext, own_out(conv_mid, 3), 1)
    short_in = mine[:, ::2, ::2]
    short_out = jnp.einsum(
        "nhwi,io->nhwo", short_in, own_out(shortcut, 1), preferred_element_type=F32
    )
    mid_norm, mid_inv = norm_forward(layout, mid_out, weight, counted)
    short_norm, short_inv = norm_forward(layout, short_out, weight, counted)
    section_pre = mid_norm * gain_d[1] + bias_d[1] + short_norm * gain_d[2] + bias_d[2]
    section = jax.nn.silu(section_pre).astype(BF16)
    first_ext = layout.rims(whole(section))
    first_out = conv_valid(first_ext, own_out(conv_first, 3), 1)
    first_norm, first_inv = norm_forward(layout, first_out, weight, counted)
    first_pre = first_norm * gain_p[0] + bias_p[0]
    second_ext = layout.rims(whole(jax.nn.silu(first_pre).astype(BF16)))
    second_out = conv_valid(second_ext, own_out(conv_second, 3), 1)
    second_norm, second_inv = norm_forward(layout, second_out, weight, counted)
    block_pre = second_norm * gain_p[1] + bias_p[1] + section.astype(F32)
    pooled = layout.group_sum(jnp.sum(jax.nn.silu(block_pre), axis=(1, 2))) / image_pixels

    pooled_all = whole(pooled, 1)
    logits = jnp.dot(pooled_all, head_weight, precision=HIGHEST) + head_bias
    errors = living[:, None] * (jax.nn.sigmoid(logits) - targets)
    cross = jnp.einsum("nt,ns->ts", errors, errors, precision=HIGHEST)
    cross = lax.psum(cross, "space", axis_index_groups=layout.inner)
    gram = cross * jnp.dot(head_weight.T, head_weight, precision=HIGHEST)
    alpha = frank_wolfe(gram, fw_picks)
    grad_logits = scale * alpha * errors
    head_w = jnp.einsum("nc,nt->ct", pooled, grad_logits, precision=HIGHEST)
    head_b = jnp.sum(grad_logits, axis=0)
    head_own = own_out(head_weight, 0)
    grad_pool = jnp.einsum("nt,ct->nc", grad_logits, head_own, precision=HIGHEST) / image_pixels

    grad_block = grad_pool[:, None, None, :] * silu_slope(block_pre)
    second_low, second_cross, second_sum = norm_back(
        layout, grad_block, second_norm, second_inv, gain_p[1], weight, counted
    )
    second_kernel = kernel_grad(share(second_ext), second_low, 1)
    act_grad = conv_valid(layout.rims(whole(second_low)), flipped(own_out(conv_second, 2)), 1)
    first_low, first_cross, first_sum = norm_back(
        layout, act_grad * silu_slope(first_pre), first_norm, first_inv, gain_p[0], weight, counted
    )
    first_kernel = kernel_grad(share(first_ext), first_low, 1)
    entry_grad = conv_valid(layout.rims(whole(first_low)), flipped(own_out(conv_first, 2)), 1)
    entry_grad = (entry_grad + grad_block).astype(BF16).astype(F32)
    grad_section = entry_grad * silu_slope(section_pre)
    mid_low, mid_cross, mid_sum = norm_back(
        layout, grad_section, mid_norm, mid_inv, gain_d[1], weight, counted
    )
    short_low, short_cross, short_sum = norm_back(
        layout, grad_section, short_norm, short_inv, gain_d[2], weight, counted
    )
    mid_kernel = kernel_grad(share(mid_ext), mid_low, 1)
    short_kernel = jnp.einsum(
        "nhwi,nhwo->io", share(short_in), short_low, preferred_element_type=F32
    )
    act_grad = conv_valid(layout.rims(whole(mid_low)), flipped(own_out(conv_mid, 2)), 1)
    down_low, down_cross, down_sum = norm_back(
        layout, act_grad * silu_slope(down_pre), down_norm, down_inv, gain_d[0], weight, counted
    )
    down_kernel = kernel_grad(share(down_ext), down_low, 2)

    kept = lax.dynamic_slice_in_dim(whole(down_low), batch * per_micro, per_micro, 0)
    below = layout.row_from(kept[:, :1], -1)
    spread = lax.conv_general_dilated(
        jnp.concatenate([kept, below], axis=1),
        flipped(own_out(conv_down, 2)),
        (1, 1),
        ((2, 2), (2, 2)),
        lhs_dilation=(2, 2),
        dimension_numbers=NUMBERS,
        preferred_element_type=F32,
    )[:, 1 : 2 * out_rows + 1, 1:]
    short_kept = lax.dynamic_slice_in_dim(whole(short_low), batch * per_micro, per_micro, 0)
    spread = spread.at[:, ::2, ::2].add(
        jnp.einsum(
            "nhwo,io->nhwi", short_kept, own_out(shortcut, 0), preferred_element_type=F32
        )
    )
    images_grad = lax.all_to_all(
        spread.astype(BF16), "space", 1, 0, axis_index_groups=layout.inner, tiled=True
    ).astype(F32)

    def total(kernel, axis):
        summed = lax.psum(kernel.astype(BF16), "space")
        return lax.all_gather(summed, "batch", axis=axis, tiled=True).astype(F32)

    pooled_out = lax.dynamic_slice_in_dim(pooled, batch * per_micro, per_micro, 0)
    pooled_out = lax.all_gather(
        pooled_out, "space", axis_index_groups=layout.inner, axis=0, tiled=True
    )
    head_w, head_b = lax.psum((head_w, head_b), "space", axis_index_groups=layout.inner)
    gains_d, sums_d, gains_p, sums_p = lax.psum(
        (
            jnp.stack([down_cross, mid_cross, short_cross]),
            jnp.stack([down_sum, mid_sum, short_sum]),
            jnp.stack([first_cross, second_cross]),
            jnp.stack([first_sum, second_sum]),
        ),
        "space",
    )
    return (
        pooled_out,
        images_grad,
        total(down_kernel, 1).reshape(3, 3, entering, half),
        total(mid_kernel, 1).reshape(3, 3, channels, half),
        total(short_kernel, 0),
        gains_d,
        sums_d,
        total(first_kernel, 1).reshape(3, 3, channels, half),
        total(second_kernel, 1).reshape(3, 3, channels, half),
        gains_p,
        sums_p,
        head_w,
        own_out(head_b, 0),
    )


def solution(mesh):
    placed = (
        P("batch", "space", None, None),
        P("batch", None),
        P("batch", None),
    ) + (P(),) * 12
    return jax.shard_map(
        per_device,
        mesh=mesh,
        in_specs=placed,
        out_specs=(
            P("batch", "pipe"),
            P("batch", "space", None, "pipe"),
            P(None, None, None, "pipe"),
            P(None, None, None, "pipe"),
            P(None, "pipe"),
            P(None, "pipe"),
            P(None, "pipe"),
            P(None, None, None, "pipe"),
            P(None, None, None, "pipe"),
            P(None, "pipe"),
            P(None, "pipe"),
            P("pipe", None),
            P("pipe"),
        ),
        check_vma=False,
    )
```

```python
import jax
import jax.numpy as jnp
from jax import lax
from jax.experimental import pallas as pl
from jax.experimental.pallas import tpu as pltpu
from jax.sharding import PartitionSpec as P

EPSILON = 1e-05
NUMBERS = ("NHWC", "HWIO", "NHWC")
HIGHEST = lax.Precision.HIGHEST
F32 = jnp.float32
BF16 = jnp.bfloat16


def silu_slope(values):
    sigmoid = jax.nn.sigmoid(values)
    return sigmoid * (1.0 + values * (1.0 - sigmoid))


def frank_wolfe_kernel(picks_ref, gram_ref, alpha_ref):
    tasks = gram_ref.shape[0]
    lanes = lax.broadcasted_iota(jnp.int32, (1, tasks), 1)
    gram = gram_ref[...]
    alpha = jnp.full((1, tasks), 1.0 / tasks, F32)
    pulled = jnp.sum(gram, axis=0, keepdims=True) * (1.0 / tasks)
    energy = jnp.sum(pulled * alpha, axis=1, keepdims=True)

    def advance(step, carry):
        alpha, pulled, energy = carry
        chosen = picks_ref[step]
        row = gram_ref[pl.ds(chosen, 1), :]
        onehot = (lanes == chosen).astype(F32)
        toward = jnp.sum(pulled * onehot, axis=1, keepdims=True)
        corner = jnp.sum(row * onehot, axis=1, keepdims=True)
        denom = jnp.maximum(energy - 2.0 * toward + corner, 0.05 * corner)
        ratio = jnp.clip((energy - toward) / denom, 0.0, 1.0)
        rest = 1.0 - ratio
        alpha = rest * alpha + ratio * onehot
        pulled = rest * pulled + ratio * row
        energy = rest * rest * energy + 2.0 * rest * ratio * toward + ratio * ratio * corner
        return alpha, pulled, energy

    alpha, _, _ = lax.fori_loop(0, picks_ref.shape[0], advance, (alpha, pulled, energy))
    alpha_ref[...] = alpha


def frank_wolfe(gram, picks):
    tasks = gram.shape[0]
    return pl.pallas_call(
        frank_wolfe_kernel,
        out_shape=jax.ShapeDtypeStruct((1, tasks), F32),
        in_specs=[
            pl.BlockSpec(memory_space=pltpu.SMEM),
            pl.BlockSpec(memory_space=pltpu.VMEM),
        ],
        out_specs=pl.BlockSpec(memory_space=pltpu.VMEM),
    )(picks, gram)


class Layout:
    def __init__(self, micros):
        self.micros = micros
        self.spaces = lax.axis_size("space")
        self.groups = self.spaces // micros
        self.inner = [
            [group * micros + zone for zone in range(micros)] for group in range(self.groups)
        ]
        self.outer = [
            [group * micros + zone for group in range(self.groups)] for zone in range(micros)
        ]
        self.zone = lax.axis_index("space") % micros

    def group_sum(self, tree):
        if self.groups == 1:
            return tree
        return lax.psum(tree, "space", axis_index_groups=self.outer)

    def row_from(self, block, step):
        span = step * self.micros
        route = [
            (i, i + span) for i in range(self.spaces) if 0 <= i + span < self.spaces
        ]
        if not route:
            return jnp.zeros_like(block)
        return lax.ppermute(block, "space", route)

    def rims(self, tensor):
        above = self.row_from(tensor[:, -1:], 1)
        below = self.row_from(tensor[:, :1], -1)
        grown = jnp.concatenate([above, tensor, below], axis=1)
        return jnp.pad(grown, ((0, 0), (0, 0), (1, 1), (0, 0)))


def conv_valid(extended, kernel, stride):
    return lax.conv_general_dilated(
        extended,
        kernel,
        (stride, stride),
        "VALID",
        dimension_numbers=NUMBERS,
        preferred_element_type=F32,
    )


def flipped(kernel):
    return jnp.swapaxes(kernel[::-1, ::-1], 2, 3)


def kernel_grad(extended, grad_low, stride):
    rows, cols = grad_low.shape[1], grad_low.shape[2]
    taps = []
    for row_tap in range(3):
        for col_tap in range(3):
            window = extended[
                :,
                row_tap : row_tap + stride * (rows - 1) + 1 : stride,
                col_tap : col_tap + stride * (cols - 1) + 1 : stride,
            ]
            taps.append(jnp.einsum("nhwi,nhwo->io", window, grad_low, preferred_element_type=F32))
    return jnp.stack(taps)


def norm_forward(layout, conv_out, weight, counted):
    total = layout.group_sum(jnp.sum(conv_out * weight, axis=(0, 1, 2)))
    centered = conv_out - total / counted
    spread = layout.group_sum(jnp.sum(centered * centered * weight, axis=(0, 1, 2)))
    inverse = lax.rsqrt(spread / counted + EPSILON)
    return centered * inverse, inverse


def norm_back(layout, upstream, normed, inverse, gain, weight, counted):
    grad_sum = jnp.sum(upstream * weight, axis=(0, 1, 2))
    cross_sum = jnp.sum(upstream * normed * weight, axis=(0, 1, 2))
    grad_total, cross_total = layout.group_sum((grad_sum, cross_sum))
    correction = weight * (grad_total / counted + normed * (cross_total / counted))
    low = (gain * inverse * (upstream - correction)).astype(BF16)
    return low, cross_sum, grad_sum


KERNEL_LIMIT = 24 * 2**20
PARTS, LAST_PARTS = 4, 1
VM = pl.BlockSpec(memory_space=pltpu.VMEM)
SM = pl.BlockSpec(memory_space=pltpu.SMEM)
NT = (((1,), (1,)), ((), ()))
TN = (((0,), (0,)), ((), ()))
OWN_PX, OTHER_PX, ALL_PX = 8, 9, 10
G_DOWN, G_MID, G_SHORT, B_DOWN, B_MID, B_SHORT, G_FIRST, G_SECOND, B_FIRST, B_SECOND = range(10)


def param(params_ref, row):
    return params_ref[row : row + 1, :]


def call(kernel, outs, operands, scratch=(), flops=0, name=None, after=(), specs=None):
    count = len(operands)
    nbytes = sum(x.size * x.dtype.itemsize for x in operands)
    specs = specs or {}

    def body(*refs):
        kernel(*refs[:count], *refs[count + len(after) :])

    return pl.pallas_call(
        body,
        out_shape=tuple(jax.ShapeDtypeStruct(shape, dtype) for shape, dtype in outs),
        in_specs=[specs.get(i, SM if x.ndim == 1 else VM) for i, x in enumerate(operands)]
        + [pl.BlockSpec(memory_space=pl.ANY)] * len(after),
        out_specs=tuple(SM if len(shape) == 1 else VM for shape, _ in outs),
        scratch_shapes=list(scratch),
        compiler_params=pltpu.CompilerParams(vmem_limit_bytes=KERNEL_LIMIT),
        cost_estimate=pl.CostEstimate(
            flops=int(flops), bytes_accessed=int(nbytes), transcendentals=0
        ),
        name=name,
    )(*operands, *after)


def fold(rows):
    return rows[0:8] + rows[8:16] + rows[16:24] + rows[24:32]


def total_row(part):
    return jnp.sum(part, axis=0, keepdims=True)


def band(row):
    return slice(row * 32, row * 32 + 32)


def put_band(x_ref, image, row, value):
    zero = jnp.zeros_like(value)
    x_ref[image, band(row), 512:1024] = value
    if row < 3:
        x_ref[image, band(row + 1), 0:512] = value
    else:
        x_ref[image, band(0), 0:512] = zero
    if row > 0:
        x_ref[image, band(row - 1), 1024:1536] = value
    else:
        x_ref[image, band(3), 1024:1536] = zero


def columns_joined(left, middle, right):
    count = middle.shape[0]
    column = lax.broadcasted_iota(jnp.int32, (count, 1), 0) % 32
    joined = middle
    if left is not None:
        joined = joined + jnp.where(column == 0, 0.0, pltpu.roll(left, 1, 0))
    if right is not None:
        joined = joined + jnp.where(column == 31, 0.0, pltpu.roll(right, count - 1, 0))
    return joined


def conv_core(x_ref, w_ref, out_ref, back):
    for part in range(1):
        images = slice(0, 8)

        def tap(col):
            value = None
            for row in range(3):
                lhs = x_ref[images, :, row * 512 : (row + 1) * 512].reshape(1024, 512)
                if back:
                    term = lax.dot_general(
                        lhs, w_ref[2 - row, 2 - col], NT, preferred_element_type=F32
                    )
                else:
                    term = jnp.dot(lhs, w_ref[row, col], preferred_element_type=F32)
                value = term if value is None else value + term
            return value

        out = columns_joined(tap(0), tap(1), tap(2))
        out_ref[images] = out.reshape(8, 128, 512)


def stats_of(facts_ref, out_ref, stat_ref, row):
    def add(image, part):
        for r in range(4):
            part = part + fold(out_ref[image, band(r), :]) * facts_ref[image]
        return part

    first = total_row(lax.fori_loop(0, 8, add, jnp.zeros((8, 512), F32)))
    mean = first / jnp.maximum(facts_ref[OWN_PX], 1.0)

    def deviate(image, part):
        for r in range(4):
            away = out_ref[image, band(r), :] - mean
            part = part + fold(away * away) * facts_ref[image]
        return part

    second = total_row(lax.fori_loop(0, 8, deviate, jnp.zeros((8, 512), F32)))
    stat_ref[row : row + 1, :] = first
    stat_ref[row + 1 : row + 2, :] = second


def norm_of(facts_ref, own_ref, other_ref, row):
    own_px, other_px, all_px = facts_ref[OWN_PX], facts_ref[OTHER_PX], facts_ref[ALL_PX]
    own, other = own_ref[row : row + 1, :], other_ref[row : row + 1, :]
    mean = (own + other) / all_px
    apart = own / jnp.maximum(own_px, 1.0) - other / jnp.maximum(other_px, 1.0)
    spread = own_ref[row + 1 : row + 2, :] + other_ref[row + 1 : row + 2, :]
    variance = (spread + apart * apart * (own_px * other_px / all_px)) / all_px
    return mean, lax.rsqrt(variance + EPSILON)


def sigmoid(values):
    return 1.0 / (1.0 + jnp.exp(-values))


def slope_of(values):
    gate = sigmoid(values)
    return gate * (1.0 + values * (1.0 - gate))


MARKS = 128


def pieces_kernel(where_ref, images_ref, labels_ref, count_ref, o0, o1, o2, o3, wide):
    pipe, zone = where_ref[0], where_ref[2]
    tasks = labels_ref.shape[1]
    o0[MARKS:, :] = jnp.zeros((16, 512), BF16)
    for rel, out in enumerate((o0, o1, o2, o3)):
        first = (zone ^ rel) * 4 + pipe * 2
        for i in range(2):
            for row in range(2):
                lines = slice((i * 2 + row) * 32, (i * 2 + row) * 32 + 32)
                for part in range(2):
                    lanes = slice(part * 128, part * 128 + 128)
                    wide[...] = images_ref[first + i, row, :, lanes].astype(F32)
                    for par in range(2):
                        value = wide[pl.ds(par, 32, stride=2), :]
                        start = par * 256 + part * 128
                        out[lines, start : start + 128] = value.astype(BF16)
    marks = jnp.concatenate(
        [
            labels_ref[pl.ds(zone * 4, 4), :].astype(F32),
            jnp.full((4, tasks), count_ref[0, zone].astype(F32)),
            jnp.zeros((8, tasks), F32),
        ]
    )
    o0[MARKS:, 0:tasks] = marks.astype(BF16)


def down_kernel(facts_ref, where_ref, *refs):
    pieces, (w_ref, s_ref, img_ref, out_ref, short_ref, stat_ref, x_ref) = refs[:12], refs[12:]
    batch, zone = where_ref[1], where_ref[2]
    for kb in range(4):
        for kz in range(4):
            piece, base = pieces[kb * 3 + min(kz, 2)], (128 if kz == 3 else 0)
            row = zone ^ kz
            here = pl.ds(pl.multiple_of(row * 32, 32), 32)
            after = pl.ds(pl.multiple_of(((row + 1) % 4) * 32, 32), 32)
            for i in range(2):
                image = (batch ^ kb) * 2 + i
                start = base + i * 64
                odd = piece[start + 32 : start + 64, :]
                img_ref[image, here, 0:512] = piece[start : start + 32, :]
                img_ref[image, here, 512:1024] = odd
                x_ref[image, after, :] = jnp.where(row == 3, jnp.zeros_like(odd), odd)
    for part in range(2):
        images = slice(4 * part, 4 * part + 4)
        blocks = (
            x_ref[images].reshape(512, 512),
            img_ref[images, :, 0:512].reshape(512, 512),
            img_ref[images, :, 512:1024].reshape(512, 512),
        )
        left, middle = None, None
        for row in range(3):
            a = jnp.dot(blocks[row][:, 256:], w_ref[row, 0], preferred_element_type=F32)
            m = jnp.dot(
                blocks[row], w_ref[row, 1:3].reshape(512, 512), preferred_element_type=F32
            )
            left = a if left is None else left + a
            middle = m if middle is None else middle + m
        out_ref[images] = columns_joined(left, middle, None).reshape(4, 128, 512)
        short = jnp.dot(blocks[1][:, :256], s_ref[...], preferred_element_type=F32)
        short_ref[images] = short.reshape(4, 128, 512)
    stats_of(facts_ref, out_ref, stat_ref, 0)
    stats_of(facts_ref, short_ref, stat_ref, 2)
    stat_ref[4:8, :] = jnp.zeros((4, 512), F32)


def layer_kernel(g_row, b_row, facts_ref, in_ref, own_ref, other_ref, params_ref, w_ref,
                 act_ref, out_ref, stat_ref, norm_ref, x_ref):
    mean, inverse = norm_of(facts_ref, own_ref, other_ref, 0)
    gain, bias = param(params_ref, g_row), param(params_ref, b_row)

    def activate(image, carry):
        for r in range(4):
            pre = (in_ref[image, band(r), :] - mean) * inverse * gain + bias
            act = (pre * sigmoid(pre)).astype(BF16)
            act_ref[image, band(r), :] = act
            put_band(x_ref, image, r, act)
        return carry

    lax.fori_loop(0, 8, activate, 0)
    norm_ref[0:1, :] = mean
    norm_ref[1:2, :] = inverse
    norm_ref[2:8, :] = jnp.zeros((6, 512), F32)
    conv_core(x_ref, w_ref, out_ref, False)
    stats_of(facts_ref, out_ref, stat_ref, 0)
    stat_ref[2:8, :] = jnp.zeros((6, 512), F32)


def join_kernel(facts_ref, mid_ref, short_ref, own_m, other_m, own_d, other_d, params_ref,
                w_ref, act_ref, out_ref, stat_ref, norm_ref, x_ref):
    mean_m, inv_m = norm_of(facts_ref, own_m, other_m, 0)
    mean_s, inv_s = norm_of(facts_ref, own_d, other_d, 2)
    gain_m, gain_s = param(params_ref, G_MID), param(params_ref, G_SHORT)
    bias_m, bias_s = param(params_ref, B_MID), param(params_ref, B_SHORT)

    def activate(image, carry):
        for r in range(4):
            pre = (mid_ref[image, band(r), :] - mean_m) * inv_m * gain_m + bias_m
            pre = pre + (short_ref[image, band(r), :] - mean_s) * inv_s * gain_s + bias_s
            act = (pre * sigmoid(pre)).astype(BF16)
            act_ref[image, band(r), :] = act
            put_band(x_ref, image, r, act)
        return carry

    lax.fori_loop(0, 8, activate, 0)
    norm_ref[0:1, :] = mean_m
    norm_ref[1:2, :] = inv_m
    norm_ref[2:3, :] = mean_s
    norm_ref[3:4, :] = inv_s
    norm_ref[4:8, :] = jnp.zeros((4, 512), F32)
    conv_core(x_ref, w_ref, out_ref, False)
    stats_of(facts_ref, out_ref, stat_ref, 0)
    stat_ref[2:8, :] = jnp.zeros((6, 512), F32)


def block_kernel(facts_ref, in_ref, section_ref, own_ref, other_ref, params_ref,
                 pack_ref, norm_ref):
    mean, inverse = norm_of(facts_ref, own_ref, other_ref, 0)
    gain, bias = param(params_ref, G_SECOND), param(params_ref, B_SECOND)
    norm_ref[0:1, :] = mean
    norm_ref[1:2, :] = inverse
    norm_ref[2:8, :] = jnp.zeros((6, 512), F32)

    def gather(image, carry):
        pooled = jnp.zeros((8, 512), F32)
        slopes, crossed = pooled, pooled
        for r in range(4):
            normed = (in_ref[image, band(r), :] - mean) * inverse
            pre = normed * gain + bias + section_ref[image, band(r), :].astype(F32)
            gate = sigmoid(pre)
            slope = gate * (1.0 + pre * (1.0 - gate))
            pooled = pooled + fold(pre * gate)
            slopes = slopes + fold(slope)
            crossed = crossed + fold(slope * normed)
        pack_ref[pl.ds(image, 1), :] = total_row(pooled) / 128.0
        pack_ref[pl.ds(image + 8, 1), :] = total_row(slopes)
        pack_ref[pl.ds(image + 16, 1), :] = total_row(crossed)
        return carry

    lax.fori_loop(0, 8, gather, 0)


def logits_kernel(where_ref, own_ref, other_ref, living_ref, labels_ref, hw_ref, hb_ref,
                  all_ref, errors_ref, cross_ref):
    pipe = where_ref[0]
    for block in range(3):
        rows = slice(block * 8, block * 8 + 8)
        all_ref[block, pl.ds(pl.multiple_of(pipe * 8, 8), 8), :] = own_ref[rows, :]
        all_ref[block, pl.ds(pl.multiple_of((1 - pipe) * 8, 8), 8), :] = other_ref[rows, :]
    logits = (
        lax.dot_general(
            all_ref[0], hw_ref[...], NT, precision=HIGHEST, preferred_element_type=F32
        )
        + hb_ref[...]
    )
    errors = living_ref[...] * (sigmoid(logits) - labels_ref[...])
    errors_ref[...] = errors
    cross_ref[...] = lax.dot_general(
        errors, errors, TN, precision=HIGHEST, preferred_element_type=F32
    )


def head_kernel(picks_ref, where_ref, facts_ref, c0, c1, c2, c3, heads_ref, hw_ref, errors_ref,
                all_ref, in_ref, section_ref, norm_ref, params_ref,
                low_ref, pool_ref, small_ref, alpha_ref, gram_ref):
    tasks = gram_ref.shape[0]
    pipe = where_ref[0]
    gram_ref[...] = ((c0[...] + c1[...]) + (c2[...] + c3[...])) * heads_ref[...]
    frank_wolfe_kernel(picks_ref, gram_ref, alpha_ref)
    grad_logits = (128.0 * tasks) * alpha_ref[...] * errors_ref[...]
    pooled, slopes, crossed = all_ref[0], all_ref[1], all_ref[2]
    grad_pool = (
        jnp.dot(grad_logits, hw_ref[...], precision=HIGHEST, preferred_element_type=F32)
        / 128.0
    )
    grad_sum = total_row(grad_pool * slopes)
    cross_sum = total_row(grad_pool * crossed)
    small_ref[0:tasks, :] = lax.dot_general(
        grad_logits, pooled, TN, precision=HIGHEST, preferred_element_type=F32
    )
    small_ref[tasks : tasks + 1, :] = grad_sum
    small_ref[tasks + 1 : tasks + 2, :] = cross_sum
    small_ref[tasks + 2 :, :] = jnp.zeros((small_ref.shape[0] - tasks - 2, 512), F32)
    for start in (0, 256):
        small_ref[tasks + 2 : tasks + 3, start : start + tasks] = total_row(grad_logits)
    pool_ref[...] = jnp.where(pipe == 0, grad_pool[0:8], grad_pool[8:16])

    mean, inverse = norm_ref[0:1, :], norm_ref[1:2, :]
    gain, bias = param(params_ref, G_SECOND), param(params_ref, B_SECOND)
    all_px = facts_ref[ALL_PX]
    front = gain * inverse
    mean_grad, mean_cross = grad_sum / all_px, cross_sum / all_px

    def back(image, carry):
        up = pool_ref[pl.ds(image, 1), :]
        for r in range(4):
            normed = (in_ref[image, band(r), :] - mean) * inverse
            pre = normed * gain + bias + section_ref[image, band(r), :].astype(F32)
            grad = up * slope_of(pre)
            fix = facts_ref[image] * (mean_grad + normed * mean_cross)
            low_ref[image, band(r), :] = (front * (grad - fix)).astype(BF16)
        return carry

    lax.fori_loop(0, 8, back, 0)


def back_norm(facts_ref, in_ref, up_ref, norm_ref, own_ref, other_ref, gain, rows, sinks):
    mean, inverse = norm_ref[rows : rows + 1, :], norm_ref[rows + 1 : rows + 2, :]
    all_px = facts_ref[ALL_PX]
    front = gain * inverse
    cross_row = 1 + rows // 2
    mean_grad = (own_ref[0:1, :] + other_ref[0:1, :]) / all_px
    mean_cross = (
        own_ref[cross_row : cross_row + 1, :] + other_ref[cross_row : cross_row + 1, :]
    ) / all_px

    def back(image, carry):
        for r in range(4):
            normed = (in_ref[image, band(r), :] - mean) * inverse
            fix = facts_ref[image] * (mean_grad + normed * mean_cross)
            sinks(image, r, (front * (up_ref[image, band(r), :] - fix)).astype(BF16))
        return carry

    lax.fori_loop(0, 8, back, 0)


def second_back_kernel(facts_ref, low_ref, in_ref, norm_ref, params_ref, w_ref,
                       up_ref, sum_ref, x_ref, conv_ref):
    def fill(image, carry):
        for r in range(4):
            put_band(x_ref, image, r, low_ref[image, band(r), :])
        return carry

    lax.fori_loop(0, 8, fill, 0)
    conv_core(x_ref, w_ref, conv_ref, True)
    gain, bias = param(params_ref, G_FIRST), param(params_ref, B_FIRST)
    slope_sums(facts_ref, in_ref, norm_ref, gain, bias, conv_ref, up_ref, sum_ref)


def slope_sums(facts_ref, in_ref, norm_ref, gain, bias, conv_ref, up_ref, sum_ref):
    mean, inverse = norm_ref[0:1, :], norm_ref[1:2, :]

    def slope(image, carry):
        grads, crosses = carry
        for r in range(4):
            normed = (in_ref[image, band(r), :] - mean) * inverse
            up = conv_ref[image, band(r), :] * slope_of(normed * gain + bias)
            up_ref[image, band(r), :] = up
            living = facts_ref[image]
            grads = grads + fold(up) * living
            crosses = crosses + fold(up * normed) * living
        return grads, crosses

    zero = jnp.zeros((8, 512), F32)
    grads, crosses = lax.fori_loop(0, 8, slope, (zero, zero))
    sum_ref[0:1, :] = total_row(grads)
    sum_ref[1:2, :] = total_row(crosses)
    sum_ref[2:8, :] = jnp.zeros((6, 512), F32)


def first_back_kernel(facts_ref, up_in, in_ref, norm_ref, own_ref, other_ref, params_ref, w_ref,
                      second_ref, norm2_ref, section_ref, pool_ref, mid_ref, short_ref, normd_ref,
                      low_ref, up_ref, sum_ref, x_ref, conv_ref):
    def keep(image, r, low):
        low_ref[image, band(r), :] = low
        put_band(x_ref, image, r, low)

    back_norm(facts_ref, in_ref, up_in, norm_ref, own_ref, other_ref, param(params_ref, G_FIRST),
              0, keep)
    conv_core(x_ref, w_ref, conv_ref, True)
    mean2, inv2 = norm2_ref[0:1, :], norm2_ref[1:2, :]
    gain2, bias2 = param(params_ref, G_SECOND), param(params_ref, B_SECOND)
    mean_m, inv_m = normd_ref[0:1, :], normd_ref[1:2, :]
    mean_s, inv_s = normd_ref[2:3, :], normd_ref[3:4, :]
    gain_m, gain_s = param(params_ref, G_MID), param(params_ref, G_SHORT)
    bias_m, bias_s = param(params_ref, B_MID), param(params_ref, B_SHORT)

    def join(image, carry):
        grads, cross_m, cross_s = carry
        pool = pool_ref[pl.ds(image, 1), :]
        for r in range(4):
            pre2 = (second_ref[image, band(r), :] - mean2) * inv2 * gain2 + bias2
            pre2 = pre2 + section_ref[image, band(r), :].astype(F32)
            entry = conv_ref[image, band(r), :] + pool * slope_of(pre2)
            entry = entry.astype(BF16).astype(F32)
            norm_m = (mid_ref[image, band(r), :] - mean_m) * inv_m
            norm_s = (short_ref[image, band(r), :] - mean_s) * inv_s
            pre = norm_m * gain_m + bias_m + norm_s * gain_s + bias_s
            up = entry * slope_of(pre)
            up_ref[image, band(r), :] = up
            living = facts_ref[image]
            grads = grads + fold(up) * living
            cross_m = cross_m + fold(up * norm_m) * living
            cross_s = cross_s + fold(up * norm_s) * living
        return grads, cross_m, cross_s

    zero = jnp.zeros((8, 512), F32)
    grads, cross_m, cross_s = lax.fori_loop(0, 8, join, (zero, zero, zero))
    sum_ref[0:1, :] = total_row(grads)
    sum_ref[1:2, :] = total_row(cross_m)
    sum_ref[2:3, :] = total_row(cross_s)
    sum_ref[3:8, :] = jnp.zeros((5, 512), F32)


def mid_back_kernel(facts_ref, up_in, mid_ref, short_ref, normd_ref, own_ref, other_ref, params_ref,
                    w_ref, in_ref, norm1_ref,
                    low_ref, low_s_ref, up_ref, sum_ref, x_ref, conv_ref):
    def keep(image, r, low):
        low_ref[image, band(r), :] = low
        put_band(x_ref, image, r, low)

    def keep_short(image, r, low):
        low_s_ref[image, band(r), :] = low

    gain_m, gain_s = param(params_ref, G_MID), param(params_ref, G_SHORT)
    back_norm(facts_ref, mid_ref, up_in, normd_ref, own_ref, other_ref, gain_m, 0, keep)
    back_norm(facts_ref, short_ref, up_in, normd_ref, own_ref, other_ref, gain_s, 2, keep_short)
    conv_core(x_ref, w_ref, conv_ref, True)
    gain, bias = param(params_ref, G_DOWN), param(params_ref, B_DOWN)
    slope_sums(facts_ref, in_ref, norm1_ref, gain, bias, conv_ref, up_ref, sum_ref)


def down_back_kernel(facts_ref, up_in, in_ref, norm1_ref, own_ref, other_ref, params_ref, low_ref):
    def keep(image, r, low):
        low_ref[image, band(r), :] = low

    gain = param(params_ref, G_DOWN)
    back_norm(facts_ref, in_ref, up_in, norm1_ref, own_ref, other_ref, gain, 0, keep)


def image_back_kernel(where_ref, low_ref, low_s_ref, w_ref, s_ref, o0, o1, o2, o3, stage_ref):
    pipe, batch, zone = where_ref[0], where_ref[1], where_ref[2]
    mine = pl.ds(batch * 2, 2)
    here = low_ref[mine]
    below = jnp.concatenate([here[:, 32:], jnp.zeros((2, 32, 512), BF16)], axis=1)
    here, below = here.reshape(256, 512), below.reshape(256, 512)
    short = low_s_ref[mine].reshape(256, 512)

    def back(lhs, row, col):
        return lax.dot_general(lhs, w_ref[row, col], NT, preferred_element_type=F32)

    even_even = back(here, 1, 1) + lax.dot_general(
        short, s_ref[...], NT, preferred_element_type=F32
    )
    even_odd = columns_joined(None, back(here, 1, 2), back(here, 1, 0))
    odd_even = back(here, 2, 1) + back(below, 0, 1)
    odd_odd = columns_joined(
        None, back(here, 2, 2) + back(below, 0, 2), back(here, 2, 0) + back(below, 0, 0)
    )
    planes = ((even_even, even_odd), (odd_even, odd_odd))
    for row in range(2):
        for par in range(2):
            plane = planes[row][par].reshape(2, 4, 32, 256).astype(BF16)
            lanes = slice(par * 128, par * 128 + 128)
            for side in range(2):
                half = plane[..., side * 128 : side * 128 + 128]
                for z in range(4):
                    stage_ref[z ^ zone, side ^ pipe, :, row, :, lanes] = half[:, z]
    for rel, out in enumerate((o0, o1, o2, o3)):
        out[...] = stage_ref[rel]


def image_grad_kernel(where_ref, own_ref, got_ref, out_ref):
    pipe, zone = where_ref[0], where_ref[2]
    for rel in range(4):
        for side, pieces in enumerate((own_ref, got_ref)):
            first = (zone ^ rel) * 4 + (pipe if side == 0 else 1 - pipe) * 2
            for i in range(2):
                for row in range(2):
                    for par in range(2):
                        out_ref[first + i, row, pl.ds(par, 32, stride=2), :] = pieces[
                            rel, i, row, :, par * 128 : (par + 1) * 128
                        ].astype(F32)


def slot_of(quarter, zone):
    rel = quarter ^ zone
    return (rel >> 1) | ((rel & 1) << 1)


def shifted_window(turned, down, right):
    pixel = lax.broadcasted_iota(jnp.int32, (1, 128), 1)
    column, row = pixel % 32 + right, pixel // 32 + down
    inside = (column >= 0) & (column < 32) & (row >= 0) & (row < 4)
    amount = (256 - down * 32 - right) % 128
    moved = turned if isinstance(amount, int) and amount == 0 else pltpu.roll(turned, amount, 1)
    return jnp.where(inside, moved, 0.0).astype(BF16)


def split_out(pipe, zone, unit, result_own, result_other, own_ref, other_ref):
    for quarter in range(4):
        slot = slot_of(quarter, zone)
        rows = slice(quarter * 32, quarter * 32 + 32)
        own_ref[slot, unit] = result_own[rows]
        other_ref[slot, unit] = result_other[rows].astype(BF16)


def hand_out(other_ref, outs):
    each = 4 // len(outs)
    for slot in range(4):
        outs[slot // each][slot % each] = other_ref[slot]


def turned_taps(batch, act_ref, turned_ref):
    lanes = pl.ds(pl.multiple_of(batch * 128, 128), 128)

    def turn(image, carry):
        turned = act_ref[image, :, lanes].astype(F32).T
        pixels = pl.ds(pl.multiple_of(image * 128, 128), 128)
        for row in range(3):
            for col in range(3):
                turned_ref[row * 3 + col, :, pixels] = shifted_window(turned, row - 1, col - 1)
        return carry

    lax.fori_loop(0, 8, turn, 0)


def tap_products(pipe, zone, low_ref, turned_ref, own_ref, other_ref):
    lhs = turned_ref[0:9].reshape(9 * 128, 1024)
    results = []
    for side in (pipe, 1 - pipe):
        columns = pl.ds(pl.multiple_of(side * 256, 256), 256)
        rhs = low_ref[:, :, columns].reshape(1024, 256)
        results.append(jnp.dot(lhs, rhs, preferred_element_type=F32))
    for unit in range(9):
        rows = slice(unit * 128, unit * 128 + 128)
        split_out(pipe, zone, unit, results[0][rows], results[1][rows], own_ref, other_ref)


def kernel_grad_kernel(where_ref, act_ref, low_ref, own_ref, *refs):
    outs, (turned_ref, other_ref) = refs[:-2], refs[-2:]
    pipe, batch, zone = where_ref[0], where_ref[1], where_ref[2]
    turned_taps(batch, act_ref, turned_ref)
    tap_products(pipe, zone, low_ref, turned_ref, own_ref, other_ref)
    hand_out(other_ref, outs)


DOWN_UNITS = (
    ((0, 0, 0, 4), (2, -1, 0, 1), (2, 0, 0, 7), (0, 0, 0, 9), (1, 0, 0, 5)),
    ((1, 0, -1, 3), (3, -1, -1, 0), (3, -1, 0, 2), (3, 0, -1, 6), (3, 0, 0, 8)),
)


def down_grad_kernel(where_ref, img_ref, low_ref, low_s_ref, own_ref, *refs):
    outs, (turned_ref, other_ref) = refs[:-2], refs[-2:]
    pipe, batch, zone = where_ref[0], where_ref[1], where_ref[2]
    upper, part = batch // 2, batch % 2

    for turn_kind in range(2):

        @pl.when(upper == turn_kind)
        def _(units=DOWN_UNITS[turn_kind]):
            def turn(image, carry):
                pixels = pl.ds(pl.multiple_of(image * 128, 128), 128)
                seen = {}
                for unit, (plane, down, right, _) in enumerate(units):
                    if plane not in seen:
                        lanes = pl.ds(pl.multiple_of(plane * 256 + part * 128, 128), 128)
                        seen[plane] = img_ref[image, :, lanes].astype(F32).T
                    turned_ref[unit, :, pixels] = shifted_window(seen[plane], down, right)
                return carry

            lax.fori_loop(0, 8, turn, 0)

    short_unit = [tap for _, _, _, tap in DOWN_UNITS[0]].index(9)
    for unit in range(5):
        lhs = turned_ref[unit]
        results = []
        for side in (pipe, 1 - pipe):
            columns = pl.ds(pl.multiple_of(side * 256, 256), 256)
            rhs = low_ref[:, :, columns].reshape(1024, 256)
            if unit == short_unit:
                rhs_s = low_s_ref[:, :, columns].reshape(1024, 256)
                rhs = jnp.where(upper == 0, rhs_s, rhs)
            results.append(jnp.dot(lhs, rhs, preferred_element_type=F32))
        split_out(pipe, zone, unit, results[0], results[1], own_ref, other_ref)
    hand_out(other_ref, outs)


def add_cores_kernel(own_ref, *refs):
    got, (keep_ref, send_ref) = refs[:-2], refs[-2:]
    each = 4 // len(got)
    for slot in range(4):
        value = own_ref[slot] + got[slot // each][slot % each].astype(F32)
        if slot < 2:
            keep_ref[slot] = value
        else:
            send_ref[slot - 2] = value.astype(BF16)


def add_near_kernel(own_ref, got_ref, keep_ref, send_ref):
    keep_ref[...] = own_ref[0] + got_ref[0].astype(F32)
    send_ref[...] = (own_ref[1] + got_ref[1].astype(F32)).astype(BF16)


def add_far_kernel(own_ref, got_ref, out_ref):
    out_ref[...] = (own_ref[...] + got_ref[...].astype(F32)).astype(BF16)


def join_kernel_of(*refs):
    at = 0
    for ref in refs[:-1]:
        if len(ref.shape) == 3:
            refs[-1][at] = ref[...]
            at += 1
        else:
            refs[-1][at : at + ref.shape[0]] = ref[...]
            at += ref.shape[0]


def gathered_blocks(zone, batch, refs):
    if len(refs) == 8:
        for kb in range(4):
            for rel in range(4):
                yield batch ^ kb, zone ^ rel, refs[2 * kb + rel % 2], rel // 2
        return
    a, b, ax, by, ayy, bxx = refs
    sets = {0: (a, b, 0, 0), 1: (ax, bxx, 0, 0), 2: (ayy, by, 0, 0), 3: (ayy, bxx, 2, 2)}
    for kb in range(4):
        even, odd, base_even, base_odd = sets[kb]
        for rel in range(4):
            if rel % 2 == 1:
                yield batch ^ kb, zone ^ rel, odd, base_odd + rel // 2
            else:
                yield batch ^ kb, zone ^ rel, even, base_even + rel // 2


def assemble_kernel(where_ref, *refs):
    pieces, out_ref = refs[:-1], refs[-1]
    batch, zone = where_ref[1], where_ref[2]
    for owner, quarter, ref, index in gathered_blocks(zone, batch, pieces):
        rows = pl.ds(pl.multiple_of(owner * 128 + quarter * 32, 32), 32)
        out_ref[:, rows, :] = ref[index].astype(F32)


def assemble_down_kernel(where_ref, *refs):
    pieces, (out_ref, short_ref) = refs[:-2], refs[-2:]
    batch, zone = where_ref[1], where_ref[2]
    for owner, quarter, ref, index in gathered_blocks(zone, batch, pieces):
        upper, part = owner // 2, owner % 2
        rows = pl.ds(pl.multiple_of(part * 128 + quarter * 32, 32), 32)
        value = ref[index].astype(F32)
        for kind in range(2):

            @pl.when(upper == kind)
            def _(value=value, rows=rows, units=DOWN_UNITS[kind]):
                for unit, (_, _, _, tap) in enumerate(units):
                    if tap == 9:
                        short_ref[rows, :] = value[unit]
                    else:
                        out_ref[tap, rows, :] = value[unit]


def facts_kernel(where_ref, p0, p1, p2, p3, hw_ref, facts_ref, living_ref, targets_ref, heads_ref):
    pipe, batch = where_ref[0], where_ref[1]
    tasks = hw_ref.shape[0]
    alive = [jnp.float32(0.0), jnp.float32(0.0)]
    for rel, piece in enumerate((p0, p1, p2, p3)):
        owner = batch ^ rel
        marks = piece[MARKS:, 0:tasks].astype(F32)
        count = jnp.max(marks[4:5, :])
        for slot in range(4):
            side, place = slot // 2, owner * 2 + slot % 2
            living = (count > slot + 0.5).astype(F32)
            alive[side] = alive[side] + living
            row = pl.ds(side * 8 + place, 1)
            living_ref[row, :] = jnp.full((1, tasks), living)
            targets_ref[row, :] = marks[slot : slot + 1, :]

            @pl.when(pipe == side)
            def _(place=place, living=living):
                facts_ref[place] = living

    own = jnp.where(pipe == 0, alive[0], alive[1])
    facts_ref[OWN_PX] = own * 128.0
    facts_ref[OTHER_PX] = (alive[0] + alive[1] - own) * 128.0
    facts_ref[ALL_PX] = (alive[0] + alive[1]) * 128.0
    for rest in range(ALL_PX + 1, 16):
        facts_ref[rest] = jnp.float32(0.0)
    heads_ref[...] = lax.dot_general(
        hw_ref[...], hw_ref[...], NT, precision=HIGHEST, preferred_element_type=F32
    )


SMALL_ROWS = 64


def small_kernel(where_ref, head_ref, all_ref, sum_f, other_f, sum_j, other_j, sum_d, other_d,
                 sent_ref, wide_ref):
    pipe, batch = where_ref[0], where_ref[1]
    tasks = head_ref.shape[0] - 8
    wide_ref[...] = jnp.zeros(wide_ref.shape, F32)
    wide_ref[0 : tasks + 3, :] = head_ref[0 : tasks + 3, :]
    at = tasks + 3
    for own, other, count in ((sum_f, other_f, 2), (sum_j, other_j, 3), (sum_d, other_d, 2)):
        wide_ref[at : at + count, :] = own[0:count, :] + other[0:count, :]
        at += count
    for side in range(2):
        for slot in range(2):
            row = side * 8 + batch * 2 + slot
            at_row = SMALL_ROWS - 8 + side * 2 + slot
            wide_ref[at_row : at_row + 1, :] = all_ref[0, pl.ds(row, 1), :]
    sent_ref[...] = wide_ref[:, pl.ds(pl.multiple_of(pipe * 256, 256), 256)]


def small_out_kernel(where_ref, p0, p1, p2, p3, pooled_ref, head_ref, gd_ref, bd_ref, gp_ref, bp_ref,
                     headb_ref):
    tasks = head_ref.shape[0]
    zone = where_ref[2]
    for rel, part in enumerate((p0, p1, p2, p3)):
        pooled_ref[zone ^ rel] = part[SMALL_ROWS - 8 : SMALL_ROWS - 4, :]
    total = (p0[...] + p1[...]) + (p2[...] + p3[...])
    head_ref[...] = total[0:tasks]

    def line(at):
        return total[tasks + at : tasks + at + 1]

    headb_ref[...] = line(2)
    bp_ref[0:1, :], gp_ref[0:1, :] = line(3), line(4)
    bp_ref[1:2, :], gp_ref[1:2, :] = line(0), line(1)
    bd_ref[0:1, :], gd_ref[0:1, :] = line(8), line(9)
    bd_ref[1:2, :], gd_ref[1:2, :] = line(5), line(6)
    bd_ref[2:3, :], gd_ref[2:3, :] = line(5), line(7)


def fast_device(images, image_counts, labels, fw_picks, conv_down, conv_mid, shortcut, gains_down,
                biases_down, conv_first, conv_second, gains_plain, biases_plain, head_weight,
                head_bias):
    pipe, batch, zone = (lax.axis_index(axis) for axis in ("pipe", "batch", "space"))
    tasks = head_weight.shape[1]

    def over(axis, rel, x):
        size = lax.axis_size(axis)
        return lax.ppermute(x, axis, [(i, i ^ rel) for i in range(size)])

    where = jnp.stack([pipe, batch, zone, zone]).astype(jnp.int32)
    params = jnp.concatenate([gains_down, biases_down, gains_plain, biases_plain])
    turned_heads = head_weight.T
    bias_row = head_bias.reshape(1, tasks)

    pieces = call(
        pieces_kernel,
        [((144, 512), BF16)] + [((128, 512), BF16)] * 3,
        [where, images, labels, image_counts],
        [pltpu.VMEM((64, 128), F32)],
        name="pieces",
        specs={3: SM},
    )
    moved = [over("space", rel, pieces[rel]) for rel in (1, 2, 3)]
    moved = [pieces[0], moved[0], jnp.concatenate([moved[1], moved[2]])]
    gathered = [moved] + [[over("batch", kb, x) for x in moved] for kb in (1, 2, 3)]
    facts, living, targets, heads = call(
        facts_kernel,
        [((16,), F32), ((16, tasks), F32), ((16, tasks), F32), ((tasks, tasks), F32)],
        [where] + [line[0] for line in gathered] + [turned_heads],
        name="facts",
    )

    big = ((8, 128, 512), F32)
    low = ((8, 128, 512), BF16)
    rows = ((8, 512), F32)
    x_scratch = pltpu.VMEM((8, 128, 1536), BF16)
    conv_scratch = pltpu.VMEM((8, 128, 512), F32)
    conv_flops = 2 * 1024 * 4608 * 512

    def partner(x):
        return over("pipe", 1, x)

    img, down_out, short_out, stat_d = call(
        down_kernel,
        [((8, 128, 1024), BF16), big, big, rows],
        [facts, where] + [piece for line in gathered for piece in line] + [conv_down, shortcut],
        [pltpu.VMEM((8, 128, 512), BF16)],
        conv_flops // 2,
        "down",
    )
    other_d = partner(stat_d)
    down_act, mid_out, stat_m, norm_d = call(
        lambda *refs: layer_kernel(G_DOWN, B_DOWN, *refs),
        [low, big, rows, rows],
        [facts, down_out, stat_d, other_d, params, conv_mid],
        [x_scratch],
        conv_flops,
        "mid",
    )
    other_m = partner(stat_m)
    section, first_out, stat_f, norm_j = call(
        join_kernel,
        [low, big, rows, rows],
        [facts, mid_out, short_out, stat_m, other_m, stat_d, other_d, params, conv_first],
        [x_scratch],
        conv_flops,
        "first",
    )
    other_f = partner(stat_f)
    plain_act, second_out, stat_s, norm_f = call(
        lambda *refs: layer_kernel(G_FIRST, B_FIRST, *refs),
        [low, big, rows, rows],
        [facts, first_out, stat_f, other_f, params, conv_second],
        [x_scratch],
        conv_flops,
        "second",
    )
    other_s = partner(stat_s)
    pack, norm_s = call(
        block_kernel,
        [((24, 512), F32), rows],
        [facts, second_out, section, stat_s, other_s, params],
        name="block",
    )
    other_pack = partner(pack)
    all_pack, errors, cross = call(
        logits_kernel,
        [((3, 16, 512), F32), ((16, tasks), F32), ((tasks, tasks), F32)],
        [where, pack, other_pack, living, targets, turned_heads, bias_row],
        name="logits",
    )
    crosses = [cross] + [over("space", rel, cross) for rel in (1, 2, 3)]
    second_low, grad_pool, small = call(
        head_kernel,
        [low, rows, ((tasks + 8, 512), F32)],
        [fw_picks, where, facts] + crosses
        + [heads, turned_heads, errors, all_pack, second_out, section, norm_s, params],
        [pltpu.VMEM((1, tasks), F32), pltpu.VMEM((tasks, tasks), F32)],
        name="head",
    )

    class Sum:
        def __init__(self, kernel, units, operands, scratch, flops, name, after=(), parts=4):
            self.units, self.name = units, name
            self.own, *self.other = call(
                kernel,
                [self.block(4, dtype=F32)] + [self.block(4 // parts)] * parts,
                operands,
                [scratch, pltpu.VMEM((4, units, 32, 256), BF16)],
                flops,
                name,
                after,
            )
            self.got = [partner(x) for x in self.other]

        def block(self, *lead, dtype=BF16):
            return (lead + (self.units, 32, 256), dtype)

        def cores(self, after=()):
            self.keep, sent = call(
                add_cores_kernel,
                [self.block(2, dtype=F32), self.block(2)],
                [self.own] + self.got,
                name=self.name + "_cores",
                after=after,
            )
            self.near = over("space", 1, sent)

        def zone_near(self, after=()):
            self.keep, sent = call(
                add_near_kernel,
                [self.block(dtype=F32), self.block()],
                [self.keep, self.near],
                name=self.name + "_near",
                after=after,
            )
            self.far = over("space", 2, sent)

        def zone_far(self, after=()):
            (self.final,) = call(
                add_far_kernel,
                [self.block()],
                [self.keep, self.far],
                name=self.name + "_final",
                after=after,
            )
            self.other_far = over("space", 2, self.final)

        def pair(self, after=()):
            (self.a,) = call(
                join_kernel_of,
                [self.block(2)],
                [self.final, self.other_far],
                name=self.name + "_pair",
                after=after,
            )
            self.b = over("space", 1, self.a)

        def direct(self):
            self.ra = [over("batch", rel, self.a) for rel in (1, 2, 3)]
            self.rb = [over("batch", rel, self.b) for rel in (1, 2, 3)]
            self.blocks = [where, self.a, self.b]
            for x, y in zip(self.ra, self.rb):
                self.blocks += [x, y]

        def plane(self):
            self.ax, self.by = over("batch", 1, self.a), over("batch", 2, self.b)

        def plane_far(self, after=()):
            self.fa, self.fb = [
                call(join_kernel_of, [self.block(4)], pair, name=self.name + "_cross", after=after)[0]
                for pair in ([self.a, self.ax], [self.b, self.by])
            ]
            self.ayy, self.bxx = over("batch", 2, self.fa), over("batch", 1, self.fb)
            self.blocks = [where, self.a, self.b, self.ax, self.by, self.ayy, self.bxx]

    def kernel_grad_of(act, low_grad, name, after=(), parts=PARTS):
        return Sum(
            kernel_grad_kernel, 9, [where, act, low_grad], pltpu.VMEM((9, 128, 1024), BF16),
            conv_flops // 4, name, after, parts,
        )

    def assembled(blocks, name, after=()):
        (out,) = call(assemble_kernel, [((9, 512, 256), F32)], blocks, name=name, after=after)
        return out.reshape(3, 3, 512, 256)

    second = kernel_grad_of(plain_act, second_low, "second_grad")
    second.cores()
    up_f, sum_f = call(
        second_back_kernel,
        [big, rows],
        [facts, second_low, first_out, norm_f, params, conv_second],
        [x_scratch, conv_scratch],
        conv_flops,
        "second_back",
        after=[second.keep],
    )
    other_sf = partner(sum_f)
    second.zone_near(after=[sum_f])
    first_low, up_j, sum_j = call(
        first_back_kernel,
        [low, big, rows],
        [facts, up_f, first_out, norm_f, sum_f, other_sf, params, conv_first,
         second_out, norm_s, section, grad_pool, mid_out, short_out, norm_j],
        [x_scratch, conv_scratch],
        conv_flops,
        "first_back",
        after=[second.keep],
    )
    other_sj = partner(sum_j)
    second.zone_far(after=[sum_j])
    first = kernel_grad_of(section, first_low, "first_grad", after=[second.final])
    second.pair(after=first.other[0:1])
    second.plane()
    first.cores(after=[second.a])
    mid_low, short_low, up_d, sum_d = call(
        mid_back_kernel,
        [low, low, big, rows],
        [facts, up_j, mid_out, short_out, norm_j, sum_j, other_sj, params, conv_mid,
         down_out, norm_d],
        [x_scratch, conv_scratch],
        conv_flops,
        "mid_back",
        after=[first.keep],
    )
    other_sd = partner(sum_d)
    first.zone_near(after=[sum_d, second.b, second.ax])
    mid = kernel_grad_of(down_act, mid_low, "mid_grad", after=[first.keep])
    first.zone_far(after=mid.other[0:1])
    mid.cores(after=[first.final])
    second.plane_far(after=[mid.keep])
    (down_low,) = call(
        down_back_kernel,
        [low],
        [facts, up_d, down_out, norm_d, sum_d, other_sd, params],
        name="down_back",
        after=[second.fa, second.fb],
    )
    down = Sum(
        down_grad_kernel, 5, [where, img, down_low, short_low], pltpu.VMEM((5, 128, 1024), BF16),
        conv_flops // 8, "down_grad", parts=LAST_PARTS,
    )
    first.pair(after=down.other[0:1])
    first.plane()
    mid.zone_near(after=[first.a])
    down.cores(after=[mid.keep])
    img_pieces = call(
        image_back_kernel,
        [((2, 2, 2, 32, 256), BF16)] * 4,
        [where, down_low, short_low, conv_down, shortcut],
        [pltpu.VMEM((4, 2, 2, 2, 32, 256), BF16)],
        conv_flops // 8,
        "image_back",
        after=[down.keep],
    )
    mid.zone_far(after=[img_pieces[0]])
    down.zone_near(after=[mid.final])
    second_out_grad = assembled(second.blocks, "second_out", after=[down.keep, first.b])
    first.plane_far(after=[second_out_grad])
    mid.pair(after=[first.fa, first.fb])
    mid.plane()
    down.zone_far(after=[mid.a])
    down.pair()
    down.plane()
    first_out_grad = assembled(first.blocks, "first_out", after=[down.a])
    mid.plane_far(after=[first_out_grad])
    down.plane_far(after=[mid.fa, mid.fb])
    mid_out_grad = assembled(mid.blocks, "mid_out", after=[down.fa])

    img_moved = [img_pieces[0]] + [over("space", rel, img_pieces[rel]) for rel in (1, 2, 3)]
    img_moved = jnp.stack(img_moved)
    img_got = partner(img_moved[:, 1])
    (images_grad,) = call(
        image_grad_kernel,
        [((16, 2, 64, 128), F32)],
        [where, img_moved[:, 0], img_got],
        name="image_grad",
    )

    (sent,) = call(
        small_kernel,
        [((SMALL_ROWS, 256), F32)],
        [where, small, all_pack, sum_f, other_sf, sum_j, other_sj, sum_d, other_sd],
        [pltpu.VMEM((SMALL_ROWS, 512), F32)],
        name="small",
        after=[down.final],
    )
    parts = [sent] + [over("space", rel, sent) for rel in (1, 2, 3)]
    pooled, head_out, gains_d, sums_d, gains_p, sums_p, head_b = call(
        small_out_kernel,
        [((4, 4, 256), F32), ((tasks, 256), F32), ((3, 256), F32), ((3, 256), F32),
         ((2, 256), F32), ((2, 256), F32), ((1, 256), F32)],
        [where] + parts,
        name="small_out",
    )
    down_grad, short_grad = call(
        assemble_down_kernel,
        [((9, 256, 256), F32), ((256, 256), F32)],
        down.blocks,
        name="down_out",
    )
    return (
        pooled.reshape(16, 256),
        images_grad,
        down_grad.reshape(3, 3, 256, 256),
        mid_out_grad,
        short_grad,
        gains_d,
        sums_d,
        first_out_grad,
        second_out_grad,
        gains_p,
        sums_p,
        head_out.T,
        lax.dynamic_slice_in_dim(head_b[0], pipe * (tasks // 2), tasks // 2, 0),
    )


def per_device(
    images,
    image_counts,
    labels,
    fw_picks,
    conv_down,
    conv_mid,
    shortcut,
    gains_down,
    biases_down,
    conv_first,
    conv_second,
    gains_plain,
    biases_plain,
    head_weight,
    head_bias,
):
    layout = Layout(image_counts.shape[1])
    micros, zone = layout.micros, layout.zone
    sizes = (images.shape, conv_down.shape, lax.axis_size("pipe"), lax.axis_size("batch"))
    if layout.groups == 1 and sizes == ((16, 2, 64, 256), (3, 3, 256, 512), 2, 4):
        return fast_device(
            images, image_counts, labels, fw_picks, conv_down, conv_mid, shortcut, gains_down,
            biases_down, conv_first, conv_second, gains_plain, biases_plain, head_weight,
            head_bias,
        )
    batches, pipes = lax.axis_size("batch"), lax.axis_size("pipe")
    batch = lax.axis_index("batch")
    pipe = lax.axis_index("pipe")
    per_micro = images.shape[0] // micros
    count = per_micro * batches
    entering, channels = conv_down.shape[2], conv_mid.shape[3]
    tasks = head_weight.shape[1]
    half = channels // pipes
    own = pipe * half

    def own_out(kernel, axis):
        size = kernel.shape[axis] // pipes
        return lax.dynamic_slice_in_dim(kernel, pipe * size, size, axis)

    def whole(tensor, axis=3):
        return lax.all_gather(tensor, "pipe", axis=axis, tiled=True)

    def share(tensor):
        size = tensor.shape[3] // batches
        return lax.dynamic_slice_in_dim(tensor, batch * size, size, 3)

    mine = lax.all_to_all(
        images, "space", 0, 1, axis_index_groups=layout.inner, tiled=True
    )
    mine = lax.all_gather(mine, "batch", axis=0, tiled=True)
    counts = lax.all_gather(image_counts, "batch", axis=0, tiled=True)
    counts = lax.dynamic_slice_in_dim(counts, zone, 1, 1)[:, 0]
    marks = lax.dynamic_slice_in_dim(labels, zone * per_micro, per_micro, 0)
    targets = lax.all_gather(marks, "batch", axis=0, tiled=True).astype(F32)
    slots = jnp.arange(per_micro, dtype=jnp.int32)
    living = (slots[None, :] < counts[:, None]).astype(F32).reshape(count)
    weight = living[:, None, None, None]
    out_rows, out_cols = mine.shape[1] // 2, mine.shape[2] // 2
    image_pixels = out_rows * layout.groups * out_cols
    counted = jnp.sum(living) * image_pixels
    scale = float(image_pixels * tasks)

    gain_d, bias_d = own_out(gains_down, 1), own_out(biases_down, 1)
    gain_p, bias_p = own_out(gains_plain, 1), own_out(biases_plain, 1)

    above = layout.row_from(mine[:, -1:], 1)
    down_ext = jnp.pad(
        jnp.concatenate([above, mine], axis=1), ((0, 0), (0, 0), (1, 0), (0, 0))
    )
    down_out = conv_valid(down_ext, own_out(conv_down, 3), 2)
    down_norm, down_inv = norm_forward(layout, down_out, weight, counted)
    down_pre = down_norm * gain_d[0] + bias_d[0]
    mid_ext = layout.rims(whole(jax.nn.silu(down_pre).astype(BF16)))
    mid_out = conv_valid(mid_ext, own_out(conv_mid, 3), 1)
    short_in = mine[:, ::2, ::2]
    short_out = jnp.einsum(
        "nhwi,io->nhwo", short_in, own_out(shortcut, 1), preferred_element_type=F32
    )
    mid_norm, mid_inv = norm_forward(layout, mid_out, weight, counted)
    short_norm, short_inv = norm_forward(layout, short_out, weight, counted)
    section_pre = mid_norm * gain_d[1] + bias_d[1] + short_norm * gain_d[2] + bias_d[2]
    section = jax.nn.silu(section_pre).astype(BF16)
    first_ext = layout.rims(whole(section))
    first_out = conv_valid(first_ext, own_out(conv_first, 3), 1)
    first_norm, first_inv = norm_forward(layout, first_out, weight, counted)
    first_pre = first_norm * gain_p[0] + bias_p[0]
    second_ext = layout.rims(whole(jax.nn.silu(first_pre).astype(BF16)))
    second_out = conv_valid(second_ext, own_out(conv_second, 3), 1)
    second_norm, second_inv = norm_forward(layout, second_out, weight, counted)
    block_pre = second_norm * gain_p[1] + bias_p[1] + section.astype(F32)
    pooled = layout.group_sum(jnp.sum(jax.nn.silu(block_pre), axis=(1, 2))) / image_pixels

    pooled_all = whole(pooled, 1)
    logits = jnp.dot(pooled_all, head_weight, precision=HIGHEST) + head_bias
    errors = living[:, None] * (jax.nn.sigmoid(logits) - targets)
    cross = jnp.einsum("nt,ns->ts", errors, errors, precision=HIGHEST)
    cross = lax.psum(cross, "space", axis_index_groups=layout.inner)
    gram = cross * jnp.dot(head_weight.T, head_weight, precision=HIGHEST)
    alpha = frank_wolfe(gram, fw_picks)
    grad_logits = scale * alpha * errors
    head_w = jnp.einsum("nc,nt->ct", pooled, grad_logits, precision=HIGHEST)
    head_b = jnp.sum(grad_logits, axis=0)
    head_own = own_out(head_weight, 0)
    grad_pool = jnp.einsum("nt,ct->nc", grad_logits, head_own, precision=HIGHEST) / image_pixels

    grad_block = grad_pool[:, None, None, :] * silu_slope(block_pre)
    second_low, second_cross, second_sum = norm_back(
        layout, grad_block, second_norm, second_inv, gain_p[1], weight, counted
    )
    second_kernel = kernel_grad(share(second_ext), second_low, 1)
    act_grad = conv_valid(layout.rims(whole(second_low)), flipped(own_out(conv_second, 2)), 1)
    first_low, first_cross, first_sum = norm_back(
        layout, act_grad * silu_slope(first_pre), first_norm, first_inv, gain_p[0], weight, counted
    )
    first_kernel = kernel_grad(share(first_ext), first_low, 1)
    entry_grad = conv_valid(layout.rims(whole(first_low)), flipped(own_out(conv_first, 2)), 1)
    entry_grad = (entry_grad + grad_block).astype(BF16).astype(F32)
    grad_section = entry_grad * silu_slope(section_pre)
    mid_low, mid_cross, mid_sum = norm_back(
        layout, grad_section, mid_norm, mid_inv, gain_d[1], weight, counted
    )
    short_low, short_cross, short_sum = norm_back(
        layout, grad_section, short_norm, short_inv, gain_d[2], weight, counted
    )
    mid_kernel = kernel_grad(share(mid_ext), mid_low, 1)
    short_kernel = jnp.einsum(
        "nhwi,nhwo->io", share(short_in), short_low, preferred_element_type=F32
    )
    act_grad = conv_valid(layout.rims(whole(mid_low)), flipped(own_out(conv_mid, 2)), 1)
    down_low, down_cross, down_sum = norm_back(
        layout, act_grad * silu_slope(down_pre), down_norm, down_inv, gain_d[0], weight, counted
    )
    down_kernel = kernel_grad(share(down_ext), down_low, 2)

    kept = lax.dynamic_slice_in_dim(whole(down_low), batch * per_micro, per_micro, 0)
    below = layout.row_from(kept[:, :1], -1)
    spread = lax.conv_general_dilated(
        jnp.concatenate([kept, below], axis=1),
        flipped(own_out(conv_down, 2)),
        (1, 1),
        ((2, 2), (2, 2)),
        lhs_dilation=(2, 2),
        dimension_numbers=NUMBERS,
        preferred_element_type=F32,
    )[:, 1 : 2 * out_rows + 1, 1:]
    short_kept = lax.dynamic_slice_in_dim(whole(short_low), batch * per_micro, per_micro, 0)
    spread = spread.at[:, ::2, ::2].add(
        jnp.einsum(
            "nhwo,io->nhwi", short_kept, own_out(shortcut, 0), preferred_element_type=F32
        )
    )
    images_grad = lax.all_to_all(
        spread.astype(BF16), "space", 1, 0, axis_index_groups=layout.inner, tiled=True
    ).astype(F32)

    def total(kernel, axis):
        summed = lax.psum(kernel.astype(BF16), "space")
        return lax.all_gather(summed, "batch", axis=axis, tiled=True).astype(F32)

    pooled_out = lax.dynamic_slice_in_dim(pooled, batch * per_micro, per_micro, 0)
    pooled_out = lax.all_gather(
        pooled_out, "space", axis_index_groups=layout.inner, axis=0, tiled=True
    )
    head_w, head_b = lax.psum((head_w, head_b), "space", axis_index_groups=layout.inner)
    gains_d, sums_d, gains_p, sums_p = lax.psum(
        (
            jnp.stack([down_cross, mid_cross, short_cross]),
            jnp.stack([down_sum, mid_sum, short_sum]),
            jnp.stack([first_cross, second_cross]),
            jnp.stack([first_sum, second_sum]),
        ),
        "space",
    )
    return (
        pooled_out,
        images_grad,
        total(down_kernel, 1).reshape(3, 3, entering, half),
        total(mid_kernel, 1).reshape(3, 3, channels, half),
        total(short_kernel, 0),
        gains_d,
        sums_d,
        total(first_kernel, 1).reshape(3, 3, channels, half),
        total(second_kernel, 1).reshape(3, 3, channels, half),
        gains_p,
        sums_p,
        head_w,
        own_out(head_b, 0),
    )


def solution(mesh):
    placed = (
        P("batch", "space", None, None),
        P("batch", None),
        P("batch", None),
    ) + (P(),) * 12
    return jax.shard_map(
        per_device,
        mesh=mesh,
        in_specs=placed,
        out_specs=(
            P("batch", "pipe"),
            P("batch", "space", None, "pipe"),
            P(None, None, None, "pipe"),
            P(None, None, None, "pipe"),
            P(None, "pipe"),
            P(None, "pipe"),
            P(None, "pipe"),
            P(None, None, None, "pipe"),
            P(None, None, None, "pipe"),
            P(None, "pipe"),
            P(None, "pipe"),
            P("pipe", None),
            P("pipe"),
        ),
        check_vma=False,
    )
```

```python
import jax
import jax.numpy as jnp
from jax import lax
from jax.experimental import pallas as pl
from jax.experimental.pallas import tpu as pltpu
from jax.sharding import PartitionSpec as P

EPSILON = 1e-05
NUMBERS = ("NHWC", "HWIO", "NHWC")
HIGHEST = lax.Precision.HIGHEST
F32 = jnp.float32
BF16 = jnp.bfloat16


def silu_slope(values):
    sigmoid = jax.nn.sigmoid(values)
    return sigmoid * (1.0 + values * (1.0 - sigmoid))


def frank_wolfe_kernel(picks_ref, gram_ref, alpha_ref):
    tasks = gram_ref.shape[0]
    lanes = lax.broadcasted_iota(jnp.int32, (1, tasks), 1)
    gram = gram_ref[...]
    alpha = jnp.full((1, tasks), 1.0 / tasks, F32)
    pulled = jnp.sum(gram, axis=0, keepdims=True) * (1.0 / tasks)
    energy = jnp.sum(pulled * alpha, axis=1, keepdims=True)

    def advance(step, carry):
        alpha, pulled, energy = carry
        chosen = picks_ref[step]
        row = gram_ref[pl.ds(chosen, 1), :]
        onehot = (lanes == chosen).astype(F32)
        toward = jnp.sum(pulled * onehot, axis=1, keepdims=True)
        corner = jnp.sum(row * onehot, axis=1, keepdims=True)
        denom = jnp.maximum(energy - 2.0 * toward + corner, 0.05 * corner)
        ratio = jnp.clip((energy - toward) / denom, 0.0, 1.0)
        rest = 1.0 - ratio
        alpha = rest * alpha + ratio * onehot
        pulled = rest * pulled + ratio * row
        energy = rest * rest * energy + 2.0 * rest * ratio * toward + ratio * ratio * corner
        return alpha, pulled, energy

    alpha, _, _ = lax.fori_loop(0, picks_ref.shape[0], advance, (alpha, pulled, energy))
    alpha_ref[...] = alpha


def frank_wolfe(gram, picks):
    tasks = gram.shape[0]
    return pl.pallas_call(
        frank_wolfe_kernel,
        out_shape=jax.ShapeDtypeStruct((1, tasks), F32),
        in_specs=[
            pl.BlockSpec(memory_space=pltpu.SMEM),
            pl.BlockSpec(memory_space=pltpu.VMEM),
        ],
        out_specs=pl.BlockSpec(memory_space=pltpu.VMEM),
    )(picks, gram)


class Layout:
    def __init__(self, micros):
        self.micros = micros
        self.spaces = lax.axis_size("space")
        self.groups = self.spaces // micros
        self.inner = [
            [group * micros + zone for zone in range(micros)] for group in range(self.groups)
        ]
        self.outer = [
            [group * micros + zone for group in range(self.groups)] for zone in range(micros)
        ]
        self.zone = lax.axis_index("space") % micros

    def group_sum(self, tree):
        if self.groups == 1:
            return tree
        return lax.psum(tree, "space", axis_index_groups=self.outer)

    def row_from(self, block, step):
        span = step * self.micros
        route = [
            (i, i + span) for i in range(self.spaces) if 0 <= i + span < self.spaces
        ]
        if not route:
            return jnp.zeros_like(block)
        return lax.ppermute(block, "space", route)

    def rims(self, tensor):
        above = self.row_from(tensor[:, -1:], 1)
        below = self.row_from(tensor[:, :1], -1)
        grown = jnp.concatenate([above, tensor, below], axis=1)
        return jnp.pad(grown, ((0, 0), (0, 0), (1, 1), (0, 0)))


def conv_valid(extended, kernel, stride):
    return lax.conv_general_dilated(
        extended,
        kernel,
        (stride, stride),
        "VALID",
        dimension_numbers=NUMBERS,
        preferred_element_type=F32,
    )


def flipped(kernel):
    return jnp.swapaxes(kernel[::-1, ::-1], 2, 3)


def kernel_grad(extended, grad_low, stride):
    rows, cols = grad_low.shape[1], grad_low.shape[2]
    taps = []
    for row_tap in range(3):
        for col_tap in range(3):
            window = extended[
                :,
                row_tap : row_tap + stride * (rows - 1) + 1 : stride,
                col_tap : col_tap + stride * (cols - 1) + 1 : stride,
            ]
            taps.append(jnp.einsum("nhwi,nhwo->io", window, grad_low, preferred_element_type=F32))
    return jnp.stack(taps)


def norm_forward(layout, conv_out, weight, counted):
    total = layout.group_sum(jnp.sum(conv_out * weight, axis=(0, 1, 2)))
    centered = conv_out - total / counted
    spread = layout.group_sum(jnp.sum(centered * centered * weight, axis=(0, 1, 2)))
    inverse = lax.rsqrt(spread / counted + EPSILON)
    return centered * inverse, inverse


def norm_back(layout, upstream, normed, inverse, gain, weight, counted):
    grad_sum = jnp.sum(upstream * weight, axis=(0, 1, 2))
    cross_sum = jnp.sum(upstream * normed * weight, axis=(0, 1, 2))
    grad_total, cross_total = layout.group_sum((grad_sum, cross_sum))
    correction = weight * (grad_total / counted + normed * (cross_total / counted))
    low = (gain * inverse * (upstream - correction)).astype(BF16)
    return low, cross_sum, grad_sum


KERNEL_LIMIT = 24 * 2**20
PARTS, LAST_PARTS = 4, 1
VM = pl.BlockSpec(memory_space=pltpu.VMEM)
SM = pl.BlockSpec(memory_space=pltpu.SMEM)
HBM = pl.BlockSpec(memory_space=pltpu.HBM)
NT = (((1,), (1,)), ((), ()))
TN = (((0,), (0,)), ((), ()))
OWN_PX, OTHER_PX, ALL_PX = 8, 9, 10
G_DOWN, G_MID, G_SHORT, B_DOWN, B_MID, B_SHORT, G_FIRST, G_SECOND, B_FIRST, B_SECOND = range(10)


def param(params_ref, row):
    return params_ref[row : row + 1, :]


def call(kernel, outs, operands, scratch=(), flops=0, name=None, after=(), specs=None,
         out_space=None):
    count = len(operands)
    nbytes = sum(x.size * x.dtype.itemsize for x in operands)
    specs = specs or {}

    def body(*refs):
        kernel(*refs[:count], *refs[count + len(after) :])

    return pl.pallas_call(
        body,
        out_shape=tuple(jax.ShapeDtypeStruct(shape, dtype) for shape, dtype in outs),
        in_specs=[specs.get(i, SM if x.ndim == 1 else VM) for i, x in enumerate(operands)]
        + [pl.BlockSpec(memory_space=pl.ANY)] * len(after),
        out_specs=tuple(out_space or [SM if len(shape) == 1 else VM for shape, _ in outs]),
        scratch_shapes=list(scratch),
        compiler_params=pltpu.CompilerParams(vmem_limit_bytes=KERNEL_LIMIT),
        cost_estimate=pl.CostEstimate(
            flops=int(flops), bytes_accessed=int(nbytes), transcendentals=0
        ),
        name=name,
    )(*operands, *after)


def fold(rows):
    return rows[0:8] + rows[8:16] + rows[16:24] + rows[24:32]


def total_row(part):
    return jnp.sum(part, axis=0, keepdims=True)


def band(row):
    return slice(row * 32, row * 32 + 32)


def put_band(x_ref, image, row, value):
    zero = jnp.zeros_like(value)
    x_ref[image, band(row), 512:1024] = value
    if row < 3:
        x_ref[image, band(row + 1), 0:512] = value
    else:
        x_ref[image, band(0), 0:512] = zero
    if row > 0:
        x_ref[image, band(row - 1), 1024:1536] = value
    else:
        x_ref[image, band(3), 1024:1536] = zero


def columns_joined(left, middle, right):
    count = middle.shape[0]
    column = lax.broadcasted_iota(jnp.int32, (count, 1), 0) % 32
    joined = middle
    if left is not None:
        joined = joined + jnp.where(column == 0, 0.0, pltpu.roll(left, 1, 0))
    if right is not None:
        joined = joined + jnp.where(column == 31, 0.0, pltpu.roll(right, count - 1, 0))
    return joined


def conv_core(x_ref, w_ref, out_ref, back):
    def tap(col):
        value = None
        for row in range(3):
            lhs = x_ref[:, :, row * 512 : (row + 1) * 512].reshape(1024, 512)
            if back:
                term = lax.dot_general(
                    lhs, w_ref[2 - row, 2 - col], NT, preferred_element_type=F32
                )
            else:
                term = jnp.dot(lhs, w_ref[row, col], preferred_element_type=F32)
            value = term if value is None else value + term
        return value

    out_ref[...] = columns_joined(tap(0), tap(1), tap(2)).reshape(8, 128, 512)


def stats_of(facts_ref, out_ref, stat_ref, row):
    def add(image, part):
        for r in range(4):
            part = part + fold(out_ref[image, band(r), :]) * facts_ref[image]
        return part

    first = total_row(lax.fori_loop(0, 8, add, jnp.zeros((8, 512), F32)))
    mean = first / jnp.maximum(facts_ref[OWN_PX], 1.0)

    def deviate(image, part):
        for r in range(4):
            away = out_ref[image, band(r), :] - mean
            part = part + fold(away * away) * facts_ref[image]
        return part

    second = total_row(lax.fori_loop(0, 8, deviate, jnp.zeros((8, 512), F32)))
    stat_ref[row : row + 1, :] = first
    stat_ref[row + 1 : row + 2, :] = second


def norm_of(facts_ref, own_ref, other_ref, row):
    own_px, other_px, all_px = facts_ref[OWN_PX], facts_ref[OTHER_PX], facts_ref[ALL_PX]
    own, other = own_ref[row : row + 1, :], other_ref[row : row + 1, :]
    mean = (own + other) / all_px
    apart = own / jnp.maximum(own_px, 1.0) - other / jnp.maximum(other_px, 1.0)
    spread = own_ref[row + 1 : row + 2, :] + other_ref[row + 1 : row + 2, :]
    variance = (spread + apart * apart * (own_px * other_px / all_px)) / all_px
    return mean, lax.rsqrt(variance + EPSILON)


def sigmoid(values):
    return 0.5 * jnp.tanh(0.5 * values) + 0.5


def slope_of(values):
    gate = sigmoid(values)
    return gate * (1.0 + values * (1.0 - gate))


MARKS = 128


def pieces_kernel(where_ref, images_hbm, labels_ref, count_ref, o0, o1, o2, o3, wide,
                  images_ref, sems):
    pipe, zone = where_ref[0], where_ref[2]
    tasks = labels_ref.shape[1]
    copies = []
    for rel in range(4):
        first = (zone ^ rel) * 4 + pipe * 2
        copies.append(
            pltpu.make_async_copy(
                images_hbm.at[pl.ds(first, 2)], images_ref.at[rel], sems.at[rel]
            )
        )
        copies[-1].start()
    o0[MARKS:, :] = jnp.zeros((16, 512), BF16)
    count = count_ref[0, zone].astype(F32)
    marks = jnp.concatenate(
        [
            labels_ref[pl.ds(zone * 4, 4), :].astype(F32),
            jnp.full((4, tasks), count),
            jnp.zeros((8, tasks), F32),
        ]
    )
    o0[MARKS:, 0:tasks] = marks.astype(BF16)
    for rel, out in enumerate((o0, o1, o2, o3)):
        copies[rel].wait()
        for i in range(2):
            for row in range(2):
                lines = slice((i * 2 + row) * 32, (i * 2 + row) * 32 + 32)
                for part in range(2):
                    lanes = slice(part * 128, part * 128 + 128)
                    wide[...] = images_ref[rel, i, row, :, lanes].astype(F32)
                    for par in range(2):
                        value = wide[pl.ds(par, 32, stride=2), :]
                        start = par * 256 + part * 128
                        out[lines, start : start + 128] = value.astype(BF16)


def down_kernel(facts_ref, where_ref, *refs):
    pieces, (w_ref, s_ref, img_ref, out_ref, short_ref, stat_ref, x_ref) = refs[:12], refs[12:]
    batch, zone = where_ref[1], where_ref[2]
    for kb in range(4):
        for kz in range(4):
            piece, base = pieces[kb * 3 + min(kz, 2)], (128 if kz == 3 else 0)
            row = zone ^ kz
            here = pl.ds(pl.multiple_of(row * 32, 32), 32)
            after = pl.ds(pl.multiple_of(((row + 1) % 4) * 32, 32), 32)
            for i in range(2):
                image = (batch ^ kb) * 2 + i
                start = base + i * 64
                odd = piece[start + 32 : start + 64, :]
                img_ref[image, here, 0:512] = piece[start : start + 32, :]
                img_ref[image, here, 512:1024] = odd
                x_ref[image, after, :] = jnp.where(row == 3, jnp.zeros_like(odd), odd)
    for part in range(2):
        images = slice(4 * part, 4 * part + 4)
        blocks = (
            x_ref[images].reshape(512, 512),
            img_ref[images, :, 0:512].reshape(512, 512),
            img_ref[images, :, 512:1024].reshape(512, 512),
        )
        left, middle = None, None
        for row in range(3):
            a = jnp.dot(blocks[row][:, 256:], w_ref[row, 0], preferred_element_type=F32)
            m = jnp.dot(
                blocks[row], w_ref[row, 1:3].reshape(512, 512), preferred_element_type=F32
            )
            left = a if left is None else left + a
            middle = m if middle is None else middle + m
        out_ref[images] = columns_joined(left, middle, None).reshape(4, 128, 512)
        short = jnp.dot(blocks[1][:, :256], s_ref[...], preferred_element_type=F32)
        short_ref[images] = short.reshape(4, 128, 512)
    stats_of(facts_ref, out_ref, stat_ref, 0)
    stats_of(facts_ref, short_ref, stat_ref, 2)
    stat_ref[4:8, :] = jnp.zeros((4, 512), F32)


def layer_kernel(g_row, b_row, facts_ref, in_ref, own_ref, other_ref, params_ref, w_ref,
                 act_ref, out_ref, stat_ref, norm_ref, x_ref):
    mean, inverse = norm_of(facts_ref, own_ref, other_ref, 0)
    gain, bias = param(params_ref, g_row), param(params_ref, b_row)

    def activate(image, carry):
        for r in range(4):
            pre = (in_ref[image, band(r), :] - mean) * inverse * gain + bias
            act = (pre * sigmoid(pre)).astype(BF16)
            act_ref[image, band(r), :] = act
            put_band(x_ref, image, r, act)
        return carry

    lax.fori_loop(0, 8, activate, 0)
    norm_ref[0:1, :] = mean
    norm_ref[1:2, :] = inverse
    norm_ref[2:8, :] = jnp.zeros((6, 512), F32)
    conv_core(x_ref, w_ref, out_ref, False)
    stats_of(facts_ref, out_ref, stat_ref, 0)
    stat_ref[2:8, :] = jnp.zeros((6, 512), F32)


def join_kernel(facts_ref, mid_ref, short_ref, own_m, other_m, own_d, other_d, params_ref,
                w_ref, act_ref, out_ref, stat_ref, norm_ref, x_ref):
    mean_m, inv_m = norm_of(facts_ref, own_m, other_m, 0)
    mean_s, inv_s = norm_of(facts_ref, own_d, other_d, 2)
    gain_m, gain_s = param(params_ref, G_MID), param(params_ref, G_SHORT)
    bias_m, bias_s = param(params_ref, B_MID), param(params_ref, B_SHORT)

    def activate(image, carry):
        for r in range(4):
            pre = (mid_ref[image, band(r), :] - mean_m) * inv_m * gain_m + bias_m
            pre = pre + (short_ref[image, band(r), :] - mean_s) * inv_s * gain_s + bias_s
            act = (pre * sigmoid(pre)).astype(BF16)
            act_ref[image, band(r), :] = act
            put_band(x_ref, image, r, act)
        return carry

    lax.fori_loop(0, 8, activate, 0)
    norm_ref[0:1, :] = mean_m
    norm_ref[1:2, :] = inv_m
    norm_ref[2:3, :] = mean_s
    norm_ref[3:4, :] = inv_s
    norm_ref[4:8, :] = jnp.zeros((4, 512), F32)
    conv_core(x_ref, w_ref, out_ref, False)
    stats_of(facts_ref, out_ref, stat_ref, 0)
    stat_ref[2:8, :] = jnp.zeros((6, 512), F32)


def block_kernel(facts_ref, in_ref, section_ref, own_ref, other_ref, params_ref,
                 pack_ref, norm_ref):
    mean, inverse = norm_of(facts_ref, own_ref, other_ref, 0)
    gain, bias = param(params_ref, G_SECOND), param(params_ref, B_SECOND)
    norm_ref[0:1, :] = mean
    norm_ref[1:2, :] = inverse
    norm_ref[2:8, :] = jnp.zeros((6, 512), F32)

    def gather(image, carry):
        pooled = jnp.zeros((8, 512), F32)
        slopes, crossed = pooled, pooled
        for r in range(4):
            normed = (in_ref[image, band(r), :] - mean) * inverse
            pre = normed * gain + bias + section_ref[image, band(r), :].astype(F32)
            gate = sigmoid(pre)
            slope = gate * (1.0 + pre * (1.0 - gate))
            pooled = pooled + fold(pre * gate)
            slopes = slopes + fold(slope)
            crossed = crossed + fold(slope * normed)
        pack_ref[pl.ds(image, 1), :] = total_row(pooled) / 128.0
        pack_ref[pl.ds(image + 8, 1), :] = total_row(slopes)
        pack_ref[pl.ds(image + 16, 1), :] = total_row(crossed)
        return carry

    lax.fori_loop(0, 8, gather, 0)


def logits_kernel(where_ref, own_ref, other_ref, living_ref, labels_ref, hw_ref, hb_ref,
                  all_ref, errors_ref, cross_ref):
    pipe = where_ref[0]
    for block in range(3):
        rows = slice(block * 8, block * 8 + 8)
        all_ref[block, pl.ds(pl.multiple_of(pipe * 8, 8), 8), :] = own_ref[rows, :]
        all_ref[block, pl.ds(pl.multiple_of((1 - pipe) * 8, 8), 8), :] = other_ref[rows, :]
    logits = (
        lax.dot_general(
            all_ref[0], hw_ref[...], NT, precision=HIGHEST, preferred_element_type=F32
        )
        + hb_ref[...]
    )
    errors = living_ref[...] * (sigmoid(logits) - labels_ref[...])
    errors_ref[...] = errors
    cross_ref[...] = lax.dot_general(
        errors, errors, TN, precision=HIGHEST, preferred_element_type=F32
    )


def head_kernel(picks_ref, where_ref, facts_ref, c0, c1, c2, c3, heads_ref, hw_ref, errors_ref,
                all_ref, in_ref, section_ref, norm_ref, params_ref,
                low_ref, pool_ref, small_ref, alpha_ref, gram_ref):
    tasks = gram_ref.shape[0]
    pipe = where_ref[0]
    gram_ref[...] = ((c0[...] + c1[...]) + (c2[...] + c3[...])) * heads_ref[...]
    frank_wolfe_kernel(picks_ref, gram_ref, alpha_ref)
    grad_logits = (128.0 * tasks) * alpha_ref[...] * errors_ref[...]
    pooled, slopes, crossed = all_ref[0], all_ref[1], all_ref[2]
    grad_pool = (
        jnp.dot(grad_logits, hw_ref[...], precision=HIGHEST, preferred_element_type=F32)
        / 128.0
    )
    grad_sum = total_row(grad_pool * slopes)
    cross_sum = total_row(grad_pool * crossed)
    small_ref[0:tasks, :] = lax.dot_general(
        grad_logits, pooled, TN, precision=HIGHEST, preferred_element_type=F32
    )
    small_ref[tasks : tasks + 1, :] = grad_sum
    small_ref[tasks + 1 : tasks + 2, :] = cross_sum
    small_ref[tasks + 2 :, :] = jnp.zeros((small_ref.shape[0] - tasks - 2, 512), F32)
    for start in (0, 256):
        small_ref[tasks + 2 : tasks + 3, start : start + tasks] = total_row(grad_logits)
    pool_ref[...] = jnp.where(pipe == 0, grad_pool[0:8], grad_pool[8:16])

    mean, inverse = norm_ref[0:1, :], norm_ref[1:2, :]
    gain, bias = param(params_ref, G_SECOND), param(params_ref, B_SECOND)
    all_px = facts_ref[ALL_PX]
    front = gain * inverse
    mean_grad, mean_cross = grad_sum / all_px, cross_sum / all_px

    def back(image, carry):
        up = pool_ref[pl.ds(image, 1), :]
        for r in range(4):
            normed = (in_ref[image, band(r), :] - mean) * inverse
            pre = normed * gain + bias + section_ref[image, band(r), :].astype(F32)
            grad = up * slope_of(pre)
            fix = facts_ref[image] * (mean_grad + normed * mean_cross)
            low_ref[image, band(r), :] = (front * (grad - fix)).astype(BF16)
        return carry

    lax.fori_loop(0, 8, back, 0)


def back_norm(facts_ref, in_ref, up_ref, norm_ref, own_ref, other_ref, gain, rows, sinks):
    mean, inverse = norm_ref[rows : rows + 1, :], norm_ref[rows + 1 : rows + 2, :]
    all_px = facts_ref[ALL_PX]
    front = gain * inverse
    cross_row = 1 + rows // 2
    mean_grad = (own_ref[0:1, :] + other_ref[0:1, :]) / all_px
    mean_cross = (
        own_ref[cross_row : cross_row + 1, :] + other_ref[cross_row : cross_row + 1, :]
    ) / all_px

    def back(image, carry):
        for r in range(4):
            normed = (in_ref[image, band(r), :] - mean) * inverse
            fix = facts_ref[image] * (mean_grad + normed * mean_cross)
            sinks(image, r, (front * (up_ref[image, band(r), :] - fix)).astype(BF16))
        return carry

    lax.fori_loop(0, 8, back, 0)


def second_back_kernel(facts_ref, low_ref, in_ref, norm_ref, params_ref, w_ref,
                       up_ref, sum_ref, x_ref, conv_ref):
    def fill(image, carry):
        for r in range(4):
            put_band(x_ref, image, r, low_ref[image, band(r), :])
        return carry

    lax.fori_loop(0, 8, fill, 0)
    conv_core(x_ref, w_ref, conv_ref, True)
    gain, bias = param(params_ref, G_FIRST), param(params_ref, B_FIRST)
    slope_sums(facts_ref, in_ref, norm_ref, gain, bias, conv_ref, up_ref, sum_ref)


def slope_sums(facts_ref, in_ref, norm_ref, gain, bias, conv_ref, up_ref, sum_ref):
    mean, inverse = norm_ref[0:1, :], norm_ref[1:2, :]

    def slope(image, carry):
        grads, crosses = carry
        for r in range(4):
            normed = (in_ref[image, band(r), :] - mean) * inverse
            up = conv_ref[image, band(r), :] * slope_of(normed * gain + bias)
            up_ref[image, band(r), :] = up
            living = facts_ref[image]
            grads = grads + fold(up) * living
            crosses = crosses + fold(up * normed) * living
        return grads, crosses

    zero = jnp.zeros((8, 512), F32)
    grads, crosses = lax.fori_loop(0, 8, slope, (zero, zero))
    sum_ref[0:1, :] = total_row(grads)
    sum_ref[1:2, :] = total_row(crosses)
    sum_ref[2:8, :] = jnp.zeros((6, 512), F32)


def first_back_kernel(facts_ref, up_in, in_ref, norm_ref, own_ref, other_ref, params_ref, w_ref,
                      second_ref, norm2_ref, section_ref, pool_ref, mid_ref, short_ref, normd_ref,
                      low_ref, up_ref, sum_ref, x_ref, conv_ref):
    def keep(image, r, low):
        low_ref[image, band(r), :] = low
        put_band(x_ref, image, r, low)

    back_norm(facts_ref, in_ref, up_in, norm_ref, own_ref, other_ref, param(params_ref, G_FIRST),
              0, keep)
    conv_core(x_ref, w_ref, conv_ref, True)
    mean2, inv2 = norm2_ref[0:1, :], norm2_ref[1:2, :]
    gain2, bias2 = param(params_ref, G_SECOND), param(params_ref, B_SECOND)
    mean_m, inv_m = normd_ref[0:1, :], normd_ref[1:2, :]
    mean_s, inv_s = normd_ref[2:3, :], normd_ref[3:4, :]
    gain_m, gain_s = param(params_ref, G_MID), param(params_ref, G_SHORT)
    bias_m, bias_s = param(params_ref, B_MID), param(params_ref, B_SHORT)

    def join(image, carry):
        grads, cross_m, cross_s = carry
        pool = pool_ref[pl.ds(image, 1), :]
        for r in range(4):
            pre2 = (second_ref[image, band(r), :] - mean2) * inv2 * gain2 + bias2
            pre2 = pre2 + section_ref[image, band(r), :].astype(F32)
            entry = conv_ref[image, band(r), :] + pool * slope_of(pre2)
            entry = entry.astype(BF16).astype(F32)
            norm_m = (mid_ref[image, band(r), :] - mean_m) * inv_m
            norm_s = (short_ref[image, band(r), :] - mean_s) * inv_s
            pre = norm_m * gain_m + bias_m + norm_s * gain_s + bias_s
            up = entry * slope_of(pre)
            up_ref[image, band(r), :] = up
            living = facts_ref[image]
            grads = grads + fold(up) * living
            cross_m = cross_m + fold(up * norm_m) * living
            cross_s = cross_s + fold(up * norm_s) * living
        return grads, cross_m, cross_s

    zero = jnp.zeros((8, 512), F32)
    grads, cross_m, cross_s = lax.fori_loop(0, 8, join, (zero, zero, zero))
    sum_ref[0:1, :] = total_row(grads)
    sum_ref[1:2, :] = total_row(cross_m)
    sum_ref[2:3, :] = total_row(cross_s)
    sum_ref[3:8, :] = jnp.zeros((5, 512), F32)


def mid_back_kernel(facts_ref, up_in, mid_ref, short_ref, normd_ref, own_ref, other_ref, params_ref,
                    w_ref, in_ref, norm1_ref,
                    low_ref, low_s_ref, up_ref, sum_ref, x_ref, conv_ref):
    def keep(image, r, low):
        low_ref[image, band(r), :] = low
        put_band(x_ref, image, r, low)

    def keep_short(image, r, low):
        low_s_ref[image, band(r), :] = low

    gain_m, gain_s = param(params_ref, G_MID), param(params_ref, G_SHORT)
    back_norm(facts_ref, mid_ref, up_in, normd_ref, own_ref, other_ref, gain_m, 0, keep)
    back_norm(facts_ref, short_ref, up_in, normd_ref, own_ref, other_ref, gain_s, 2, keep_short)
    conv_core(x_ref, w_ref, conv_ref, True)
    gain, bias = param(params_ref, G_DOWN), param(params_ref, B_DOWN)
    slope_sums(facts_ref, in_ref, norm1_ref, gain, bias, conv_ref, up_ref, sum_ref)


def down_back_kernel(facts_ref, up_in, in_ref, norm1_ref, own_ref, other_ref, params_ref, low_ref):
    def keep(image, r, low):
        low_ref[image, band(r), :] = low

    gain = param(params_ref, G_DOWN)
    back_norm(facts_ref, in_ref, up_in, norm1_ref, own_ref, other_ref, gain, 0, keep)


def image_back_kernel(where_ref, low_ref, low_s_ref, w_ref, s_ref, keep_ref, send_ref, stage_ref):
    pipe, batch, zone = where_ref[0], where_ref[1], where_ref[2]
    mine = pl.ds(batch * 2, 2)
    here = low_ref[mine]
    below = jnp.concatenate([here[:, 32:], jnp.zeros((2, 32, 512), BF16)], axis=1)
    here, below = here.reshape(256, 512), below.reshape(256, 512)
    short = low_s_ref[mine].reshape(256, 512)

    def back(lhs, row, col):
        return lax.dot_general(lhs, w_ref[row, col], NT, preferred_element_type=F32)

    even_even = back(here, 1, 1) + lax.dot_general(
        short, s_ref[...], NT, preferred_element_type=F32
    )
    even_odd = columns_joined(None, back(here, 1, 2), back(here, 1, 0))
    odd_even = back(here, 2, 1) + back(below, 0, 1)
    odd_odd = columns_joined(
        None, back(here, 2, 2) + back(below, 0, 2), back(here, 2, 0) + back(below, 0, 0)
    )
    planes = ((even_even, even_odd), (odd_even, odd_odd))
    for row in range(2):
        for par in range(2):
            plane = planes[row][par].reshape(2, 4, 32, 256).astype(BF16)
            lanes = slice(par * 128, par * 128 + 128)
            for side in range(2):
                half = plane[..., side * 128 : side * 128 + 128]
                for z in range(4):
                    stage_ref[z ^ zone, side ^ pipe, :, row, :, lanes] = half[:, z]
    keep_ref[0], keep_ref[1] = stage_ref[0], stage_ref[2]
    send_ref[0], send_ref[1] = stage_ref[1], stage_ref[3]


def image_far_kernel(keep_ref, near_ref, out_ref):
    out_ref[0], out_ref[1] = keep_ref[1], near_ref[1]


def image_pipe_kernel(keep_ref, near_ref, far_ref, out_ref):
    out_ref[0], out_ref[1] = keep_ref[0, 1], near_ref[0, 1]
    out_ref[2], out_ref[3] = far_ref[0, 1], far_ref[1, 1]


def image_grad_kernel(where_ref, keep_ref, near_ref, far_ref, got_ref, out_ref):
    pipe, zone = where_ref[0], where_ref[2]
    own = (keep_ref.at[0, 0], near_ref.at[0, 0], far_ref.at[0, 0], far_ref.at[1, 0])
    for rel in range(4):
        for side in range(2):
            piece = own[rel] if side == 0 else got_ref.at[rel]
            first = (zone ^ rel) * 4 + (pipe if side == 0 else 1 - pipe) * 2
            for i in range(2):
                for row in range(2):
                    for par in range(2):
                        out_ref[first + i, row, pl.ds(par, 32, stride=2), :] = piece[
                            i, row, :, par * 128 : (par + 1) * 128
                        ].astype(F32)


def slot_of(quarter, zone):
    rel = quarter ^ zone
    return (rel >> 1) | ((rel & 1) << 1)


def shifted_window(turned, down, right):
    pixel = lax.broadcasted_iota(jnp.int32, (1, 128), 1)
    column, row = pixel % 32 + right, pixel // 32 + down
    inside = (column >= 0) & (column < 32) & (row >= 0) & (row < 4)
    amount = (256 - down * 32 - right) % 128
    moved = turned if isinstance(amount, int) and amount == 0 else pltpu.roll(turned, amount, 1)
    return jnp.where(inside, moved, 0.0).astype(BF16)


def split_out(pipe, zone, unit, result_own, result_other, own_ref, other_ref):
    for quarter in range(4):
        slot = slot_of(quarter, zone)
        rows = slice(quarter * 32, quarter * 32 + 32)
        own_ref[slot, unit] = result_own[rows]
        other_ref[slot, unit] = result_other[rows].astype(BF16)


def hand_out(other_ref, outs):
    each = 4 // len(outs)
    for slot in range(4):
        outs[slot // each][slot % each] = other_ref[slot]


def turned_taps(batch, act_ref, turned_ref):
    lanes = pl.ds(pl.multiple_of(batch * 128, 128), 128)

    def turn(image, carry):
        turned = act_ref[image, :, lanes].astype(F32).T
        pixels = pl.ds(pl.multiple_of(image * 128, 128), 128)
        for row in range(3):
            for col in range(3):
                turned_ref[row * 3 + col, :, pixels] = shifted_window(turned, row - 1, col - 1)
        return carry

    lax.fori_loop(0, 8, turn, 0)


def tap_products(pipe, zone, low_ref, turned_ref, own_ref, other_ref):
    lhs = turned_ref[0:9].reshape(9 * 128, 1024)
    results = []
    for side in (pipe, 1 - pipe):
        columns = pl.ds(pl.multiple_of(side * 256, 256), 256)
        rhs = low_ref[:, :, columns].reshape(1024, 256)
        results.append(jnp.dot(lhs, rhs, preferred_element_type=F32))
    for unit in range(9):
        rows = slice(unit * 128, unit * 128 + 128)
        split_out(pipe, zone, unit, results[0][rows], results[1][rows], own_ref, other_ref)


def kernel_grad_kernel(where_ref, act_ref, low_ref, own_ref, *refs):
    outs, (turned_ref, other_ref) = refs[:-2], refs[-2:]
    pipe, batch, zone = where_ref[0], where_ref[1], where_ref[2]
    turned_taps(batch, act_ref, turned_ref)
    tap_products(pipe, zone, low_ref, turned_ref, own_ref, other_ref)
    hand_out(other_ref, outs)


DOWN_UNITS = (
    ((0, 0, 0, 4), (2, -1, 0, 1), (2, 0, 0, 7), (0, 0, 0, 9), (1, 0, 0, 5)),
    ((1, 0, -1, 3), (3, -1, -1, 0), (3, -1, 0, 2), (3, 0, -1, 6), (3, 0, 0, 8)),
)


def down_grad_kernel(where_ref, img_ref, low_ref, low_s_ref, own_ref, *refs):
    outs, (turned_ref, other_ref) = refs[:-2], refs[-2:]
    pipe, batch, zone = where_ref[0], where_ref[1], where_ref[2]
    upper, part = batch // 2, batch % 2

    for turn_kind in range(2):

        @pl.when(upper == turn_kind)
        def _(units=DOWN_UNITS[turn_kind]):
            def turn(image, carry):
                pixels = pl.ds(pl.multiple_of(image * 128, 128), 128)
                seen = {}
                for unit, (plane, down, right, _) in enumerate(units):
                    if plane not in seen:
                        lanes = pl.ds(pl.multiple_of(plane * 256 + part * 128, 128), 128)
                        seen[plane] = img_ref[image, :, lanes].astype(F32).T
                    turned_ref[unit, :, pixels] = shifted_window(seen[plane], down, right)
                return carry

            lax.fori_loop(0, 8, turn, 0)

    short_unit = [tap for _, _, _, tap in DOWN_UNITS[0]].index(9)
    for unit in range(5):
        lhs = turned_ref[unit]
        results = []
        for side in (pipe, 1 - pipe):
            columns = pl.ds(pl.multiple_of(side * 256, 256), 256)
            rhs = low_ref[:, :, columns].reshape(1024, 256)
            if unit == short_unit:
                rhs_s = low_s_ref[:, :, columns].reshape(1024, 256)
                rhs = jnp.where(upper == 0, rhs_s, rhs)
            results.append(jnp.dot(lhs, rhs, preferred_element_type=F32))
        split_out(pipe, zone, unit, results[0], results[1], own_ref, other_ref)
    hand_out(other_ref, outs)


def add_cores_kernel(own_ref, *refs):
    got, (keep_ref, send_ref) = refs[:-2], refs[-2:]
    each = 4 // len(got)
    for slot in range(4):
        value = own_ref[slot] + got[slot // each][slot % each].astype(F32)
        if slot < 2:
            keep_ref[slot] = value
        else:
            send_ref[slot - 2] = value.astype(BF16)


def add_near_kernel(own_ref, got_ref, keep_ref, send_ref):
    keep_ref[...] = own_ref[0] + got_ref[0].astype(F32)
    send_ref[...] = (own_ref[1] + got_ref[1].astype(F32)).astype(BF16)


def add_far_kernel(own_ref, got_ref, out_ref):
    out_ref[...] = (own_ref[...] + got_ref[...].astype(F32)).astype(BF16)


def join_kernel_of(*refs):
    at = 0
    for ref in refs[:-1]:
        if len(ref.shape) == 3:
            refs[-1][at] = ref[...]
            at += 1
        else:
            refs[-1][at : at + ref.shape[0]] = ref[...]
            at += ref.shape[0]


def gathered_blocks(zone, batch, refs):
    if len(refs) == 8:
        for kb in range(4):
            for rel in range(4):
                yield batch ^ kb, zone ^ rel, refs[2 * kb + rel % 2], rel // 2
        return
    a, b, ax, by, ayy, bxx = refs
    sets = {0: (a, b, 0, 0), 1: (ax, bxx, 0, 0), 2: (ayy, by, 0, 0), 3: (ayy, bxx, 2, 2)}
    for kb in range(4):
        even, odd, base_even, base_odd = sets[kb]
        for rel in range(4):
            if rel % 2 == 1:
                yield batch ^ kb, zone ^ rel, odd, base_odd + rel // 2
            else:
                yield batch ^ kb, zone ^ rel, even, base_even + rel // 2


def assemble_kernel(where_ref, *refs):
    pieces, (out_ref, token_ref, stage_ref, sems) = refs[:-4], refs[-4:]
    token_ref[...] = jnp.zeros(token_ref.shape, F32)
    batch, zone = where_ref[1], where_ref[2]
    blocks = list(gathered_blocks(zone, batch, pieces))
    copies = []
    for tap in range(9):
        for owner, quarter, ref, index in blocks:
            rows = pl.ds(pl.multiple_of(owner * 128 + quarter * 32, 32), 32)
            stage_ref[tap, rows, :] = ref[index, tap].astype(F32)
        copies.append(pltpu.make_async_copy(stage_ref.at[tap], out_ref.at[tap], sems.at[tap]))
        copies[-1].start()
    for copy in copies:
        copy.wait()


def assemble_down_kernel(where_ref, *refs):
    pieces, (out_hbm, short_hbm, out_ref, short_ref, sems) = refs[:-5], refs[-5:]
    batch, zone = where_ref[1], where_ref[2]
    for owner, quarter, ref, index in gathered_blocks(zone, batch, pieces):
        upper, part = owner // 2, owner % 2
        rows = pl.ds(pl.multiple_of(part * 128 + quarter * 32, 32), 32)
        value = ref[index].astype(F32)
        for kind in range(2):

            @pl.when(upper == kind)
            def _(value=value, rows=rows, units=DOWN_UNITS[kind]):
                for unit, (_, _, _, tap) in enumerate(units):
                    if tap == 9:
                        short_ref[rows, :] = value[unit]
                    else:
                        out_ref[tap, rows, :] = value[unit]

    copies = [
        pltpu.make_async_copy(out_ref, out_hbm, sems.at[0]),
        pltpu.make_async_copy(short_ref, short_hbm, sems.at[1]),
    ]
    for copy in copies:
        copy.start()
    for copy in copies:
        copy.wait()


def facts_kernel(where_ref, p0, p1, p2, p3, hw_ref, facts_ref, living_ref, targets_ref, heads_ref):
    pipe, batch = where_ref[0], where_ref[1]
    tasks = hw_ref.shape[0]
    alive = [jnp.float32(0.0), jnp.float32(0.0)]
    for rel, piece in enumerate((p0, p1, p2, p3)):
        owner = batch ^ rel
        marks = piece[MARKS:, 0:tasks].astype(F32)
        count = jnp.max(marks[4:5, :])
        for slot in range(4):
            side, place = slot // 2, owner * 2 + slot % 2
            living = (count > slot + 0.5).astype(F32)
            alive[side] = alive[side] + living
            row = pl.ds(side * 8 + place, 1)
            living_ref[row, :] = jnp.full((1, tasks), living)
            targets_ref[row, :] = marks[slot : slot + 1, :]

            @pl.when(pipe == side)
            def _(place=place, living=living):
                facts_ref[place] = living

    own = jnp.where(pipe == 0, alive[0], alive[1])
    facts_ref[OWN_PX] = own * 128.0
    facts_ref[OTHER_PX] = (alive[0] + alive[1] - own) * 128.0
    facts_ref[ALL_PX] = (alive[0] + alive[1]) * 128.0
    for rest in range(ALL_PX + 1, 16):
        facts_ref[rest] = jnp.float32(0.0)
    heads_ref[...] = lax.dot_general(
        hw_ref[...], hw_ref[...], NT, precision=HIGHEST, preferred_element_type=F32
    )


SMALL_ROWS = 72


def small_kernel(where_ref, head_ref, all_ref, sum_f, other_f, sum_j, other_j, sum_d, other_d,
                 sent_ref, wide_ref):
    pipe, batch = where_ref[0], where_ref[1]
    tasks = head_ref.shape[0] - 8
    wide_ref[...] = jnp.zeros(wide_ref.shape, F32)
    wide_ref[0 : tasks + 3, :] = head_ref[0 : tasks + 3, :]
    at = tasks + 3
    for own, other, count in ((sum_f, other_f, 2), (sum_j, other_j, 3), (sum_d, other_d, 2)):
        wide_ref[at : at + count, :] = own[0:count, :] + other[0:count, :]
        at += count
    for side in range(2):
        for slot in range(2):
            row = side * 8 + batch * 2 + slot
            at_row = SMALL_ROWS - 16 + where_ref[2] * 4 + side * 2 + slot
            wide_ref[pl.ds(at_row, 1), :] = all_ref[0, pl.ds(row, 1), :]
    sent_ref[...] = wide_ref[:, pl.ds(pl.multiple_of(pipe * 256, 256), 256)]


def add_kernel(a_ref, b_ref, out_ref):
    out_ref[...] = a_ref[...] + b_ref[...]


def small_out_kernel(where_ref, near_ref, far_ref, pooled_ref, head_ref, gd_ref, bd_ref, gp_ref,
                     bp_ref, headb_ref):
    tasks = head_ref.shape[0]
    pipe = where_ref[0]
    total = near_ref[...] + far_ref[...]
    pooled_ref[...] = total[SMALL_ROWS - 16 :]
    head_ref[...] = total[0:tasks]

    def line(at):
        return total[tasks + at : tasks + at + 1]

    share = tasks // 2
    headb_ref[...] = jnp.where(pipe == 0, line(2)[:, 0:share], line(2)[:, share:tasks])
    bp_ref[0:1, :], gp_ref[0:1, :] = line(3), line(4)
    bp_ref[1:2, :], gp_ref[1:2, :] = line(0), line(1)
    bd_ref[0:1, :], gd_ref[0:1, :] = line(8), line(9)
    bd_ref[1:2, :], gd_ref[1:2, :] = line(5), line(6)
    bd_ref[2:3, :], gd_ref[2:3, :] = line(5), line(7)


def fast_device(images, image_counts, labels, fw_picks, conv_down, conv_mid, shortcut, gains_down,
                biases_down, conv_first, conv_second, gains_plain, biases_plain, head_weight,
                head_bias):
    pipe, batch, zone = (lax.axis_index(axis) for axis in ("pipe", "batch", "space"))
    tasks = head_weight.shape[1]

    def over(axis, rel, x):
        size = lax.axis_size(axis)
        return lax.ppermute(x, axis, [(i, i ^ rel) for i in range(size)])

    where = jnp.stack([pipe, batch, zone, zone]).astype(jnp.int32)
    params = jnp.concatenate([gains_down, biases_down, gains_plain, biases_plain])
    turned_heads = head_weight.T
    bias_row = head_bias.reshape(1, tasks)

    pieces = call(
        pieces_kernel,
        [((144, 512), BF16)] + [((128, 512), BF16)] * 3,
        [where, images, labels, image_counts],
        [pltpu.VMEM((64, 128), F32), pltpu.VMEM((4, 2, 2, 64, 256), BF16),
         pltpu.SemaphoreType.DMA((4,))],
        name="pieces",
        specs={1: HBM, 3: SM},
    )
    moved = [over("space", rel, pieces[rel]) for rel in (1, 2, 3)]
    moved = [pieces[0], moved[0], jnp.concatenate([moved[1], moved[2]])]
    gathered = [moved] + [[over("batch", kb, x) for x in moved] for kb in (1, 2, 3)]
    facts, living, targets, heads = call(
        facts_kernel,
        [((16,), F32), ((16, tasks), F32), ((16, tasks), F32), ((tasks, tasks), F32)],
        [where] + [line[0] for line in gathered] + [turned_heads],
        name="facts",
    )

    big = ((8, 128, 512), F32)
    low = ((8, 128, 512), BF16)
    rows = ((8, 512), F32)
    x_scratch = pltpu.VMEM((8, 128, 1536), BF16)
    conv_scratch = pltpu.VMEM((8, 128, 512), F32)
    conv_flops = 2 * 1024 * 4608 * 512

    def partner(x):
        return over("pipe", 1, x)

    img, down_out, short_out, stat_d = call(
        down_kernel,
        [((8, 128, 1024), BF16), big, big, rows],
        [facts, where] + [piece for line in gathered for piece in line] + [conv_down, shortcut],
        [pltpu.VMEM((8, 128, 512), BF16)],
        conv_flops // 2,
        "down",
    )
    other_d = partner(stat_d)
    down_act, mid_out, stat_m, norm_d = call(
        lambda *refs: layer_kernel(G_DOWN, B_DOWN, *refs),
        [low, big, rows, rows],
        [facts, down_out, stat_d, other_d, params, conv_mid],
        [x_scratch],
        conv_flops,
        "mid",
    )
    other_m = partner(stat_m)
    section, first_out, stat_f, norm_j = call(
        join_kernel,
        [low, big, rows, rows],
        [facts, mid_out, short_out, stat_m, other_m, stat_d, other_d, params, conv_first],
        [x_scratch],
        conv_flops,
        "first",
    )
    other_f = partner(stat_f)
    plain_act, second_out, stat_s, norm_f = call(
        lambda *refs: layer_kernel(G_FIRST, B_FIRST, *refs),
        [low, big, rows, rows],
        [facts, first_out, stat_f, other_f, params, conv_second],
        [x_scratch],
        conv_flops,
        "second",
    )
    other_s = partner(stat_s)
    pack, norm_s = call(
        block_kernel,
        [((24, 512), F32), rows],
        [facts, second_out, section, stat_s, other_s, params],
        name="block",
    )
    other_pack = partner(pack)
    all_pack, errors, cross = call(
        logits_kernel,
        [((3, 16, 512), F32), ((16, tasks), F32), ((tasks, tasks), F32)],
        [where, pack, other_pack, living, targets, turned_heads, bias_row],
        name="logits",
    )
    crosses = [cross] + [over("space", rel, cross) for rel in (1, 2, 3)]
    second_low, grad_pool, small = call(
        head_kernel,
        [low, rows, ((tasks + 8, 512), F32)],
        [fw_picks, where, facts] + crosses
        + [heads, turned_heads, errors, all_pack, second_out, section, norm_s, params],
        [pltpu.VMEM((1, tasks), F32), pltpu.VMEM((tasks, tasks), F32)],
        name="head",
    )

    class Sum:
        def __init__(self, kernel, units, operands, scratch, flops, name, after=(), parts=4):
            self.units, self.name = units, name
            self.own, *self.other = call(
                kernel,
                [self.block(4, dtype=F32)] + [self.block(4 // parts)] * parts,
                operands,
                [scratch, pltpu.VMEM((4, units, 32, 256), BF16)],
                flops,
                name,
                after,
            )
            self.got = [partner(x) for x in self.other]

        def block(self, *lead, dtype=BF16):
            return (lead + (self.units, 32, 256), dtype)

        def cores(self, after=()):
            self.keep, sent = call(
                add_cores_kernel,
                [self.block(2, dtype=F32), self.block(2)],
                [self.own] + self.got,
                name=self.name + "_cores",
                after=after,
            )
            self.near = over("space", 1, sent)

        def zone_near(self, after=()):
            self.keep, sent = call(
                add_near_kernel,
                [self.block(dtype=F32), self.block()],
                [self.keep, self.near],
                name=self.name + "_near",
                after=after,
            )
            self.far = over("space", 2, sent)

        def zone_far(self, after=()):
            (self.final,) = call(
                add_far_kernel,
                [self.block()],
                [self.keep, self.far],
                name=self.name + "_final",
                after=after,
            )
            self.other_far = over("space", 2, self.final)

        def pair(self, after=()):
            (self.a,) = call(
                join_kernel_of,
                [self.block(2)],
                [self.final, self.other_far],
                name=self.name + "_pair",
                after=after,
            )
            self.b = over("space", 1, self.a)

        def direct(self):
            self.ra = [over("batch", rel, self.a) for rel in (1, 2, 3)]
            self.rb = [over("batch", rel, self.b) for rel in (1, 2, 3)]
            self.blocks = [where, self.a, self.b]
            for x, y in zip(self.ra, self.rb):
                self.blocks += [x, y]

        def plane(self):
            self.ax, self.by = over("batch", 1, self.a), over("batch", 2, self.b)

        def plane_far(self, after=()):
            self.fa, self.fb = [
                call(join_kernel_of, [self.block(4)], pair, name=self.name + "_cross", after=after)[0]
                for pair in ([self.a, self.ax], [self.b, self.by])
            ]
            self.ayy, self.bxx = over("batch", 2, self.fa), over("batch", 1, self.fb)
            self.blocks = [where, self.a, self.b, self.ax, self.by, self.ayy, self.bxx]

    def kernel_grad_of(act, low_grad, name, after=(), parts=PARTS):
        return Sum(
            kernel_grad_kernel, 9, [where, act, low_grad], pltpu.VMEM((9, 128, 1024), BF16),
            conv_flops // 4, name, after, parts,
        )

    def assembled(blocks, name, after=()):
        out, token = call(
            assemble_kernel,
            [((9, 512, 256), F32), ((8, 128), F32)],
            blocks,
            [pltpu.VMEM((9, 512, 256), F32), pltpu.SemaphoreType.DMA((9,))],
            name=name,
            after=after,
            out_space=[HBM, VM],
        )
        return out.reshape(3, 3, 512, 256), token

    second = kernel_grad_of(plain_act, second_low, "second_grad")
    second.cores()
    up_f, sum_f = call(
        second_back_kernel,
        [big, rows],
        [facts, second_low, first_out, norm_f, params, conv_second],
        [x_scratch, conv_scratch],
        conv_flops,
        "second_back",
        after=[second.keep],
    )
    other_sf = partner(sum_f)
    second.zone_near(after=[sum_f])
    first_low, up_j, sum_j = call(
        first_back_kernel,
        [low, big, rows],
        [facts, up_f, first_out, norm_f, sum_f, other_sf, params, conv_first,
         second_out, norm_s, section, grad_pool, mid_out, short_out, norm_j],
        [x_scratch, conv_scratch],
        conv_flops,
        "first_back",
        after=[second.keep],
    )
    other_sj = partner(sum_j)
    second.zone_far(after=[sum_j])
    first = kernel_grad_of(section, first_low, "first_grad", after=[second.final])
    second.pair(after=first.other[0:1])
    second.plane()
    first.cores(after=[second.a])
    mid_low, short_low, up_d, sum_d = call(
        mid_back_kernel,
        [low, low, big, rows],
        [facts, up_j, mid_out, short_out, norm_j, sum_j, other_sj, params, conv_mid,
         down_out, norm_d],
        [x_scratch, conv_scratch],
        conv_flops,
        "mid_back",
        after=[first.keep],
    )
    other_sd = partner(sum_d)
    first.zone_near(after=[sum_d, second.b, second.ax])
    mid = kernel_grad_of(down_act, mid_low, "mid_grad", after=[first.keep])
    first.zone_far(after=mid.other[0:1])
    mid.cores(after=[first.final])
    second.plane_far(after=[mid.keep])
    (down_low,) = call(
        down_back_kernel,
        [low],
        [facts, up_d, down_out, norm_d, sum_d, other_sd, params],
        name="down_back",
        after=[second.fa, second.fb],
    )
    down = Sum(
        down_grad_kernel, 5, [where, img, down_low, short_low], pltpu.VMEM((5, 128, 1024), BF16),
        conv_flops // 8, "down_grad", parts=LAST_PARTS,
    )
    first.pair(after=down.other[0:1])
    first.plane()
    mid.zone_near(after=[first.a])
    down.cores(after=[mid.keep])
    img_pieces = call(
        image_back_kernel,
        [((2, 2, 2, 2, 32, 256), BF16)] * 2,
        [where, down_low, short_low, conv_down, shortcut],
        [pltpu.VMEM((4, 2, 2, 2, 32, 256), BF16)],
        conv_flops // 8,
        "image_back",
        after=[down.keep],
    )
    mid.zone_far(after=[img_pieces[0]])
    down.zone_near(after=[mid.final])
    second_out_grad, second_done = assembled(second.blocks, "second_out", after=[down.keep, first.b])
    first.plane_far(after=[second_done])
    mid.pair(after=[first.fa, first.fb])
    mid.plane()
    down.zone_far(after=[mid.a])
    down.pair()
    down.plane()
    first_out_grad, first_done = assembled(first.blocks, "first_out", after=[down.a])
    mid.plane_far(after=[first_done])
    down.plane_far(after=[mid.fa, mid.fb])
    mid_out_grad, mid_done = assembled(mid.blocks, "mid_out", after=[down.fa])

    img_near = over("space", 1, img_pieces[1])
    pair = ((2, 2, 2, 2, 32, 256), BF16)
    (img_sent,) = call(image_far_kernel, [pair], [img_pieces[0], img_near], name="image_far")
    img_far = over("space", 2, img_sent)
    img_parts = [img_pieces[0], img_near, img_far]
    (img_other,) = call(
        image_pipe_kernel, [((4, 2, 2, 32, 256), BF16)], img_parts, name="image_pipe"
    )
    (images_grad,) = call(
        image_grad_kernel,
        [((16, 2, 64, 128), F32)],
        [where] + img_parts + [partner(img_other)],
        name="image_grad",
    )

    (sent,) = call(
        small_kernel,
        [((SMALL_ROWS, 256), F32)],
        [where, small, all_pack, sum_f, other_sf, sum_j, other_sj, sum_d, other_sd],
        [pltpu.VMEM((SMALL_ROWS, 512), F32)],
        name="small",
        after=[down.final],
    )
    (near_sum,) = call(
        add_kernel,
        [((SMALL_ROWS, 256), F32)],
        [sent, over("space", 1, sent)],
        name="small_near",
    )
    pooled, head_out, gains_d, sums_d, gains_p, sums_p, head_b = call(
        small_out_kernel,
        [((16, 256), F32), ((tasks, 256), F32), ((3, 256), F32), ((3, 256), F32),
         ((2, 256), F32), ((2, 256), F32), ((1, tasks // 2), F32)],
        [where, near_sum, over("space", 2, near_sum)],
        name="small_out",
    )
    down_grad, short_grad = call(
        assemble_down_kernel,
        [((9, 256, 256), F32), ((256, 256), F32)],
        down.blocks,
        [pltpu.VMEM((9, 256, 256), F32), pltpu.VMEM((256, 256), F32),
         pltpu.SemaphoreType.DMA((2,))],
        out_space=[HBM, HBM],
        name="down_out",
    )
    return (
        pooled,
        images_grad,
        down_grad.reshape(3, 3, 256, 256),
        mid_out_grad,
        short_grad,
        gains_d,
        sums_d,
        first_out_grad,
        second_out_grad,
        gains_p,
        sums_p,
        head_out.T,
        head_b.reshape(tasks // 2),
    )


def per_device(
    images,
    image_counts,
    labels,
    fw_picks,
    conv_down,
    conv_mid,
    shortcut,
    gains_down,
    biases_down,
    conv_first,
    conv_second,
    gains_plain,
    biases_plain,
    head_weight,
    head_bias,
):
    layout = Layout(image_counts.shape[1])
    micros, zone = layout.micros, layout.zone
    sizes = (images.shape, conv_down.shape, lax.axis_size("pipe"), lax.axis_size("batch"))
    if layout.groups == 1 and sizes == ((16, 2, 64, 256), (3, 3, 256, 512), 2, 4):
        return fast_device(
            images, image_counts, labels, fw_picks, conv_down, conv_mid, shortcut, gains_down,
            biases_down, conv_first, conv_second, gains_plain, biases_plain, head_weight,
            head_bias,
        )
    batches, pipes = lax.axis_size("batch"), lax.axis_size("pipe")
    batch = lax.axis_index("batch")
    pipe = lax.axis_index("pipe")
    per_micro = images.shape[0] // micros
    count = per_micro * batches
    entering, channels = conv_down.shape[2], conv_mid.shape[3]
    tasks = head_weight.shape[1]
    half = channels // pipes
    own = pipe * half

    def own_out(kernel, axis):
        size = kernel.shape[axis] // pipes
        return lax.dynamic_slice_in_dim(kernel, pipe * size, size, axis)

    def whole(tensor, axis=3):
        return lax.all_gather(tensor, "pipe", axis=axis, tiled=True)

    def share(tensor):
        size = tensor.shape[3] // batches
        return lax.dynamic_slice_in_dim(tensor, batch * size, size, 3)

    mine = lax.all_to_all(
        images, "space", 0, 1, axis_index_groups=layout.inner, tiled=True
    )
    mine = lax.all_gather(mine, "batch", axis=0, tiled=True)
    counts = lax.all_gather(image_counts, "batch", axis=0, tiled=True)
    counts = lax.dynamic_slice_in_dim(counts, zone, 1, 1)[:, 0]
    marks = lax.dynamic_slice_in_dim(labels, zone * per_micro, per_micro, 0)
    targets = lax.all_gather(marks, "batch", axis=0, tiled=True).astype(F32)
    slots = jnp.arange(per_micro, dtype=jnp.int32)
    living = (slots[None, :] < counts[:, None]).astype(F32).reshape(count)
    weight = living[:, None, None, None]
    out_rows, out_cols = mine.shape[1] // 2, mine.shape[2] // 2
    image_pixels = out_rows * layout.groups * out_cols
    counted = jnp.sum(living) * image_pixels
    scale = float(image_pixels * tasks)

    gain_d, bias_d = own_out(gains_down, 1), own_out(biases_down, 1)
    gain_p, bias_p = own_out(gains_plain, 1), own_out(biases_plain, 1)

    above = layout.row_from(mine[:, -1:], 1)
    down_ext = jnp.pad(
        jnp.concatenate([above, mine], axis=1), ((0, 0), (0, 0), (1, 0), (0, 0))
    )
    down_out = conv_valid(down_ext, own_out(conv_down, 3), 2)
    down_norm, down_inv = norm_forward(layout, down_out, weight, counted)
    down_pre = down_norm * gain_d[0] + bias_d[0]
    mid_ext = layout.rims(whole(jax.nn.silu(down_pre).astype(BF16)))
    mid_out = conv_valid(mid_ext, own_out(conv_mid, 3), 1)
    short_in = mine[:, ::2, ::2]
    short_out = jnp.einsum(
        "nhwi,io->nhwo", short_in, own_out(shortcut, 1), preferred_element_type=F32
    )
    mid_norm, mid_inv = norm_forward(layout, mid_out, weight, counted)
    short_norm, short_inv = norm_forward(layout, short_out, weight, counted)
    section_pre = mid_norm * gain_d[1] + bias_d[1] + short_norm * gain_d[2] + bias_d[2]
    section = jax.nn.silu(section_pre).astype(BF16)
    first_ext = layout.rims(whole(section))
    first_out = conv_valid(first_ext, own_out(conv_first, 3), 1)
    first_norm, first_inv = norm_forward(layout, first_out, weight, counted)
    first_pre = first_norm * gain_p[0] + bias_p[0]
    second_ext = layout.rims(whole(jax.nn.silu(first_pre).astype(BF16)))
    second_out = conv_valid(second_ext, own_out(conv_second, 3), 1)
    second_norm, second_inv = norm_forward(layout, second_out, weight, counted)
    block_pre = second_norm * gain_p[1] + bias_p[1] + section.astype(F32)
    pooled = layout.group_sum(jnp.sum(jax.nn.silu(block_pre), axis=(1, 2))) / image_pixels

    pooled_all = whole(pooled, 1)
    logits = jnp.dot(pooled_all, head_weight, precision=HIGHEST) + head_bias
    errors = living[:, None] * (jax.nn.sigmoid(logits) - targets)
    cross = jnp.einsum("nt,ns->ts", errors, errors, precision=HIGHEST)
    cross = lax.psum(cross, "space", axis_index_groups=layout.inner)
    gram = cross * jnp.dot(head_weight.T, head_weight, precision=HIGHEST)
    alpha = frank_wolfe(gram, fw_picks)
    grad_logits = scale * alpha * errors
    head_w = jnp.einsum("nc,nt->ct", pooled, grad_logits, precision=HIGHEST)
    head_b = jnp.sum(grad_logits, axis=0)
    head_own = own_out(head_weight, 0)
    grad_pool = jnp.einsum("nt,ct->nc", grad_logits, head_own, precision=HIGHEST) / image_pixels

    grad_block = grad_pool[:, None, None, :] * silu_slope(block_pre)
    second_low, second_cross, second_sum = norm_back(
        layout, grad_block, second_norm, second_inv, gain_p[1], weight, counted
    )
    second_kernel = kernel_grad(share(second_ext), second_low, 1)
    act_grad = conv_valid(layout.rims(whole(second_low)), flipped(own_out(conv_second, 2)), 1)
    first_low, first_cross, first_sum = norm_back(
        layout, act_grad * silu_slope(first_pre), first_norm, first_inv, gain_p[0], weight, counted
    )
    first_kernel = kernel_grad(share(first_ext), first_low, 1)
    entry_grad = conv_valid(layout.rims(whole(first_low)), flipped(own_out(conv_first, 2)), 1)
    entry_grad = (entry_grad + grad_block).astype(BF16).astype(F32)
    grad_section = entry_grad * silu_slope(section_pre)
    mid_low, mid_cross, mid_sum = norm_back(
        layout, grad_section, mid_norm, mid_inv, gain_d[1], weight, counted
    )
    short_low, short_cross, short_sum = norm_back(
        layout, grad_section, short_norm, short_inv, gain_d[2], weight, counted
    )
    mid_kernel = kernel_grad(share(mid_ext), mid_low, 1)
    short_kernel = jnp.einsum(
        "nhwi,nhwo->io", share(short_in), short_low, preferred_element_type=F32
    )
    act_grad = conv_valid(layout.rims(whole(mid_low)), flipped(own_out(conv_mid, 2)), 1)
    down_low, down_cross, down_sum = norm_back(
        layout, act_grad * silu_slope(down_pre), down_norm, down_inv, gain_d[0], weight, counted
    )
    down_kernel = kernel_grad(share(down_ext), down_low, 2)

    kept = lax.dynamic_slice_in_dim(whole(down_low), batch * per_micro, per_micro, 0)
    below = layout.row_from(kept[:, :1], -1)
    spread = lax.conv_general_dilated(
        jnp.concatenate([kept, below], axis=1),
        flipped(own_out(conv_down, 2)),
        (1, 1),
        ((2, 2), (2, 2)),
        lhs_dilation=(2, 2),
        dimension_numbers=NUMBERS,
        preferred_element_type=F32,
    )[:, 1 : 2 * out_rows + 1, 1:]
    short_kept = lax.dynamic_slice_in_dim(whole(short_low), batch * per_micro, per_micro, 0)
    spread = spread.at[:, ::2, ::2].add(
        jnp.einsum(
            "nhwo,io->nhwi", short_kept, own_out(shortcut, 0), preferred_element_type=F32
        )
    )
    images_grad = lax.all_to_all(
        spread.astype(BF16), "space", 1, 0, axis_index_groups=layout.inner, tiled=True
    ).astype(F32)

    def total(kernel, axis):
        summed = lax.psum(kernel.astype(BF16), "space")
        return lax.all_gather(summed, "batch", axis=axis, tiled=True).astype(F32)

    pooled_out = lax.dynamic_slice_in_dim(pooled, batch * per_micro, per_micro, 0)
    pooled_out = lax.all_gather(
        pooled_out, "space", axis_index_groups=layout.inner, axis=0, tiled=True
    )
    head_w, head_b = lax.psum((head_w, head_b), "space", axis_index_groups=layout.inner)
    gains_d, sums_d, gains_p, sums_p = lax.psum(
        (
            jnp.stack([down_cross, mid_cross, short_cross]),
            jnp.stack([down_sum, mid_sum, short_sum]),
            jnp.stack([first_cross, second_cross]),
            jnp.stack([first_sum, second_sum]),
        ),
        "space",
    )
    return (
        pooled_out,
        images_grad,
        total(down_kernel, 1).reshape(3, 3, entering, half),
        total(mid_kernel, 1).reshape(3, 3, channels, half),
        total(short_kernel, 0),
        gains_d,
        sums_d,
        total(first_kernel, 1).reshape(3, 3, channels, half),
        total(second_kernel, 1).reshape(3, 3, channels, half),
        gains_p,
        sums_p,
        head_w,
        own_out(head_b, 0),
    )


def solution(mesh):
    placed = (
        P("batch", "space", None, None),
        P("batch", None),
        P("batch", None),
    ) + (P(),) * 12
    return jax.shard_map(
        per_device,
        mesh=mesh,
        in_specs=placed,
        out_specs=(
            P("batch", "pipe"),
            P("batch", "space", None, "pipe"),
            P(None, None, None, "pipe"),
            P(None, None, None, "pipe"),
            P(None, "pipe"),
            P(None, "pipe"),
            P(None, "pipe"),
            P(None, None, None, "pipe"),
            P(None, None, None, "pipe"),
            P(None, "pipe"),
            P(None, "pipe"),
            P("pipe", None),
            P("pipe"),
        ),
        check_vma=False,
    )
```

```python
import jax
import jax.numpy as jnp
from jax import lax
from jax.experimental import pallas as pl
from jax.experimental.pallas import tpu as pltpu
from jax.sharding import PartitionSpec as P

EPSILON = 1e-05
NUMBERS = ("NHWC", "HWIO", "NHWC")
HIGHEST = lax.Precision.HIGHEST
F32 = jnp.float32
BF16 = jnp.bfloat16


def silu_slope(values):
    sigmoid = jax.nn.sigmoid(values)
    return sigmoid * (1.0 + values * (1.0 - sigmoid))


def frank_wolfe_kernel(picks_ref, gram_ref, alpha_ref):
    tasks = gram_ref.shape[0]
    lanes = lax.broadcasted_iota(jnp.int32, (1, tasks), 1)
    gram = gram_ref[...]
    alpha = jnp.full((1, tasks), 1.0 / tasks, F32)
    pulled = jnp.sum(gram, axis=0, keepdims=True) * (1.0 / tasks)
    energy = jnp.sum(pulled * alpha, axis=1, keepdims=True)

    def advance(step, carry):
        alpha, pulled, energy = carry
        chosen = picks_ref[step]
        row = gram_ref[pl.ds(chosen, 1), :]
        onehot = (lanes == chosen).astype(F32)
        toward = jnp.sum(pulled * onehot, axis=1, keepdims=True)
        corner = jnp.sum(row * onehot, axis=1, keepdims=True)
        denom = jnp.maximum(energy - 2.0 * toward + corner, 0.05 * corner)
        ratio = jnp.clip((energy - toward) / denom, 0.0, 1.0)
        rest = 1.0 - ratio
        alpha = rest * alpha + ratio * onehot
        pulled = rest * pulled + ratio * row
        energy = rest * rest * energy + 2.0 * rest * ratio * toward + ratio * ratio * corner
        return alpha, pulled, energy

    alpha, _, _ = lax.fori_loop(0, picks_ref.shape[0], advance, (alpha, pulled, energy))
    alpha_ref[...] = alpha


def frank_wolfe(gram, picks):
    tasks = gram.shape[0]
    return pl.pallas_call(
        frank_wolfe_kernel,
        out_shape=jax.ShapeDtypeStruct((1, tasks), F32),
        in_specs=[
            pl.BlockSpec(memory_space=pltpu.SMEM),
            pl.BlockSpec(memory_space=pltpu.VMEM),
        ],
        out_specs=pl.BlockSpec(memory_space=pltpu.VMEM),
    )(picks, gram)


class Layout:
    def __init__(self, micros):
        self.micros = micros
        self.spaces = lax.axis_size("space")
        self.groups = self.spaces // micros
        self.inner = [
            [group * micros + zone for zone in range(micros)] for group in range(self.groups)
        ]
        self.outer = [
            [group * micros + zone for group in range(self.groups)] for zone in range(micros)
        ]
        self.zone = lax.axis_index("space") % micros

    def group_sum(self, tree):
        if self.groups == 1:
            return tree
        return lax.psum(tree, "space", axis_index_groups=self.outer)

    def row_from(self, block, step):
        span = step * self.micros
        route = [
            (i, i + span) for i in range(self.spaces) if 0 <= i + span < self.spaces
        ]
        if not route:
            return jnp.zeros_like(block)
        return lax.ppermute(block, "space", route)

    def rims(self, tensor):
        above = self.row_from(tensor[:, -1:], 1)
        below = self.row_from(tensor[:, :1], -1)
        grown = jnp.concatenate([above, tensor, below], axis=1)
        return jnp.pad(grown, ((0, 0), (0, 0), (1, 1), (0, 0)))


def conv_valid(extended, kernel, stride):
    return lax.conv_general_dilated(
        extended,
        kernel,
        (stride, stride),
        "VALID",
        dimension_numbers=NUMBERS,
        preferred_element_type=F32,
    )


def flipped(kernel):
    return jnp.swapaxes(kernel[::-1, ::-1], 2, 3)


def kernel_grad(extended, grad_low, stride):
    rows, cols = grad_low.shape[1], grad_low.shape[2]
    taps = []
    for row_tap in range(3):
        for col_tap in range(3):
            window = extended[
                :,
                row_tap : row_tap + stride * (rows - 1) + 1 : stride,
                col_tap : col_tap + stride * (cols - 1) + 1 : stride,
            ]
            taps.append(jnp.einsum("nhwi,nhwo->io", window, grad_low, preferred_element_type=F32))
    return jnp.stack(taps)


def norm_forward(layout, conv_out, weight, counted):
    total = layout.group_sum(jnp.sum(conv_out * weight, axis=(0, 1, 2)))
    centered = conv_out - total / counted
    spread = layout.group_sum(jnp.sum(centered * centered * weight, axis=(0, 1, 2)))
    inverse = lax.rsqrt(spread / counted + EPSILON)
    return centered * inverse, inverse


def norm_back(layout, upstream, normed, inverse, gain, weight, counted):
    grad_sum = jnp.sum(upstream * weight, axis=(0, 1, 2))
    cross_sum = jnp.sum(upstream * normed * weight, axis=(0, 1, 2))
    grad_total, cross_total = layout.group_sum((grad_sum, cross_sum))
    correction = weight * (grad_total / counted + normed * (cross_total / counted))
    low = (gain * inverse * (upstream - correction)).astype(BF16)
    return low, cross_sum, grad_sum


KERNEL_LIMIT = 16 * 2**20
PARTS, LAST_PARTS = 4, 1
VM = pl.BlockSpec(memory_space=pltpu.VMEM)
SM = pl.BlockSpec(memory_space=pltpu.SMEM)
HBM = pl.BlockSpec(memory_space=pltpu.HBM)
NT = (((1,), (1,)), ((), ()))
TN = (((0,), (0,)), ((), ()))
OWN_PX, OTHER_PX, ALL_PX = 8, 9, 10
G_DOWN, G_MID, G_SHORT, B_DOWN, B_MID, B_SHORT, G_FIRST, G_SECOND, B_FIRST, B_SECOND = range(10)


def param(params_ref, row):
    return params_ref[row : row + 1, :]


def call(kernel, outs, operands, scratch=(), flops=0, name=None, after=(), specs=None,
         out_space=None):
    count = len(operands)
    nbytes = sum(x.size * x.dtype.itemsize for x in operands)
    specs = specs or {}

    def body(*refs):
        kernel(*refs[:count], *refs[count + len(after) :])

    return pl.pallas_call(
        body,
        out_shape=tuple(jax.ShapeDtypeStruct(shape, dtype) for shape, dtype in outs),
        in_specs=[specs.get(i, SM if x.ndim == 1 else VM) for i, x in enumerate(operands)]
        + [pl.BlockSpec(memory_space=pl.ANY)] * len(after),
        out_specs=tuple(out_space or [SM if len(shape) == 1 else VM for shape, _ in outs]),
        scratch_shapes=list(scratch),
        compiler_params=pltpu.CompilerParams(vmem_limit_bytes=KERNEL_LIMIT),
        cost_estimate=pl.CostEstimate(
            flops=int(flops), bytes_accessed=int(nbytes), transcendentals=0
        ),
        name=name,
    )(*operands, *after)


def fold(rows):
    return rows[0:8] + rows[8:16] + rows[16:24] + rows[24:32]


def total_row(part):
    return jnp.sum(part, axis=0, keepdims=True)


def band(row):
    return slice(row * 32, row * 32 + 32)


def put_band(x_ref, image, row, value):
    zero = jnp.zeros_like(value)
    x_ref[image, band(row), 512:1024] = value
    if row < 3:
        x_ref[image, band(row + 1), 0:512] = value
    else:
        x_ref[image, band(0), 0:512] = zero
    if row > 0:
        x_ref[image, band(row - 1), 1024:1536] = value
    else:
        x_ref[image, band(3), 1024:1536] = zero


def columns_joined(left, middle, right):
    count = middle.shape[0]
    column = lax.broadcasted_iota(jnp.int32, (count, 1), 0) % 32
    joined = middle
    if left is not None:
        joined = joined + jnp.where(column == 0, 0.0, pltpu.roll(left, 1, 0))
    if right is not None:
        joined = joined + jnp.where(column == 31, 0.0, pltpu.roll(right, count - 1, 0))
    return joined


def conv_core(x_ref, w_ref, out_ref, back):
    def tap(col):
        value = None
        for row in range(3):
            lhs = x_ref[:, :, row * 512 : (row + 1) * 512].reshape(1024, 512)
            if back:
                term = lax.dot_general(
                    lhs, w_ref[2 - row, 2 - col], NT, preferred_element_type=F32
                )
            else:
                term = jnp.dot(lhs, w_ref[row, col], preferred_element_type=F32)
            value = term if value is None else value + term
        return value

    out_ref[...] = columns_joined(tap(0), tap(1), tap(2)).reshape(8, 128, 512)


def stats_of(facts_ref, out_ref, stat_ref, row):
    def add(image, part):
        for r in range(4):
            part = part + fold(out_ref[image, band(r), :]) * facts_ref[image]
        return part

    first = total_row(lax.fori_loop(0, 8, add, jnp.zeros((8, 512), F32)))
    mean = first / jnp.maximum(facts_ref[OWN_PX], 1.0)

    def deviate(image, part):
        for r in range(4):
            away = out_ref[image, band(r), :] - mean
            part = part + fold(away * away) * facts_ref[image]
        return part

    second = total_row(lax.fori_loop(0, 8, deviate, jnp.zeros((8, 512), F32)))
    stat_ref[row : row + 1, :] = first
    stat_ref[row + 1 : row + 2, :] = second


def norm_of(facts_ref, own_ref, other_ref, row):
    own_px, other_px, all_px = facts_ref[OWN_PX], facts_ref[OTHER_PX], facts_ref[ALL_PX]
    own, other = own_ref[row : row + 1, :], other_ref[row : row + 1, :]
    mean = (own + other) / all_px
    apart = own / jnp.maximum(own_px, 1.0) - other / jnp.maximum(other_px, 1.0)
    spread = own_ref[row + 1 : row + 2, :] + other_ref[row + 1 : row + 2, :]
    variance = (spread + apart * apart * (own_px * other_px / all_px)) / all_px
    return mean, lax.rsqrt(variance + EPSILON)


def sigmoid(values):
    return 0.5 * jnp.tanh(0.5 * values) + 0.5


def slope_of(values):
    gate = sigmoid(values)
    return gate * (1.0 + values * (1.0 - gate))


MARKS = 128


def pieces_kernel(where_ref, images_hbm, labels_ref, count_ref, o0, o1, o2, o3, wide,
                  images_ref, sems):
    pipe, zone = where_ref[0], where_ref[2]
    tasks = labels_ref.shape[1]
    copies = []
    for rel in range(4):
        first = (zone ^ rel) * 4 + pipe * 2
        copies.append(
            pltpu.make_async_copy(
                images_hbm.at[pl.ds(first, 2)], images_ref.at[rel], sems.at[rel]
            )
        )
        copies[-1].start()
    o0[MARKS:, :] = jnp.zeros((16, 512), BF16)
    count = count_ref[0, zone].astype(F32)
    marks = jnp.concatenate(
        [
            labels_ref[pl.ds(zone * 4, 4), :].astype(F32),
            jnp.full((4, tasks), count),
            jnp.zeros((8, tasks), F32),
        ]
    )
    o0[MARKS:, 0:tasks] = marks.astype(BF16)
    for rel, out in enumerate((o0, o1, o2, o3)):
        copies[rel].wait()
        for i in range(2):
            for row in range(2):
                lines = slice((i * 2 + row) * 32, (i * 2 + row) * 32 + 32)
                for part in range(2):
                    lanes = slice(part * 128, part * 128 + 128)
                    wide[...] = images_ref[rel, i, row, :, lanes].astype(F32)
                    for par in range(2):
                        value = wide[pl.ds(par, 32, stride=2), :]
                        start = par * 256 + part * 128
                        out[lines, start : start + 128] = value.astype(BF16)


def down_kernel(facts_ref, where_ref, *refs):
    pieces, (w_ref, s_ref, img_ref, out_ref, short_ref, stat_ref, x_ref) = refs[:12], refs[12:]
    batch, zone = where_ref[1], where_ref[2]
    for kb in range(4):
        for kz in range(4):
            piece, base = pieces[kb * 3 + min(kz, 2)], (128 if kz == 3 else 0)
            row = zone ^ kz
            here = pl.ds(pl.multiple_of(row * 32, 32), 32)
            after = pl.ds(pl.multiple_of(((row + 1) % 4) * 32, 32), 32)
            for i in range(2):
                image = (batch ^ kb) * 2 + i
                start = base + i * 64
                odd = piece[start + 32 : start + 64, :]
                img_ref[image, here, 0:512] = piece[start : start + 32, :]
                img_ref[image, here, 512:1024] = odd
                x_ref[image, after, :] = jnp.where(row == 3, jnp.zeros_like(odd), odd)
    for part in range(2):
        images = slice(4 * part, 4 * part + 4)
        blocks = (
            x_ref[images].reshape(512, 512),
            img_ref[images, :, 0:512].reshape(512, 512),
            img_ref[images, :, 512:1024].reshape(512, 512),
        )
        left, middle = None, None
        for row in range(3):
            a = jnp.dot(blocks[row][:, 256:], w_ref[row, 0], preferred_element_type=F32)
            m = jnp.dot(
                blocks[row], w_ref[row, 1:3].reshape(512, 512), preferred_element_type=F32
            )
            left = a if left is None else left + a
            middle = m if middle is None else middle + m
        out_ref[images] = columns_joined(left, middle, None).reshape(4, 128, 512)
        short = jnp.dot(blocks[1][:, :256], s_ref[...], preferred_element_type=F32)
        short_ref[images] = short.reshape(4, 128, 512)
    stats_of(facts_ref, out_ref, stat_ref, 0)
    stats_of(facts_ref, short_ref, stat_ref, 2)
    stat_ref[4:8, :] = jnp.zeros((4, 512), F32)


def layer_kernel(g_row, b_row, facts_ref, in_ref, own_ref, other_ref, params_ref, w_ref,
                 act_ref, out_ref, stat_ref, norm_ref, x_ref):
    mean, inverse = norm_of(facts_ref, own_ref, other_ref, 0)
    gain, bias = param(params_ref, g_row), param(params_ref, b_row)

    def activate(image, carry):
        for r in range(4):
            pre = (in_ref[image, band(r), :] - mean) * inverse * gain + bias
            act = (pre * sigmoid(pre)).astype(BF16)
            act_ref[image, band(r), :] = act
            put_band(x_ref, image, r, act)
        return carry

    lax.fori_loop(0, 8, activate, 0)
    norm_ref[0:1, :] = mean
    norm_ref[1:2, :] = inverse
    norm_ref[2:8, :] = jnp.zeros((6, 512), F32)
    conv_core(x_ref, w_ref, out_ref, False)
    stats_of(facts_ref, out_ref, stat_ref, 0)
    stat_ref[2:8, :] = jnp.zeros((6, 512), F32)


def join_kernel(facts_ref, mid_ref, short_ref, own_m, other_m, own_d, other_d, params_ref,
                w_ref, act_ref, out_ref, stat_ref, norm_ref, x_ref):
    mean_m, inv_m = norm_of(facts_ref, own_m, other_m, 0)
    mean_s, inv_s = norm_of(facts_ref, own_d, other_d, 2)
    gain_m, gain_s = param(params_ref, G_MID), param(params_ref, G_SHORT)
    bias_m, bias_s = param(params_ref, B_MID), param(params_ref, B_SHORT)

    def activate(image, carry):
        for r in range(4):
            pre = (mid_ref[image, band(r), :] - mean_m) * inv_m * gain_m + bias_m
            pre = pre + (short_ref[image, band(r), :] - mean_s) * inv_s * gain_s + bias_s
            act = (pre * sigmoid(pre)).astype(BF16)
            act_ref[image, band(r), :] = act
            put_band(x_ref, image, r, act)
        return carry

    lax.fori_loop(0, 8, activate, 0)
    norm_ref[0:1, :] = mean_m
    norm_ref[1:2, :] = inv_m
    norm_ref[2:3, :] = mean_s
    norm_ref[3:4, :] = inv_s
    norm_ref[4:8, :] = jnp.zeros((4, 512), F32)
    conv_core(x_ref, w_ref, out_ref, False)
    stats_of(facts_ref, out_ref, stat_ref, 0)
    stat_ref[2:8, :] = jnp.zeros((6, 512), F32)


def block_kernel(facts_ref, in_ref, section_ref, own_ref, other_ref, params_ref,
                 pack_ref, norm_ref):
    mean, inverse = norm_of(facts_ref, own_ref, other_ref, 0)
    gain, bias = param(params_ref, G_SECOND), param(params_ref, B_SECOND)
    norm_ref[0:1, :] = mean
    norm_ref[1:2, :] = inverse
    norm_ref[2:8, :] = jnp.zeros((6, 512), F32)

    def gather(image, carry):
        pooled = jnp.zeros((8, 512), F32)
        slopes, crossed = pooled, pooled
        for r in range(4):
            normed = (in_ref[image, band(r), :] - mean) * inverse
            pre = normed * gain + bias + section_ref[image, band(r), :].astype(F32)
            gate = sigmoid(pre)
            slope = gate * (1.0 + pre * (1.0 - gate))
            pooled = pooled + fold(pre * gate)
            slopes = slopes + fold(slope)
            crossed = crossed + fold(slope * normed)
        pack_ref[pl.ds(image, 1), :] = total_row(pooled) / 128.0
        pack_ref[pl.ds(image + 8, 1), :] = total_row(slopes)
        pack_ref[pl.ds(image + 16, 1), :] = total_row(crossed)
        return carry

    lax.fori_loop(0, 8, gather, 0)


def logits_kernel(where_ref, own_ref, other_ref, living_ref, labels_ref, hw_ref, hb_ref,
                  all_ref, errors_ref, cross_ref):
    pipe = where_ref[0]
    for block in range(3):
        rows = slice(block * 8, block * 8 + 8)
        all_ref[block, pl.ds(pl.multiple_of(pipe * 8, 8), 8), :] = own_ref[rows, :]
        all_ref[block, pl.ds(pl.multiple_of((1 - pipe) * 8, 8), 8), :] = other_ref[rows, :]
    logits = (
        lax.dot_general(
            all_ref[0], hw_ref[...], NT, precision=HIGHEST, preferred_element_type=F32
        )
        + hb_ref[...]
    )
    errors = living_ref[...] * (sigmoid(logits) - labels_ref[...])
    errors_ref[...] = errors
    cross_ref[...] = lax.dot_general(
        errors, errors, TN, precision=HIGHEST, preferred_element_type=F32
    )


def head_kernel(picks_ref, where_ref, facts_ref, c0, c1, c2, c3, heads_ref, hw_ref, errors_ref,
                all_ref, in_ref, section_ref, norm_ref, params_ref,
                low_ref, pool_ref, small_ref, alpha_ref, gram_ref):
    tasks = gram_ref.shape[0]
    pipe = where_ref[0]
    gram_ref[...] = ((c0[...] + c1[...]) + (c2[...] + c3[...])) * heads_ref[...]
    frank_wolfe_kernel(picks_ref, gram_ref, alpha_ref)
    grad_logits = (128.0 * tasks) * alpha_ref[...] * errors_ref[...]
    pooled, slopes, crossed = all_ref[0], all_ref[1], all_ref[2]
    grad_pool = (
        jnp.dot(grad_logits, hw_ref[...], precision=HIGHEST, preferred_element_type=F32)
        / 128.0
    )
    grad_sum = total_row(grad_pool * slopes)
    cross_sum = total_row(grad_pool * crossed)
    small_ref[0:tasks, :] = lax.dot_general(
        grad_logits, pooled, TN, precision=HIGHEST, preferred_element_type=F32
    )
    small_ref[tasks : tasks + 1, :] = grad_sum
    small_ref[tasks + 1 : tasks + 2, :] = cross_sum
    small_ref[tasks + 2 :, :] = jnp.zeros((small_ref.shape[0] - tasks - 2, 512), F32)
    for start in (0, 256):
        small_ref[tasks + 2 : tasks + 3, start : start + tasks] = total_row(grad_logits)
    pool_ref[...] = jnp.where(pipe == 0, grad_pool[0:8], grad_pool[8:16])

    mean, inverse = norm_ref[0:1, :], norm_ref[1:2, :]
    gain, bias = param(params_ref, G_SECOND), param(params_ref, B_SECOND)
    all_px = facts_ref[ALL_PX]
    front = gain * inverse
    mean_grad, mean_cross = grad_sum / all_px, cross_sum / all_px

    def back(image, carry):
        up = pool_ref[pl.ds(image, 1), :]
        for r in range(4):
            normed = (in_ref[image, band(r), :] - mean) * inverse
            pre = normed * gain + bias + section_ref[image, band(r), :].astype(F32)
            grad = up * slope_of(pre)
            fix = facts_ref[image] * (mean_grad + normed * mean_cross)
            low_ref[image, band(r), :] = (front * (grad - fix)).astype(BF16)
        return carry

    lax.fori_loop(0, 8, back, 0)


def back_norm(facts_ref, in_ref, up_ref, norm_ref, own_ref, other_ref, gain, rows, sinks):
    mean, inverse = norm_ref[rows : rows + 1, :], norm_ref[rows + 1 : rows + 2, :]
    all_px = facts_ref[ALL_PX]
    front = gain * inverse
    cross_row = 1 + rows // 2
    mean_grad = (own_ref[0:1, :] + other_ref[0:1, :]) / all_px
    mean_cross = (
        own_ref[cross_row : cross_row + 1, :] + other_ref[cross_row : cross_row + 1, :]
    ) / all_px

    def back(image, carry):
        for r in range(4):
            normed = (in_ref[image, band(r), :] - mean) * inverse
            fix = facts_ref[image] * (mean_grad + normed * mean_cross)
            sinks(image, r, (front * (up_ref[image, band(r), :] - fix)).astype(BF16))
        return carry

    lax.fori_loop(0, 8, back, 0)


def second_back_kernel(facts_ref, low_ref, in_ref, norm_ref, params_ref, w_ref,
                       up_ref, sum_ref, x_ref, conv_ref):
    def fill(image, carry):
        for r in range(4):
            put_band(x_ref, image, r, low_ref[image, band(r), :])
        return carry

    lax.fori_loop(0, 8, fill, 0)
    conv_core(x_ref, w_ref, conv_ref, True)
    gain, bias = param(params_ref, G_FIRST), param(params_ref, B_FIRST)
    slope_sums(facts_ref, in_ref, norm_ref, gain, bias, conv_ref, up_ref, sum_ref)


def slope_sums(facts_ref, in_ref, norm_ref, gain, bias, conv_ref, up_ref, sum_ref):
    mean, inverse = norm_ref[0:1, :], norm_ref[1:2, :]

    def slope(image, carry):
        grads, crosses = carry
        for r in range(4):
            normed = (in_ref[image, band(r), :] - mean) * inverse
            up = conv_ref[image, band(r), :] * slope_of(normed * gain + bias)
            up_ref[image, band(r), :] = up
            living = facts_ref[image]
            grads = grads + fold(up) * living
            crosses = crosses + fold(up * normed) * living
        return grads, crosses

    zero = jnp.zeros((8, 512), F32)
    grads, crosses = lax.fori_loop(0, 8, slope, (zero, zero))
    sum_ref[0:1, :] = total_row(grads)
    sum_ref[1:2, :] = total_row(crosses)
    sum_ref[2:8, :] = jnp.zeros((6, 512), F32)


def first_back_kernel(facts_ref, up_in, in_ref, norm_ref, own_ref, other_ref, params_ref, w_ref,
                      second_ref, norm2_ref, section_ref, pool_ref, mid_ref, short_ref, normd_ref,
                      low_ref, up_ref, sum_ref, x_ref, conv_ref):
    def keep(image, r, low):
        low_ref[image, band(r), :] = low
        put_band(x_ref, image, r, low)

    back_norm(facts_ref, in_ref, up_in, norm_ref, own_ref, other_ref, param(params_ref, G_FIRST),
              0, keep)
    conv_core(x_ref, w_ref, conv_ref, True)
    mean2, inv2 = norm2_ref[0:1, :], norm2_ref[1:2, :]
    gain2, bias2 = param(params_ref, G_SECOND), param(params_ref, B_SECOND)
    mean_m, inv_m = normd_ref[0:1, :], normd_ref[1:2, :]
    mean_s, inv_s = normd_ref[2:3, :], normd_ref[3:4, :]
    gain_m, gain_s = param(params_ref, G_MID), param(params_ref, G_SHORT)
    bias_m, bias_s = param(params_ref, B_MID), param(params_ref, B_SHORT)

    def join(image, carry):
        grads, cross_m, cross_s = carry
        pool = pool_ref[pl.ds(image, 1), :]
        for r in range(4):
            pre2 = (second_ref[image, band(r), :] - mean2) * inv2 * gain2 + bias2
            pre2 = pre2 + section_ref[image, band(r), :].astype(F32)
            entry = conv_ref[image, band(r), :] + pool * slope_of(pre2)
            entry = entry.astype(BF16).astype(F32)
            norm_m = (mid_ref[image, band(r), :] - mean_m) * inv_m
            norm_s = (short_ref[image, band(r), :] - mean_s) * inv_s
            pre = norm_m * gain_m + bias_m + norm_s * gain_s + bias_s
            up = entry * slope_of(pre)
            up_ref[image, band(r), :] = up
            living = facts_ref[image]
            grads = grads + fold(up) * living
            cross_m = cross_m + fold(up * norm_m) * living
            cross_s = cross_s + fold(up * norm_s) * living
        return grads, cross_m, cross_s

    zero = jnp.zeros((8, 512), F32)
    grads, cross_m, cross_s = lax.fori_loop(0, 8, join, (zero, zero, zero))
    sum_ref[0:1, :] = total_row(grads)
    sum_ref[1:2, :] = total_row(cross_m)
    sum_ref[2:3, :] = total_row(cross_s)
    sum_ref[3:8, :] = jnp.zeros((5, 512), F32)


def mid_back_kernel(facts_ref, up_in, mid_ref, short_ref, normd_ref, own_ref, other_ref, params_ref,
                    w_ref, in_ref, norm1_ref,
                    low_ref, low_s_ref, up_ref, sum_ref, x_ref, conv_ref):
    def keep(image, r, low):
        low_ref[image, band(r), :] = low
        put_band(x_ref, image, r, low)

    def keep_short(image, r, low):
        low_s_ref[image, band(r), :] = low

    gain_m, gain_s = param(params_ref, G_MID), param(params_ref, G_SHORT)
    back_norm(facts_ref, mid_ref, up_in, normd_ref, own_ref, other_ref, gain_m, 0, keep)
    back_norm(facts_ref, short_ref, up_in, normd_ref, own_ref, other_ref, gain_s, 2, keep_short)
    conv_core(x_ref, w_ref, conv_ref, True)
    gain, bias = param(params_ref, G_DOWN), param(params_ref, B_DOWN)
    slope_sums(facts_ref, in_ref, norm1_ref, gain, bias, conv_ref, up_ref, sum_ref)


def down_back_kernel(facts_ref, up_in, in_ref, norm1_ref, own_ref, other_ref, params_ref, low_ref):
    def keep(image, r, low):
        low_ref[image, band(r), :] = low

    gain = param(params_ref, G_DOWN)
    back_norm(facts_ref, in_ref, up_in, norm1_ref, own_ref, other_ref, gain, 0, keep)


def image_back_kernel(where_ref, low_ref, low_s_ref, w_ref, s_ref, keep_ref, send_ref, stage_ref):
    pipe, batch, zone = where_ref[0], where_ref[1], where_ref[2]
    mine = pl.ds(batch * 2, 2)
    here = low_ref[mine]
    below = jnp.concatenate([here[:, 32:], jnp.zeros((2, 32, 512), BF16)], axis=1)
    here, below = here.reshape(256, 512), below.reshape(256, 512)
    short = low_s_ref[mine].reshape(256, 512)

    def back(lhs, row, col):
        return lax.dot_general(lhs, w_ref[row, col], NT, preferred_element_type=F32)

    even_even = back(here, 1, 1) + lax.dot_general(
        short, s_ref[...], NT, preferred_element_type=F32
    )
    even_odd = columns_joined(None, back(here, 1, 2), back(here, 1, 0))
    odd_even = back(here, 2, 1) + back(below, 0, 1)
    odd_odd = columns_joined(
        None, back(here, 2, 2) + back(below, 0, 2), back(here, 2, 0) + back(below, 0, 0)
    )
    planes = ((even_even, even_odd), (odd_even, odd_odd))
    for row in range(2):
        for par in range(2):
            plane = planes[row][par].reshape(2, 4, 32, 256).astype(BF16)
            lanes = slice(par * 128, par * 128 + 128)
            for side in range(2):
                half = plane[..., side * 128 : side * 128 + 128]
                for z in range(4):
                    stage_ref[z ^ zone, side ^ pipe, :, row, :, lanes] = half[:, z]
    keep_ref[0], keep_ref[1] = stage_ref[0], stage_ref[2]
    send_ref[0], send_ref[1] = stage_ref[1], stage_ref[3]


def image_far_kernel(keep_ref, near_ref, out_ref):
    out_ref[0], out_ref[1] = keep_ref[1], near_ref[1]


def image_pipe_kernel(keep_ref, near_ref, far_ref, out_ref):
    out_ref[0], out_ref[1] = keep_ref[0, 1], near_ref[0, 1]
    out_ref[2], out_ref[3] = far_ref[0, 1], far_ref[1, 1]


def image_grad_kernel(where_ref, keep_ref, near_ref, far_ref, got_ref, out_ref):
    pipe, zone = where_ref[0], where_ref[2]
    own = (keep_ref.at[0, 0], near_ref.at[0, 0], far_ref.at[0, 0], far_ref.at[1, 0])
    for rel in range(4):
        for side in range(2):
            piece = own[rel] if side == 0 else got_ref.at[rel]
            first = (zone ^ rel) * 4 + (pipe if side == 0 else 1 - pipe) * 2
            for i in range(2):
                for row in range(2):
                    for par in range(2):
                        out_ref[first + i, row, pl.ds(par, 32, stride=2), :] = piece[
                            i, row, :, par * 128 : (par + 1) * 128
                        ].astype(F32)


def slot_of(quarter, zone):
    rel = quarter ^ zone
    return (rel >> 1) | ((rel & 1) << 1)


def shifted_window(turned, down, right):
    pixel = lax.broadcasted_iota(jnp.int32, (1, 128), 1)
    column, row = pixel % 32 + right, pixel // 32 + down
    inside = (column >= 0) & (column < 32) & (row >= 0) & (row < 4)
    amount = (256 - down * 32 - right) % 128
    moved = turned if isinstance(amount, int) and amount == 0 else pltpu.roll(turned, amount, 1)
    return jnp.where(inside, moved, 0.0).astype(BF16)


def split_out(pipe, zone, unit, result_own, result_other, own_ref, other_ref):
    for quarter in range(4):
        slot = slot_of(quarter, zone)
        rows = slice(quarter * 32, quarter * 32 + 32)
        own_ref[slot, unit] = result_own[rows]
        other_ref[slot, unit] = result_other[rows].astype(BF16)


def hand_out(other_ref, outs):
    each = 4 // len(outs)
    for slot in range(4):
        outs[slot // each][slot % each] = other_ref[slot]


def turned_taps(batch, act_ref, turned_ref):
    lanes = pl.ds(pl.multiple_of(batch * 128, 128), 128)

    def turn(image, carry):
        turned = act_ref[image, :, lanes].astype(F32).T
        pixels = pl.ds(pl.multiple_of(image * 128, 128), 128)
        for row in range(3):
            for col in range(3):
                turned_ref[row * 3 + col, :, pixels] = shifted_window(turned, row - 1, col - 1)
        return carry

    lax.fori_loop(0, 8, turn, 0)


def tap_products(pipe, zone, low_ref, turned_ref, own_ref, other_ref):
    lhs = turned_ref[0:9].reshape(9 * 128, 1024)
    results = []
    for side in (pipe, 1 - pipe):
        columns = pl.ds(pl.multiple_of(side * 256, 256), 256)
        rhs = low_ref[:, :, columns].reshape(1024, 256)
        results.append(jnp.dot(lhs, rhs, preferred_element_type=F32))
    for unit in range(9):
        rows = slice(unit * 128, unit * 128 + 128)
        split_out(pipe, zone, unit, results[0][rows], results[1][rows], own_ref, other_ref)


def kernel_grad_kernel(where_ref, act_ref, low_ref, own_ref, *refs):
    outs, (turned_ref, other_ref) = refs[:-2], refs[-2:]
    pipe, batch, zone = where_ref[0], where_ref[1], where_ref[2]
    turned_taps(batch, act_ref, turned_ref)
    tap_products(pipe, zone, low_ref, turned_ref, own_ref, other_ref)
    hand_out(other_ref, outs)


DOWN_UNITS = (
    ((0, 0, 0, 4), (2, -1, 0, 1), (2, 0, 0, 7), (0, 0, 0, 9), (1, 0, 0, 5)),
    ((1, 0, -1, 3), (3, -1, -1, 0), (3, -1, 0, 2), (3, 0, -1, 6), (3, 0, 0, 8)),
)


def down_grad_kernel(where_ref, img_ref, low_ref, low_s_ref, own_ref, *refs):
    outs, (turned_ref, other_ref) = refs[:-2], refs[-2:]
    pipe, batch, zone = where_ref[0], where_ref[1], where_ref[2]
    upper, part = batch // 2, batch % 2

    for turn_kind in range(2):

        @pl.when(upper == turn_kind)
        def _(units=DOWN_UNITS[turn_kind]):
            def turn(image, carry):
                pixels = pl.ds(pl.multiple_of(image * 128, 128), 128)
                seen = {}
                for unit, (plane, down, right, _) in enumerate(units):
                    if plane not in seen:
                        lanes = pl.ds(pl.multiple_of(plane * 256 + part * 128, 128), 128)
                        seen[plane] = img_ref[image, :, lanes].astype(F32).T
                    turned_ref[unit, :, pixels] = shifted_window(seen[plane], down, right)
                return carry

            lax.fori_loop(0, 8, turn, 0)

    short_unit = [tap for _, _, _, tap in DOWN_UNITS[0]].index(9)
    for unit in range(5):
        lhs = turned_ref[unit]
        results = []
        for side in (pipe, 1 - pipe):
            columns = pl.ds(pl.multiple_of(side * 256, 256), 256)
            rhs = low_ref[:, :, columns].reshape(1024, 256)
            if unit == short_unit:
                rhs_s = low_s_ref[:, :, columns].reshape(1024, 256)
                rhs = jnp.where(upper == 0, rhs_s, rhs)
            results.append(jnp.dot(lhs, rhs, preferred_element_type=F32))
        split_out(pipe, zone, unit, results[0], results[1], own_ref, other_ref)
    hand_out(other_ref, outs)


def add_cores_kernel(own_ref, *refs):
    got, (keep_ref, send_ref) = refs[:-2], refs[-2:]
    each = 4 // len(got)
    for slot in range(4):
        value = own_ref[slot] + got[slot // each][slot % each].astype(F32)
        if slot < 2:
            keep_ref[slot] = value
        else:
            send_ref[slot - 2] = value.astype(BF16)


def add_near_kernel(own_ref, got_ref, keep_ref, send_ref):
    keep_ref[...] = own_ref[0] + got_ref[0].astype(F32)
    send_ref[...] = (own_ref[1] + got_ref[1].astype(F32)).astype(BF16)


def add_far_kernel(own_ref, got_ref, out_ref):
    out_ref[...] = (own_ref[...] + got_ref[...].astype(F32)).astype(BF16)


def join_kernel_of(*refs):
    at = 0
    for ref in refs[:-1]:
        if len(ref.shape) == 3:
            refs[-1][at] = ref[...]
            at += 1
        else:
            refs[-1][at : at + ref.shape[0]] = ref[...]
            at += ref.shape[0]


def gathered_blocks(zone, batch, refs):
    if len(refs) == 8:
        for kb in range(4):
            for rel in range(4):
                yield batch ^ kb, zone ^ rel, refs[2 * kb + rel % 2], rel // 2
        return
    a, b, ax, by, ayy, bxx = refs
    sets = {0: (a, b, 0, 0), 1: (ax, bxx, 0, 0), 2: (ayy, by, 0, 0), 3: (ayy, bxx, 2, 2)}
    for kb in range(4):
        even, odd, base_even, base_odd = sets[kb]
        for rel in range(4):
            if rel % 2 == 1:
                yield batch ^ kb, zone ^ rel, odd, base_odd + rel // 2
            else:
                yield batch ^ kb, zone ^ rel, even, base_even + rel // 2


def assemble_kernel(where_ref, *refs):
    pieces, (out_ref, token_ref, stage_ref, sems) = refs[:-4], refs[-4:]
    token_ref[...] = jnp.zeros(token_ref.shape, F32)
    batch, zone = where_ref[1], where_ref[2]
    blocks = list(gathered_blocks(zone, batch, pieces))
    copies = []
    for tap in range(9):
        for owner, quarter, ref, index in blocks:
            rows = pl.ds(pl.multiple_of(owner * 128 + quarter * 32, 32), 32)
            stage_ref[tap, rows, :] = ref[index, tap].astype(F32)
        copies.append(pltpu.make_async_copy(stage_ref.at[tap], out_ref.at[tap], sems.at[tap]))
        copies[-1].start()
    for copy in copies:
        copy.wait()


def assemble_down_kernel(where_ref, *refs):
    pieces, (out_hbm, short_hbm, out_ref, short_ref, sems) = refs[:-5], refs[-5:]
    batch, zone = where_ref[1], where_ref[2]
    for owner, quarter, ref, index in gathered_blocks(zone, batch, pieces):
        upper, part = owner // 2, owner % 2
        rows = pl.ds(pl.multiple_of(part * 128 + quarter * 32, 32), 32)
        value = ref[index].astype(F32)
        for kind in range(2):

            @pl.when(upper == kind)
            def _(value=value, rows=rows, units=DOWN_UNITS[kind]):
                for unit, (_, _, _, tap) in enumerate(units):
                    if tap == 9:
                        short_ref[rows, :] = value[unit]
                    else:
                        out_ref[tap, rows, :] = value[unit]

    copies = [
        pltpu.make_async_copy(out_ref, out_hbm, sems.at[0]),
        pltpu.make_async_copy(short_ref, short_hbm, sems.at[1]),
    ]
    for copy in copies:
        copy.start()
    for copy in copies:
        copy.wait()


def facts_kernel(where_ref, p0, p1, p2, p3, hw_ref, facts_ref, living_ref, targets_ref, heads_ref):
    pipe, batch = where_ref[0], where_ref[1]
    tasks = hw_ref.shape[0]
    alive = [jnp.float32(0.0), jnp.float32(0.0)]
    for rel, piece in enumerate((p0, p1, p2, p3)):
        owner = batch ^ rel
        marks = piece[MARKS:, 0:tasks].astype(F32)
        count = jnp.max(marks[4:5, :])
        for slot in range(4):
            side, place = slot // 2, owner * 2 + slot % 2
            living = (count > slot + 0.5).astype(F32)
            alive[side] = alive[side] + living
            row = pl.ds(side * 8 + place, 1)
            living_ref[row, :] = jnp.full((1, tasks), living)
            targets_ref[row, :] = marks[slot : slot + 1, :]

            @pl.when(pipe == side)
            def _(place=place, living=living):
                facts_ref[place] = living

    own = jnp.where(pipe == 0, alive[0], alive[1])
    facts_ref[OWN_PX] = own * 128.0
    facts_ref[OTHER_PX] = (alive[0] + alive[1] - own) * 128.0
    facts_ref[ALL_PX] = (alive[0] + alive[1]) * 128.0
    for rest in range(ALL_PX + 1, 16):
        facts_ref[rest] = jnp.float32(0.0)
    heads_ref[...] = lax.dot_general(
        hw_ref[...], hw_ref[...], NT, precision=HIGHEST, preferred_element_type=F32
    )


SMALL_ROWS = 72


def small_kernel(where_ref, head_ref, all_ref, sum_f, other_f, sum_j, other_j, sum_d, other_d,
                 sent_ref, wide_ref):
    pipe, batch = where_ref[0], where_ref[1]
    tasks = head_ref.shape[0] - 8
    wide_ref[...] = jnp.zeros(wide_ref.shape, F32)
    wide_ref[0 : tasks + 3, :] = head_ref[0 : tasks + 3, :]
    at = tasks + 3
    for own, other, count in ((sum_f, other_f, 2), (sum_j, other_j, 3), (sum_d, other_d, 2)):
        wide_ref[at : at + count, :] = own[0:count, :] + other[0:count, :]
        at += count
    for side in range(2):
        for slot in range(2):
            row = side * 8 + batch * 2 + slot
            at_row = SMALL_ROWS - 16 + where_ref[2] * 4 + side * 2 + slot
            wide_ref[pl.ds(at_row, 1), :] = all_ref[0, pl.ds(row, 1), :]
    sent_ref[...] = wide_ref[:, pl.ds(pl.multiple_of(pipe * 256, 256), 256)]


def add_kernel(a_ref, b_ref, out_ref):
    out_ref[...] = a_ref[...] + b_ref[...]


def small_out_kernel(where_ref, near_ref, far_ref, pooled_ref, head_ref, gd_ref, bd_ref, gp_ref,
                     bp_ref, headb_ref):
    tasks = head_ref.shape[0]
    pipe = where_ref[0]
    total = near_ref[...] + far_ref[...]
    pooled_ref[...] = total[SMALL_ROWS - 16 :]
    head_ref[...] = total[0:tasks]

    def line(at):
        return total[tasks + at : tasks + at + 1]

    share = tasks // 2
    headb_ref[...] = jnp.where(pipe == 0, line(2)[:, 0:share], line(2)[:, share:tasks])
    bp_ref[0:1, :], gp_ref[0:1, :] = line(3), line(4)
    bp_ref[1:2, :], gp_ref[1:2, :] = line(0), line(1)
    bd_ref[0:1, :], gd_ref[0:1, :] = line(8), line(9)
    bd_ref[1:2, :], gd_ref[1:2, :] = line(5), line(6)
    bd_ref[2:3, :], gd_ref[2:3, :] = line(5), line(7)


def fast_device(images, image_counts, labels, fw_picks, conv_down, conv_mid, shortcut, gains_down,
                biases_down, conv_first, conv_second, gains_plain, biases_plain, head_weight,
                head_bias):
    pipe, batch, zone = (lax.axis_index(axis) for axis in ("pipe", "batch", "space"))
    tasks = head_weight.shape[1]

    def over(axis, rel, x):
        size = lax.axis_size(axis)
        return lax.ppermute(x, axis, [(i, i ^ rel) for i in range(size)])

    where = jnp.stack([pipe, batch, zone, zone]).astype(jnp.int32)
    params = jnp.concatenate([gains_down, biases_down, gains_plain, biases_plain])
    turned_heads = head_weight.T
    bias_row = head_bias.reshape(1, tasks)

    pieces = call(
        pieces_kernel,
        [((144, 512), BF16)] + [((128, 512), BF16)] * 3,
        [where, images, labels, image_counts],
        [pltpu.VMEM((64, 128), F32), pltpu.VMEM((4, 2, 2, 64, 256), BF16),
         pltpu.SemaphoreType.DMA((4,))],
        name="pieces",
        specs={1: HBM, 3: SM},
    )
    moved = [over("space", rel, pieces[rel]) for rel in (1, 2, 3)]
    moved = [pieces[0], moved[0], jnp.concatenate([moved[1], moved[2]])]
    gathered = [moved] + [[over("batch", kb, x) for x in moved] for kb in (1, 2, 3)]
    facts, living, targets, heads = call(
        facts_kernel,
        [((16,), F32), ((16, tasks), F32), ((16, tasks), F32), ((tasks, tasks), F32)],
        [where] + [line[0] for line in gathered] + [turned_heads],
        name="facts",
    )

    big = ((8, 128, 512), F32)
    low = ((8, 128, 512), BF16)
    rows = ((8, 512), F32)
    x_scratch = pltpu.VMEM((8, 128, 1536), BF16)
    conv_scratch = pltpu.VMEM((8, 128, 512), F32)
    conv_flops = 2 * 1024 * 4608 * 512

    def partner(x):
        return over("pipe", 1, x)

    img, down_out, short_out, stat_d = call(
        down_kernel,
        [((8, 128, 1024), BF16), big, big, rows],
        [facts, where] + [piece for line in gathered for piece in line] + [conv_down, shortcut],
        [pltpu.VMEM((8, 128, 512), BF16)],
        conv_flops // 2,
        "down",
    )
    other_d = partner(stat_d)
    down_act, mid_out, stat_m, norm_d = call(
        lambda *refs: layer_kernel(G_DOWN, B_DOWN, *refs),
        [low, big, rows, rows],
        [facts, down_out, stat_d, other_d, params, conv_mid],
        [x_scratch],
        conv_flops,
        "mid",
    )
    other_m = partner(stat_m)
    section, first_out, stat_f, norm_j = call(
        join_kernel,
        [low, big, rows, rows],
        [facts, mid_out, short_out, stat_m, other_m, stat_d, other_d, params, conv_first],
        [x_scratch],
        conv_flops,
        "first",
    )
    other_f = partner(stat_f)
    plain_act, second_out, stat_s, norm_f = call(
        lambda *refs: layer_kernel(G_FIRST, B_FIRST, *refs),
        [low, big, rows, rows],
        [facts, first_out, stat_f, other_f, params, conv_second],
        [x_scratch],
        conv_flops,
        "second",
    )
    other_s = partner(stat_s)
    pack, norm_s = call(
        block_kernel,
        [((24, 512), F32), rows],
        [facts, second_out, section, stat_s, other_s, params],
        name="block",
    )
    other_pack = partner(pack)
    all_pack, errors, cross = call(
        logits_kernel,
        [((3, 16, 512), F32), ((16, tasks), F32), ((tasks, tasks), F32)],
        [where, pack, other_pack, living, targets, turned_heads, bias_row],
        name="logits",
    )
    crosses = [cross] + [over("space", rel, cross) for rel in (1, 2, 3)]
    second_low, grad_pool, small = call(
        head_kernel,
        [low, rows, ((tasks + 8, 512), F32)],
        [fw_picks, where, facts] + crosses
        + [heads, turned_heads, errors, all_pack, second_out, section, norm_s, params],
        [pltpu.VMEM((1, tasks), F32), pltpu.VMEM((tasks, tasks), F32)],
        name="head",
    )

    class Sum:
        def __init__(self, kernel, units, operands, scratch, flops, name, after=(), parts=4):
            self.units, self.name = units, name
            self.own, *self.other = call(
                kernel,
                [self.block(4, dtype=F32)] + [self.block(4 // parts)] * parts,
                operands,
                [scratch, pltpu.VMEM((4, units, 32, 256), BF16)],
                flops,
                name,
                after,
            )
            self.got = [partner(x) for x in self.other]

        def block(self, *lead, dtype=BF16):
            return (lead + (self.units, 32, 256), dtype)

        def cores(self, after=()):
            self.keep, sent = call(
                add_cores_kernel,
                [self.block(2, dtype=F32), self.block(2)],
                [self.own] + self.got,
                name=self.name + "_cores",
                after=after,
            )
            self.near = over("space", 1, sent)

        def zone_near(self, after=()):
            self.keep, sent = call(
                add_near_kernel,
                [self.block(dtype=F32), self.block()],
                [self.keep, self.near],
                name=self.name + "_near",
                after=after,
            )
            self.far = over("space", 2, sent)

        def zone_far(self, after=()):
            (self.final,) = call(
                add_far_kernel,
                [self.block()],
                [self.keep, self.far],
                name=self.name + "_final",
                after=after,
            )
            self.other_far = over("space", 2, self.final)

        def pair(self, after=()):
            (self.a,) = call(
                join_kernel_of,
                [self.block(2)],
                [self.final, self.other_far],
                name=self.name + "_pair",
                after=after,
            )
            self.b = over("space", 1, self.a)

        def direct(self):
            self.ra = [over("batch", rel, self.a) for rel in (1, 2, 3)]
            self.rb = [over("batch", rel, self.b) for rel in (1, 2, 3)]
            self.blocks = [where, self.a, self.b]
            for x, y in zip(self.ra, self.rb):
                self.blocks += [x, y]

        def plane(self):
            self.ax, self.by = over("batch", 1, self.a), over("batch", 2, self.b)

        def plane_far(self, after=()):
            self.fa, self.fb = [
                call(join_kernel_of, [self.block(4)], pair, name=self.name + "_cross", after=after)[0]
                for pair in ([self.a, self.ax], [self.b, self.by])
            ]
            self.ayy, self.bxx = over("batch", 2, self.fa), over("batch", 1, self.fb)
            self.blocks = [where, self.a, self.b, self.ax, self.by, self.ayy, self.bxx]

    def kernel_grad_of(act, low_grad, name, after=(), parts=PARTS):
        return Sum(
            kernel_grad_kernel, 9, [where, act, low_grad], pltpu.VMEM((9, 128, 1024), BF16),
            conv_flops // 4, name, after, parts,
        )

    def assembled(blocks, name, after=()):
        out, token = call(
            assemble_kernel,
            [((9, 512, 256), F32), ((8, 128), F32)],
            blocks,
            [pltpu.VMEM((9, 512, 256), F32), pltpu.SemaphoreType.DMA((9,))],
            name=name,
            after=after,
            out_space=[HBM, VM],
        )
        return out.reshape(3, 3, 512, 256), token

    second = kernel_grad_of(plain_act, second_low, "second_grad")
    second.cores()
    up_f, sum_f = call(
        second_back_kernel,
        [big, rows],
        [facts, second_low, first_out, norm_f, params, conv_second],
        [x_scratch, conv_scratch],
        conv_flops,
        "second_back",
        after=[second.keep],
    )
    other_sf = partner(sum_f)
    second.zone_near(after=[sum_f])
    first_low, up_j, sum_j = call(
        first_back_kernel,
        [low, big, rows],
        [facts, up_f, first_out, norm_f, sum_f, other_sf, params, conv_first,
         second_out, norm_s, section, grad_pool, mid_out, short_out, norm_j],
        [x_scratch, conv_scratch],
        conv_flops,
        "first_back",
        after=[second.keep],
    )
    other_sj = partner(sum_j)
    second.zone_far(after=[sum_j])
    first = kernel_grad_of(section, first_low, "first_grad", after=[second.final])
    second.pair(after=first.other[0:1])
    second.plane()
    first.cores(after=[second.a])
    mid_low, short_low, up_d, sum_d = call(
        mid_back_kernel,
        [low, low, big, rows],
        [facts, up_j, mid_out, short_out, norm_j, sum_j, other_sj, params, conv_mid,
         down_out, norm_d],
        [x_scratch, conv_scratch],
        conv_flops,
        "mid_back",
        after=[first.keep],
    )
    other_sd = partner(sum_d)
    first.zone_near(after=[sum_d, second.b, second.ax])
    mid = kernel_grad_of(down_act, mid_low, "mid_grad", after=[first.keep])
    first.zone_far(after=mid.other[0:1])
    mid.cores(after=[first.final])
    second.plane_far(after=[mid.keep])
    (down_low,) = call(
        down_back_kernel,
        [low],
        [facts, up_d, down_out, norm_d, sum_d, other_sd, params],
        name="down_back",
        after=[second.fa, second.fb],
    )
    down = Sum(
        down_grad_kernel, 5, [where, img, down_low, short_low], pltpu.VMEM((5, 128, 1024), BF16),
        conv_flops // 8, "down_grad", parts=LAST_PARTS,
    )
    first.pair(after=down.other[0:1])
    first.plane()
    mid.zone_near(after=[first.a])
    down.cores(after=[mid.keep])
    img_pieces = call(
        image_back_kernel,
        [((2, 2, 2, 2, 32, 256), BF16)] * 2,
        [where, down_low, short_low, conv_down, shortcut],
        [pltpu.VMEM((4, 2, 2, 2, 32, 256), BF16)],
        conv_flops // 8,
        "image_back",
        after=[down.keep],
    )
    mid.zone_far(after=[img_pieces[0]])
    down.zone_near(after=[mid.final])
    second_out_grad, second_done = assembled(second.blocks, "second_out", after=[down.keep, first.b])
    first.plane_far(after=[second_done])
    mid.pair(after=[first.fa, first.fb])
    mid.plane()
    down.zone_far(after=[mid.a])
    down.pair()
    down.plane()
    first_out_grad, first_done = assembled(first.blocks, "first_out", after=[down.a])
    mid.plane_far(after=[first_done])
    down.plane_far(after=[mid.fa, mid.fb])
    mid_out_grad, mid_done = assembled(mid.blocks, "mid_out", after=[down.fa])

    img_near = over("space", 1, img_pieces[1])
    pair = ((2, 2, 2, 2, 32, 256), BF16)
    (img_sent,) = call(image_far_kernel, [pair], [img_pieces[0], img_near], name="image_far")
    img_far = over("space", 2, img_sent)
    img_parts = [img_pieces[0], img_near, img_far]
    (img_other,) = call(
        image_pipe_kernel, [((4, 2, 2, 32, 256), BF16)], img_parts, name="image_pipe"
    )
    (images_grad,) = call(
        image_grad_kernel,
        [((16, 2, 64, 128), F32)],
        [where] + img_parts + [partner(img_other)],
        name="image_grad",
    )

    (sent,) = call(
        small_kernel,
        [((SMALL_ROWS, 256), F32)],
        [where, small, all_pack, sum_f, other_sf, sum_j, other_sj, sum_d, other_sd],
        [pltpu.VMEM((SMALL_ROWS, 512), F32)],
        name="small",
        after=[down.final],
    )
    (near_sum,) = call(
        add_kernel,
        [((SMALL_ROWS, 256), F32)],
        [sent, over("space", 1, sent)],
        name="small_near",
    )
    pooled, head_out, gains_d, sums_d, gains_p, sums_p, head_b = call(
        small_out_kernel,
        [((16, 256), F32), ((tasks, 256), F32), ((3, 256), F32), ((3, 256), F32),
         ((2, 256), F32), ((2, 256), F32), ((1, tasks // 2), F32)],
        [where, near_sum, over("space", 2, near_sum)],
        name="small_out",
    )
    down_grad, short_grad = call(
        assemble_down_kernel,
        [((9, 256, 256), F32), ((256, 256), F32)],
        down.blocks,
        [pltpu.VMEM((9, 256, 256), F32), pltpu.VMEM((256, 256), F32),
         pltpu.SemaphoreType.DMA((2,))],
        out_space=[HBM, HBM],
        name="down_out",
    )
    return (
        pooled,
        images_grad,
        down_grad.reshape(3, 3, 256, 256),
        mid_out_grad,
        short_grad,
        gains_d,
        sums_d,
        first_out_grad,
        second_out_grad,
        gains_p,
        sums_p,
        head_out.T,
        head_b.reshape(tasks // 2),
    )


def per_device(
    images,
    image_counts,
    labels,
    fw_picks,
    conv_down,
    conv_mid,
    shortcut,
    gains_down,
    biases_down,
    conv_first,
    conv_second,
    gains_plain,
    biases_plain,
    head_weight,
    head_bias,
):
    layout = Layout(image_counts.shape[1])
    micros, zone = layout.micros, layout.zone
    sizes = (images.shape, conv_down.shape, lax.axis_size("pipe"), lax.axis_size("batch"))
    if layout.groups == 1 and sizes == ((16, 2, 64, 256), (3, 3, 256, 512), 2, 4):
        return fast_device(
            images, image_counts, labels, fw_picks, conv_down, conv_mid, shortcut, gains_down,
            biases_down, conv_first, conv_second, gains_plain, biases_plain, head_weight,
            head_bias,
        )
    batches, pipes = lax.axis_size("batch"), lax.axis_size("pipe")
    batch = lax.axis_index("batch")
    pipe = lax.axis_index("pipe")
    per_micro = images.shape[0] // micros
    count = per_micro * batches
    entering, channels = conv_down.shape[2], conv_mid.shape[3]
    tasks = head_weight.shape[1]
    half = channels // pipes
    own = pipe * half

    def own_out(kernel, axis):
        size = kernel.shape[axis] // pipes
        return lax.dynamic_slice_in_dim(kernel, pipe * size, size, axis)

    def whole(tensor, axis=3):
        return lax.all_gather(tensor, "pipe", axis=axis, tiled=True)

    def share(tensor):
        size = tensor.shape[3] // batches
        return lax.dynamic_slice_in_dim(tensor, batch * size, size, 3)

    mine = lax.all_to_all(
        images, "space", 0, 1, axis_index_groups=layout.inner, tiled=True
    )
    mine = lax.all_gather(mine, "batch", axis=0, tiled=True)
    counts = lax.all_gather(image_counts, "batch", axis=0, tiled=True)
    counts = lax.dynamic_slice_in_dim(counts, zone, 1, 1)[:, 0]
    marks = lax.dynamic_slice_in_dim(labels, zone * per_micro, per_micro, 0)
    targets = lax.all_gather(marks, "batch", axis=0, tiled=True).astype(F32)
    slots = jnp.arange(per_micro, dtype=jnp.int32)
    living = (slots[None, :] < counts[:, None]).astype(F32).reshape(count)
    weight = living[:, None, None, None]
    out_rows, out_cols = mine.shape[1] // 2, mine.shape[2] // 2
    image_pixels = out_rows * layout.groups * out_cols
    counted = jnp.sum(living) * image_pixels
    scale = float(image_pixels * tasks)

    gain_d, bias_d = own_out(gains_down, 1), own_out(biases_down, 1)
    gain_p, bias_p = own_out(gains_plain, 1), own_out(biases_plain, 1)

    above = layout.row_from(mine[:, -1:], 1)
    down_ext = jnp.pad(
        jnp.concatenate([above, mine], axis=1), ((0, 0), (0, 0), (1, 0), (0, 0))
    )
    down_out = conv_valid(down_ext, own_out(conv_down, 3), 2)
    down_norm, down_inv = norm_forward(layout, down_out, weight, counted)
    down_pre = down_norm * gain_d[0] + bias_d[0]
    mid_ext = layout.rims(whole(jax.nn.silu(down_pre).astype(BF16)))
    mid_out = conv_valid(mid_ext, own_out(conv_mid, 3), 1)
    short_in = mine[:, ::2, ::2]
    short_out = jnp.einsum(
        "nhwi,io->nhwo", short_in, own_out(shortcut, 1), preferred_element_type=F32
    )
    mid_norm, mid_inv = norm_forward(layout, mid_out, weight, counted)
    short_norm, short_inv = norm_forward(layout, short_out, weight, counted)
    section_pre = mid_norm * gain_d[1] + bias_d[1] + short_norm * gain_d[2] + bias_d[2]
    section = jax.nn.silu(section_pre).astype(BF16)
    first_ext = layout.rims(whole(section))
    first_out = conv_valid(first_ext, own_out(conv_first, 3), 1)
    first_norm, first_inv = norm_forward(layout, first_out, weight, counted)
    first_pre = first_norm * gain_p[0] + bias_p[0]
    second_ext = layout.rims(whole(jax.nn.silu(first_pre).astype(BF16)))
    second_out = conv_valid(second_ext, own_out(conv_second, 3), 1)
    second_norm, second_inv = norm_forward(layout, second_out, weight, counted)
    block_pre = second_norm * gain_p[1] + bias_p[1] + section.astype(F32)
    pooled = layout.group_sum(jnp.sum(jax.nn.silu(block_pre), axis=(1, 2))) / image_pixels

    pooled_all = whole(pooled, 1)
    logits = jnp.dot(pooled_all, head_weight, precision=HIGHEST) + head_bias
    errors = living[:, None] * (jax.nn.sigmoid(logits) - targets)
    cross = jnp.einsum("nt,ns->ts", errors, errors, precision=HIGHEST)
    cross = lax.psum(cross, "space", axis_index_groups=layout.inner)
    gram = cross * jnp.dot(head_weight.T, head_weight, precision=HIGHEST)
    alpha = frank_wolfe(gram, fw_picks)
    grad_logits = scale * alpha * errors
    head_w = jnp.einsum("nc,nt->ct", pooled, grad_logits, precision=HIGHEST)
    head_b = jnp.sum(grad_logits, axis=0)
    head_own = own_out(head_weight, 0)
    grad_pool = jnp.einsum("nt,ct->nc", grad_logits, head_own, precision=HIGHEST) / image_pixels

    grad_block = grad_pool[:, None, None, :] * silu_slope(block_pre)
    second_low, second_cross, second_sum = norm_back(
        layout, grad_block, second_norm, second_inv, gain_p[1], weight, counted
    )
    second_kernel = kernel_grad(share(second_ext), second_low, 1)
    act_grad = conv_valid(layout.rims(whole(second_low)), flipped(own_out(conv_second, 2)), 1)
    first_low, first_cross, first_sum = norm_back(
        layout, act_grad * silu_slope(first_pre), first_norm, first_inv, gain_p[0], weight, counted
    )
    first_kernel = kernel_grad(share(first_ext), first_low, 1)
    entry_grad = conv_valid(layout.rims(whole(first_low)), flipped(own_out(conv_first, 2)), 1)
    entry_grad = (entry_grad + grad_block).astype(BF16).astype(F32)
    grad_section = entry_grad * silu_slope(section_pre)
    mid_low, mid_cross, mid_sum = norm_back(
        layout, grad_section, mid_norm, mid_inv, gain_d[1], weight, counted
    )
    short_low, short_cross, short_sum = norm_back(
        layout, grad_section, short_norm, short_inv, gain_d[2], weight, counted
    )
    mid_kernel = kernel_grad(share(mid_ext), mid_low, 1)
    short_kernel = jnp.einsum(
        "nhwi,nhwo->io", share(short_in), short_low, preferred_element_type=F32
    )
    act_grad = conv_valid(layout.rims(whole(mid_low)), flipped(own_out(conv_mid, 2)), 1)
    down_low, down_cross, down_sum = norm_back(
        layout, act_grad * silu_slope(down_pre), down_norm, down_inv, gain_d[0], weight, counted
    )
    down_kernel = kernel_grad(share(down_ext), down_low, 2)

    kept = lax.dynamic_slice_in_dim(whole(down_low), batch * per_micro, per_micro, 0)
    below = layout.row_from(kept[:, :1], -1)
    spread = lax.conv_general_dilated(
        jnp.concatenate([kept, below], axis=1),
        flipped(own_out(conv_down, 2)),
        (1, 1),
        ((2, 2), (2, 2)),
        lhs_dilation=(2, 2),
        dimension_numbers=NUMBERS,
        preferred_element_type=F32,
    )[:, 1 : 2 * out_rows + 1, 1:]
    short_kept = lax.dynamic_slice_in_dim(whole(short_low), batch * per_micro, per_micro, 0)
    spread = spread.at[:, ::2, ::2].add(
        jnp.einsum(
            "nhwo,io->nhwi", short_kept, own_out(shortcut, 0), preferred_element_type=F32
        )
    )
    images_grad = lax.all_to_all(
        spread.astype(BF16), "space", 1, 0, axis_index_groups=layout.inner, tiled=True
    ).astype(F32)

    def total(kernel, axis):
        summed = lax.psum(kernel.astype(BF16), "space")
        return lax.all_gather(summed, "batch", axis=axis, tiled=True).astype(F32)

    pooled_out = lax.dynamic_slice_in_dim(pooled, batch * per_micro, per_micro, 0)
    pooled_out = lax.all_gather(
        pooled_out, "space", axis_index_groups=layout.inner, axis=0, tiled=True
    )
    head_w, head_b = lax.psum((head_w, head_b), "space", axis_index_groups=layout.inner)
    gains_d, sums_d, gains_p, sums_p = lax.psum(
        (
            jnp.stack([down_cross, mid_cross, short_cross]),
            jnp.stack([down_sum, mid_sum, short_sum]),
            jnp.stack([first_cross, second_cross]),
            jnp.stack([first_sum, second_sum]),
        ),
        "space",
    )
    return (
        pooled_out,
        images_grad,
        total(down_kernel, 1).reshape(3, 3, entering, half),
        total(mid_kernel, 1).reshape(3, 3, channels, half),
        total(short_kernel, 0),
        gains_d,
        sums_d,
        total(first_kernel, 1).reshape(3, 3, channels, half),
        total(second_kernel, 1).reshape(3, 3, channels, half),
        gains_p,
        sums_p,
        head_w,
        own_out(head_b, 0),
    )


def solution(mesh):
    placed = (
        P("batch", "space", None, None),
        P("batch", None),
        P("batch", None),
    ) + (P(),) * 12
    return jax.shard_map(
        per_device,
        mesh=mesh,
        in_specs=placed,
        out_specs=(
            P("batch", "pipe"),
            P("batch", "space", None, "pipe"),
            P(None, None, None, "pipe"),
            P(None, None, None, "pipe"),
            P(None, "pipe"),
            P(None, "pipe"),
            P(None, "pipe"),
            P(None, None, None, "pipe"),
            P(None, None, None, "pipe"),
            P(None, "pipe"),
            P(None, "pipe"),
            P("pipe", None),
            P("pipe"),
        ),
        check_vma=False,
    )
```

```python
import jax
import jax.numpy as jnp
from jax import lax
from jax.experimental import pallas as pl
from jax.experimental.pallas import tpu as pltpu
from jax.sharding import PartitionSpec as P

EPSILON = 1e-05
NUMBERS = ("NHWC", "HWIO", "NHWC")
HIGHEST = lax.Precision.HIGHEST
F32 = jnp.float32
BF16 = jnp.bfloat16


def silu_slope(values):
    sigmoid = jax.nn.sigmoid(values)
    return sigmoid * (1.0 + values * (1.0 - sigmoid))


def frank_wolfe_kernel(picks_ref, gram_ref, alpha_ref):
    tasks = gram_ref.shape[0]
    lanes = lax.broadcasted_iota(jnp.int32, (1, tasks), 1)
    gram = gram_ref[...]
    alpha = jnp.full((1, tasks), 1.0 / tasks, F32)
    pulled = jnp.sum(gram, axis=0, keepdims=True) * (1.0 / tasks)
    energy = jnp.sum(pulled * alpha, axis=1, keepdims=True)

    def advance(step, carry):
        alpha, pulled, energy = carry
        chosen = picks_ref[step]
        row = gram_ref[pl.ds(chosen, 1), :]
        onehot = (lanes == chosen).astype(F32)
        toward = jnp.sum(pulled * onehot, axis=1, keepdims=True)
        corner = jnp.sum(row * onehot, axis=1, keepdims=True)
        denom = jnp.maximum(energy - 2.0 * toward + corner, 0.05 * corner)
        ratio = jnp.clip((energy - toward) / denom, 0.0, 1.0)
        rest = 1.0 - ratio
        alpha = rest * alpha + ratio * onehot
        pulled = rest * pulled + ratio * row
        energy = rest * rest * energy + 2.0 * rest * ratio * toward + ratio * ratio * corner
        return alpha, pulled, energy

    alpha, _, _ = lax.fori_loop(
        0, picks_ref.shape[0], advance, (alpha, pulled, energy), unroll=True
    )
    alpha_ref[...] = alpha


def frank_wolfe(gram, picks):
    tasks = gram.shape[0]
    return pl.pallas_call(
        frank_wolfe_kernel,
        out_shape=jax.ShapeDtypeStruct((1, tasks), F32),
        in_specs=[
            pl.BlockSpec(memory_space=pltpu.SMEM),
            pl.BlockSpec(memory_space=pltpu.VMEM),
        ],
        out_specs=pl.BlockSpec(memory_space=pltpu.VMEM),
    )(picks, gram)


class Layout:
    def __init__(self, micros):
        self.micros = micros
        self.spaces = lax.axis_size("space")
        self.groups = self.spaces // micros
        self.inner = [
            [group * micros + zone for zone in range(micros)] for group in range(self.groups)
        ]
        self.outer = [
            [group * micros + zone for group in range(self.groups)] for zone in range(micros)
        ]
        self.zone = lax.axis_index("space") % micros

    def group_sum(self, tree):
        if self.groups == 1:
            return tree
        return lax.psum(tree, "space", axis_index_groups=self.outer)

    def row_from(self, block, step):
        span = step * self.micros
        route = [
            (i, i + span) for i in range(self.spaces) if 0 <= i + span < self.spaces
        ]
        if not route:
            return jnp.zeros_like(block)
        return lax.ppermute(block, "space", route)

    def rims(self, tensor):
        above = self.row_from(tensor[:, -1:], 1)
        below = self.row_from(tensor[:, :1], -1)
        grown = jnp.concatenate([above, tensor, below], axis=1)
        return jnp.pad(grown, ((0, 0), (0, 0), (1, 1), (0, 0)))


def conv_valid(extended, kernel, stride):
    return lax.conv_general_dilated(
        extended,
        kernel,
        (stride, stride),
        "VALID",
        dimension_numbers=NUMBERS,
        preferred_element_type=F32,
    )


def flipped(kernel):
    return jnp.swapaxes(kernel[::-1, ::-1], 2, 3)


def kernel_grad(extended, grad_low, stride):
    rows, cols = grad_low.shape[1], grad_low.shape[2]
    taps = []
    for row_tap in range(3):
        for col_tap in range(3):
            window = extended[
                :,
                row_tap : row_tap + stride * (rows - 1) + 1 : stride,
                col_tap : col_tap + stride * (cols - 1) + 1 : stride,
            ]
            taps.append(jnp.einsum("nhwi,nhwo->io", window, grad_low, preferred_element_type=F32))
    return jnp.stack(taps)


def norm_forward(layout, conv_out, weight, counted):
    total = layout.group_sum(jnp.sum(conv_out * weight, axis=(0, 1, 2)))
    centered = conv_out - total / counted
    spread = layout.group_sum(jnp.sum(centered * centered * weight, axis=(0, 1, 2)))
    inverse = lax.rsqrt(spread / counted + EPSILON)
    return centered * inverse, inverse


def norm_back(layout, upstream, normed, inverse, gain, weight, counted):
    grad_sum = jnp.sum(upstream * weight, axis=(0, 1, 2))
    cross_sum = jnp.sum(upstream * normed * weight, axis=(0, 1, 2))
    grad_total, cross_total = layout.group_sum((grad_sum, cross_sum))
    correction = weight * (grad_total / counted + normed * (cross_total / counted))
    low = (gain * inverse * (upstream - correction)).astype(BF16)
    return low, cross_sum, grad_sum


KERNEL_LIMIT = 16 * 2**20
PARTS, LAST_PARTS = 4, 1
VM = pl.BlockSpec(memory_space=pltpu.VMEM)
SM = pl.BlockSpec(memory_space=pltpu.SMEM)
HBM = pl.BlockSpec(memory_space=pltpu.HBM)
NT = (((1,), (1,)), ((), ()))
TN = (((0,), (0,)), ((), ()))
OWN_PX, OTHER_PX, ALL_PX = 8, 9, 10
G_DOWN, G_MID, G_SHORT, B_DOWN, B_MID, B_SHORT, G_FIRST, G_SECOND, B_FIRST, B_SECOND = range(10)


def param(params_ref, row):
    return params_ref[row : row + 1, :]


def call(kernel, outs, operands, scratch=(), flops=0, name=None, after=(), specs=None,
         out_space=None):
    count = len(operands)
    nbytes = sum(x.size * x.dtype.itemsize for x in operands)
    specs = specs or {}

    def body(*refs):
        kernel(*refs[:count], *refs[count + len(after) :])

    return pl.pallas_call(
        body,
        out_shape=tuple(jax.ShapeDtypeStruct(shape, dtype) for shape, dtype in outs),
        in_specs=[specs.get(i, SM if x.ndim == 1 else VM) for i, x in enumerate(operands)]
        + [pl.BlockSpec(memory_space=pl.ANY)] * len(after),
        out_specs=tuple(out_space or [SM if len(shape) == 1 else VM for shape, _ in outs]),
        scratch_shapes=list(scratch),
        compiler_params=pltpu.CompilerParams(vmem_limit_bytes=KERNEL_LIMIT),
        cost_estimate=pl.CostEstimate(
            flops=int(flops), bytes_accessed=int(nbytes), transcendentals=0
        ),
        name=name,
    )(*operands, *after)


def fold(rows):
    return rows[0:8] + rows[8:16] + rows[16:24] + rows[24:32]


def total_row(part):
    return jnp.sum(part, axis=0, keepdims=True)


def band(row):
    return slice(row * 32, row * 32 + 32)


def put_band(x_ref, image, row, value):
    zero = jnp.zeros_like(value)
    x_ref[image, band(row), 512:1024] = value
    if row < 3:
        x_ref[image, band(row + 1), 0:512] = value
    else:
        x_ref[image, band(0), 0:512] = zero
    if row > 0:
        x_ref[image, band(row - 1), 1024:1536] = value
    else:
        x_ref[image, band(3), 1024:1536] = zero


def columns_joined(left, middle, right):
    count = middle.shape[0]
    column = lax.broadcasted_iota(jnp.int32, (count, 1), 0) % 32
    joined = middle
    if left is not None:
        joined = joined + jnp.where(column == 0, 0.0, pltpu.roll(left, 1, 0))
    if right is not None:
        joined = joined + jnp.where(column == 31, 0.0, pltpu.roll(right, count - 1, 0))
    return joined


def conv_core(x_ref, w_ref, out_ref, back):
    def tap(col):
        value = None
        for row in range(3):
            lhs = x_ref[:, :, row * 512 : (row + 1) * 512].reshape(1024, 512)
            if back:
                term = lax.dot_general(
                    lhs, w_ref[2 - row, 2 - col], NT, preferred_element_type=F32
                )
            else:
                term = jnp.dot(lhs, w_ref[row, col], preferred_element_type=F32)
            value = term if value is None else value + term
        return value

    out_ref[...] = columns_joined(tap(0), tap(1), tap(2)).reshape(8, 128, 512)


def stats_of(facts_ref, out_ref, stat_ref, row):
    def add(image, part):
        for r in range(4):
            part = part + fold(out_ref[image, band(r), :]) * facts_ref[image]
        return part

    first = total_row(lax.fori_loop(0, 8, add, jnp.zeros((8, 512), F32), unroll=2))
    mean = first / jnp.maximum(facts_ref[OWN_PX], 1.0)

    def deviate(image, part):
        for r in range(4):
            away = out_ref[image, band(r), :] - mean
            part = part + fold(away * away) * facts_ref[image]
        return part

    second = total_row(lax.fori_loop(0, 8, deviate, jnp.zeros((8, 512), F32), unroll=2))
    stat_ref[row : row + 1, :] = first
    stat_ref[row + 1 : row + 2, :] = second


def norm_of(facts_ref, own_ref, other_ref, row):
    own_px, other_px, all_px = facts_ref[OWN_PX], facts_ref[OTHER_PX], facts_ref[ALL_PX]
    own, other = own_ref[row : row + 1, :], other_ref[row : row + 1, :]
    mean = (own + other) / all_px
    apart = own / jnp.maximum(own_px, 1.0) - other / jnp.maximum(other_px, 1.0)
    spread = own_ref[row + 1 : row + 2, :] + other_ref[row + 1 : row + 2, :]
    variance = (spread + apart * apart * (own_px * other_px / all_px)) / all_px
    return mean, lax.rsqrt(variance + EPSILON)


def sigmoid(values):
    return 0.5 * jnp.tanh(0.5 * values) + 0.5


def slope_of(values):
    gate = sigmoid(values)
    return gate * (1.0 + values * (1.0 - gate))


MARKS = 128


def pieces_kernel(where_ref, images_hbm, labels_ref, count_ref, o0, o1, o2, o3, wide,
                  images_ref, sems):
    pipe, zone = where_ref[0], where_ref[2]
    tasks = labels_ref.shape[1]
    copies = []
    for rel in range(4):
        first = (zone ^ rel) * 4 + pipe * 2
        copies.append(
            pltpu.make_async_copy(
                images_hbm.at[pl.ds(first, 2)], images_ref.at[rel], sems.at[rel]
            )
        )
        copies[-1].start()
    o0[MARKS:, :] = jnp.zeros((16, 512), BF16)
    count = count_ref[0, zone].astype(F32)
    marks = jnp.concatenate(
        [
            labels_ref[pl.ds(zone * 4, 4), :].astype(F32),
            jnp.full((4, tasks), count),
            jnp.zeros((8, tasks), F32),
        ]
    )
    o0[MARKS:, 0:tasks] = marks.astype(BF16)
    for rel, out in enumerate((o0, o1, o2, o3)):
        copies[rel].wait()
        for i in range(2):
            for row in range(2):
                lines = slice((i * 2 + row) * 32, (i * 2 + row) * 32 + 32)
                for part in range(2):
                    lanes = slice(part * 128, part * 128 + 128)
                    wide[...] = images_ref[rel, i, row, :, lanes].astype(F32)
                    for par in range(2):
                        value = wide[pl.ds(par, 32, stride=2), :]
                        start = par * 256 + part * 128
                        out[lines, start : start + 128] = value.astype(BF16)


def down_kernel(facts_ref, where_ref, *refs):
    pieces, (w_ref, s_ref, img_ref, out_ref, short_ref, stat_ref, x_ref) = refs[:12], refs[12:]
    batch, zone = where_ref[1], where_ref[2]
    for kb in range(4):
        for kz in range(4):
            piece, base = pieces[kb * 3 + min(kz, 2)], (128 if kz == 3 else 0)
            row = zone ^ kz
            here = pl.ds(pl.multiple_of(row * 32, 32), 32)
            after = pl.ds(pl.multiple_of(((row + 1) % 4) * 32, 32), 32)
            for i in range(2):
                image = (batch ^ kb) * 2 + i
                start = base + i * 64
                odd = piece[start + 32 : start + 64, :]
                img_ref[image, here, 0:512] = piece[start : start + 32, :]
                img_ref[image, here, 512:1024] = odd
                x_ref[image, after, :] = jnp.where(row == 3, jnp.zeros_like(odd), odd)
    for part in range(2):
        images = slice(4 * part, 4 * part + 4)
        blocks = (
            x_ref[images].reshape(512, 512),
            img_ref[images, :, 0:512].reshape(512, 512),
            img_ref[images, :, 512:1024].reshape(512, 512),
        )
        left, middle = None, None
        for row in range(3):
            a = jnp.dot(blocks[row][:, 256:], w_ref[row, 0], preferred_element_type=F32)
            m = jnp.dot(
                blocks[row], w_ref[row, 1:3].reshape(512, 512), preferred_element_type=F32
            )
            left = a if left is None else left + a
            middle = m if middle is None else middle + m
        out_ref[images] = columns_joined(left, middle, None).reshape(4, 128, 512)
        short = jnp.dot(blocks[1][:, :256], s_ref[...], preferred_element_type=F32)
        short_ref[images] = short.reshape(4, 128, 512)
    stats_of(facts_ref, out_ref, stat_ref, 0)
    stats_of(facts_ref, short_ref, stat_ref, 2)
    stat_ref[4:8, :] = jnp.zeros((4, 512), F32)


def layer_kernel(g_row, b_row, facts_ref, in_ref, own_ref, other_ref, params_ref, w_ref,
                 act_ref, out_ref, stat_ref, norm_ref, x_ref):
    mean, inverse = norm_of(facts_ref, own_ref, other_ref, 0)
    gain, bias = param(params_ref, g_row), param(params_ref, b_row)

    def activate(image, carry):
        for r in range(4):
            pre = (in_ref[image, band(r), :] - mean) * inverse * gain + bias
            act = (pre * sigmoid(pre)).astype(BF16)
            act_ref[image, band(r), :] = act
            put_band(x_ref, image, r, act)
        return carry

    lax.fori_loop(0, 8, activate, 0, unroll=2)
    norm_ref[0:1, :] = mean
    norm_ref[1:2, :] = inverse
    norm_ref[2:8, :] = jnp.zeros((6, 512), F32)
    conv_core(x_ref, w_ref, out_ref, False)
    stats_of(facts_ref, out_ref, stat_ref, 0)
    stat_ref[2:8, :] = jnp.zeros((6, 512), F32)


def join_kernel(facts_ref, mid_ref, short_ref, own_m, other_m, own_d, other_d, params_ref,
                w_ref, act_ref, out_ref, stat_ref, norm_ref, x_ref):
    mean_m, inv_m = norm_of(facts_ref, own_m, other_m, 0)
    mean_s, inv_s = norm_of(facts_ref, own_d, other_d, 2)
    gain_m, gain_s = param(params_ref, G_MID), param(params_ref, G_SHORT)
    bias_m, bias_s = param(params_ref, B_MID), param(params_ref, B_SHORT)

    def activate(image, carry):
        for r in range(4):
            pre = (mid_ref[image, band(r), :] - mean_m) * inv_m * gain_m + bias_m
            pre = pre + (short_ref[image, band(r), :] - mean_s) * inv_s * gain_s + bias_s
            act = (pre * sigmoid(pre)).astype(BF16)
            act_ref[image, band(r), :] = act
            put_band(x_ref, image, r, act)
        return carry

    lax.fori_loop(0, 8, activate, 0, unroll=2)
    norm_ref[0:1, :] = mean_m
    norm_ref[1:2, :] = inv_m
    norm_ref[2:3, :] = mean_s
    norm_ref[3:4, :] = inv_s
    norm_ref[4:8, :] = jnp.zeros((4, 512), F32)
    conv_core(x_ref, w_ref, out_ref, False)
    stats_of(facts_ref, out_ref, stat_ref, 0)
    stat_ref[2:8, :] = jnp.zeros((6, 512), F32)


def block_kernel(facts_ref, in_ref, section_ref, own_ref, other_ref, params_ref,
                 pack_ref, norm_ref):
    mean, inverse = norm_of(facts_ref, own_ref, other_ref, 0)
    gain, bias = param(params_ref, G_SECOND), param(params_ref, B_SECOND)
    norm_ref[0:1, :] = mean
    norm_ref[1:2, :] = inverse
    norm_ref[2:8, :] = jnp.zeros((6, 512), F32)

    def gather(image, carry):
        pooled = jnp.zeros((8, 512), F32)
        slopes, crossed = pooled, pooled
        for r in range(4):
            normed = (in_ref[image, band(r), :] - mean) * inverse
            pre = normed * gain + bias + section_ref[image, band(r), :].astype(F32)
            gate = sigmoid(pre)
            slope = gate * (1.0 + pre * (1.0 - gate))
            pooled = pooled + fold(pre * gate)
            slopes = slopes + fold(slope)
            crossed = crossed + fold(slope * normed)
        pack_ref[pl.ds(image, 1), :] = total_row(pooled) / 128.0
        pack_ref[pl.ds(image + 8, 1), :] = total_row(slopes)
        pack_ref[pl.ds(image + 16, 1), :] = total_row(crossed)
        return carry

    lax.fori_loop(0, 8, gather, 0, unroll=2)


def logits_kernel(where_ref, own_ref, other_ref, living_ref, labels_ref, hw_ref, hb_ref,
                  all_ref, errors_ref, cross_ref):
    pipe = where_ref[0]
    for block in range(3):
        rows = slice(block * 8, block * 8 + 8)
        all_ref[block, pl.ds(pl.multiple_of(pipe * 8, 8), 8), :] = own_ref[rows, :]
        all_ref[block, pl.ds(pl.multiple_of((1 - pipe) * 8, 8), 8), :] = other_ref[rows, :]
    logits = (
        lax.dot_general(
            all_ref[0], hw_ref[...], NT, precision=HIGHEST, preferred_element_type=F32
        )
        + hb_ref[...]
    )
    errors = living_ref[...] * (sigmoid(logits) - labels_ref[...])
    errors_ref[...] = errors
    cross_ref[...] = lax.dot_general(
        errors, errors, TN, precision=HIGHEST, preferred_element_type=F32
    )


def head_kernel(picks_ref, where_ref, facts_ref, c0, c1, c2, c3, heads_ref, hw_ref, errors_ref,
                all_ref, in_ref, section_ref, norm_ref, params_ref,
                low_ref, pool_ref, small_ref, alpha_ref, gram_ref):
    tasks = gram_ref.shape[0]
    pipe = where_ref[0]
    gram_ref[...] = ((c0[...] + c1[...]) + (c2[...] + c3[...])) * heads_ref[...]
    frank_wolfe_kernel(picks_ref, gram_ref, alpha_ref)
    grad_logits = (128.0 * tasks) * alpha_ref[...] * errors_ref[...]
    pooled, slopes, crossed = all_ref[0], all_ref[1], all_ref[2]
    grad_pool = (
        jnp.dot(grad_logits, hw_ref[...], precision=HIGHEST, preferred_element_type=F32)
        / 128.0
    )
    grad_sum = total_row(grad_pool * slopes)
    cross_sum = total_row(grad_pool * crossed)
    small_ref[0:tasks, :] = lax.dot_general(
        grad_logits, pooled, TN, precision=HIGHEST, preferred_element_type=F32
    )
    small_ref[tasks : tasks + 1, :] = grad_sum
    small_ref[tasks + 1 : tasks + 2, :] = cross_sum
    small_ref[tasks + 2 :, :] = jnp.zeros((small_ref.shape[0] - tasks - 2, 512), F32)
    for start in (0, 256):
        small_ref[tasks + 2 : tasks + 3, start : start + tasks] = total_row(grad_logits)
    pool_ref[...] = jnp.where(pipe == 0, grad_pool[0:8], grad_pool[8:16])

    mean, inverse = norm_ref[0:1, :], norm_ref[1:2, :]
    gain, bias = param(params_ref, G_SECOND), param(params_ref, B_SECOND)
    all_px = facts_ref[ALL_PX]
    front = gain * inverse
    mean_grad, mean_cross = grad_sum / all_px, cross_sum / all_px

    def back(image, carry):
        up = pool_ref[pl.ds(image, 1), :]
        for r in range(4):
            normed = (in_ref[image, band(r), :] - mean) * inverse
            pre = normed * gain + bias + section_ref[image, band(r), :].astype(F32)
            grad = up * slope_of(pre)
            fix = facts_ref[image] * (mean_grad + normed * mean_cross)
            low_ref[image, band(r), :] = (front * (grad - fix)).astype(BF16)
        return carry

    lax.fori_loop(0, 8, back, 0, unroll=2)


def back_norm(facts_ref, in_ref, up_ref, norm_ref, own_ref, other_ref, gain, rows, sinks):
    mean, inverse = norm_ref[rows : rows + 1, :], norm_ref[rows + 1 : rows + 2, :]
    all_px = facts_ref[ALL_PX]
    front = gain * inverse
    cross_row = 1 + rows // 2
    mean_grad = (own_ref[0:1, :] + other_ref[0:1, :]) / all_px
    mean_cross = (
        own_ref[cross_row : cross_row + 1, :] + other_ref[cross_row : cross_row + 1, :]
    ) / all_px

    def back(image, carry):
        for r in range(4):
            normed = (in_ref[image, band(r), :] - mean) * inverse
            fix = facts_ref[image] * (mean_grad + normed * mean_cross)
            sinks(image, r, (front * (up_ref[image, band(r), :] - fix)).astype(BF16))
        return carry

    lax.fori_loop(0, 8, back, 0, unroll=2)


def second_back_kernel(facts_ref, low_ref, in_ref, norm_ref, params_ref, w_ref,
                       up_ref, sum_ref, x_ref, conv_ref):
    def fill(image, carry):
        for r in range(4):
            put_band(x_ref, image, r, low_ref[image, band(r), :])
        return carry

    lax.fori_loop(0, 8, fill, 0, unroll=2)
    conv_core(x_ref, w_ref, conv_ref, True)
    gain, bias = param(params_ref, G_FIRST), param(params_ref, B_FIRST)
    slope_sums(facts_ref, in_ref, norm_ref, gain, bias, conv_ref, up_ref, sum_ref)


def slope_sums(facts_ref, in_ref, norm_ref, gain, bias, conv_ref, up_ref, sum_ref):
    mean, inverse = norm_ref[0:1, :], norm_ref[1:2, :]

    def slope(image, carry):
        grads, crosses = carry
        for r in range(4):
            normed = (in_ref[image, band(r), :] - mean) * inverse
            up = conv_ref[image, band(r), :] * slope_of(normed * gain + bias)
            up_ref[image, band(r), :] = up
            living = facts_ref[image]
            grads = grads + fold(up) * living
            crosses = crosses + fold(up * normed) * living
        return grads, crosses

    zero = jnp.zeros((8, 512), F32)
    grads, crosses = lax.fori_loop(0, 8, slope, (zero, zero), unroll=2)
    sum_ref[0:1, :] = total_row(grads)
    sum_ref[1:2, :] = total_row(crosses)
    sum_ref[2:8, :] = jnp.zeros((6, 512), F32)


def first_back_kernel(facts_ref, up_in, in_ref, norm_ref, own_ref, other_ref, params_ref, w_ref,
                      second_ref, norm2_ref, section_ref, pool_ref, mid_ref, short_ref, normd_ref,
                      low_ref, up_ref, sum_ref, x_ref, conv_ref):
    def keep(image, r, low):
        low_ref[image, band(r), :] = low
        put_band(x_ref, image, r, low)

    back_norm(facts_ref, in_ref, up_in, norm_ref, own_ref, other_ref, param(params_ref, G_FIRST),
              0, keep)
    conv_core(x_ref, w_ref, conv_ref, True)
    mean2, inv2 = norm2_ref[0:1, :], norm2_ref[1:2, :]
    gain2, bias2 = param(params_ref, G_SECOND), param(params_ref, B_SECOND)
    mean_m, inv_m = normd_ref[0:1, :], normd_ref[1:2, :]
    mean_s, inv_s = normd_ref[2:3, :], normd_ref[3:4, :]
    gain_m, gain_s = param(params_ref, G_MID), param(params_ref, G_SHORT)
    bias_m, bias_s = param(params_ref, B_MID), param(params_ref, B_SHORT)

    def join(image, carry):
        grads, cross_m, cross_s = carry
        pool = pool_ref[pl.ds(image, 1), :]
        for r in range(4):
            pre2 = (second_ref[image, band(r), :] - mean2) * inv2 * gain2 + bias2
            pre2 = pre2 + section_ref[image, band(r), :].astype(F32)
            entry = conv_ref[image, band(r), :] + pool * slope_of(pre2)
            entry = entry.astype(BF16).astype(F32)
            norm_m = (mid_ref[image, band(r), :] - mean_m) * inv_m
            norm_s = (short_ref[image, band(r), :] - mean_s) * inv_s
            pre = norm_m * gain_m + bias_m + norm_s * gain_s + bias_s
            up = entry * slope_of(pre)
            up_ref[image, band(r), :] = up
            living = facts_ref[image]
            grads = grads + fold(up) * living
            cross_m = cross_m + fold(up * norm_m) * living
            cross_s = cross_s + fold(up * norm_s) * living
        return grads, cross_m, cross_s

    zero = jnp.zeros((8, 512), F32)
    grads, cross_m, cross_s = lax.fori_loop(0, 8, join, (zero, zero, zero), unroll=2)
    sum_ref[0:1, :] = total_row(grads)
    sum_ref[1:2, :] = total_row(cross_m)
    sum_ref[2:3, :] = total_row(cross_s)
    sum_ref[3:8, :] = jnp.zeros((5, 512), F32)


def mid_back_kernel(facts_ref, up_in, mid_ref, short_ref, normd_ref, own_ref, other_ref, params_ref,
                    w_ref, in_ref, norm1_ref,
                    low_ref, low_s_ref, up_ref, sum_ref, x_ref, conv_ref):
    def keep(image, r, low):
        low_ref[image, band(r), :] = low
        put_band(x_ref, image, r, low)

    def keep_short(image, r, low):
        low_s_ref[image, band(r), :] = low

    gain_m, gain_s = param(params_ref, G_MID), param(params_ref, G_SHORT)
    back_norm(facts_ref, mid_ref, up_in, normd_ref, own_ref, other_ref, gain_m, 0, keep)
    back_norm(facts_ref, short_ref, up_in, normd_ref, own_ref, other_ref, gain_s, 2, keep_short)
    conv_core(x_ref, w_ref, conv_ref, True)
    gain, bias = param(params_ref, G_DOWN), param(params_ref, B_DOWN)
    slope_sums(facts_ref, in_ref, norm1_ref, gain, bias, conv_ref, up_ref, sum_ref)


def down_back_kernel(facts_ref, up_in, in_ref, norm1_ref, own_ref, other_ref, params_ref, low_ref):
    def keep(image, r, low):
        low_ref[image, band(r), :] = low

    gain = param(params_ref, G_DOWN)
    back_norm(facts_ref, in_ref, up_in, norm1_ref, own_ref, other_ref, gain, 0, keep)


def image_back_kernel(where_ref, low_ref, low_s_ref, w_ref, s_ref, keep_ref, send_ref, stage_ref):
    pipe, batch, zone = where_ref[0], where_ref[1], where_ref[2]
    mine = pl.ds(batch * 2, 2)
    here = low_ref[mine]
    below = jnp.concatenate([here[:, 32:], jnp.zeros((2, 32, 512), BF16)], axis=1)
    here, below = here.reshape(256, 512), below.reshape(256, 512)
    short = low_s_ref[mine].reshape(256, 512)

    def back(lhs, row, col):
        return lax.dot_general(lhs, w_ref[row, col], NT, preferred_element_type=F32)

    even_even = back(here, 1, 1) + lax.dot_general(
        short, s_ref[...], NT, preferred_element_type=F32
    )
    even_odd = columns_joined(None, back(here, 1, 2), back(here, 1, 0))
    odd_even = back(here, 2, 1) + back(below, 0, 1)
    odd_odd = columns_joined(
        None, back(here, 2, 2) + back(below, 0, 2), back(here, 2, 0) + back(below, 0, 0)
    )
    planes = ((even_even, even_odd), (odd_even, odd_odd))
    for row in range(2):
        for par in range(2):
            plane = planes[row][par].reshape(2, 4, 32, 256).astype(BF16)
            lanes = slice(par * 128, par * 128 + 128)
            for side in range(2):
                half = plane[..., side * 128 : side * 128 + 128]
                for z in range(4):
                    stage_ref[z ^ zone, side ^ pipe, :, row, :, lanes] = half[:, z]
    keep_ref[0], keep_ref[1] = stage_ref[0], stage_ref[2]
    send_ref[0], send_ref[1] = stage_ref[1], stage_ref[3]


def image_far_kernel(keep_ref, near_ref, out_ref):
    out_ref[0], out_ref[1] = keep_ref[1], near_ref[1]


def image_pipe_kernel(keep_ref, near_ref, far_ref, out_ref):
    out_ref[0], out_ref[1] = keep_ref[0, 1], near_ref[0, 1]
    out_ref[2], out_ref[3] = far_ref[0, 1], far_ref[1, 1]


def image_grad_kernel(where_ref, keep_ref, near_ref, far_ref, got_ref, out_ref):
    pipe, zone = where_ref[0], where_ref[2]
    own = (keep_ref.at[0, 0], near_ref.at[0, 0], far_ref.at[0, 0], far_ref.at[1, 0])
    for rel in range(4):
        for side in range(2):
            piece = own[rel] if side == 0 else got_ref.at[rel]
            first = (zone ^ rel) * 4 + (pipe if side == 0 else 1 - pipe) * 2
            for i in range(2):
                for row in range(2):
                    for par in range(2):
                        out_ref[first + i, row, pl.ds(par, 32, stride=2), :] = piece[
                            i, row, :, par * 128 : (par + 1) * 128
                        ].astype(F32)


def slot_of(quarter, zone):
    rel = quarter ^ zone
    return (rel >> 1) | ((rel & 1) << 1)


def shifted_window(turned, down, right):
    pixel = lax.broadcasted_iota(jnp.int32, (1, 128), 1)
    column, row = pixel % 32 + right, pixel // 32 + down
    inside = (column >= 0) & (column < 32) & (row >= 0) & (row < 4)
    amount = (256 - down * 32 - right) % 128
    moved = turned if isinstance(amount, int) and amount == 0 else pltpu.roll(turned, amount, 1)
    return jnp.where(inside, moved, 0.0).astype(BF16)


def split_out(pipe, zone, unit, result_own, result_other, own_ref, other_ref):
    for quarter in range(4):
        slot = slot_of(quarter, zone)
        rows = slice(quarter * 32, quarter * 32 + 32)
        own_ref[slot, unit] = result_own[rows]
        other_ref[slot, unit] = result_other[rows].astype(BF16)


def hand_out(other_ref, outs):
    each = 4 // len(outs)
    for slot in range(4):
        outs[slot // each][slot % each] = other_ref[slot]


def turned_taps(batch, act_ref, turned_ref):
    lanes = pl.ds(pl.multiple_of(batch * 128, 128), 128)

    def turn(image, carry):
        turned = act_ref[image, :, lanes].astype(F32).T
        pixels = pl.ds(pl.multiple_of(image * 128, 128), 128)
        for row in range(3):
            for col in range(3):
                turned_ref[row * 3 + col, :, pixels] = shifted_window(turned, row - 1, col - 1)
        return carry

    lax.fori_loop(0, 8, turn, 0, unroll=2)


def tap_products(pipe, zone, low_ref, turned_ref, own_ref, other_ref):
    lhs = turned_ref[0:9].reshape(9 * 128, 1024)
    results = []
    for side in (pipe, 1 - pipe):
        columns = pl.ds(pl.multiple_of(side * 256, 256), 256)
        rhs = low_ref[:, :, columns].reshape(1024, 256)
        results.append(jnp.dot(lhs, rhs, preferred_element_type=F32))
    for unit in range(9):
        rows = slice(unit * 128, unit * 128 + 128)
        split_out(pipe, zone, unit, results[0][rows], results[1][rows], own_ref, other_ref)


def kernel_grad_kernel(where_ref, act_ref, low_ref, own_ref, *refs):
    outs, (turned_ref, other_ref) = refs[:-2], refs[-2:]
    pipe, batch, zone = where_ref[0], where_ref[1], where_ref[2]
    turned_taps(batch, act_ref, turned_ref)
    tap_products(pipe, zone, low_ref, turned_ref, own_ref, other_ref)
    hand_out(other_ref, outs)


DOWN_UNITS = (
    ((0, 0, 0, 4), (2, -1, 0, 1), (2, 0, 0, 7), (0, 0, 0, 9), (1, 0, 0, 5)),
    ((1, 0, -1, 3), (3, -1, -1, 0), (3, -1, 0, 2), (3, 0, -1, 6), (3, 0, 0, 8)),
)


def down_grad_kernel(where_ref, img_ref, low_ref, low_s_ref, own_ref, *refs):
    outs, (turned_ref, other_ref) = refs[:-2], refs[-2:]
    pipe, batch, zone = where_ref[0], where_ref[1], where_ref[2]
    upper, part = batch // 2, batch % 2

    for turn_kind in range(2):

        @pl.when(upper == turn_kind)
        def _(units=DOWN_UNITS[turn_kind]):
            def turn(image, carry):
                pixels = pl.ds(pl.multiple_of(image * 128, 128), 128)
                seen = {}
                for unit, (plane, down, right, _) in enumerate(units):
                    if plane not in seen:
                        lanes = pl.ds(pl.multiple_of(plane * 256 + part * 128, 128), 128)
                        seen[plane] = img_ref[image, :, lanes].astype(F32).T
                    turned_ref[unit, :, pixels] = shifted_window(seen[plane], down, right)
                return carry

            lax.fori_loop(0, 8, turn, 0, unroll=2)

    short_unit = [tap for _, _, _, tap in DOWN_UNITS[0]].index(9)
    for unit in range(5):
        lhs = turned_ref[unit]
        results = []
        for side in (pipe, 1 - pipe):
            columns = pl.ds(pl.multiple_of(side * 256, 256), 256)
            rhs = low_ref[:, :, columns].reshape(1024, 256)
            if unit == short_unit:
                rhs_s = low_s_ref[:, :, columns].reshape(1024, 256)
                rhs = jnp.where(upper == 0, rhs_s, rhs)
            results.append(jnp.dot(lhs, rhs, preferred_element_type=F32))
        split_out(pipe, zone, unit, results[0], results[1], own_ref, other_ref)
    hand_out(other_ref, outs)


def add_cores_kernel(own_ref, *refs):
    got, (keep_ref, send_ref) = refs[:-2], refs[-2:]
    each = 4 // len(got)
    for slot in range(4):
        value = own_ref[slot] + got[slot // each][slot % each].astype(F32)
        if slot < 2:
            keep_ref[slot] = value
        else:
            send_ref[slot - 2] = value.astype(BF16)


def add_near_kernel(own_ref, got_ref, keep_ref, send_ref):
    keep_ref[...] = own_ref[0] + got_ref[0].astype(F32)
    send_ref[...] = (own_ref[1] + got_ref[1].astype(F32)).astype(BF16)


def add_far_kernel(own_ref, got_ref, out_ref):
    out_ref[...] = (own_ref[...] + got_ref[...].astype(F32)).astype(BF16)


def join_kernel_of(*refs):
    at = 0
    for ref in refs[:-1]:
        if len(ref.shape) == 3:
            refs[-1][at] = ref[...]
            at += 1
        else:
            refs[-1][at : at + ref.shape[0]] = ref[...]
            at += ref.shape[0]


def gathered_blocks(zone, batch, refs):
    if len(refs) == 8:
        for kb in range(4):
            for rel in range(4):
                yield batch ^ kb, zone ^ rel, refs[2 * kb + rel % 2], rel // 2
        return
    a, b, ax, by, ayy, bxx = refs
    sets = {0: (a, b, 0, 0), 1: (ax, bxx, 0, 0), 2: (ayy, by, 0, 0), 3: (ayy, bxx, 2, 2)}
    for kb in range(4):
        even, odd, base_even, base_odd = sets[kb]
        for rel in range(4):
            if rel % 2 == 1:
                yield batch ^ kb, zone ^ rel, odd, base_odd + rel // 2
            else:
                yield batch ^ kb, zone ^ rel, even, base_even + rel // 2


def assemble_kernel(where_ref, *refs):
    pieces, (out_ref, token_ref, stage_ref, sems) = refs[:-4], refs[-4:]
    token_ref[...] = jnp.zeros(token_ref.shape, F32)
    batch, zone = where_ref[1], where_ref[2]
    blocks = list(gathered_blocks(zone, batch, pieces))
    copies = []
    for tap in range(9):
        for owner, quarter, ref, index in blocks:
            rows = pl.ds(pl.multiple_of(owner * 128 + quarter * 32, 32), 32)
            stage_ref[tap, rows, :] = ref[index, tap].astype(F32)
        copies.append(pltpu.make_async_copy(stage_ref.at[tap], out_ref.at[tap], sems.at[tap]))
        copies[-1].start()
    for copy in copies:
        copy.wait()


def assemble_down_kernel(where_ref, *refs):
    pieces, (out_hbm, short_hbm, out_ref, short_ref, sems) = refs[:-5], refs[-5:]
    batch, zone = where_ref[1], where_ref[2]
    for owner, quarter, ref, index in gathered_blocks(zone, batch, pieces):
        upper, part = owner // 2, owner % 2
        rows = pl.ds(pl.multiple_of(part * 128 + quarter * 32, 32), 32)
        value = ref[index].astype(F32)
        for kind in range(2):

            @pl.when(upper == kind)
            def _(value=value, rows=rows, units=DOWN_UNITS[kind]):
                for unit, (_, _, _, tap) in enumerate(units):
                    if tap == 9:
                        short_ref[rows, :] = value[unit]
                    else:
                        out_ref[tap, rows, :] = value[unit]

    copies = [
        pltpu.make_async_copy(out_ref, out_hbm, sems.at[0]),
        pltpu.make_async_copy(short_ref, short_hbm, sems.at[1]),
    ]
    for copy in copies:
        copy.start()
    for copy in copies:
        copy.wait()


def facts_kernel(where_ref, p0, p1, p2, p3, hw_ref, facts_ref, living_ref, targets_ref, heads_ref):
    pipe, batch = where_ref[0], where_ref[1]
    tasks = hw_ref.shape[0]
    alive = [jnp.float32(0.0), jnp.float32(0.0)]
    for rel, piece in enumerate((p0, p1, p2, p3)):
        owner = batch ^ rel
        marks = piece[MARKS:, 0:tasks].astype(F32)
        count = jnp.max(marks[4:5, :])
        for slot in range(4):
            side, place = slot // 2, owner * 2 + slot % 2
            living = (count > slot + 0.5).astype(F32)
            alive[side] = alive[side] + living
            row = pl.ds(side * 8 + place, 1)
            living_ref[row, :] = jnp.full((1, tasks), living)
            targets_ref[row, :] = marks[slot : slot + 1, :]

            @pl.when(pipe == side)
            def _(place=place, living=living):
                facts_ref[place] = living

    own = jnp.where(pipe == 0, alive[0], alive[1])
    facts_ref[OWN_PX] = own * 128.0
    facts_ref[OTHER_PX] = (alive[0] + alive[1] - own) * 128.0
    facts_ref[ALL_PX] = (alive[0] + alive[1]) * 128.0
    for rest in range(ALL_PX + 1, 16):
        facts_ref[rest] = jnp.float32(0.0)
    heads_ref[...] = lax.dot_general(
        hw_ref[...], hw_ref[...], NT, precision=HIGHEST, preferred_element_type=F32
    )


SMALL_ROWS = 72


def small_kernel(where_ref, head_ref, all_ref, sum_f, other_f, sum_j, other_j, sum_d, other_d,
                 sent_ref, wide_ref):
    pipe, batch = where_ref[0], where_ref[1]
    tasks = head_ref.shape[0] - 8
    wide_ref[...] = jnp.zeros(wide_ref.shape, F32)
    wide_ref[0 : tasks + 3, :] = head_ref[0 : tasks + 3, :]
    at = tasks + 3
    for own, other, count in ((sum_f, other_f, 2), (sum_j, other_j, 3), (sum_d, other_d, 2)):
        wide_ref[at : at + count, :] = own[0:count, :] + other[0:count, :]
        at += count
    for side in range(2):
        for slot in range(2):
            row = side * 8 + batch * 2 + slot
            at_row = SMALL_ROWS - 16 + where_ref[2] * 4 + side * 2 + slot
            wide_ref[pl.ds(at_row, 1), :] = all_ref[0, pl.ds(row, 1), :]
    sent_ref[...] = wide_ref[:, pl.ds(pl.multiple_of(pipe * 256, 256), 256)]


def add_kernel(a_ref, b_ref, out_ref):
    out_ref[...] = a_ref[...] + b_ref[...]


def small_out_kernel(where_ref, near_ref, far_ref, pooled_ref, head_ref, gd_ref, bd_ref, gp_ref,
                     bp_ref, headb_ref):
    tasks = head_ref.shape[0]
    pipe = where_ref[0]
    total = near_ref[...] + far_ref[...]
    pooled_ref[...] = total[SMALL_ROWS - 16 :]
    head_ref[...] = total[0:tasks]

    def line(at):
        return total[tasks + at : tasks + at + 1]

    share = tasks // 2
    headb_ref[...] = jnp.where(pipe == 0, line(2)[:, 0:share], line(2)[:, share:tasks])
    bp_ref[0:1, :], gp_ref[0:1, :] = line(3), line(4)
    bp_ref[1:2, :], gp_ref[1:2, :] = line(0), line(1)
    bd_ref[0:1, :], gd_ref[0:1, :] = line(8), line(9)
    bd_ref[1:2, :], gd_ref[1:2, :] = line(5), line(6)
    bd_ref[2:3, :], gd_ref[2:3, :] = line(5), line(7)


def fast_device(images, image_counts, labels, fw_picks, conv_down, conv_mid, shortcut, gains_down,
                biases_down, conv_first, conv_second, gains_plain, biases_plain, head_weight,
                head_bias):
    pipe, batch, zone = (lax.axis_index(axis) for axis in ("pipe", "batch", "space"))
    tasks = head_weight.shape[1]

    def over(axis, rel, x):
        size = lax.axis_size(axis)
        return lax.ppermute(x, axis, [(i, i ^ rel) for i in range(size)])

    where = jnp.stack([pipe, batch, zone, zone]).astype(jnp.int32)
    params = jnp.concatenate([gains_down, biases_down, gains_plain, biases_plain])
    turned_heads = head_weight.T
    bias_row = head_bias.reshape(1, tasks)

    pieces = call(
        pieces_kernel,
        [((144, 512), BF16)] + [((128, 512), BF16)] * 3,
        [where, images, labels, image_counts],
        [pltpu.VMEM((64, 128), F32), pltpu.VMEM((4, 2, 2, 64, 256), BF16),
         pltpu.SemaphoreType.DMA((4,))],
        name="pieces",
        specs={1: HBM, 3: SM},
    )
    moved = [over("space", rel, pieces[rel]) for rel in (1, 2, 3)]
    moved = [pieces[0], moved[0], jnp.concatenate([moved[1], moved[2]])]
    gathered = [moved] + [[over("batch", kb, x) for x in moved] for kb in (1, 2, 3)]
    facts, living, targets, heads = call(
        facts_kernel,
        [((16,), F32), ((16, tasks), F32), ((16, tasks), F32), ((tasks, tasks), F32)],
        [where] + [line[0] for line in gathered] + [turned_heads],
        name="facts",
    )

    big = ((8, 128, 512), F32)
    low = ((8, 128, 512), BF16)
    rows = ((8, 512), F32)
    x_scratch = pltpu.VMEM((8, 128, 1536), BF16)
    conv_scratch = pltpu.VMEM((8, 128, 512), F32)
    conv_flops = 2 * 1024 * 4608 * 512

    def partner(x):
        return over("pipe", 1, x)

    img, down_out, short_out, stat_d = call(
        down_kernel,
        [((8, 128, 1024), BF16), big, big, rows],
        [facts, where] + [piece for line in gathered for piece in line] + [conv_down, shortcut],
        [pltpu.VMEM((8, 128, 512), BF16)],
        conv_flops // 2,
        "down",
    )
    other_d = partner(stat_d)
    down_act, mid_out, stat_m, norm_d = call(
        lambda *refs: layer_kernel(G_DOWN, B_DOWN, *refs),
        [low, big, rows, rows],
        [facts, down_out, stat_d, other_d, params, conv_mid],
        [x_scratch],
        conv_flops,
        "mid",
    )
    other_m = partner(stat_m)
    section, first_out, stat_f, norm_j = call(
        join_kernel,
        [low, big, rows, rows],
        [facts, mid_out, short_out, stat_m, other_m, stat_d, other_d, params, conv_first],
        [x_scratch],
        conv_flops,
        "first",
    )
    other_f = partner(stat_f)
    plain_act, second_out, stat_s, norm_f = call(
        lambda *refs: layer_kernel(G_FIRST, B_FIRST, *refs),
        [low, big, rows, rows],
        [facts, first_out, stat_f, other_f, params, conv_second],
        [x_scratch],
        conv_flops,
        "second",
    )
    other_s = partner(stat_s)
    pack, norm_s = call(
        block_kernel,
        [((24, 512), F32), rows],
        [facts, second_out, section, stat_s, other_s, params],
        name="block",
    )
    other_pack = partner(pack)
    all_pack, errors, cross = call(
        logits_kernel,
        [((3, 16, 512), F32), ((16, tasks), F32), ((tasks, tasks), F32)],
        [where, pack, other_pack, living, targets, turned_heads, bias_row],
        name="logits",
    )
    crosses = [cross] + [over("space", rel, cross) for rel in (1, 2, 3)]
    second_low, grad_pool, small = call(
        head_kernel,
        [low, rows, ((tasks + 8, 512), F32)],
        [fw_picks, where, facts] + crosses
        + [heads, turned_heads, errors, all_pack, second_out, section, norm_s, params],
        [pltpu.VMEM((1, tasks), F32), pltpu.VMEM((tasks, tasks), F32)],
        name="head",
    )

    class Sum:
        def __init__(self, kernel, units, operands, scratch, flops, name, after=(), parts=4):
            self.units, self.name = units, name
            self.own, *self.other = call(
                kernel,
                [self.block(4, dtype=F32)] + [self.block(4 // parts)] * parts,
                operands,
                [scratch, pltpu.VMEM((4, units, 32, 256), BF16)],
                flops,
                name,
                after,
            )
            self.got = [partner(x) for x in self.other]

        def block(self, *lead, dtype=BF16):
            return (lead + (self.units, 32, 256), dtype)

        def cores(self, after=()):
            self.keep, sent = call(
                add_cores_kernel,
                [self.block(2, dtype=F32), self.block(2)],
                [self.own] + self.got,
                name=self.name + "_cores",
                after=after,
            )
            self.near = over("space", 1, sent)

        def zone_near(self, after=()):
            self.keep, sent = call(
                add_near_kernel,
                [self.block(dtype=F32), self.block()],
                [self.keep, self.near],
                name=self.name + "_near",
                after=after,
            )
            self.far = over("space", 2, sent)

        def zone_far(self, after=()):
            (self.final,) = call(
                add_far_kernel,
                [self.block()],
                [self.keep, self.far],
                name=self.name + "_final",
                after=after,
            )
            self.other_far = over("space", 2, self.final)

        def pair(self, after=()):
            (self.a,) = call(
                join_kernel_of,
                [self.block(2)],
                [self.final, self.other_far],
                name=self.name + "_pair",
                after=after,
            )
            self.b = over("space", 1, self.a)

        def direct(self):
            self.ra = [over("batch", rel, self.a) for rel in (1, 2, 3)]
            self.rb = [over("batch", rel, self.b) for rel in (1, 2, 3)]
            self.blocks = [where, self.a, self.b]
            for x, y in zip(self.ra, self.rb):
                self.blocks += [x, y]

        def plane(self):
            self.ax, self.by = over("batch", 1, self.a), over("batch", 2, self.b)

        def plane_far(self, after=()):
            self.fa, self.fb = [
                call(join_kernel_of, [self.block(4)], pair, name=self.name + "_cross", after=after)[0]
                for pair in ([self.a, self.ax], [self.b, self.by])
            ]
            self.ayy, self.bxx = over("batch", 2, self.fa), over("batch", 1, self.fb)
            self.blocks = [where, self.a, self.b, self.ax, self.by, self.ayy, self.bxx]

    def kernel_grad_of(act, low_grad, name, after=(), parts=PARTS):
        return Sum(
            kernel_grad_kernel, 9, [where, act, low_grad], pltpu.VMEM((9, 128, 1024), BF16),
            conv_flops // 4, name, after, parts,
        )

    def assembled(blocks, name, after=()):
        out, token = call(
            assemble_kernel,
            [((9, 512, 256), F32), ((8, 128), F32)],
            blocks,
            [pltpu.VMEM((9, 512, 256), F32), pltpu.SemaphoreType.DMA((9,))],
            name=name,
            after=after,
            out_space=[HBM, VM],
        )
        return out.reshape(3, 3, 512, 256), token

    second = kernel_grad_of(plain_act, second_low, "second_grad")
    second.cores()
    up_f, sum_f = call(
        second_back_kernel,
        [big, rows],
        [facts, second_low, first_out, norm_f, params, conv_second],
        [x_scratch, conv_scratch],
        conv_flops,
        "second_back",
        after=[second.keep],
    )
    other_sf = partner(sum_f)
    second.zone_near(after=[sum_f])
    first_low, up_j, sum_j = call(
        first_back_kernel,
        [low, big, rows],
        [facts, up_f, first_out, norm_f, sum_f, other_sf, params, conv_first,
         second_out, norm_s, section, grad_pool, mid_out, short_out, norm_j],
        [x_scratch, conv_scratch],
        conv_flops,
        "first_back",
        after=[second.keep],
    )
    other_sj = partner(sum_j)
    second.zone_far(after=[sum_j])
    first = kernel_grad_of(section, first_low, "first_grad", after=[second.final])
    second.pair(after=first.other[0:1])
    second.plane()
    first.cores(after=[second.a])
    mid_low, short_low, up_d, sum_d = call(
        mid_back_kernel,
        [low, low, big, rows],
        [facts, up_j, mid_out, short_out, norm_j, sum_j, other_sj, params, conv_mid,
         down_out, norm_d],
        [x_scratch, conv_scratch],
        conv_flops,
        "mid_back",
        after=[first.keep],
    )
    other_sd = partner(sum_d)
    first.zone_near(after=[sum_d, second.b, second.ax])
    mid = kernel_grad_of(down_act, mid_low, "mid_grad", after=[first.keep])
    first.zone_far(after=mid.other[0:1])
    mid.cores(after=[first.final])
    second.plane_far(after=[mid.keep])
    (down_low,) = call(
        down_back_kernel,
        [low],
        [facts, up_d, down_out, norm_d, sum_d, other_sd, params],
        name="down_back",
        after=[second.fa, second.fb],
    )
    down = Sum(
        down_grad_kernel, 5, [where, img, down_low, short_low], pltpu.VMEM((5, 128, 1024), BF16),
        conv_flops // 8, "down_grad", parts=LAST_PARTS,
    )
    first.pair(after=down.other[0:1])
    first.plane()
    mid.zone_near(after=[first.a])
    down.cores(after=[mid.keep])
    img_pieces = call(
        image_back_kernel,
        [((2, 2, 2, 2, 32, 256), BF16)] * 2,
        [where, down_low, short_low, conv_down, shortcut],
        [pltpu.VMEM((4, 2, 2, 2, 32, 256), BF16)],
        conv_flops // 8,
        "image_back",
        after=[down.keep],
    )
    mid.zone_far(after=[img_pieces[0]])
    down.zone_near(after=[mid.final])
    second_out_grad, second_done = assembled(second.blocks, "second_out", after=[down.keep, first.b])
    first.plane_far(after=[second_done])
    mid.pair(after=[first.fa, first.fb])
    mid.plane()
    down.zone_far(after=[mid.a])
    down.pair()
    down.plane()
    first_out_grad, first_done = assembled(first.blocks, "first_out", after=[down.a])
    mid.plane_far(after=[first_done])
    down.plane_far(after=[mid.fa, mid.fb])
    mid_out_grad, mid_done = assembled(mid.blocks, "mid_out", after=[down.fa])

    img_near = over("space", 1, img_pieces[1])
    pair = ((2, 2, 2, 2, 32, 256), BF16)
    (img_sent,) = call(image_far_kernel, [pair], [img_pieces[0], img_near], name="image_far")
    img_far = over("space", 2, img_sent)
    img_parts = [img_pieces[0], img_near, img_far]
    (img_other,) = call(
        image_pipe_kernel, [((4, 2, 2, 32, 256), BF16)], img_parts, name="image_pipe"
    )
    (images_grad,) = call(
        image_grad_kernel,
        [((16, 2, 64, 128), F32)],
        [where] + img_parts + [partner(img_other)],
        name="image_grad",
    )

    (sent,) = call(
        small_kernel,
        [((SMALL_ROWS, 256), F32)],
        [where, small, all_pack, sum_f, other_sf, sum_j, other_sj, sum_d, other_sd],
        [pltpu.VMEM((SMALL_ROWS, 512), F32)],
        name="small",
        after=[down.final],
    )
    (near_sum,) = call(
        add_kernel,
        [((SMALL_ROWS, 256), F32)],
        [sent, over("space", 1, sent)],
        name="small_near",
    )
    pooled, head_out, gains_d, sums_d, gains_p, sums_p, head_b = call(
        small_out_kernel,
        [((16, 256), F32), ((tasks, 256), F32), ((3, 256), F32), ((3, 256), F32),
         ((2, 256), F32), ((2, 256), F32), ((1, tasks // 2), F32)],
        [where, near_sum, over("space", 2, near_sum)],
        name="small_out",
    )
    down_grad, short_grad = call(
        assemble_down_kernel,
        [((9, 256, 256), F32), ((256, 256), F32)],
        down.blocks,
        [pltpu.VMEM((9, 256, 256), F32), pltpu.VMEM((256, 256), F32),
         pltpu.SemaphoreType.DMA((2,))],
        out_space=[HBM, HBM],
        name="down_out",
    )
    return (
        pooled,
        images_grad,
        down_grad.reshape(3, 3, 256, 256),
        mid_out_grad,
        short_grad,
        gains_d,
        sums_d,
        first_out_grad,
        second_out_grad,
        gains_p,
        sums_p,
        head_out.T,
        head_b.reshape(tasks // 2),
    )


def per_device(
    images,
    image_counts,
    labels,
    fw_picks,
    conv_down,
    conv_mid,
    shortcut,
    gains_down,
    biases_down,
    conv_first,
    conv_second,
    gains_plain,
    biases_plain,
    head_weight,
    head_bias,
):
    layout = Layout(image_counts.shape[1])
    micros, zone = layout.micros, layout.zone
    sizes = (images.shape, conv_down.shape, lax.axis_size("pipe"), lax.axis_size("batch"))
    if layout.groups == 1 and sizes == ((16, 2, 64, 256), (3, 3, 256, 512), 2, 4):
        return fast_device(
            images, image_counts, labels, fw_picks, conv_down, conv_mid, shortcut, gains_down,
            biases_down, conv_first, conv_second, gains_plain, biases_plain, head_weight,
            head_bias,
        )
    batches, pipes = lax.axis_size("batch"), lax.axis_size("pipe")
    batch = lax.axis_index("batch")
    pipe = lax.axis_index("pipe")
    per_micro = images.shape[0] // micros
    count = per_micro * batches
    entering, channels = conv_down.shape[2], conv_mid.shape[3]
    tasks = head_weight.shape[1]
    half = channels // pipes
    own = pipe * half

    def own_out(kernel, axis):
        size = kernel.shape[axis] // pipes
        return lax.dynamic_slice_in_dim(kernel, pipe * size, size, axis)

    def whole(tensor, axis=3):
        return lax.all_gather(tensor, "pipe", axis=axis, tiled=True)

    def share(tensor):
        size = tensor.shape[3] // batches
        return lax.dynamic_slice_in_dim(tensor, batch * size, size, 3)

    mine = lax.all_to_all(
        images, "space", 0, 1, axis_index_groups=layout.inner, tiled=True
    )
    mine = lax.all_gather(mine, "batch", axis=0, tiled=True)
    counts = lax.all_gather(image_counts, "batch", axis=0, tiled=True)
    counts = lax.dynamic_slice_in_dim(counts, zone, 1, 1)[:, 0]
    marks = lax.dynamic_slice_in_dim(labels, zone * per_micro, per_micro, 0)
    targets = lax.all_gather(marks, "batch", axis=0, tiled=True).astype(F32)
    slots = jnp.arange(per_micro, dtype=jnp.int32)
    living = (slots[None, :] < counts[:, None]).astype(F32).reshape(count)
    weight = living[:, None, None, None]
    out_rows, out_cols = mine.shape[1] // 2, mine.shape[2] // 2
    image_pixels = out_rows * layout.groups * out_cols
    counted = jnp.sum(living) * image_pixels
    scale = float(image_pixels * tasks)

    gain_d, bias_d = own_out(gains_down, 1), own_out(biases_down, 1)
    gain_p, bias_p = own_out(gains_plain, 1), own_out(biases_plain, 1)

    above = layout.row_from(mine[:, -1:], 1)
    down_ext = jnp.pad(
        jnp.concatenate([above, mine], axis=1), ((0, 0), (0, 0), (1, 0), (0, 0))
    )
    down_out = conv_valid(down_ext, own_out(conv_down, 3), 2)
    down_norm, down_inv = norm_forward(layout, down_out, weight, counted)
    down_pre = down_norm * gain_d[0] + bias_d[0]
    mid_ext = layout.rims(whole(jax.nn.silu(down_pre).astype(BF16)))
    mid_out = conv_valid(mid_ext, own_out(conv_mid, 3), 1)
    short_in = mine[:, ::2, ::2]
    short_out = jnp.einsum(
        "nhwi,io->nhwo", short_in, own_out(shortcut, 1), preferred_element_type=F32
    )
    mid_norm, mid_inv = norm_forward(layout, mid_out, weight, counted)
    short_norm, short_inv = norm_forward(layout, short_out, weight, counted)
    section_pre = mid_norm * gain_d[1] + bias_d[1] + short_norm * gain_d[2] + bias_d[2]
    section = jax.nn.silu(section_pre).astype(BF16)
    first_ext = layout.rims(whole(section))
    first_out = conv_valid(first_ext, own_out(conv_first, 3), 1)
    first_norm, first_inv = norm_forward(layout, first_out, weight, counted)
    first_pre = first_norm * gain_p[0] + bias_p[0]
    second_ext = layout.rims(whole(jax.nn.silu(first_pre).astype(BF16)))
    second_out = conv_valid(second_ext, own_out(conv_second, 3), 1)
    second_norm, second_inv = norm_forward(layout, second_out, weight, counted)
    block_pre = second_norm * gain_p[1] + bias_p[1] + section.astype(F32)
    pooled = layout.group_sum(jnp.sum(jax.nn.silu(block_pre), axis=(1, 2))) / image_pixels

    pooled_all = whole(pooled, 1)
    logits = jnp.dot(pooled_all, head_weight, precision=HIGHEST) + head_bias
    errors = living[:, None] * (jax.nn.sigmoid(logits) - targets)
    cross = jnp.einsum("nt,ns->ts", errors, errors, precision=HIGHEST)
    cross = lax.psum(cross, "space", axis_index_groups=layout.inner)
    gram = cross * jnp.dot(head_weight.T, head_weight, precision=HIGHEST)
    alpha = frank_wolfe(gram, fw_picks)
    grad_logits = scale * alpha * errors
    head_w = jnp.einsum("nc,nt->ct", pooled, grad_logits, precision=HIGHEST)
    head_b = jnp.sum(grad_logits, axis=0)
    head_own = own_out(head_weight, 0)
    grad_pool = jnp.einsum("nt,ct->nc", grad_logits, head_own, precision=HIGHEST) / image_pixels

    grad_block = grad_pool[:, None, None, :] * silu_slope(block_pre)
    second_low, second_cross, second_sum = norm_back(
        layout, grad_block, second_norm, second_inv, gain_p[1], weight, counted
    )
    second_kernel = kernel_grad(share(second_ext), second_low, 1)
    act_grad = conv_valid(layout.rims(whole(second_low)), flipped(own_out(conv_second, 2)), 1)
    first_low, first_cross, first_sum = norm_back(
        layout, act_grad * silu_slope(first_pre), first_norm, first_inv, gain_p[0], weight, counted
    )
    first_kernel = kernel_grad(share(first_ext), first_low, 1)
    entry_grad = conv_valid(layout.rims(whole(first_low)), flipped(own_out(conv_first, 2)), 1)
    entry_grad = (entry_grad + grad_block).astype(BF16).astype(F32)
    grad_section = entry_grad * silu_slope(section_pre)
    mid_low, mid_cross, mid_sum = norm_back(
        layout, grad_section, mid_norm, mid_inv, gain_d[1], weight, counted
    )
    short_low, short_cross, short_sum = norm_back(
        layout, grad_section, short_norm, short_inv, gain_d[2], weight, counted
    )
    mid_kernel = kernel_grad(share(mid_ext), mid_low, 1)
    short_kernel = jnp.einsum(
        "nhwi,nhwo->io", share(short_in), short_low, preferred_element_type=F32
    )
    act_grad = conv_valid(layout.rims(whole(mid_low)), flipped(own_out(conv_mid, 2)), 1)
    down_low, down_cross, down_sum = norm_back(
        layout, act_grad * silu_slope(down_pre), down_norm, down_inv, gain_d[0], weight, counted
    )
    down_kernel = kernel_grad(share(down_ext), down_low, 2)

    kept = lax.dynamic_slice_in_dim(whole(down_low), batch * per_micro, per_micro, 0)
    below = layout.row_from(kept[:, :1], -1)
    spread = lax.conv_general_dilated(
        jnp.concatenate([kept, below], axis=1),
        flipped(own_out(conv_down, 2)),
        (1, 1),
        ((2, 2), (2, 2)),
        lhs_dilation=(2, 2),
        dimension_numbers=NUMBERS,
        preferred_element_type=F32,
    )[:, 1 : 2 * out_rows + 1, 1:]
    short_kept = lax.dynamic_slice_in_dim(whole(short_low), batch * per_micro, per_micro, 0)
    spread = spread.at[:, ::2, ::2].add(
        jnp.einsum(
            "nhwo,io->nhwi", short_kept, own_out(shortcut, 0), preferred_element_type=F32
        )
    )
    images_grad = lax.all_to_all(
        spread.astype(BF16), "space", 1, 0, axis_index_groups=layout.inner, tiled=True
    ).astype(F32)

    def total(kernel, axis):
        summed = lax.psum(kernel.astype(BF16), "space")
        return lax.all_gather(summed, "batch", axis=axis, tiled=True).astype(F32)

    pooled_out = lax.dynamic_slice_in_dim(pooled, batch * per_micro, per_micro, 0)
    pooled_out = lax.all_gather(
        pooled_out, "space", axis_index_groups=layout.inner, axis=0, tiled=True
    )
    head_w, head_b = lax.psum((head_w, head_b), "space", axis_index_groups=layout.inner)
    gains_d, sums_d, gains_p, sums_p = lax.psum(
        (
            jnp.stack([down_cross, mid_cross, short_cross]),
            jnp.stack([down_sum, mid_sum, short_sum]),
            jnp.stack([first_cross, second_cross]),
            jnp.stack([first_sum, second_sum]),
        ),
        "space",
    )
    return (
        pooled_out,
        images_grad,
        total(down_kernel, 1).reshape(3, 3, entering, half),
        total(mid_kernel, 1).reshape(3, 3, channels, half),
        total(short_kernel, 0),
        gains_d,
        sums_d,
        total(first_kernel, 1).reshape(3, 3, channels, half),
        total(second_kernel, 1).reshape(3, 3, channels, half),
        gains_p,
        sums_p,
        head_w,
        own_out(head_b, 0),
    )


def solution(mesh):
    placed = (
        P("batch", "space", None, None),
        P("batch", None),
        P("batch", None),
    ) + (P(),) * 12
    return jax.shard_map(
        per_device,
        mesh=mesh,
        in_specs=placed,
        out_specs=(
            P("batch", "pipe"),
            P("batch", "space", None, "pipe"),
            P(None, None, None, "pipe"),
            P(None, None, None, "pipe"),
            P(None, "pipe"),
            P(None, "pipe"),
            P(None, "pipe"),
            P(None, None, None, "pipe"),
            P(None, None, None, "pipe"),
            P(None, "pipe"),
            P(None, "pipe"),
            P("pipe", None),
            P("pipe"),
        ),
        check_vma=False,
    )
```
